32 devices in a mesh: seq: 8 (over z, x), sub: 4 (over y, core).
Axes of the slice: x: 2, y: 2, z: 4, core: 2. Of those that a mesh axis runs over, the one named last changes fastest.
Arguments:
- first_half: float32 [1, 4096, 1024], P(None, ('seq', 'sub')), may hold values from -6 to 6
- second_half: float32 [1, 4096, 1024], P(None, ('seq', 'sub')), may hold values from -6 to 6
- grad_first: float32 [1, 4096, 1024], P(None, ('seq', 'sub')), may hold values from -6 to 6
- grad_second: float32 [1, 4096, 1024], P(None, ('seq', 'sub')), may hold values from -6 to 6
- attend_gain: bfloat16 [1, 1024], P(None, ('seq', 'sub')), may hold values from 0.5 to 1.5
- attend_shift: bfloat16 [1, 1024], P(None, ('seq', 'sub')), may hold values from -3 to 3
- query_key_weight: bfloat16 [1, 1024, 1024], P(None, ('seq', 'sub')), may hold values from -3 to 3
- value_projection_weight: bfloat16 [1, 1024, 1024], P(None, ('seq', 'sub')), may hold values from -0.1875 to 0.1875
- output_projection_weight: bfloat16 [1, 1024, 1024], P(None, ('seq', 'sub')), may hold values from -0.75 to 0.75
- feed_gain: bfloat16 [1, 1024], P(None, ('seq', 'sub')), may hold values from 0.5 to 1.5
- feed_shift: bfloat16 [1, 1024], P(None, ('seq', 'sub')), may hold values from -3 to 3
- upper_projection_weight: bfloat16 [1, 1024, 4096], P(None, ('seq', 'sub')), may hold values from -0.1875 to 0.1875
- upper_projection_bias: bfloat16 [1, 4096], P(None, ('seq', 'sub')), may hold values from -3 to 3
- lower_projection_weight: bfloat16 [1, 4096, 1024], P(None, ('seq', 'sub')), may hold values from -0.09375 to 0.09375
- lower_projection_bias: bfloat16 [1, 1024], P(None, ('seq', 'sub')), may hold values from -3 to 3
- sort_order: int32 [1, 4, 1, 4096], P(None, None, None, ('seq', 'sub')), may hold values from 0 to 4095, as said below
- sort_place: int32 [1, 4, 1, 4096], P(None, None, None, ('seq', 'sub')), may hold values from 0 to 4095, as said below
Outputs:
- first_out: float32 [1, 4096, 1024], P(None, ('seq', 'sub'))
- second_out: float32 [1, 4096, 1024], P(None, ('seq', 'sub'))
- first_grad: float32 [1, 4096, 1024], P(None, ('seq', 'sub'))
- second_grad: float32 [1, 4096, 1024], P(None, ('seq', 'sub'))
- attend_gain_grad: float32 [1, 1024], P(None, ('seq', 'sub'))
- attend_shift_grad: float32 [1, 1024], P(None, ('seq', 'sub'))
- shared_weight_grad: float32 [1, 1024, 1024], P(None, ('seq', 'sub'))
- value_weight_grad: float32 [1, 1024, 1024], P(None, ('seq', 'sub'))
- output_weight_grad: float32 [1, 1024, 1024], P(None, ('seq', 'sub'))
- feed_gain_grad: float32 [1, 1024], P(None, ('seq', 'sub'))
- feed_shift_grad: float32 [1, 1024], P(None, ('seq', 'sub'))
- up_weight_grad: float32 [1, 1024, 4096], P(None, ('seq', 'sub'))
- up_bias_grad: float32 [1, 4096], P(None, ('seq', 'sub'))
- down_weight_grad: float32 [1, 4096, 1024], P(None, ('seq', 'sub'))
- down_bias_grad: float32 [1, 1024], P(None, ('seq', 'sub'))
The draws below stay inside these ranges and needn't reach their ends.
Inputs may be any that keep to these rules, and one draw needn't show every extreme that they name: For every layer, round and sequence, sort_place is a permutation of the places and sort_order is its inverse. Of the 128 tokens of a sequence that one device holds, at most 8 take places that another single device holds, in every round; in every round some pairs of devices have exactly 8. `sort_order`: the inverse of sort_place.
All inputs are finite; a program needn't handle non-finite values.
Results may differ from the reference program's by a relative error of at most 0.015.
Values may be sent and summed in bfloat16 or wider, within the bound.
A program may use at most 128 MiB of HBM per device.

```python
import jax
import jax.numpy as jnp
import numpy as np
from jax import lax

D = 1024
HEADS = 8
HEAD_DIM = 128
FF = 4096
BLOCK = 64
ROUNDS = 4
LAYERS = 1
SEQS = 1
BLOCKS_DEV = 2
SEQ_LEN = 4096
CAP = 8
N_SEQ = 8
N_SUB = 4


def routing(key):
    row_count = BLOCK * BLOCKS_DEV
    devices = N_SEQ * N_SUB
    batch_size = LAYERS * ROUNDS * SEQS
    big_groups = row_count // (2 * CAP)
    half_groups = row_count // CAP
    groups = big_groups + half_groups
    member = jnp.asarray(np.repeat(np.arange(groups), [CAP] * big_groups + [CAP // 2] * half_groups), dtype=jnp.int32)
    key_shift, key_device, key_within, key_arrive = jax.random.split(key, 4)
    shifts = jax.vmap(lambda sub_key: jax.random.permutation(sub_key, devices)[:groups])(jax.random.split(key_shift, batch_size))
    device_order = jax.vmap(lambda sub_key: jax.random.permutation(sub_key, devices))(jax.random.split(key_device, batch_size))
    within = jax.vmap(lambda sub_key: jax.random.permutation(sub_key, row_count))(jax.random.split(key_within, batch_size * devices)).reshape(batch_size, devices, row_count)
    arrive = jax.vmap(lambda sub_key: jax.random.permutation(sub_key, row_count))(jax.random.split(key_arrive, batch_size * devices)).reshape(batch_size, devices, row_count)
    batch_index = jnp.arange(batch_size)[:, None, None]
    target = (device_order[:, :, None] + shifts[batch_index, member[within]]) % devices
    placed = target * row_count + arrive[batch_index, target, within]
    return placed.reshape(LAYERS, ROUNDS, SEQS, devices * row_count).astype(jnp.int32)


def draw_sort_place(key, part):
    return routing(key)


def draw_sort_order(key, part):
    return jnp.argsort(routing(key), axis=-1).astype(jnp.int32)


def strengthened(array, own_key, source, target, blocks, factor):
    def block_of(position):
        return (jnp.arange(array.shape[position]) // (array.shape[position] // blocks)).reshape((-1,) + (1,) * (array.ndim - 1 - position))

    first = jax.random.permutation(own_key, blocks)[block_of(target)]
    second = (block_of(target) + blocks // 2) % blocks
    return jnp.where((block_of(source) == first) | (block_of(source) == second), factor * array, array)


def block_scale(rng, shape, cuts, least, high):
    loudness, own = 1.0, jax.random.fold_in(rng, 6)
    for position, parts in cuts:
        draws = jnp.exp(jax.random.uniform(jax.random.fold_in(own, position), (parts,), jnp.float32, least / len(cuts), high / len(cuts)))
        loudness = loudness * jnp.repeat(draws, shape[position] // parts).reshape([-1 if axis == position else 1 for axis in range(len(shape))])
    return loudness


def bell_draw(own_key, dims, scale, most, cuts=(), kind=jnp.bfloat16):
    array = jax.random.normal(own_key, dims, jnp.float32) * scale
    if len(cuts) > 0:
        array = block_scale(own_key, dims, cuts, -0.22, 0.18) * array
    return jnp.clip(array, min=-most, max=most).astype(kind)


def bell_draw_with(own_key, dims, scale, bound, cuts, heavy, kind=jnp.bfloat16):
    values = scale * jax.random.normal(own_key, dims, jnp.float32)
    if cuts:
        values = values * block_scale(own_key, dims, cuts, -0.22, 0.18)
    return jnp.clip(strengthened(values, jax.random.fold_in(own_key, 3), *heavy), -bound, bound).astype(kind)


def setup_inputs(seed: int = 0) -> dict:
    keys = jax.random.split(jax.random.key(seed), 18)
    return {
        "first_half": bell_draw_with(keys[0], (SEQS, SEQ_LEN, D), 1.0, 6.0, ((1, 32),), (1, 2, 32, 2.75), jnp.float32),
        "second_half": bell_draw_with(keys[1], (SEQS, SEQ_LEN, D), 1.0, 6.0, ((1, 32),), (1, 2, 32, 2.75), jnp.float32),
        "grad_first": bell_draw(keys[2], (SEQS, SEQ_LEN, D), 1.0, 6.0, ((1, 32),), jnp.float32),
        "grad_second": bell_draw(keys[3], (SEQS, SEQ_LEN, D), 1.0, 6.0, ((1, 32),), jnp.float32),
        "attend_gain": jnp.clip(1.0 + 0.1 * jax.random.normal(keys[4], (LAYERS, D), jnp.float32), 0.5, 1.5).astype(jnp.bfloat16),
        "attend_shift": bell_draw(keys[5], (LAYERS, D), 0.5, 3.0, ((1, 32),)),
        "query_key_weight": bell_draw(keys[6], (LAYERS, D, D), (D // (2 * HEAD_DIM)) ** -0.5, 3.0, ((1, 32),)),
        "value_projection_weight": bell_draw(keys[7], (LAYERS, D, D), D ** -0.5, 0.1875, ((1, 32),)),
        "output_projection_weight": bell_draw(keys[8], (LAYERS, D, D), (D // 16) ** -0.5, 0.75, ((1, 32),)),
        "feed_gain": jnp.clip(1.0 + 0.1 * jax.random.normal(keys[9], (LAYERS, D), jnp.float32), 0.5, 1.5).astype(jnp.bfloat16),
        "feed_shift": bell_draw(keys[10], (LAYERS, D), 0.5, 3.0, ((1, 32),)),
        "upper_projection_weight": bell_draw(keys[11], (LAYERS, D, FF), D ** -0.5, 0.1875, ((1, 32),)),
        "upper_projection_bias": bell_draw(keys[12], (LAYERS, FF), 0.5, 3.0, ((1, 32),)),
        "lower_projection_weight": bell_draw(keys[13], (LAYERS, FF, D), FF ** -0.5, 0.09375, ((1, 32),)),
        "lower_projection_bias": bell_draw(keys[14], (LAYERS, D), 0.5, 3.0, ((1, 32),)),
        "sort_order": draw_sort_order(jax.random.fold_in(keys[17], 71), 0),
        "sort_place": draw_sort_place(jax.random.fold_in(keys[17], 71), 0),
    }


@jax.custom_vjp
def reduced_precision(v):
    return lax.optimization_barrier(v.astype(jnp.bfloat16)).astype(jnp.float32)

@jax.custom_vjp
def reduced_backward(v):
    return v

def low_keep(v):
    return (reduced_precision(v), None)

def low_pass(kept, grad):
    return (grad,)

def back_keep(v):
    return (v, None)

def back_low(kept, grad):
    return (reduced_precision(grad),)
reduced_precision.defvjp(low_keep, low_pass)
reduced_backward.defvjp(back_keep, back_low)

def layer_norm(value_vectors, scaling, shifts):
    center = lax.optimization_barrier(jnp.mean(value_vectors, axis=-1, keepdims=True))
    offset = value_vectors - center
    spread = lax.optimization_barrier(jnp.mean(offset * offset, axis=-1, keepdims=True))
    return offset * lax.rsqrt(spread + 1e-05) * scaling + shifts

def gelu_exact(value_vectors):
    return jax.nn.gelu(value_vectors, approximate=False)

def combine_rounds(outputs, totals):
    highest = lax.optimization_barrier(jnp.max(totals, axis=0, keepdims=True))
    weights = jnp.exp(totals - highest)
    weights = weights / lax.optimization_barrier(jnp.sum(weights, axis=0, keepdims=True))
    by_head = outputs.reshape(outputs.shape[:-1] + (totals.shape[-1], -1))
    return lax.optimization_barrier(jnp.sum(weights[..., None] * by_head, axis=0)).reshape(outputs.shape[1:])

def round_attention(shared_all, value_all, orders, places):
    length = orders.shape[0]
    blocks = length // BLOCK
    shared_sorted = reduced_backward(shared_all)[orders]
    value_sorted = reduced_backward(value_all)[orders]
    queries = shared_sorted.reshape(blocks, BLOCK, HEADS, HEAD_DIM)
    key_rows = jnp.concatenate([jnp.roll(queries, 1, axis=0), queries], axis=1)
    value_heads = value_sorted.reshape(blocks, BLOCK, HEADS, HEAD_DIM)
    value_keys = jnp.concatenate([jnp.roll(value_heads, 1, axis=0), value_heads], axis=1)
    query_pos = orders.reshape(blocks, BLOCK)
    key_pos = jnp.concatenate([jnp.roll(query_pos, 1, axis=0), query_pos], axis=1)
    key_scale = lax.rsqrt(lax.optimization_barrier(jnp.mean(key_rows * key_rows, axis=-1)) + 1e-06) / HEAD_DIM
    raw_scores = reduced_backward(jnp.einsum('cqhd,ckhd->chqk', queries, key_rows, precision=lax.Precision.HIGHEST))
    scores = raw_scores * jnp.transpose(key_scale, (0, 2, 1))[:, :, None, :]
    is_later = (key_pos[:, None, :] > query_pos[:, :, None])[:, None]
    is_self = (key_pos[:, None, :] == query_pos[:, :, None])[:, None]
    scores = jnp.where(is_later, -1000000000.0, jnp.where(is_self, -100000.0, scores))
    highest = lax.optimization_barrier(jnp.max(scores, axis=-1, keepdims=True))
    log_total = highest + jnp.log(lax.optimization_barrier(jnp.sum(jnp.exp(scores - highest), axis=-1, keepdims=True)))
    probability = reduced_precision(jnp.exp(scores - log_total))
    mixed = jnp.einsum('chqk,ckhd->cqhd', probability, value_keys, precision=lax.Precision.HIGHEST)
    mixed = mixed.reshape(length, HEADS * HEAD_DIM)
    log_total = jnp.transpose(log_total[..., 0], (0, 2, 1)).reshape(length, HEADS)
    return (reduced_backward(mixed[places]), reduced_backward(log_total[places]))

def sequence_attention(packed):
    shared_seq, value_seq, orders, places = packed
    outputs = []
    totals = []
    for round_index in range(ROUNDS):
        mixed, log_total = round_attention(shared_seq, value_seq, orders[round_index], places[round_index])
        outputs.append(mixed)
        totals.append(log_total)
    return combine_rounds(jnp.stack(outputs), jnp.stack(totals))

def layer(first_stream_state, second_stream_state, weights, orders, places):
    attend_gain, attend_shift, query_key_weight, value_projection_weight, output_projection_weight, feed_gain, feed_shift, upper_projection_weight, upper_projection_bias, lower_projection_weight, lower_projection_bias = weights
    normalized_input = reduced_precision(layer_norm(second_stream_state, attend_gain, attend_shift))
    shared_query_key = reduced_backward(reduced_precision(jnp.einsum('ikw,wt->ikt', normalized_input, query_key_weight, precision=lax.Precision.HIGHEST)))
    value_vectors = reduced_backward(reduced_precision(jnp.einsum('ikw,wt->ikt', normalized_input, value_projection_weight, precision=lax.Precision.HIGHEST)))
    attention_result = lax.map(jax.checkpoint(sequence_attention), (shared_query_key, value_vectors, jnp.transpose(orders, (1, 0, 2)), jnp.transpose(places, (1, 0, 2))))
    first_stream_state = first_stream_state + reduced_backward(jnp.einsum('ikw,wt->ikt', reduced_precision(attention_result), output_projection_weight, precision=lax.Precision.HIGHEST))
    feed_forward_input = reduced_precision(layer_norm(first_stream_state, feed_gain, feed_shift))
    prior_state = reduced_backward(jnp.einsum('jcp,px->jcx', feed_forward_input, upper_projection_weight, precision=lax.Precision.HIGHEST) + upper_projection_bias)
    hidden_activation = reduced_precision(gelu_exact(prior_state))
    second_stream_state = second_stream_state + reduced_backward(jnp.einsum('bxo,ot->bxt', hidden_activation, lower_projection_weight, precision=lax.Precision.HIGHEST) + lower_projection_bias)
    return (first_stream_state, second_stream_state)

def reference(first_half, second_half, grad_first, grad_second, attend_gain, attend_shift, query_key_weight, value_projection_weight, output_projection_weight, feed_gain, feed_shift, upper_projection_weight, upper_projection_bias, lower_projection_weight, lower_projection_bias, sort_order, sort_place):
    weights = tuple((weight_arg.astype(jnp.float32) for weight_arg in (attend_gain, attend_shift, query_key_weight, value_projection_weight, output_projection_weight, feed_gain, feed_shift, upper_projection_weight, upper_projection_bias, lower_projection_weight, lower_projection_bias)))

    def forward(first_stream_state, second_stream_state, *stack):
        for layer_index in range(LAYERS):
            first_stream_state, second_stream_state = layer(first_stream_state, second_stream_state, tuple((piece_all[layer_index] for piece_all in stack)), sort_order[layer_index], sort_place[layer_index])
        return (first_stream_state, second_stream_state)
    outputs, pullback = jax.vjp(forward, first_half, second_half, *weights)
    gradients = pullback((grad_first, grad_second))
    return (outputs[0], outputs[1], gradients[0], gradients[1], gradients[2], gradients[3], gradients[4], gradients[5], gradients[6], gradients[7], gradients[8], gradients[9], gradients[10], gradients[11], gradients[12])
```

```python
import jax
import jax.numpy as jnp
from jax import lax
from jax.sharding import PartitionSpec as P

HEADS = 8
HEAD_DIM = 128
BLOCK = 64


def from_behind(block, axis, distance):
    devices = range(lax.axis_size(axis))
    route = [((i - distance) % len(devices), i) for i in devices]
    return lax.ppermute(block, axis, route)


def layer_norm(value_vectors, scaling, shifts):
    center = jnp.mean(value_vectors, axis=-1, keepdims=True)
    offset = value_vectors - center
    spread = jnp.mean(offset * offset, axis=-1, keepdims=True)
    return offset * lax.rsqrt(spread + 1e-05) * scaling + shifts


def gelu_exact(value_vectors):
    return jax.nn.gelu(value_vectors, approximate=False)


def combine_rounds(outputs, totals):
    highest = jnp.max(totals, axis=0, keepdims=True)
    weights = jnp.exp(totals - highest)
    weights = weights / jnp.sum(weights, axis=0, keepdims=True)
    by_head = outputs.reshape(outputs.shape[:-1] + (totals.shape[-1], -1))
    return jnp.sum(weights[..., None] * by_head, axis=0).reshape(outputs.shape[1:])


def home_slots(places, row_count):
    target = places // row_count
    prior_state = (target[:, None, :] == target[:, :, None]) & (
        places[:, None, :] < places[:, :, None]
    )
    return (target, jnp.sum(prior_state.astype(jnp.int32), axis=2))


def sorted_slots(orders, row_count):
    source = orders // row_count
    ladder = jnp.arange(row_count, dtype=jnp.int32)
    prior_state = (source[:, None, :] == source[:, :, None]) & (
        ladder[None, None, :] < ladder[None, :, None]
    )
    return (source, jnp.sum(prior_state.astype(jnp.int32), axis=2))


def slot_lookup(owners, slot_index, devices, capacity):
    groups, row_count = owners.shape
    flat_index = owners * capacity + slot_index
    lookup = jnp.full((groups, devices * capacity), row_count, jnp.int32)
    filler = jnp.broadcast_to(jnp.arange(row_count, dtype=jnp.int32), (groups, row_count))
    lookup = lookup.at[jnp.arange(groups)[:, None], flat_index].set(filler)
    return jnp.transpose(lookup.reshape(groups, devices, capacity), (1, 0, 2))


def gather_slots(value_vectors, member, lookup):
    padding = jnp.zeros((value_vectors.shape[0], 1) + value_vectors.shape[2:], value_vectors.dtype)
    padded = jnp.concatenate([value_vectors, padding], axis=1)
    return padded[member[None, :, None], lookup]


def settle(received, owners, slot_index):
    return received[owners, jnp.arange(owners.shape[0])[:, None], slot_index]


def build_routes(orders, places, devices, capacity):
    rounds, sequences, row_count = orders.shape
    order_flat = orders.reshape(rounds * sequences, row_count)
    target, home_slot = home_slots(places.reshape(rounds * sequences, row_count), row_count)
    source, sorted_slot = sorted_slots(order_flat, row_count)
    home_lookup = slot_lookup(target, home_slot, devices, capacity)
    back_lookup = slot_lookup(source, sorted_slot, devices, capacity)
    return (target, home_slot, source, sorted_slot, home_lookup, back_lookup, order_flat)


def trade_rows(first_part, second_part):
    return (
        lax.all_to_all(first_part, ("seq", "sub"), split_axis=0, concat_axis=0, tiled=True),
        lax.all_to_all(second_part, ("seq", "sub"), split_axis=0, concat_axis=0, tiled=True),
    )


def trade_results(first_part, second_part):
    return (
        lax.all_to_all(first_part, ("seq", "sub"), split_axis=0, concat_axis=0, tiled=True),
        lax.all_to_all(second_part, ("seq", "sub"), split_axis=0, concat_axis=0, tiled=True),
    )


def window(rows_here, rows_left):
    groups = rows_here.shape[0]
    extended = jnp.concatenate([rows_left, rows_here], axis=1)
    extended = extended.reshape((groups, -1, BLOCK) + rows_here.shape[2:])
    return jnp.concatenate([extended[:, :-1], extended[:, 1:]], axis=2)


def score_parts(shared_rows, order_rows, halo_shared, halo_order):
    groups, row_count, features = shared_rows.shape
    blocks = row_count // BLOCK
    queries = shared_rows.reshape(groups, blocks, BLOCK, HEADS, HEAD_DIM)
    key_rows = window(shared_rows, halo_shared).reshape(groups, blocks, 2 * BLOCK, HEADS, HEAD_DIM)
    key_float = key_rows.astype(jnp.float32)
    mean_square = jnp.mean(key_float * key_float, axis=-1) + 1e-06
    key_scale = lax.rsqrt(mean_square) / HEAD_DIM
    raw_scores = jnp.einsum(
        "gcqhd,gckhd->gchqk", queries, key_rows, preferred_element_type=jnp.float32
    )
    query_pos = order_rows.reshape(groups, blocks, BLOCK)
    key_pos = window(order_rows, halo_order)
    is_later = (key_pos[:, :, None, :] > query_pos[:, :, :, None])[:, :, None]
    is_self = (key_pos[:, :, None, :] == query_pos[:, :, :, None])[:, :, None]
    scale_row = jnp.transpose(key_scale, (0, 1, 3, 2))[:, :, :, None, :]
    scores = jnp.where(
        is_later, -1000000000.0, jnp.where(is_self, -100000.0, raw_scores * scale_row)
    )
    highest = jnp.max(scores, axis=-1, keepdims=True)
    log_total = highest + jnp.log(jnp.sum(jnp.exp(scores - highest), axis=-1, keepdims=True))
    probability = jnp.exp(scores - log_total)
    return (
        queries,
        key_rows,
        key_float,
        mean_square,
        key_scale,
        scale_row,
        raw_scores,
        is_later | is_self,
        log_total,
        probability,
    )


def attend(shared_rows, value_rows, order_rows, halo):
    halo_shared, halo_value, halo_order = halo
    parts = score_parts(shared_rows, order_rows, halo_shared, halo_order)
    groups, row_count, features = shared_rows.shape
    value_keys = window(value_rows, halo_value).reshape(
        groups, row_count // BLOCK, 2 * BLOCK, HEADS, HEAD_DIM
    )
    mixed = jnp.einsum(
        "gchqk,gckhd->gcqhd",
        parts[9].astype(jnp.bfloat16),
        value_keys,
        preferred_element_type=jnp.float32,
    )
    log_total = jnp.transpose(parts[8][..., 0], (0, 1, 3, 2)).reshape(groups, row_count, HEADS)
    return (mixed.reshape(groups, row_count, features), log_total)


def fold_window(grads_window, groups, row_count, features):
    grads_window = grads_window.reshape(groups, row_count // BLOCK, 2 * BLOCK, features)
    empty = jnp.zeros((groups, 1, BLOCK, features), jnp.float32)
    extended = jnp.concatenate([grads_window[:, :, :BLOCK], empty], axis=1) + jnp.concatenate(
        [empty, grads_window[:, :, BLOCK:]], axis=1
    )
    return (extended[:, 1:].reshape(groups, row_count, features), extended[:, 0])


def attend_back(shared_rows, value_rows, order_rows, halo, grad_out, grad_total):
    halo_shared, halo_value, halo_order = halo
    (
        queries,
        key_rows,
        key_float,
        mean_square,
        key_scale,
        scale_row,
        raw_scores,
        masked,
        log_total,
        probability,
    ) = score_parts(shared_rows, order_rows, halo_shared, halo_order)
    groups, row_count, features = shared_rows.shape
    blocks = row_count // BLOCK
    value_keys = window(value_rows, halo_value).reshape(groups, blocks, 2 * BLOCK, HEADS, HEAD_DIM)
    prob_low = probability.astype(jnp.bfloat16)
    grad_heads = grad_out.reshape(groups, blocks, BLOCK, HEADS, HEAD_DIM)
    grad_log = jnp.transpose(
        grad_total.astype(jnp.float32).reshape(groups, blocks, BLOCK, HEADS), (0, 1, 3, 2)
    )[..., None]
    grad_prob = jnp.einsum(
        "gcqhd,gckhd->gchqk", grad_heads, value_keys, preferred_element_type=jnp.float32
    )
    inner = jnp.sum(probability * grad_prob, axis=-1, keepdims=True)
    grad_score = jnp.where(masked, 0.0, probability * (grad_prob - inner + grad_log))
    grad_scale = jnp.transpose(jnp.sum(grad_score * raw_scores, axis=3), (0, 1, 3, 2))
    grad_raw = (grad_score * scale_row).astype(jnp.bfloat16)
    grad_query = jnp.einsum(
        "gchqk,gckhd->gcqhd", grad_raw, key_rows, preferred_element_type=jnp.float32
    )
    grad_key = jnp.einsum(
        "gchqk,gcqhd->gckhd", grad_raw, queries, preferred_element_type=jnp.float32
    )
    grad_key = grad_key - (grad_scale * key_scale / mean_square)[..., None] * key_float / HEAD_DIM
    grad_value = jnp.einsum(
        "gchqk,gcqhd->gckhd", prob_low, grad_heads, preferred_element_type=jnp.float32
    )
    key_home, key_left = fold_window(grad_key, groups, row_count, features)
    value_home, value_left = fold_window(grad_value, groups, row_count, features)
    back_key, back_value = from_behind((key_left, value_left), ("seq", "sub"), -1)
    grad_shared = grad_query.reshape(groups, row_count, features) + key_home
    grad_shared = grad_shared.at[:, row_count - BLOCK :].add(back_key)
    grad_values = value_home.at[:, row_count - BLOCK :].add(back_value)
    return (grad_shared, grad_values)


def sorted_attention(shared_query_key, value_vectors, routes):
    target, home_slot, source, sorted_slot, home_lookup, back_lookup, order_flat = routes
    groups = target.shape[0]
    member = jnp.arange(groups) % shared_query_key.shape[0]
    got_shared, got_values = trade_rows(
        gather_slots(shared_query_key, member, home_lookup),
        gather_slots(value_vectors, member, home_lookup),
    )
    shared_rows = settle(got_shared, source, sorted_slot)
    value_rows = settle(got_values, source, sorted_slot)
    halo = from_behind(
        (shared_rows[:, -BLOCK:], value_rows[:, -BLOCK:], order_flat[:, -BLOCK:]), ("seq", "sub"), 1
    )
    mixed, log_total = attend(shared_rows, value_rows, order_flat, halo)
    all_groups = jnp.arange(groups)
    got_mixed, got_total = trade_results(
        gather_slots(mixed, all_groups, back_lookup),
        gather_slots(log_total, all_groups, back_lookup),
    )
    return (
        settle(got_mixed, target, home_slot),
        settle(got_total, target, home_slot),
        (shared_rows, value_rows, halo),
    )


def round_outputs(normalized_input, query_key_weight, value_projection_weight, routes, rounds):
    shared_query_key = jnp.einsum(
        "srd,de->sre", normalized_input, query_key_weight, preferred_element_type=jnp.float32
    ).astype(jnp.bfloat16)
    value_vectors = jnp.einsum(
        "srd,de->sre", normalized_input, value_projection_weight, preferred_element_type=jnp.float32
    ).astype(jnp.bfloat16)
    mixed, log_total, kept = sorted_attention(shared_query_key, value_vectors, routes)
    sequences, row_count, features = normalized_input.shape
    outputs = mixed.reshape(rounds, sequences, row_count, features)
    totals = log_total.reshape(rounds, sequences, row_count, HEADS)
    return (shared_query_key, value_vectors, outputs, totals, kept)


def collect(weight_stack, layer_index):
    (
        attend_gain,
        attend_shift,
        query_key_weight,
        value_projection_weight,
        output_projection_weight,
        feed_gain,
        feed_shift,
        upper_projection_weight,
        upper_projection_bias,
        lower_projection_weight,
        lower_projection_bias,
    ) = tuple((shard_piece[layer_index] for shard_piece in weight_stack))
    return (
        lax.all_gather(attend_gain, ("seq", "sub"), axis=0, tiled=True),
        lax.all_gather(attend_shift, ("seq", "sub"), axis=0, tiled=True),
        lax.all_gather(query_key_weight, ("seq", "sub"), axis=0, tiled=True),
        lax.all_gather(value_projection_weight, ("seq", "sub"), axis=0, tiled=True),
        lax.all_gather(output_projection_weight, ("seq", "sub"), axis=0, tiled=True),
        lax.all_gather(feed_gain, ("seq", "sub"), axis=0, tiled=True),
        lax.all_gather(feed_shift, ("seq", "sub"), axis=0, tiled=True),
        lax.all_gather(upper_projection_weight, ("seq", "sub"), axis=0, tiled=True),
        lax.all_gather(upper_projection_bias, ("seq", "sub"), axis=0, tiled=True),
        lax.all_gather(lower_projection_weight, ("seq", "sub"), axis=0, tiled=True),
        lax.all_gather(lower_projection_bias, ("seq", "sub"), axis=0, tiled=True),
    )


def spread_grads(level_grads):
    (
        attend_gain,
        attend_shift,
        query_key_weight,
        value_projection_weight,
        output_projection_weight,
        feed_gain,
        feed_shift,
        upper_projection_weight,
        upper_projection_bias,
        lower_projection_weight,
        lower_projection_bias,
    ) = level_grads
    return (
        lax.psum_scatter(attend_gain, ("seq", "sub"), scatter_dimension=0, tiled=True),
        lax.psum_scatter(attend_shift, ("seq", "sub"), scatter_dimension=0, tiled=True),
        lax.psum_scatter(query_key_weight.astype(jnp.bfloat16), ("seq", "sub"), scatter_dimension=0, tiled=True),
        lax.psum_scatter(value_projection_weight.astype(jnp.bfloat16), ("seq", "sub"), scatter_dimension=0, tiled=True),
        lax.psum_scatter(output_projection_weight.astype(jnp.bfloat16), ("seq", "sub"), scatter_dimension=0, tiled=True),
        lax.psum_scatter(feed_gain, ("seq", "sub"), scatter_dimension=0, tiled=True),
        lax.psum_scatter(feed_shift, ("seq", "sub"), scatter_dimension=0, tiled=True),
        lax.psum_scatter(upper_projection_weight.astype(jnp.bfloat16), ("seq", "sub"), scatter_dimension=0, tiled=True),
        lax.psum_scatter(upper_projection_bias, ("seq", "sub"), scatter_dimension=0, tiled=True),
        lax.psum_scatter(lower_projection_weight.astype(jnp.bfloat16), ("seq", "sub"), scatter_dimension=0, tiled=True),
        lax.psum_scatter(lower_projection_bias, ("seq", "sub"), scatter_dimension=0, tiled=True),
    )


def layer_pass(first_half, second_half, grad_one, grad_two, params, routes, rounds):
    (
        attend_gain,
        attend_shift,
        query_key_weight,
        value_projection_weight,
        output_projection_weight,
        feed_gain,
        feed_shift,
        upper_projection_weight,
        upper_projection_bias,
        lower_projection_weight,
        lower_projection_bias,
    ) = params
    attend_norm, attend_pull = jax.vjp(
        layer_norm, second_half, attend_gain.astype(jnp.float32), attend_shift.astype(jnp.float32)
    )
    normalized_input = attend_norm.astype(jnp.bfloat16)
    shared_query_key, value_vectors, outputs, totals, kept = round_outputs(
        normalized_input, query_key_weight, value_projection_weight, routes, rounds
    )
    attention_result, combine_pull = jax.vjp(combine_rounds, outputs, totals)
    attended_low = attention_result.astype(jnp.bfloat16)
    top_one = first_half + jnp.einsum(
        "srd,de->sre", attended_low, output_projection_weight, preferred_element_type=jnp.float32
    )
    feed_norm, feed_pull = jax.vjp(
        layer_norm, top_one, feed_gain.astype(jnp.float32), feed_shift.astype(jnp.float32)
    )
    feed_forward_input = feed_norm.astype(jnp.bfloat16)
    prior_state = jnp.einsum(
        "srd,df->srf",
        feed_forward_input,
        upper_projection_weight,
        preferred_element_type=jnp.float32,
    ) + upper_projection_bias.astype(jnp.float32)
    hidden_activation, active_pull = jax.vjp(gelu_exact, prior_state)
    active_low = hidden_activation.astype(jnp.bfloat16)
    feed_out = jnp.einsum(
        "srf,fd->srd", active_low, lower_projection_weight, preferred_element_type=jnp.float32
    ) + lower_projection_bias.astype(jnp.float32)
    top_two = second_half + feed_out
    feed_grad = grad_two.astype(jnp.bfloat16)
    down_weight_grad = jnp.einsum(
        "srf,srd->fd", active_low, feed_grad, preferred_element_type=jnp.float32
    )
    down_bias_grad = jnp.sum(feed_grad.astype(jnp.float32), axis=(0, 1))
    active_grad = jnp.einsum(
        "srd,fd->srf", feed_grad, lower_projection_weight, preferred_element_type=jnp.float32
    )
    before_grad = active_pull(active_grad)[0].astype(jnp.bfloat16)
    up_weight_grad = jnp.einsum(
        "srd,srf->df", feed_forward_input, before_grad, preferred_element_type=jnp.float32
    )
    up_bias_grad = jnp.sum(before_grad.astype(jnp.float32), axis=(0, 1))
    norm_grad = jnp.einsum(
        "srf,df->srd", before_grad, upper_projection_weight, preferred_element_type=jnp.float32
    )
    one_part, feed_gain_grad, feed_shift_grad = feed_pull(norm_grad)
    total_one = grad_one + one_part
    out_grad = total_one.astype(jnp.bfloat16)
    output_weight_grad = jnp.einsum(
        "srd,sre->de", attended_low, out_grad, preferred_element_type=jnp.float32
    )
    attended_grad = jnp.einsum(
        "sre,de->srd", out_grad, output_projection_weight, preferred_element_type=jnp.float32
    )
    outputs_grad, totals_grad = combine_pull(attended_grad)
    target, home_slot, source, sorted_slot, home_lookup, back_lookup, order_flat = routes
    sequences, row_count, features = top_one.shape
    groups = rounds * sequences
    all_groups = jnp.arange(groups)
    outputs_low = outputs_grad.astype(jnp.bfloat16).reshape(groups, row_count, features)
    totals_low = totals_grad.astype(jnp.bfloat16).reshape(groups, row_count, HEADS)
    got_out, got_total = trade_rows(
        gather_slots(outputs_low, all_groups, home_lookup),
        gather_slots(totals_low, all_groups, home_lookup),
    )
    shared_rows, value_rows, halo = kept
    grad_shared, grad_values = attend_back(
        shared_rows,
        value_rows,
        order_flat,
        halo,
        settle(got_out, source, sorted_slot),
        settle(got_total, source, sorted_slot),
    )
    home_shared, home_values = trade_rows(
        gather_slots(grad_shared.astype(jnp.bfloat16), all_groups, back_lookup),
        gather_slots(grad_values.astype(jnp.bfloat16), all_groups, back_lookup),
    )
    shared_grad = jnp.sum(
        settle(home_shared, target, home_slot)
        .astype(jnp.float32)
        .reshape(rounds, sequences, row_count, features),
        axis=0,
    ).astype(jnp.bfloat16)
    values_grad = jnp.sum(
        settle(home_values, target, home_slot)
        .astype(jnp.float32)
        .reshape(rounds, sequences, row_count, features),
        axis=0,
    ).astype(jnp.bfloat16)
    shared_weight_grad = jnp.einsum(
        "srd,sre->de", normalized_input, shared_grad, preferred_element_type=jnp.float32
    )
    value_weight_grad = jnp.einsum(
        "srd,sre->de", normalized_input, values_grad, preferred_element_type=jnp.float32
    )
    normed_grad = jnp.einsum(
        "sre,de->srd", shared_grad, query_key_weight, preferred_element_type=jnp.float32
    ) + jnp.einsum(
        "sre,de->srd", values_grad, value_projection_weight, preferred_element_type=jnp.float32
    )
    two_part, attend_gain_grad, attend_shift_grad = attend_pull(normed_grad)
    total_two = grad_two + two_part
    level_grads = (
        attend_gain_grad,
        attend_shift_grad,
        shared_weight_grad,
        value_weight_grad,
        output_weight_grad,
        feed_gain_grad,
        feed_shift_grad,
        up_weight_grad,
        up_bias_grad,
        down_weight_grad,
        down_bias_grad,
    )
    return (top_one, top_two, total_one, total_two, level_grads)


def on_device(
    first_half,
    second_half,
    grad_first,
    grad_second,
    attend_gain,
    attend_shift,
    query_key_weight,
    value_projection_weight,
    output_projection_weight,
    feed_gain,
    feed_shift,
    upper_projection_weight,
    upper_projection_bias,
    lower_projection_weight,
    lower_projection_bias,
    sort_order,
    sort_place,
):
    weight_stack = (
        attend_gain,
        attend_shift,
        query_key_weight,
        value_projection_weight,
        output_projection_weight,
        feed_gain,
        feed_shift,
        upper_projection_weight,
        upper_projection_bias,
        lower_projection_weight,
        lower_projection_bias,
    )
    devices = lax.axis_size(("seq", "sub"))
    rounds = sort_order.shape[1]
    row_count = first_half.shape[1]
    capacity = 2 * max(1, row_count // devices)
    params = collect(weight_stack, 0)
    routes = build_routes(sort_order[0], sort_place[0], devices, capacity)
    first_out, second_out, first_grad, second_grad, level_grads = layer_pass(
        first_half, second_half, grad_first, grad_second, params, routes, rounds
    )
    stacked = tuple((entry[None].astype(jnp.float32) for entry in spread_grads(level_grads)))
    return (first_out, second_out, first_grad, second_grad) + stacked


def solution(mesh):
    return jax.shard_map(
        on_device,
        mesh=mesh,
        in_specs=(
            P(None, ("seq", "sub"), None),
            P(None, ("seq", "sub"), None),
            P(None, ("seq", "sub"), None),
            P(None, ("seq", "sub"), None),
            P(None, ("seq", "sub")),
            P(None, ("seq", "sub")),
            P(None, ("seq", "sub"), None),
            P(None, ("seq", "sub"), None),
            P(None, ("seq", "sub"), None),
            P(None, ("seq", "sub")),
            P(None, ("seq", "sub")),
            P(None, ("seq", "sub"), None),
            P(None, ("seq", "sub")),
            P(None, ("seq", "sub"), None),
            P(None, ("seq", "sub")),
            P(None, None, None, ("seq", "sub")),
            P(None, None, None, ("seq", "sub")),
        ),
        out_specs=(
            P(None, ("seq", "sub"), None),
            P(None, ("seq", "sub"), None),
            P(None, ("seq", "sub"), None),
            P(None, ("seq", "sub"), None),
            P(None, ("seq", "sub")),
            P(None, ("seq", "sub")),
            P(None, ("seq", "sub"), None),
            P(None, ("seq", "sub"), None),
            P(None, ("seq", "sub"), None),
            P(None, ("seq", "sub")),
            P(None, ("seq", "sub")),
            P(None, ("seq", "sub"), None),
            P(None, ("seq", "sub")),
            P(None, ("seq", "sub"), None),
            P(None, ("seq", "sub")),
        ),
        check_vma=False,
    )
```

```python
import functools

import jax
import jax.numpy as jnp
from jax import lax
from jax.experimental import pallas as pl
from jax.experimental.pallas import tpu as pltpu
from jax.sharding import PartitionSpec as P

HEADS = 8
HEAD_DIM = 128
BLOCK = 64
LATER = -1000000000.0
SELF = -100000.0
OUTSIDE = -3e38


def from_behind(block, axis, distance):
    devices = range(lax.axis_size(axis))
    route = [((i - distance) % len(devices), i) for i in devices]
    return lax.ppermute(block, axis, route)


def layer_norm(value_vectors, scaling, shifts):
    center = jnp.mean(value_vectors, axis=-1, keepdims=True)
    offset = value_vectors - center
    spread = jnp.mean(offset * offset, axis=-1, keepdims=True)
    return offset * lax.rsqrt(spread + 1e-05) * scaling + shifts


def gelu_exact(value_vectors):
    return jax.nn.gelu(value_vectors, approximate=False)


def combine_rounds(outputs, totals):
    highest = jnp.max(totals, axis=0, keepdims=True)
    weights = jnp.exp(totals - highest)
    weights = weights / jnp.sum(weights, axis=0, keepdims=True)
    by_head = outputs.reshape(outputs.shape[:-1] + (totals.shape[-1], -1))
    return jnp.sum(weights[..., None] * by_head, axis=0).reshape(outputs.shape[1:])


def home_slots(places, row_count):
    target = places // row_count
    prior_state = (target[:, None, :] == target[:, :, None]) & (
        places[:, None, :] < places[:, :, None]
    )
    return (target, jnp.sum(prior_state.astype(jnp.int32), axis=2))


def sorted_slots(orders, row_count):
    source = orders // row_count
    ladder = jnp.arange(row_count, dtype=jnp.int32)
    prior_state = (source[:, None, :] == source[:, :, None]) & (
        ladder[None, None, :] < ladder[None, :, None]
    )
    return (source, jnp.sum(prior_state.astype(jnp.int32), axis=2))


def slot_lookup(owners, slot_index, devices, capacity):
    groups, row_count = owners.shape
    flat_index = owners * capacity + slot_index
    lookup = jnp.full((groups, devices * capacity), row_count, jnp.int32)
    filler = jnp.broadcast_to(jnp.arange(row_count, dtype=jnp.int32), (groups, row_count))
    lookup = lookup.at[jnp.arange(groups)[:, None], flat_index].set(filler)
    return jnp.transpose(lookup.reshape(groups, devices, capacity), (1, 0, 2))


def gather_slots(value_vectors, member, lookup):
    padding = jnp.zeros((value_vectors.shape[0], 1) + value_vectors.shape[2:], value_vectors.dtype)
    padded = jnp.concatenate([value_vectors, padding], axis=1)
    return padded[member[None, :, None], lookup]


def settle(received, owners, slot_index):
    return received[owners, jnp.arange(owners.shape[0])[:, None], slot_index]


def build_routes(orders, places, devices, capacity):
    rounds, sequences, row_count = orders.shape
    order_flat = orders.reshape(rounds * sequences, row_count)
    target, home_slot = home_slots(places.reshape(rounds * sequences, row_count), row_count)
    source, sorted_slot = sorted_slots(order_flat, row_count)
    home_lookup = slot_lookup(target, home_slot, devices, capacity)
    back_lookup = slot_lookup(source, sorted_slot, devices, capacity)
    return (target, home_slot, source, sorted_slot, home_lookup, back_lookup, order_flat)


def trade_rows(first_part, second_part):
    return (
        lax.all_to_all(first_part, ("seq", "sub"), split_axis=0, concat_axis=0, tiled=True),
        lax.all_to_all(second_part, ("seq", "sub"), split_axis=0, concat_axis=0, tiled=True),
    )


def trade_results(first_part, second_part):
    return (
        lax.all_to_all(first_part, ("seq", "sub"), split_axis=0, concat_axis=0, tiled=True),
        lax.all_to_all(second_part, ("seq", "sub"), split_axis=0, concat_axis=0, tiled=True),
    )


def window(rows_here, rows_left):
    groups = rows_here.shape[0]
    extended = jnp.concatenate([rows_left, rows_here], axis=1)
    extended = extended.reshape((groups, -1, BLOCK) + rows_here.shape[2:])
    return jnp.concatenate([extended[:, :-1], extended[:, 1:]], axis=2)


def score_parts(shared_rows, order_rows, halo_shared, halo_order):
    groups, row_count, features = shared_rows.shape
    blocks = row_count // BLOCK
    queries = shared_rows.reshape(groups, blocks, BLOCK, HEADS, HEAD_DIM)
    key_rows = window(shared_rows, halo_shared).reshape(groups, blocks, 2 * BLOCK, HEADS, HEAD_DIM)
    key_float = key_rows.astype(jnp.float32)
    mean_square = jnp.mean(key_float * key_float, axis=-1) + 1e-06
    key_scale = lax.rsqrt(mean_square) / HEAD_DIM
    raw_scores = jnp.einsum(
        "gcqhd,gckhd->gchqk", queries, key_rows, preferred_element_type=jnp.float32
    )
    query_pos = order_rows.reshape(groups, blocks, BLOCK)
    key_pos = window(order_rows, halo_order)
    is_later = (key_pos[:, :, None, :] > query_pos[:, :, :, None])[:, :, None]
    is_self = (key_pos[:, :, None, :] == query_pos[:, :, :, None])[:, :, None]
    scale_row = jnp.transpose(key_scale, (0, 1, 3, 2))[:, :, :, None, :]
    scores = jnp.where(
        is_later, -1000000000.0, jnp.where(is_self, -100000.0, raw_scores * scale_row)
    )
    highest = jnp.max(scores, axis=-1, keepdims=True)
    log_total = highest + jnp.log(jnp.sum(jnp.exp(scores - highest), axis=-1, keepdims=True))
    probability = jnp.exp(scores - log_total)
    return (
        queries,
        key_rows,
        key_float,
        mean_square,
        key_scale,
        scale_row,
        raw_scores,
        is_later | is_self,
        log_total,
        probability,
    )


def attend(shared_rows, value_rows, order_rows, halo):
    halo_shared, halo_value, halo_order = halo
    parts = score_parts(shared_rows, order_rows, halo_shared, halo_order)
    groups, row_count, features = shared_rows.shape
    value_keys = window(value_rows, halo_value).reshape(
        groups, row_count // BLOCK, 2 * BLOCK, HEADS, HEAD_DIM
    )
    mixed = jnp.einsum(
        "gchqk,gckhd->gcqhd",
        parts[9].astype(jnp.bfloat16),
        value_keys,
        preferred_element_type=jnp.float32,
    )
    log_total = jnp.transpose(parts[8][..., 0], (0, 1, 3, 2)).reshape(groups, row_count, HEADS)
    return (mixed.reshape(groups, row_count, features), log_total)


def fold_window(grads_window, groups, row_count, features):
    grads_window = grads_window.reshape(groups, row_count // BLOCK, 2 * BLOCK, features)
    empty = jnp.zeros((groups, 1, BLOCK, features), jnp.float32)
    extended = jnp.concatenate([grads_window[:, :, :BLOCK], empty], axis=1) + jnp.concatenate(
        [empty, grads_window[:, :, BLOCK:]], axis=1
    )
    return (extended[:, 1:].reshape(groups, row_count, features), extended[:, 0])


def attend_back(shared_rows, value_rows, order_rows, halo, grad_out, grad_total):
    halo_shared, halo_value, halo_order = halo
    (
        queries,
        key_rows,
        key_float,
        mean_square,
        key_scale,
        scale_row,
        raw_scores,
        masked,
        log_total,
        probability,
    ) = score_parts(shared_rows, order_rows, halo_shared, halo_order)
    groups, row_count, features = shared_rows.shape
    blocks = row_count // BLOCK
    value_keys = window(value_rows, halo_value).reshape(groups, blocks, 2 * BLOCK, HEADS, HEAD_DIM)
    prob_low = probability.astype(jnp.bfloat16)
    grad_heads = grad_out.reshape(groups, blocks, BLOCK, HEADS, HEAD_DIM)
    grad_log = jnp.transpose(
        grad_total.astype(jnp.float32).reshape(groups, blocks, BLOCK, HEADS), (0, 1, 3, 2)
    )[..., None]
    grad_prob = jnp.einsum(
        "gcqhd,gckhd->gchqk", grad_heads, value_keys, preferred_element_type=jnp.float32
    )
    inner = jnp.sum(probability * grad_prob, axis=-1, keepdims=True)
    grad_score = jnp.where(masked, 0.0, probability * (grad_prob - inner + grad_log))
    grad_scale = jnp.transpose(jnp.sum(grad_score * raw_scores, axis=3), (0, 1, 3, 2))
    grad_raw = (grad_score * scale_row).astype(jnp.bfloat16)
    grad_query = jnp.einsum(
        "gchqk,gckhd->gcqhd", grad_raw, key_rows, preferred_element_type=jnp.float32
    )
    grad_key = jnp.einsum(
        "gchqk,gcqhd->gckhd", grad_raw, queries, preferred_element_type=jnp.float32
    )
    grad_key = grad_key - (grad_scale * key_scale / mean_square)[..., None] * key_float / HEAD_DIM
    grad_value = jnp.einsum(
        "gchqk,gcqhd->gckhd", prob_low, grad_heads, preferred_element_type=jnp.float32
    )
    key_home, key_left = fold_window(grad_key, groups, row_count, features)
    value_home, value_left = fold_window(grad_value, groups, row_count, features)
    back_key, back_value = from_behind((key_left, value_left), ("seq", "sub"), -1)
    grad_shared = grad_query.reshape(groups, row_count, features) + key_home
    grad_shared = grad_shared.at[:, row_count - BLOCK :].add(back_key)
    grad_values = value_home.at[:, row_count - BLOCK :].add(back_value)
    return (grad_shared, grad_values)


def sorted_attention(shared_query_key, value_vectors, routes):
    target, home_slot, source, sorted_slot, home_lookup, back_lookup, order_flat = routes
    groups = target.shape[0]
    member = jnp.arange(groups) % shared_query_key.shape[0]
    got_shared, got_values = trade_rows(
        gather_slots(shared_query_key, member, home_lookup),
        gather_slots(value_vectors, member, home_lookup),
    )
    shared_rows = settle(got_shared, source, sorted_slot)
    value_rows = settle(got_values, source, sorted_slot)
    halo = from_behind(
        (shared_rows[:, -BLOCK:], value_rows[:, -BLOCK:], order_flat[:, -BLOCK:]), ("seq", "sub"), 1
    )
    mixed, log_total = attend(shared_rows, value_rows, order_flat, halo)
    all_groups = jnp.arange(groups)
    got_mixed, got_total = trade_results(
        gather_slots(mixed, all_groups, back_lookup),
        gather_slots(log_total, all_groups, back_lookup),
    )
    return (
        settle(got_mixed, target, home_slot),
        settle(got_total, target, home_slot),
        (shared_rows, value_rows, halo),
    )


def round_outputs(normalized_input, query_key_weight, value_projection_weight, routes, rounds):
    shared_query_key = jnp.einsum(
        "srd,de->sre", normalized_input, query_key_weight, preferred_element_type=jnp.float32
    ).astype(jnp.bfloat16)
    value_vectors = jnp.einsum(
        "srd,de->sre", normalized_input, value_projection_weight, preferred_element_type=jnp.float32
    ).astype(jnp.bfloat16)
    mixed, log_total, kept = sorted_attention(shared_query_key, value_vectors, routes)
    sequences, row_count, features = normalized_input.shape
    outputs = mixed.reshape(rounds, sequences, row_count, features)
    totals = log_total.reshape(rounds, sequences, row_count, HEADS)
    return (shared_query_key, value_vectors, outputs, totals, kept)


def collect(weight_stack, layer_index):
    (
        attend_gain,
        attend_shift,
        query_key_weight,
        value_projection_weight,
        output_projection_weight,
        feed_gain,
        feed_shift,
        upper_projection_weight,
        upper_projection_bias,
        lower_projection_weight,
        lower_projection_bias,
    ) = tuple((shard_piece[layer_index] for shard_piece in weight_stack))
    return (
        lax.all_gather(attend_gain, ("seq", "sub"), axis=0, tiled=True),
        lax.all_gather(attend_shift, ("seq", "sub"), axis=0, tiled=True),
        lax.all_gather(query_key_weight, ("seq", "sub"), axis=0, tiled=True),
        lax.all_gather(value_projection_weight, ("seq", "sub"), axis=0, tiled=True),
        lax.all_gather(output_projection_weight, ("seq", "sub"), axis=0, tiled=True),
        lax.all_gather(feed_gain, ("seq", "sub"), axis=0, tiled=True),
        lax.all_gather(feed_shift, ("seq", "sub"), axis=0, tiled=True),
        lax.all_gather(upper_projection_weight, ("seq", "sub"), axis=0, tiled=True),
        lax.all_gather(upper_projection_bias, ("seq", "sub"), axis=0, tiled=True),
        lax.all_gather(lower_projection_weight, ("seq", "sub"), axis=0, tiled=True),
        lax.all_gather(lower_projection_bias, ("seq", "sub"), axis=0, tiled=True),
    )


def spread_grads(level_grads):
    (
        attend_gain,
        attend_shift,
        query_key_weight,
        value_projection_weight,
        output_projection_weight,
        feed_gain,
        feed_shift,
        upper_projection_weight,
        upper_projection_bias,
        lower_projection_weight,
        lower_projection_bias,
    ) = level_grads
    return (
        lax.psum_scatter(attend_gain, ("seq", "sub"), scatter_dimension=0, tiled=True),
        lax.psum_scatter(attend_shift, ("seq", "sub"), scatter_dimension=0, tiled=True),
        lax.psum_scatter(query_key_weight.astype(jnp.bfloat16), ("seq", "sub"), scatter_dimension=0, tiled=True),
        lax.psum_scatter(value_projection_weight.astype(jnp.bfloat16), ("seq", "sub"), scatter_dimension=0, tiled=True),
        lax.psum_scatter(output_projection_weight.astype(jnp.bfloat16), ("seq", "sub"), scatter_dimension=0, tiled=True),
        lax.psum_scatter(feed_gain, ("seq", "sub"), scatter_dimension=0, tiled=True),
        lax.psum_scatter(feed_shift, ("seq", "sub"), scatter_dimension=0, tiled=True),
        lax.psum_scatter(upper_projection_weight.astype(jnp.bfloat16), ("seq", "sub"), scatter_dimension=0, tiled=True),
        lax.psum_scatter(upper_projection_bias, ("seq", "sub"), scatter_dimension=0, tiled=True),
        lax.psum_scatter(lower_projection_weight.astype(jnp.bfloat16), ("seq", "sub"), scatter_dimension=0, tiled=True),
        lax.psum_scatter(lower_projection_bias, ("seq", "sub"), scatter_dimension=0, tiled=True),
    )


def layer_pass(first_half, second_half, grad_one, grad_two, params, routes, rounds):
    (
        attend_gain,
        attend_shift,
        query_key_weight,
        value_projection_weight,
        output_projection_weight,
        feed_gain,
        feed_shift,
        upper_projection_weight,
        upper_projection_bias,
        lower_projection_weight,
        lower_projection_bias,
    ) = params
    attend_norm, attend_pull = jax.vjp(
        layer_norm, second_half, attend_gain.astype(jnp.float32), attend_shift.astype(jnp.float32)
    )
    normalized_input = attend_norm.astype(jnp.bfloat16)
    shared_query_key, value_vectors, outputs, totals, kept = round_outputs(
        normalized_input, query_key_weight, value_projection_weight, routes, rounds
    )
    attention_result, combine_pull = jax.vjp(combine_rounds, outputs, totals)
    attended_low = attention_result.astype(jnp.bfloat16)
    top_one = first_half + jnp.einsum(
        "srd,de->sre", attended_low, output_projection_weight, preferred_element_type=jnp.float32
    )
    feed_norm, feed_pull = jax.vjp(
        layer_norm, top_one, feed_gain.astype(jnp.float32), feed_shift.astype(jnp.float32)
    )
    feed_forward_input = feed_norm.astype(jnp.bfloat16)
    prior_state = jnp.einsum(
        "srd,df->srf",
        feed_forward_input,
        upper_projection_weight,
        preferred_element_type=jnp.float32,
    ) + upper_projection_bias.astype(jnp.float32)
    hidden_activation, active_pull = jax.vjp(gelu_exact, prior_state)
    active_low = hidden_activation.astype(jnp.bfloat16)
    feed_out = jnp.einsum(
        "srf,fd->srd", active_low, lower_projection_weight, preferred_element_type=jnp.float32
    ) + lower_projection_bias.astype(jnp.float32)
    top_two = second_half + feed_out
    feed_grad = grad_two.astype(jnp.bfloat16)
    down_weight_grad = jnp.einsum(
        "srf,srd->fd", active_low, feed_grad, preferred_element_type=jnp.float32
    )
    down_bias_grad = jnp.sum(feed_grad.astype(jnp.float32), axis=(0, 1))
    active_grad = jnp.einsum(
        "srd,fd->srf", feed_grad, lower_projection_weight, preferred_element_type=jnp.float32
    )
    before_grad = active_pull(active_grad)[0].astype(jnp.bfloat16)
    up_weight_grad = jnp.einsum(
        "srd,srf->df", feed_forward_input, before_grad, preferred_element_type=jnp.float32
    )
    up_bias_grad = jnp.sum(before_grad.astype(jnp.float32), axis=(0, 1))
    norm_grad = jnp.einsum(
        "srf,df->srd", before_grad, upper_projection_weight, preferred_element_type=jnp.float32
    )
    one_part, feed_gain_grad, feed_shift_grad = feed_pull(norm_grad)
    total_one = grad_one + one_part
    out_grad = total_one.astype(jnp.bfloat16)
    output_weight_grad = jnp.einsum(
        "srd,sre->de", attended_low, out_grad, preferred_element_type=jnp.float32
    )
    attended_grad = jnp.einsum(
        "sre,de->srd", out_grad, output_projection_weight, preferred_element_type=jnp.float32
    )
    outputs_grad, totals_grad = combine_pull(attended_grad)
    target, home_slot, source, sorted_slot, home_lookup, back_lookup, order_flat = routes
    sequences, row_count, features = top_one.shape
    groups = rounds * sequences
    all_groups = jnp.arange(groups)
    outputs_low = outputs_grad.astype(jnp.bfloat16).reshape(groups, row_count, features)
    totals_low = totals_grad.astype(jnp.bfloat16).reshape(groups, row_count, HEADS)
    got_out, got_total = trade_rows(
        gather_slots(outputs_low, all_groups, home_lookup),
        gather_slots(totals_low, all_groups, home_lookup),
    )
    shared_rows, value_rows, halo = kept
    grad_shared, grad_values = attend_back(
        shared_rows,
        value_rows,
        order_flat,
        halo,
        settle(got_out, source, sorted_slot),
        settle(got_total, source, sorted_slot),
    )
    home_shared, home_values = trade_rows(
        gather_slots(grad_shared.astype(jnp.bfloat16), all_groups, back_lookup),
        gather_slots(grad_values.astype(jnp.bfloat16), all_groups, back_lookup),
    )
    shared_grad = jnp.sum(
        settle(home_shared, target, home_slot)
        .astype(jnp.float32)
        .reshape(rounds, sequences, row_count, features),
        axis=0,
    ).astype(jnp.bfloat16)
    values_grad = jnp.sum(
        settle(home_values, target, home_slot)
        .astype(jnp.float32)
        .reshape(rounds, sequences, row_count, features),
        axis=0,
    ).astype(jnp.bfloat16)
    shared_weight_grad = jnp.einsum(
        "srd,sre->de", normalized_input, shared_grad, preferred_element_type=jnp.float32
    )
    value_weight_grad = jnp.einsum(
        "srd,sre->de", normalized_input, values_grad, preferred_element_type=jnp.float32
    )
    normed_grad = jnp.einsum(
        "sre,de->srd", shared_grad, query_key_weight, preferred_element_type=jnp.float32
    ) + jnp.einsum(
        "sre,de->srd", values_grad, value_projection_weight, preferred_element_type=jnp.float32
    )
    two_part, attend_gain_grad, attend_shift_grad = attend_pull(normed_grad)
    total_two = grad_two + two_part
    level_grads = (
        attend_gain_grad,
        attend_shift_grad,
        shared_weight_grad,
        value_weight_grad,
        output_weight_grad,
        feed_gain_grad,
        feed_shift_grad,
        up_weight_grad,
        up_bias_grad,
        down_weight_grad,
        down_bias_grad,
    )
    return (top_one, top_two, total_one, total_two, level_grads)


def general_plan(
    first_half,
    second_half,
    grad_first,
    grad_second,
    attend_gain,
    attend_shift,
    query_key_weight,
    value_projection_weight,
    output_projection_weight,
    feed_gain,
    feed_shift,
    upper_projection_weight,
    upper_projection_bias,
    lower_projection_weight,
    lower_projection_bias,
    sort_order,
    sort_place,
):
    weight_stack = (
        attend_gain,
        attend_shift,
        query_key_weight,
        value_projection_weight,
        output_projection_weight,
        feed_gain,
        feed_shift,
        upper_projection_weight,
        upper_projection_bias,
        lower_projection_weight,
        lower_projection_bias,
    )
    devices = lax.axis_size(("seq", "sub"))
    rounds = sort_order.shape[1]
    row_count = first_half.shape[1]
    capacity = 2 * max(1, row_count // devices)
    params = collect(weight_stack, 0)
    routes = build_routes(sort_order[0], sort_place[0], devices, capacity)
    first_out, second_out, first_grad, second_grad, level_grads = layer_pass(
        first_half, second_half, grad_first, grad_second, params, routes, rounds
    )
    stacked = tuple((entry[None].astype(jnp.float32) for entry in spread_grads(level_grads)))
    return (first_out, second_out, first_grad, second_grad) + stacked


def exchange(items, name, collective_id, n_seq, n_sub):
    per_plane = 2 * n_sub
    size = {"plane": per_plane, "z": n_seq // 2, "all": n_seq * n_sub}
    axes = sorted({item[0] for item in items})
    count = len(items)
    slots = max(size[axis] for axis in axes)

    def body(*refs):
        sources, targets = refs[:count], refs[count : 2 * count]
        send, receive, own = refs[2 * count :]
        seq, sub = lax.axis_index("seq"), lax.axis_index("sub")
        here = {
            "plane": lax.rem(seq, 2) * n_sub + sub,
            "z": seq // 2,
            "all": seq * n_sub + sub,
        }

        def device(axis, index):
            if axis == "all":
                return (index // n_sub, lax.rem(index, n_sub))
            if axis == "z":
                return (index * 2 + lax.rem(seq, 2), sub)
            return ((seq // 2) * 2 + index // n_sub, lax.rem(index, n_sub))

        barrier = pltpu.get_barrier_semaphore()
        greeted = 0
        for axis in ["all"] if "all" in axes else axes:
            for step in range(1, size[axis]):
                peer = lax.rem(here[axis] + step, size[axis])
                pl.semaphore_signal(
                    barrier, inc=1, device_id=device(axis, peer), device_id_type=pl.DeviceIdType.MESH
                )
                greeted += 1
        copies = []
        for index, (axis, _, _, source, target) in enumerate(items):
            copies.append(
                pltpu.make_async_copy(
                    source(sources[index], here[axis]),
                    target(targets[index], here[axis]),
                    own.at[index],
                )
            )
            copies[-1].start()
        pl.semaphore_wait(barrier, greeted)
        for step in range(1, slots):
            for index, (axis, _, _, source, target) in enumerate(items):
                if step >= size[axis]:
                    continue
                peer = lax.rem(here[axis] + step, size[axis])
                copies.append(
                    pltpu.make_async_remote_copy(
                        src_ref=source(sources[index], peer),
                        dst_ref=target(targets[index], here[axis]),
                        send_sem=send.at[index, step],
                        recv_sem=receive.at[index, step],
                        device_id=device(axis, peer),
                        device_id_type=pl.DeviceIdType.MESH,
                    )
                )
                copies[-1].start()
        for copy in copies:
            copy.wait()

    return pl.pallas_call(
        body,
        out_shape=[item[2] for item in items],
        in_specs=[pl.BlockSpec(memory_space=pl.ANY)] * count,
        out_specs=[pl.BlockSpec(memory_space=pl.ANY)] * count,
        scratch_shapes=[
            pltpu.SemaphoreType.DMA((count, slots)),
            pltpu.SemaphoreType.DMA((count, slots)),
            pltpu.SemaphoreType.DMA((count,)),
        ],
        compiler_params=pltpu.CompilerParams(collective_id=collective_id, has_side_effects=True),
        name=name,
    )(*[item[1] for item in items])


def gathered(axis, array, devices):
    shape = jax.ShapeDtypeStruct((devices,) + array.shape, array.dtype)
    return (axis, array, shape, lambda ref, peer: ref, lambda ref, here: ref.at[here])


def traded(axis, array):
    shape = jax.ShapeDtypeStruct(array.shape, array.dtype)
    return (axis, array, shape, lambda ref, peer: ref.at[peer], lambda ref, here: ref.at[here])


def pick_rows(table, index_ref, start, count):
    return jnp.concatenate(
        [table[pl.ds(index_ref[start + row], 1), :] for row in range(count)], axis=0
    )


def across(column):
    return jnp.broadcast_to(column, (128, 128)).T


def down(row):
    return jnp.broadcast_to(row, (128, 128)).T


def dot(a, b, contract):
    return lax.dot_general(a, b, (contract, ((), ())), preferred_element_type=jnp.float32)


def window_masks():
    query = lax.broadcasted_iota(jnp.int32, (128, 128), 0) // BLOCK
    key = lax.broadcasted_iota(jnp.int32, (128, 128), 1) // BLOCK
    return (query == 0) & (key == 1), key <= query


def key_scales(keys):
    rows = keys.astype(jnp.float32)
    mean_square = jnp.mean(rows * rows, axis=-1, keepdims=True) + 1e-06
    return rows, mean_square, lax.rsqrt(mean_square) / HEAD_DIM


def masked_scores(raw, scale, query_pos, key_pos, inside):
    scores = jnp.where(
        key_pos > query_pos, LATER, jnp.where(key_pos == query_pos, SELF, raw * scale)
    )
    return jnp.where(inside, scores, OUTSIDE)


def attend_kernel(
    tiles, order, place, order_rows, shared, values, shared_sorted, values_sorted, total_sorted,
    mixed_home, total_home, table, mixed, scales,
):
    def load(tile, carry):
        rows = pl.ds(pl.multiple_of(tile * 128, 128), 128)
        table[rows, :128] = shared[rows, :].astype(jnp.float32)
        table[rows, 128:] = values[rows, :].astype(jnp.float32)
        return carry

    lax.fori_loop(0, tiles, load, 0)

    def sort(step, carry):
        start = pl.multiple_of(step * 32, 32)
        picked = pick_rows(table, order, start, 32).astype(jnp.bfloat16)
        shared_sorted[pl.ds(start, 32), :] = picked[:, :128]
        values_sorted[pl.ds(start, 32), :] = picked[:, 128:]
        return carry

    lax.fori_loop(0, tiles * 4, sort, 0)
    inside_left, inside_here = window_masks()
    scales[0] = across(key_scales(shared_sorted[(tiles - 1) * 128 :, :])[2])

    def attend_tile(tile, carry):
        left = lax.rem(tile + tiles - 1, tiles)
        rows = pl.ds(pl.multiple_of(tile * 128, 128), 128)
        rows_left = pl.ds(pl.multiple_of(left * 128, 128), 128)
        here, before = shared_sorted[rows, :], shared_sorted[rows_left, :]
        scale_left = scales[0]
        scale_here = across(key_scales(here)[2])
        scales[0] = scale_here
        pos_here, pos_left = order_rows[pl.ds(tile, 1), :], order_rows[pl.ds(left, 1), :]
        query_pos = down(pos_here)
        score_left = masked_scores(
            dot(here, before, ((1,), (1,))), scale_left, query_pos, pos_left, inside_left
        )
        score_here = masked_scores(
            dot(here, here, ((1,), (1,))), scale_here, query_pos, pos_here, inside_here
        )
        highest = jnp.maximum(
            jnp.max(score_left, axis=-1, keepdims=True), jnp.max(score_here, axis=-1, keepdims=True)
        )
        total = highest + jnp.log(
            jnp.sum(jnp.exp(score_left - highest) + jnp.exp(score_here - highest), axis=-1, keepdims=True)
        )
        prob_left = jnp.exp(score_left - total).astype(jnp.bfloat16)
        prob_here = jnp.exp(score_here - total).astype(jnp.bfloat16)
        mixed[rows, :128] = dot(prob_left, values_sorted[rows_left, :], ((1,), (0,))) + dot(
            prob_here, values_sorted[rows, :], ((1,), (0,))
        )
        total = jnp.broadcast_to(total, (128, 128))
        mixed[rows, 128:] = total
        total_sorted[rows, :] = total
        return carry

    lax.fori_loop(0, tiles, attend_tile, 0)

    def unsort(tile, carry):
        totals = []
        for part in range(4):
            start = pl.multiple_of(tile * 128 + part * 32, 32)
            picked = pick_rows(mixed, place, start, 32)
            mixed_home[pl.ds(start, 32), :] = picked[:, :128].astype(jnp.bfloat16)
            totals.append(picked[:, 128:])
        total_home[lax.rem(tile, 8), pl.ds(tile // 8, 1), :] = jnp.concatenate(totals, axis=0).T[:1, :]
        return carry

    lax.fori_loop(0, tiles, unsort, 0)


def attend_back_kernel(
    tiles, order, place, order_rows, shared_sorted, values_sorted, total_sorted, grad_mixed, grad_total,
    grad_shared_home, grad_values_home, table, grad_sorted, grad_total_sorted, scales, scale_sums, sums,
):
    def load(tile, carry):
        rows = pl.ds(pl.multiple_of(tile * 128, 128), 128)
        table[rows, :128] = grad_mixed[rows, :].astype(jnp.float32)
        table[rows, 128:] = down(grad_total[lax.rem(tile, 8), pl.ds(tile // 8, 1), :])
        sums[rows, :] = jnp.zeros((128, 256), jnp.float32)
        return carry

    lax.fori_loop(0, tiles, load, 0)

    def sort(step, carry):
        start = pl.multiple_of(step * 32, 32)
        picked = pick_rows(table, order, start, 32)
        grad_sorted[pl.ds(start, 32), :] = picked[:, :128].astype(jnp.bfloat16)
        grad_total_sorted[pl.ds(start, 32), :] = picked[:, 128:]
        return carry

    lax.fori_loop(0, tiles * 4, sort, 0)
    inside_left, inside_here = window_masks()
    scales[0] = across(key_scales(shared_sorted[(tiles - 1) * 128 :, :])[2])
    scale_sums[...] = jnp.zeros_like(scale_sums)

    def back_tile(tile, carry):
        left = lax.rem(tile + tiles - 1, tiles)
        rows = pl.ds(pl.multiple_of(tile * 128, 128), 128)
        rows_left = pl.ds(pl.multiple_of(left * 128, 128), 128)
        here, before = shared_sorted[rows, :], shared_sorted[rows_left, :]
        scale_left = scales[0]
        scale_here = across(key_scales(here)[2])
        scales[0] = scale_here
        pos_here, pos_left = order_rows[pl.ds(tile, 1), :], order_rows[pl.ds(left, 1), :]
        query_pos = down(pos_here)
        raw_left = dot(here, before, ((1,), (1,)))
        raw_here = dot(here, here, ((1,), (1,)))
        total = total_sorted[rows, :]
        prob_left = jnp.exp(
            masked_scores(raw_left, scale_left, query_pos, pos_left, inside_left) - total
        )
        prob_here = jnp.exp(
            masked_scores(raw_here, scale_here, query_pos, pos_here, inside_here) - total
        )
        grad = grad_sorted[rows, :]
        grad_prob_left = dot(grad, values_sorted[rows_left, :], ((1,), (1,)))
        grad_prob_here = dot(grad, values_sorted[rows, :], ((1,), (1,)))
        inner = jnp.sum(
            prob_left * grad_prob_left + prob_here * grad_prob_here, axis=-1, keepdims=True
        )
        shift = grad_total_sorted[rows, :] - inner
        keep_left = inside_left & (pos_left < query_pos)
        keep_here = inside_here & (pos_here < query_pos)
        grad_score_left = jnp.where(keep_left, prob_left * (grad_prob_left + shift), 0.0)
        grad_score_here = jnp.where(keep_here, prob_here * (grad_prob_here + shift), 0.0)
        scale_sums[pl.ds(left, 1), :] += jnp.sum(grad_score_left * raw_left, axis=0, keepdims=True)
        scale_sums[pl.ds(tile, 1), :] += jnp.sum(grad_score_here * raw_here, axis=0, keepdims=True)
        grad_raw_left = (grad_score_left * scale_left).astype(jnp.bfloat16)
        grad_raw_here = (grad_score_here * scale_here).astype(jnp.bfloat16)
        sums[rows, :128] += (
            dot(grad_raw_left, before, ((1,), (0,)))
            + dot(grad_raw_here, here, ((1,), (0,)))
            + dot(grad_raw_here, here, ((0,), (0,)))
        )
        sums[rows_left, :128] += dot(grad_raw_left, here, ((0,), (0,)))
        sums[rows, 128:] += dot(prob_here.astype(jnp.bfloat16), grad, ((0,), (0,)))
        sums[rows_left, 128:] += dot(prob_left.astype(jnp.bfloat16), grad, ((0,), (0,)))
        return carry

    lax.fori_loop(0, tiles, back_tile, 0)

    def finish(tile, carry):
        rows = pl.ds(pl.multiple_of(tile * 128, 128), 128)
        keys, mean_square, scale = key_scales(shared_sorted[rows, :])
        factor = down(scale_sums[pl.ds(tile, 1), :]) * (scale / (mean_square * HEAD_DIM))
        sums[rows, :128] -= factor * keys
        return carry

    lax.fori_loop(0, tiles, finish, 0)

    def unsort(step, carry):
        start = pl.multiple_of(step * 32, 32)
        picked = pick_rows(sums, place, start, 32).astype(jnp.bfloat16)
        grad_shared_home[pl.ds(start, 32), :] = picked[:, :128]
        grad_values_home[pl.ds(start, 32), :] = picked[:, 128:]
        return carry

    lax.fori_loop(0, tiles * 4, unsort, 0)


VMEM = pl.BlockSpec(memory_space=pltpu.VMEM)
SMEM = pl.BlockSpec(memory_space=pltpu.SMEM)


def attend_head(order, place, order_rows, shared, values):
    length = shared.shape[0]
    rows = jax.ShapeDtypeStruct((length, HEAD_DIM), jnp.bfloat16)
    return pl.pallas_call(
        functools.partial(attend_kernel, length // 128),
        out_shape=[
            rows,
            rows,
            jax.ShapeDtypeStruct((length, HEAD_DIM), jnp.float32),
            rows,
            jax.ShapeDtypeStruct((8, 8, 128), jnp.float32),
        ],
        in_specs=[SMEM, SMEM, VMEM, VMEM, VMEM],
        out_specs=[VMEM] * 5,
        scratch_shapes=[
            pltpu.VMEM((length, 256), jnp.float32),
            pltpu.VMEM((length, 256), jnp.float32),
            pltpu.VMEM((1, 128, 128), jnp.float32),
        ],
        compiler_params=pltpu.CompilerParams(vmem_limit_bytes=40 << 20),
        name="attend",
    )(order, place, order_rows, shared, values)


def attend_head_back(order, place, order_rows, shared_sorted, values_sorted, total_sorted, grad, grad_total):
    length = grad.shape[0]
    rows = jax.ShapeDtypeStruct((length, HEAD_DIM), jnp.bfloat16)
    return pl.pallas_call(
        functools.partial(attend_back_kernel, length // 128),
        out_shape=[rows, rows],
        in_specs=[SMEM, SMEM] + [VMEM] * 6,
        out_specs=[VMEM] * 2,
        scratch_shapes=[
            pltpu.VMEM((length, 256), jnp.float32),
            pltpu.VMEM((length, HEAD_DIM), jnp.bfloat16),
            pltpu.VMEM((length, HEAD_DIM), jnp.float32),
            pltpu.VMEM((1, 128, 128), jnp.float32),
            pltpu.VMEM((length // 128, 128), jnp.float32),
            pltpu.VMEM((length, 256), jnp.float32),
        ],
        compiler_params=pltpu.CompilerParams(vmem_limit_bytes=40 << 20),
        name="attend_back",
    )(order, place, order_rows, shared_sorted, values_sorted, total_sorted, grad, grad_total)


def matmul(a, b, contract=((1,), (0,))):
    return dot(a, b, contract)


def plane_plan(
    n_seq,
    n_sub,
    first_half,
    second_half,
    grad_first,
    grad_second,
    attend_gain,
    attend_shift,
    query_key_weight,
    value_projection_weight,
    output_projection_weight,
    feed_gain,
    feed_shift,
    upper_projection_weight,
    upper_projection_bias,
    lower_projection_weight,
    lower_projection_bias,
    sort_order,
    sort_place,
):
    low, full = jnp.bfloat16, jnp.float32
    devices, planes, per_plane = n_seq * n_sub, n_seq // 2, 2 * n_sub
    rows, width = first_half.shape[1:]
    hidden = upper_projection_weight.shape[2]
    tokens = devices * rows
    line = planes * rows
    part = hidden // per_plane
    seq, sub = lax.axis_index("seq"), lax.axis_index("sub")
    me_p = lax.rem(seq, 2) * n_sub + sub
    trade = functools.partial(exchange, n_seq=n_seq, n_sub=n_sub)
    shape = jax.ShapeDtypeStruct
    x1, x2, g1, g2 = (a[0] for a in (first_half, second_half, grad_first, grad_second))
    wqk, wv, wo = query_key_weight[0], value_projection_weight[0], output_projection_weight[0]
    wup, wdown = upper_projection_weight[0], lower_projection_weight[0]
    own = width // devices
    pair = 2 * HEAD_DIM

    def row_of(*vectors):
        return jnp.concatenate([v[0].astype(full) for v in vectors])[None]

    small = jnp.concatenate(
        [
            sort_order[0, :, 0].astype(full),
            sort_place[0, :, 0].astype(full),
            row_of(attend_gain, attend_shift, feed_gain, feed_shift),
            row_of(upper_projection_bias),
            jnp.pad(row_of(lower_projection_bias), ((0, 5), (0, rows - own))),
        ],
        axis=0,
    )
    small = jnp.pad(small, ((0, 16 - small.shape[0]), (0, 0)))

    def columns(array):
        return (
            "z",
            array,
            shape((planes, own, pair), low),
            lambda ref, peer: ref.at[:, pl.ds(pl.multiple_of(peer * pair, pair), pair)],
            lambda ref, here: ref.at[here],
        )

    def upper_part(chunk):
        return (
            "plane",
            wup,
            shape((per_plane, own, rows), low),
            lambda ref, peer: ref.at[
                :, pl.ds(pl.multiple_of((chunk * per_plane + peer) * rows, rows), rows)
            ],
            lambda ref, here: ref.at[here],
        )

    all_small, wqk_line, wv_line, *wup_rows = trade(
        [gathered("all", small, devices), columns(wqk), columns(wv)]
        + [upper_part(chunk) for chunk in range(planes)],
        "share_small",
        1,
    )
    wup_rows = jnp.concatenate([a.reshape(per_plane * own, rows) for a in wup_rows], axis=1)
    gain_a, shift_a, gain_f, shift_f = (
        all_small[:, 8, k * own : (k + 1) * own].reshape(width) for k in range(4)
    )
    bias_down = all_small[:, 10, :own].reshape(width)
    bias_up = jnp.take(
        all_small[:, 9].reshape(planes, per_plane, rows), me_p, axis=1
    ).reshape(planes * rows)
    order_rows = jnp.take(all_small[:, :4], sub, axis=1)
    order = order_rows.astype(jnp.int32).reshape(tokens)
    place = jnp.take(all_small[:, 4:8], sub, axis=1).astype(jnp.int32).reshape(tokens)

    normed, attend_pull = jax.vjp(layer_norm, x2, gain_a, shift_a)
    normed = normed.astype(low)

    def rows_over_plane(array):
        return (
            "plane",
            array,
            shape((planes, per_plane) + array.shape[1:], low),
            lambda ref, peer: ref,
            lambda ref, here: ref.at[:, here],
        )

    normed_line, wqk_pair, wv_pair, wo_pair = trade(
        [
            gathered("z", normed, planes),
            rows_over_plane(wqk_line),
            rows_over_plane(wv_line),
            gathered("plane", wo, per_plane),
        ],
        "share_normed",
        2,
    )
    normed_line = normed_line.reshape(line, width)
    wqk_pair, wv_pair = wqk_pair.reshape(width, pair), wv_pair.reshape(width, pair)
    wo_pair = wo_pair.reshape(pair, width)
    shared = matmul(normed_line, wqk_pair).astype(low).reshape(planes, rows, pair)
    values = matmul(normed_line, wv_pair).astype(low).reshape(planes, rows, pair)

    def to_head(array):
        return (
            "plane",
            array,
            shape((planes, per_plane, rows, HEAD_DIM), low),
            lambda ref, peer: ref.at[
                :, :, pl.ds(pl.multiple_of((peer // n_sub) * HEAD_DIM, HEAD_DIM), HEAD_DIM)
            ],
            lambda ref, here: ref.at[:, here],
        )

    head_shared, head_values, wup_part = trade(
        [to_head(shared), to_head(values), gathered("z", wup_rows, planes)], "to_heads", 3
    )
    wup_part = wup_part.reshape(width, part)
    shared_sorted, values_sorted, total_sorted, mixed, total = attend_head(
        order,
        place,
        order_rows,
        head_shared.reshape(tokens, HEAD_DIM),
        head_values.reshape(tokens, HEAD_DIM),
    )

    def to_tokens(array):
        array = array.reshape(planes, per_plane, rows, HEAD_DIM)
        return (
            "plane",
            array,
            shape((per_plane, planes, rows, HEAD_DIM), low),
            lambda ref, peer: ref.at[:, peer],
            lambda ref, here: ref.at[here],
        )

    mixed, total = trade([to_tokens(mixed), traded("plane", total)], "heads_out", 4)
    mixed = mixed.reshape(2, n_sub, line, HEAD_DIM).astype(full)
    total = total[:, :planes].reshape(2, n_sub, line)
    weights = jnp.exp(total - jnp.max(total, axis=1, keepdims=True))
    weights = weights / jnp.sum(weights, axis=1, keepdims=True)
    attended = jnp.sum(weights[..., None] * mixed, axis=1)
    attended = jnp.swapaxes(attended, 0, 1).reshape(line, pair).astype(low)
    y1_parts = matmul(attended, wo_pair).astype(low).reshape(planes, rows, width)

    df = g2.astype(low)
    y1_parts, df_plane = trade(
        [traded("z", y1_parts), gathered("plane", df, per_plane)], "sum_first", 5
    )
    y1 = x1 + jnp.sum(y1_parts.astype(full), axis=0)
    h2, feed_pull = jax.vjp(layer_norm, y1, gain_f, shift_f)
    h2_plane, wdown_part = trade(
        [gathered("plane", h2.astype(low), per_plane), gathered("z", wdown, planes)], "share_feed", 6
    )
    h2_plane = h2_plane.reshape(per_plane * rows, width)
    df_plane = df_plane.reshape(per_plane * rows, width)
    wdown_part = wdown_part.reshape(part, width)
    pre = matmul(h2_plane, wup_part) + bias_up
    act, act_pull = jax.vjp(gelu_exact, pre)
    act = act.astype(low)
    y2_parts = matmul(act, wdown_part).astype(low).reshape(per_plane, rows, width)
    dpre = act_pull(matmul(df_plane, wdown_part, ((1,), (1,))))[0].astype(low)
    dh2_parts = matmul(dpre, wup_part, ((1,), (1,))).astype(low).reshape(per_plane, rows, width)
    down_grad = matmul(act, df_plane, ((0,), (0,))).astype(low).reshape(planes, rows, width)
    up_grad = matmul(h2_plane, dpre, ((0,), (0,))).astype(low).reshape(planes, width // planes, part)
    up_bias_grad = jnp.sum(dpre.astype(full), axis=0)
    down_bias_grad = jnp.sum(df.astype(full), axis=0)

    dh2_parts, up_grad = trade([traded("plane", dh2_parts), traded("z", up_grad)], "sum_feed_grad", 7)
    one_part, feed_gain_grad, feed_shift_grad = feed_pull(jnp.sum(dh2_parts.astype(full), axis=0))
    g1 = g1 + one_part
    up_grad = jnp.sum(up_grad.astype(full), axis=0).reshape(per_plane, own, part)

    dout_line, y2_parts = trade(
        [gathered("z", g1.astype(low), planes), traded("plane", y2_parts)], "share_out_grad", 8
    )
    y2 = x2 + (jnp.sum(y2_parts.astype(full), axis=0) + bias_down)
    dout_line = dout_line.reshape(line, width)
    datt = matmul(dout_line, wo_pair, ((1,), (1,))).reshape(line, 2, HEAD_DIM)
    datt = jnp.swapaxes(datt, 0, 1)[:, None]
    out_grad = matmul(attended, dout_line, ((0,), (0,))).astype(low).reshape(per_plane, own, width)
    dweights = jnp.sum(datt * mixed, axis=-1)
    dmixed = (weights[..., None] * datt).astype(low).reshape(per_plane, planes, rows, HEAD_DIM)
    dtotal = weights * (dweights - jnp.sum(weights * dweights, axis=1, keepdims=True))
    dtotal = dtotal.astype(low).astype(full).reshape(per_plane, planes, rows)
    dtotal = jnp.pad(dtotal, ((0, 0), (0, 8 - planes), (0, 0)))
    back_to_heads = (
        "plane",
        dmixed,
        shape((planes, per_plane, rows, HEAD_DIM), low),
        lambda ref, peer: ref.at[peer],
        lambda ref, here: ref.at[:, here],
    )
    dmixed, dtotal, out_grad = trade(
        [back_to_heads, traded("plane", dtotal), traded("plane", out_grad)], "grads_to_heads", 9
    )
    dshared, dvalues = attend_head_back(
        order,
        place,
        order_rows,
        shared_sorted,
        values_sorted,
        total_sorted,
        dmixed.reshape(tokens, HEAD_DIM),
        dtotal,
    )
    dshared, dvalues, down_grad = trade(
        [to_tokens(dshared), to_tokens(dvalues), traded("z", down_grad)], "grads_from_heads", 10
    )

    def over_rounds(array):
        array = jnp.sum(array.reshape(2, n_sub, line, HEAD_DIM).astype(full), axis=1)
        return jnp.swapaxes(array, 0, 1).reshape(line, pair).astype(low)

    dshared, dvalues = over_rounds(dshared), over_rounds(dvalues)
    de_parts = matmul(dshared, wqk_pair, ((1,), (1,))) + matmul(dvalues, wv_pair, ((1,), (1,)))
    de_parts = de_parts.astype(low).reshape(planes, rows, width)

    def to_owners(grad):
        return (
            "plane",
            grad.astype(low).reshape(planes, per_plane, own, pair),
            shape((per_plane, planes, own, pair), low),
            lambda ref, peer: ref.at[:, peer],
            lambda ref, here: ref.at[here],
        )

    de_parts, shared_grad, value_grad, up_grad = trade(
        [
            traded("z", de_parts),
            to_owners(matmul(normed_line, dshared, ((0,), (0,)))),
            to_owners(matmul(normed_line, dvalues, ((0,), (0,)))),
            traded("plane", up_grad),
        ],
        "sum_second_grad",
        11,
    )
    two_part, attend_gain_grad, attend_shift_grad = attend_pull(
        jnp.sum(de_parts.astype(full), axis=0)
    )
    g2 = g2 + two_part
    shared_grad = jnp.sum(shared_grad.astype(full), axis=0)
    value_grad = jnp.sum(value_grad.astype(full), axis=0)
    vectors = [attend_gain_grad, attend_shift_grad, feed_gain_grad, feed_shift_grad]
    vectors = jnp.concatenate([v.reshape(devices, 1, own) for v in vectors], axis=2)
    down_bias_grad = jnp.pad(
        down_bias_grad.reshape(devices, 1, own), ((0, 0), (0, 0), (0, rows - own))
    )
    up_bias_grad = jnp.where(
        jnp.arange(per_plane)[None, :, None] == me_p, up_bias_grad.reshape(planes, 1, rows), 0.0
    ).reshape(devices, 1, rows)
    vectors = jnp.concatenate(
        [vectors, down_bias_grad, up_bias_grad, jnp.zeros((devices, 5, rows), full)], axis=1
    )
    vectors, shared_grad, value_grad = trade(
        [traded("all", vectors), traded("z", shared_grad), traded("z", value_grad)], "sum_small", 12
    )
    vectors = jnp.sum(vectors, axis=0)
    pieces = [vectors[0, k * own : (k + 1) * own] for k in range(4)]
    shared_grad, value_grad = (
        jnp.swapaxes(a, 0, 1).reshape(own, width) for a in (shared_grad, value_grad)
    )
    up_grad = jnp.transpose(up_grad.reshape(per_plane, own, planes, rows), (1, 2, 0, 3))
    outputs = (
        y1,
        y2,
        g1,
        g2,
        pieces[0],
        pieces[1],
        shared_grad,
        value_grad,
        jnp.sum(out_grad.astype(full), axis=0),
        pieces[2],
        pieces[3],
        up_grad.reshape(own, hidden),
        vectors[2],
        jnp.sum(down_grad.astype(full), axis=0),
        vectors[1, :own],
    )
    return tuple((a[None] for a in outputs))


def on_device(n_seq, n_sub, *arguments):
    sequences, rows, width = arguments[0].shape
    rounds = arguments[-1].shape[1]
    fits = (
        sequences == 1
        and rows == 2 * BLOCK
        and rounds == n_sub
        and HEADS == n_seq
        and width == HEADS * HEAD_DIM
    )
    if fits:
        return plane_plan(n_seq, n_sub, *arguments)
    return general_plan(*arguments)


def solution(mesh):
    return jax.shard_map(
        functools.partial(on_device, mesh.shape["seq"], mesh.shape["sub"]),
        mesh=mesh,
        in_specs=(
            P(None, ("seq", "sub"), None),
            P(None, ("seq", "sub"), None),
            P(None, ("seq", "sub"), None),
            P(None, ("seq", "sub"), None),
            P(None, ("seq", "sub")),
            P(None, ("seq", "sub")),
            P(None, ("seq", "sub"), None),
            P(None, ("seq", "sub"), None),
            P(None, ("seq", "sub"), None),
            P(None, ("seq", "sub")),
            P(None, ("seq", "sub")),
            P(None, ("seq", "sub"), None),
            P(None, ("seq", "sub")),
            P(None, ("seq", "sub"), None),
            P(None, ("seq", "sub")),
            P(None, None, None, ("seq", "sub")),
            P(None, None, None, ("seq", "sub")),
        ),
        out_specs=(
            P(None, ("seq", "sub"), None),
            P(None, ("seq", "sub"), None),
            P(None, ("seq", "sub"), None),
            P(None, ("seq", "sub"), None),
            P(None, ("seq", "sub")),
            P(None, ("seq", "sub")),
            P(None, ("seq", "sub"), None),
            P(None, ("seq", "sub"), None),
            P(None, ("seq", "sub"), None),
            P(None, ("seq", "sub")),
            P(None, ("seq", "sub")),
            P(None, ("seq", "sub"), None),
            P(None, ("seq", "sub")),
            P(None, ("seq", "sub"), None),
            P(None, ("seq", "sub")),
        ),
        check_vma=False,
    )
```

```python
import functools

import jax
import jax.numpy as jnp
from jax import lax
from jax.experimental import pallas as pl
from jax.experimental.pallas import tpu as pltpu
from jax.sharding import PartitionSpec as P

HEADS = 8
HEAD_DIM = 128
BLOCK = 64
LATER = -1000000000.0
SELF = -100000.0
OUTSIDE = -3e38


def from_behind(block, axis, distance):
    devices = range(lax.axis_size(axis))
    route = [((i - distance) % len(devices), i) for i in devices]
    return lax.ppermute(block, axis, route)


def layer_norm(value_vectors, scaling, shifts):
    center = jnp.mean(value_vectors, axis=-1, keepdims=True)
    offset = value_vectors - center
    spread = jnp.mean(offset * offset, axis=-1, keepdims=True)
    return offset * lax.rsqrt(spread + 1e-05) * scaling + shifts


def gelu_exact(value_vectors):
    return jax.nn.gelu(value_vectors, approximate=False)


def combine_rounds(outputs, totals):
    highest = jnp.max(totals, axis=0, keepdims=True)
    weights = jnp.exp(totals - highest)
    weights = weights / jnp.sum(weights, axis=0, keepdims=True)
    by_head = outputs.reshape(outputs.shape[:-1] + (totals.shape[-1], -1))
    return jnp.sum(weights[..., None] * by_head, axis=0).reshape(outputs.shape[1:])


def home_slots(places, row_count):
    target = places // row_count
    prior_state = (target[:, None, :] == target[:, :, None]) & (
        places[:, None, :] < places[:, :, None]
    )
    return (target, jnp.sum(prior_state.astype(jnp.int32), axis=2))


def sorted_slots(orders, row_count):
    source = orders // row_count
    ladder = jnp.arange(row_count, dtype=jnp.int32)
    prior_state = (source[:, None, :] == source[:, :, None]) & (
        ladder[None, None, :] < ladder[None, :, None]
    )
    return (source, jnp.sum(prior_state.astype(jnp.int32), axis=2))


def slot_lookup(owners, slot_index, devices, capacity):
    groups, row_count = owners.shape
    flat_index = owners * capacity + slot_index
    lookup = jnp.full((groups, devices * capacity), row_count, jnp.int32)
    filler = jnp.broadcast_to(jnp.arange(row_count, dtype=jnp.int32), (groups, row_count))
    lookup = lookup.at[jnp.arange(groups)[:, None], flat_index].set(filler)
    return jnp.transpose(lookup.reshape(groups, devices, capacity), (1, 0, 2))


def gather_slots(value_vectors, member, lookup):
    padding = jnp.zeros((value_vectors.shape[0], 1) + value_vectors.shape[2:], value_vectors.dtype)
    padded = jnp.concatenate([value_vectors, padding], axis=1)
    return padded[member[None, :, None], lookup]


def settle(received, owners, slot_index):
    return received[owners, jnp.arange(owners.shape[0])[:, None], slot_index]


def build_routes(orders, places, devices, capacity):
    rounds, sequences, row_count = orders.shape
    order_flat = orders.reshape(rounds * sequences, row_count)
    target, home_slot = home_slots(places.reshape(rounds * sequences, row_count), row_count)
    source, sorted_slot = sorted_slots(order_flat, row_count)
    home_lookup = slot_lookup(target, home_slot, devices, capacity)
    back_lookup = slot_lookup(source, sorted_slot, devices, capacity)
    return (target, home_slot, source, sorted_slot, home_lookup, back_lookup, order_flat)


def trade_rows(first_part, second_part):
    return (
        lax.all_to_all(first_part, ("seq", "sub"), split_axis=0, concat_axis=0, tiled=True),
        lax.all_to_all(second_part, ("seq", "sub"), split_axis=0, concat_axis=0, tiled=True),
    )


def trade_results(first_part, second_part):
    return (
        lax.all_to_all(first_part, ("seq", "sub"), split_axis=0, concat_axis=0, tiled=True),
        lax.all_to_all(second_part, ("seq", "sub"), split_axis=0, concat_axis=0, tiled=True),
    )


def window(rows_here, rows_left):
    groups = rows_here.shape[0]
    extended = jnp.concatenate([rows_left, rows_here], axis=1)
    extended = extended.reshape((groups, -1, BLOCK) + rows_here.shape[2:])
    return jnp.concatenate([extended[:, :-1], extended[:, 1:]], axis=2)


def score_parts(shared_rows, order_rows, halo_shared, halo_order):
    groups, row_count, features = shared_rows.shape
    blocks = row_count // BLOCK
    queries = shared_rows.reshape(groups, blocks, BLOCK, HEADS, HEAD_DIM)
    key_rows = window(shared_rows, halo_shared).reshape(groups, blocks, 2 * BLOCK, HEADS, HEAD_DIM)
    key_float = key_rows.astype(jnp.float32)
    mean_square = jnp.mean(key_float * key_float, axis=-1) + 1e-06
    key_scale = lax.rsqrt(mean_square) / HEAD_DIM
    raw_scores = jnp.einsum(
        "gcqhd,gckhd->gchqk", queries, key_rows, preferred_element_type=jnp.float32
    )
    query_pos = order_rows.reshape(groups, blocks, BLOCK)
    key_pos = window(order_rows, halo_order)
    is_later = (key_pos[:, :, None, :] > query_pos[:, :, :, None])[:, :, None]
    is_self = (key_pos[:, :, None, :] == query_pos[:, :, :, None])[:, :, None]
    scale_row = jnp.transpose(key_scale, (0, 1, 3, 2))[:, :, :, None, :]
    scores = jnp.where(
        is_later, -1000000000.0, jnp.where(is_self, -100000.0, raw_scores * scale_row)
    )
    highest = jnp.max(scores, axis=-1, keepdims=True)
    log_total = highest + jnp.log(jnp.sum(jnp.exp(scores - highest), axis=-1, keepdims=True))
    probability = jnp.exp(scores - log_total)
    return (
        queries,
        key_rows,
        key_float,
        mean_square,
        key_scale,
        scale_row,
        raw_scores,
        is_later | is_self,
        log_total,
        probability,
    )


def attend(shared_rows, value_rows, order_rows, halo):
    halo_shared, halo_value, halo_order = halo
    parts = score_parts(shared_rows, order_rows, halo_shared, halo_order)
    groups, row_count, features = shared_rows.shape
    value_keys = window(value_rows, halo_value).reshape(
        groups, row_count // BLOCK, 2 * BLOCK, HEADS, HEAD_DIM
    )
    mixed = jnp.einsum(
        "gchqk,gckhd->gcqhd",
        parts[9].astype(jnp.bfloat16),
        value_keys,
        preferred_element_type=jnp.float32,
    )
    log_total = jnp.transpose(parts[8][..., 0], (0, 1, 3, 2)).reshape(groups, row_count, HEADS)
    return (mixed.reshape(groups, row_count, features), log_total)


def fold_window(grads_window, groups, row_count, features):
    grads_window = grads_window.reshape(groups, row_count // BLOCK, 2 * BLOCK, features)
    empty = jnp.zeros((groups, 1, BLOCK, features), jnp.float32)
    extended = jnp.concatenate([grads_window[:, :, :BLOCK], empty], axis=1) + jnp.concatenate(
        [empty, grads_window[:, :, BLOCK:]], axis=1
    )
    return (extended[:, 1:].reshape(groups, row_count, features), extended[:, 0])


def attend_back(shared_rows, value_rows, order_rows, halo, grad_out, grad_total):
    halo_shared, halo_value, halo_order = halo
    (
        queries,
        key_rows,
        key_float,
        mean_square,
        key_scale,
        scale_row,
        raw_scores,
        masked,
        log_total,
        probability,
    ) = score_parts(shared_rows, order_rows, halo_shared, halo_order)
    groups, row_count, features = shared_rows.shape
    blocks = row_count // BLOCK
    value_keys = window(value_rows, halo_value).reshape(groups, blocks, 2 * BLOCK, HEADS, HEAD_DIM)
    prob_low = probability.astype(jnp.bfloat16)
    grad_heads = grad_out.reshape(groups, blocks, BLOCK, HEADS, HEAD_DIM)
    grad_log = jnp.transpose(
        grad_total.astype(jnp.float32).reshape(groups, blocks, BLOCK, HEADS), (0, 1, 3, 2)
    )[..., None]
    grad_prob = jnp.einsum(
        "gcqhd,gckhd->gchqk", grad_heads, value_keys, preferred_element_type=jnp.float32
    )
    inner = jnp.sum(probability * grad_prob, axis=-1, keepdims=True)
    grad_score = jnp.where(masked, 0.0, probability * (grad_prob - inner + grad_log))
    grad_scale = jnp.transpose(jnp.sum(grad_score * raw_scores, axis=3), (0, 1, 3, 2))
    grad_raw = (grad_score * scale_row).astype(jnp.bfloat16)
    grad_query = jnp.einsum(
        "gchqk,gckhd->gcqhd", grad_raw, key_rows, preferred_element_type=jnp.float32
    )
    grad_key = jnp.einsum(
        "gchqk,gcqhd->gckhd", grad_raw, queries, preferred_element_type=jnp.float32
    )
    grad_key = grad_key - (grad_scale * key_scale / mean_square)[..., None] * key_float / HEAD_DIM
    grad_value = jnp.einsum(
        "gchqk,gcqhd->gckhd", prob_low, grad_heads, preferred_element_type=jnp.float32
    )
    key_home, key_left = fold_window(grad_key, groups, row_count, features)
    value_home, value_left = fold_window(grad_value, groups, row_count, features)
    back_key, back_value = from_behind((key_left, value_left), ("seq", "sub"), -1)
    grad_shared = grad_query.reshape(groups, row_count, features) + key_home
    grad_shared = grad_shared.at[:, row_count - BLOCK :].add(back_key)
    grad_values = value_home.at[:, row_count - BLOCK :].add(back_value)
    return (grad_shared, grad_values)


def sorted_attention(shared_query_key, value_vectors, routes):
    target, home_slot, source, sorted_slot, home_lookup, back_lookup, order_flat = routes
    groups = target.shape[0]
    member = jnp.arange(groups) % shared_query_key.shape[0]
    got_shared, got_values = trade_rows(
        gather_slots(shared_query_key, member, home_lookup),
        gather_slots(value_vectors, member, home_lookup),
    )
    shared_rows = settle(got_shared, source, sorted_slot)
    value_rows = settle(got_values, source, sorted_slot)
    halo = from_behind(
        (shared_rows[:, -BLOCK:], value_rows[:, -BLOCK:], order_flat[:, -BLOCK:]), ("seq", "sub"), 1
    )
    mixed, log_total = attend(shared_rows, value_rows, order_flat, halo)
    all_groups = jnp.arange(groups)
    got_mixed, got_total = trade_results(
        gather_slots(mixed, all_groups, back_lookup),
        gather_slots(log_total, all_groups, back_lookup),
    )
    return (
        settle(got_mixed, target, home_slot),
        settle(got_total, target, home_slot),
        (shared_rows, value_rows, halo),
    )


def round_outputs(normalized_input, query_key_weight, value_projection_weight, routes, rounds):
    shared_query_key = jnp.einsum(
        "srd,de->sre", normalized_input, query_key_weight, preferred_element_type=jnp.float32
    ).astype(jnp.bfloat16)
    value_vectors = jnp.einsum(
        "srd,de->sre", normalized_input, value_projection_weight, preferred_element_type=jnp.float32
    ).astype(jnp.bfloat16)
    mixed, log_total, kept = sorted_attention(shared_query_key, value_vectors, routes)
    sequences, row_count, features = normalized_input.shape
    outputs = mixed.reshape(rounds, sequences, row_count, features)
    totals = log_total.reshape(rounds, sequences, row_count, HEADS)
    return (shared_query_key, value_vectors, outputs, totals, kept)


def collect(weight_stack, layer_index):
    (
        attend_gain,
        attend_shift,
        query_key_weight,
        value_projection_weight,
        output_projection_weight,
        feed_gain,
        feed_shift,
        upper_projection_weight,
        upper_projection_bias,
        lower_projection_weight,
        lower_projection_bias,
    ) = tuple((shard_piece[layer_index] for shard_piece in weight_stack))
    return (
        lax.all_gather(attend_gain, ("seq", "sub"), axis=0, tiled=True),
        lax.all_gather(attend_shift, ("seq", "sub"), axis=0, tiled=True),
        lax.all_gather(query_key_weight, ("seq", "sub"), axis=0, tiled=True),
        lax.all_gather(value_projection_weight, ("seq", "sub"), axis=0, tiled=True),
        lax.all_gather(output_projection_weight, ("seq", "sub"), axis=0, tiled=True),
        lax.all_gather(feed_gain, ("seq", "sub"), axis=0, tiled=True),
        lax.all_gather(feed_shift, ("seq", "sub"), axis=0, tiled=True),
        lax.all_gather(upper_projection_weight, ("seq", "sub"), axis=0, tiled=True),
        lax.all_gather(upper_projection_bias, ("seq", "sub"), axis=0, tiled=True),
        lax.all_gather(lower_projection_weight, ("seq", "sub"), axis=0, tiled=True),
        lax.all_gather(lower_projection_bias, ("seq", "sub"), axis=0, tiled=True),
    )


def spread_grads(level_grads):
    (
        attend_gain,
        attend_shift,
        query_key_weight,
        value_projection_weight,
        output_projection_weight,
        feed_gain,
        feed_shift,
        upper_projection_weight,
        upper_projection_bias,
        lower_projection_weight,
        lower_projection_bias,
    ) = level_grads
    return (
        lax.psum_scatter(attend_gain, ("seq", "sub"), scatter_dimension=0, tiled=True),
        lax.psum_scatter(attend_shift, ("seq", "sub"), scatter_dimension=0, tiled=True),
        lax.psum_scatter(query_key_weight.astype(jnp.bfloat16), ("seq", "sub"), scatter_dimension=0, tiled=True),
        lax.psum_scatter(value_projection_weight.astype(jnp.bfloat16), ("seq", "sub"), scatter_dimension=0, tiled=True),
        lax.psum_scatter(output_projection_weight.astype(jnp.bfloat16), ("seq", "sub"), scatter_dimension=0, tiled=True),
        lax.psum_scatter(feed_gain, ("seq", "sub"), scatter_dimension=0, tiled=True),
        lax.psum_scatter(feed_shift, ("seq", "sub"), scatter_dimension=0, tiled=True),
        lax.psum_scatter(upper_projection_weight.astype(jnp.bfloat16), ("seq", "sub"), scatter_dimension=0, tiled=True),
        lax.psum_scatter(upper_projection_bias, ("seq", "sub"), scatter_dimension=0, tiled=True),
        lax.psum_scatter(lower_projection_weight.astype(jnp.bfloat16), ("seq", "sub"), scatter_dimension=0, tiled=True),
        lax.psum_scatter(lower_projection_bias, ("seq", "sub"), scatter_dimension=0, tiled=True),
    )


def layer_pass(first_half, second_half, grad_one, grad_two, params, routes, rounds):
    (
        attend_gain,
        attend_shift,
        query_key_weight,
        value_projection_weight,
        output_projection_weight,
        feed_gain,
        feed_shift,
        upper_projection_weight,
        upper_projection_bias,
        lower_projection_weight,
        lower_projection_bias,
    ) = params
    attend_norm, attend_pull = jax.vjp(
        layer_norm, second_half, attend_gain.astype(jnp.float32), attend_shift.astype(jnp.float32)
    )
    normalized_input = attend_norm.astype(jnp.bfloat16)
    shared_query_key, value_vectors, outputs, totals, kept = round_outputs(
        normalized_input, query_key_weight, value_projection_weight, routes, rounds
    )
    attention_result, combine_pull = jax.vjp(combine_rounds, outputs, totals)
    attended_low = attention_result.astype(jnp.bfloat16)
    top_one = first_half + jnp.einsum(
        "srd,de->sre", attended_low, output_projection_weight, preferred_element_type=jnp.float32
    )
    feed_norm, feed_pull = jax.vjp(
        layer_norm, top_one, feed_gain.astype(jnp.float32), feed_shift.astype(jnp.float32)
    )
    feed_forward_input = feed_norm.astype(jnp.bfloat16)
    prior_state = jnp.einsum(
        "srd,df->srf",
        feed_forward_input,
        upper_projection_weight,
        preferred_element_type=jnp.float32,
    ) + upper_projection_bias.astype(jnp.float32)
    hidden_activation, active_pull = jax.vjp(gelu_exact, prior_state)
    active_low = hidden_activation.astype(jnp.bfloat16)
    feed_out = jnp.einsum(
        "srf,fd->srd", active_low, lower_projection_weight, preferred_element_type=jnp.float32
    ) + lower_projection_bias.astype(jnp.float32)
    top_two = second_half + feed_out
    feed_grad = grad_two.astype(jnp.bfloat16)
    down_weight_grad = jnp.einsum(
        "srf,srd->fd", active_low, feed_grad, preferred_element_type=jnp.float32
    )
    down_bias_grad = jnp.sum(feed_grad.astype(jnp.float32), axis=(0, 1))
    active_grad = jnp.einsum(
        "srd,fd->srf", feed_grad, lower_projection_weight, preferred_element_type=jnp.float32
    )
    before_grad = active_pull(active_grad)[0].astype(jnp.bfloat16)
    up_weight_grad = jnp.einsum(
        "srd,srf->df", feed_forward_input, before_grad, preferred_element_type=jnp.float32
    )
    up_bias_grad = jnp.sum(before_grad.astype(jnp.float32), axis=(0, 1))
    norm_grad = jnp.einsum(
        "srf,df->srd", before_grad, upper_projection_weight, preferred_element_type=jnp.float32
    )
    one_part, feed_gain_grad, feed_shift_grad = feed_pull(norm_grad)
    total_one = grad_one + one_part
    out_grad = total_one.astype(jnp.bfloat16)
    output_weight_grad = jnp.einsum(
        "srd,sre->de", attended_low, out_grad, preferred_element_type=jnp.float32
    )
    attended_grad = jnp.einsum(
        "sre,de->srd", out_grad, output_projection_weight, preferred_element_type=jnp.float32
    )
    outputs_grad, totals_grad = combine_pull(attended_grad)
    target, home_slot, source, sorted_slot, home_lookup, back_lookup, order_flat = routes
    sequences, row_count, features = top_one.shape
    groups = rounds * sequences
    all_groups = jnp.arange(groups)
    outputs_low = outputs_grad.astype(jnp.bfloat16).reshape(groups, row_count, features)
    totals_low = totals_grad.astype(jnp.bfloat16).reshape(groups, row_count, HEADS)
    got_out, got_total = trade_rows(
        gather_slots(outputs_low, all_groups, home_lookup),
        gather_slots(totals_low, all_groups, home_lookup),
    )
    shared_rows, value_rows, halo = kept
    grad_shared, grad_values = attend_back(
        shared_rows,
        value_rows,
        order_flat,
        halo,
        settle(got_out, source, sorted_slot),
        settle(got_total, source, sorted_slot),
    )
    home_shared, home_values = trade_rows(
        gather_slots(grad_shared.astype(jnp.bfloat16), all_groups, back_lookup),
        gather_slots(grad_values.astype(jnp.bfloat16), all_groups, back_lookup),
    )
    shared_grad = jnp.sum(
        settle(home_shared, target, home_slot)
        .astype(jnp.float32)
        .reshape(rounds, sequences, row_count, features),
        axis=0,
    ).astype(jnp.bfloat16)
    values_grad = jnp.sum(
        settle(home_values, target, home_slot)
        .astype(jnp.float32)
        .reshape(rounds, sequences, row_count, features),
        axis=0,
    ).astype(jnp.bfloat16)
    shared_weight_grad = jnp.einsum(
        "srd,sre->de", normalized_input, shared_grad, preferred_element_type=jnp.float32
    )
    value_weight_grad = jnp.einsum(
        "srd,sre->de", normalized_input, values_grad, preferred_element_type=jnp.float32
    )
    normed_grad = jnp.einsum(
        "sre,de->srd", shared_grad, query_key_weight, preferred_element_type=jnp.float32
    ) + jnp.einsum(
        "sre,de->srd", values_grad, value_projection_weight, preferred_element_type=jnp.float32
    )
    two_part, attend_gain_grad, attend_shift_grad = attend_pull(normed_grad)
    total_two = grad_two + two_part
    level_grads = (
        attend_gain_grad,
        attend_shift_grad,
        shared_weight_grad,
        value_weight_grad,
        output_weight_grad,
        feed_gain_grad,
        feed_shift_grad,
        up_weight_grad,
        up_bias_grad,
        down_weight_grad,
        down_bias_grad,
    )
    return (top_one, top_two, total_one, total_two, level_grads)


def general_plan(
    first_half,
    second_half,
    grad_first,
    grad_second,
    attend_gain,
    attend_shift,
    query_key_weight,
    value_projection_weight,
    output_projection_weight,
    feed_gain,
    feed_shift,
    upper_projection_weight,
    upper_projection_bias,
    lower_projection_weight,
    lower_projection_bias,
    sort_order,
    sort_place,
):
    weight_stack = (
        attend_gain,
        attend_shift,
        query_key_weight,
        value_projection_weight,
        output_projection_weight,
        feed_gain,
        feed_shift,
        upper_projection_weight,
        upper_projection_bias,
        lower_projection_weight,
        lower_projection_bias,
    )
    devices = lax.axis_size(("seq", "sub"))
    rounds = sort_order.shape[1]
    row_count = first_half.shape[1]
    capacity = 2 * max(1, row_count // devices)
    params = collect(weight_stack, 0)
    routes = build_routes(sort_order[0], sort_place[0], devices, capacity)
    first_out, second_out, first_grad, second_grad, level_grads = layer_pass(
        first_half, second_half, grad_first, grad_second, params, routes, rounds
    )
    stacked = tuple((entry[None].astype(jnp.float32) for entry in spread_grads(level_grads)))
    return (first_out, second_out, first_grad, second_grad) + stacked


class Links:
    def __init__(self, planes, send, receive, local):
        self.send, self.receive, self.local = send, receive, local
        self.used, self.used_local = 0, 0
        self.planes = planes
        seq, sub = lax.axis_index("seq"), lax.axis_index("sub")
        self.z, self.x = seq // 2, lax.rem(seq, 2)
        self.y, self.core = sub // 2, lax.rem(sub, 2)
        self.p = self.x * 4 + sub

    def near(self, step):
        x = 1 - self.x if step & 4 else self.x
        y = 1 - self.y if step & 2 else self.y
        core = 1 - self.core if step & 1 else self.core
        return (self.z * 2 + x, y * 2 + core), x * 4 + y * 2 + core

    def along(self, step):
        to = lax.rem(self.z + step, self.planes)
        back = lax.rem(self.z + self.planes - step, self.planes)
        return (to * 2 + self.x, self.y * 2 + self.core), to, back

    def greet(self):
        barrier = pltpu.get_barrier_semaphore()
        targets = [self.near(step)[0] for step in range(1, 8)]
        targets += [self.along(step)[0] for step in range(1, self.planes)]
        for target in targets:
            pl.semaphore_signal(barrier, inc=1, device_id=target, device_id_type=pl.DeviceIdType.MESH)
        self.greeted = len(targets)

    def meet(self):
        pl.semaphore_wait(pltpu.get_barrier_semaphore(), self.greeted)

    def push(self, source, target, device):
        copy = pltpu.make_async_remote_copy(
            src_ref=source,
            dst_ref=target,
            send_sem=self.send.at[self.used],
            recv_sem=self.receive.at[self.used],
            device_id=device,
            device_id_type=pl.DeviceIdType.MESH,
        )
        self.used += 1
        copy.start()
        return copy

    def keep(self, source, target):
        copy = pltpu.make_async_copy(source, target, self.local.at[self.used_local])
        self.used_local += 1
        copy.start()
        return copy


COPIES = 96


def link_scratch():
    return [
        pltpu.SemaphoreType.DMA((COPIES,)),
        pltpu.SemaphoreType.DMA((COPIES,)),
        pltpu.SemaphoreType.DMA((16,)),
    ]


def along_z(source, target):
    def transfer(links, here, there):
        own = links.keep(source(here, links.z), target(there, links.z))
        copies = []
        for step in range(1, links.planes):
            device, to, _ = links.along(step)
            copies.append(links.push(source(here, to), target(there, links.z), device))
        yield
        own.wait()
        for copy in copies:
            copy.wait()

    return transfer


def over_plane(source, target):
    def transfer(links, here, there):
        own = links.keep(source(here, links.p), target(there, links.p))
        copies = []
        for step in (6, 7, 4, 5, 2, 3, 1):
            device, to = links.near(step)
            copies.append(links.push(source(here, to), target(there, links.p), device))
        yield
        own.wait()
        for copy in copies:
            copy.wait()

    return transfer


def over_chips(source, target):
    def transfer(links, here, there):
        own = links.keep(source(here, links.p), target(there, links.p))
        copies = []
        for step in (6, 4, 2):
            device, to = links.near(step)
            copies.append(links.push(source(here, to), target(there, links.p), device))
        sibling, _ = links.near(1)
        passed = [links.push(source(here, links.p), target(there, links.p), sibling)]
        yield
        for step, copy in zip((6, 4, 2), copies):
            copy.wait_recv()
            _, sender = links.near(step)
            passed.append(links.push(target(there, sender), target(there, sender), sibling))
        yield
        own.wait()
        for copy in copies:
            copy.wait_send()
        for copy in passed:
            copy.wait()

    return transfer


def everywhere(links, here, there):
    own = links.keep(here, there.at[links.z, links.p])
    copies = []
    for step in (6, 7, 4, 5, 2, 3, 1):
        copies.append(links.push(here, there.at[links.z, links.p], links.near(step)[0]))
    yield
    own.wait()
    for copy in copies:
        copy.wait()
    copies = []
    for step in range(1, links.planes):
        copies.append(links.push(there.at[links.z], there.at[links.z], links.along(step)[0]))
    yield
    for copy in copies:
        copy.wait()


def drive(transfers):
    while transfers:
        left = []
        for transfer in transfers:
            try:
                next(transfer)
                left.append(transfer)
            except StopIteration:
                pass
        transfers = left


def exchange(items, name, collective_id, planes):
    count = len(items)

    def body(*refs):
        links = Links(planes, *refs[2 * count :])
        links.greet()
        links.meet()
        drive([item[0](links, refs[k], refs[count + k]) for k, item in enumerate(items)])

    return pl.pallas_call(
        body,
        out_shape=[item[2] for item in items],
        in_specs=[pl.BlockSpec(memory_space=pl.ANY)] * count,
        out_specs=[pl.BlockSpec(memory_space=pl.ANY)] * count,
        scratch_shapes=link_scratch(),
        compiler_params=pltpu.CompilerParams(collective_id=collective_id, has_side_effects=True),
        name=name,
    )(*[item[1] for item in items])


def whole(ref, index):
    return ref


def block(ref, index):
    return ref.at[index]


def second(ref, index):
    return ref.at[:, index]


def like(kind, array, *shape):
    return (kind, array, jax.ShapeDtypeStruct(shape, array.dtype))


def pick_rows(table, index_ref, start, count):
    return jnp.concatenate(
        [table[pl.ds(index_ref[start + row], 1), :] for row in range(count)], axis=0
    )


def across(column):
    return jnp.broadcast_to(column, (128, 128)).T


def down(row):
    return jnp.broadcast_to(row, (128, 128)).T


def dot(a, b, contract):
    return lax.dot_general(a, b, (contract, ((), ())), preferred_element_type=jnp.float32)


def window_masks():
    query = lax.broadcasted_iota(jnp.int32, (128, 128), 0) // BLOCK
    key = lax.broadcasted_iota(jnp.int32, (128, 128), 1) // BLOCK
    return (query == 0) & (key == 1), key <= query


def key_scales(keys):
    rows = keys.astype(jnp.float32)
    mean_square = jnp.mean(rows * rows, axis=-1, keepdims=True) + 1e-06
    return rows, mean_square, lax.rsqrt(mean_square) / HEAD_DIM


def masked_scores(raw, scale, query_pos, key_pos, inside):
    scores = jnp.where(
        key_pos > query_pos, LATER, jnp.where(key_pos == query_pos, SELF, raw * scale)
    )
    return jnp.where(inside, scores, OUTSIDE)


def tile_rows(tile):
    return pl.ds(pl.multiple_of(tile * 128, 128), 128)


def sort_pair(order, table, first, second, tile):
    for part in range(4):
        start = pl.multiple_of(tile * 128 + part * 32, 32)
        picked = pick_rows(table, order, start, 32)
        first[pl.ds(start, 32), :] = picked[:, :128].astype(first.dtype)
        second[pl.ds(start, 32), :] = picked[:, 128:].astype(second.dtype)


def attend_kernel(
    tiles, unroll, order, place, order_rows, shared, values, shared_sorted, values_sorted, total_sorted,
    mixed_home, total_home, table, mixed, scales,
):
    def load(tile, carry):
        rows = tile_rows(tile)
        table[rows, :128] = shared[rows, :].astype(jnp.float32)
        table[rows, 128:] = values[rows, :].astype(jnp.float32)
        return carry

    lax.fori_loop(0, tiles, load, 0)
    sort = functools.partial(sort_pair, order, table, shared_sorted, values_sorted)
    for tile in [tiles - 1] + list(range(unroll)):
        sort(tile)
    inside_left, inside_here = window_masks()
    scales[0] = across(key_scales(shared_sorted[(tiles - 1) * 128 :, :])[2])

    def attend_tiles(step, carry):
        first = step * unroll
        numbers = [lax.rem(first + tiles - 1, tiles)] + [first + k for k in range(unroll)]
        keys = [shared_sorted[tile_rows(t), :] for t in numbers]
        vals = [values_sorted[tile_rows(t), :] for t in numbers]
        places = [order_rows[pl.ds(t, 1), :] for t in numbers]
        scale = [scales[0]] + [across(key_scales(k)[2]) for k in keys[1:]]
        scales[0] = scale[-1]
        for k in range(unroll):
            sort(lax.rem(first + unroll + k, tiles))
        for k in range(unroll):
            rows = tile_rows(first + k)
            query_pos = down(places[k + 1])
            score_left = masked_scores(
                dot(keys[k + 1], keys[k], ((1,), (1,))), scale[k], query_pos, places[k], inside_left
            )
            score_here = masked_scores(
                dot(keys[k + 1], keys[k + 1], ((1,), (1,))),
                scale[k + 1],
                query_pos,
                places[k + 1],
                inside_here,
            )
            highest = jnp.max(jnp.maximum(score_left, score_here), axis=-1, keepdims=True)
            total = highest + jnp.log(
                jnp.sum(
                    jnp.exp(score_left - highest) + jnp.exp(score_here - highest),
                    axis=-1,
                    keepdims=True,
                )
            )
            prob_left = jnp.exp(score_left - total).astype(jnp.bfloat16)
            prob_here = jnp.exp(score_here - total).astype(jnp.bfloat16)
            mixed[rows, :128] = dot(prob_left, vals[k], ((1,), (0,))) + dot(
                prob_here, vals[k + 1], ((1,), (0,))
            )
            total = jnp.broadcast_to(total, (128, 128))
            mixed[rows, 128:] = total
            total_sorted[rows, :] = total
        return carry

    lax.fori_loop(0, tiles // unroll, attend_tiles, 0)

    def unsort(tile, carry):
        totals = []
        for part in range(4):
            start = pl.multiple_of(tile * 128 + part * 32, 32)
            picked = pick_rows(mixed, place, start, 32)
            mixed_home[pl.ds(start, 32), :] = picked[:, :128].astype(jnp.bfloat16)
            totals.append(picked[:, 128:])
        total_home[lax.rem(tile, 8), pl.ds(tile // 8, 1), :] = jnp.concatenate(totals, axis=0).T[:1, :]
        return carry

    lax.fori_loop(0, tiles, unsort, 0)


def attend_back_kernel(
    tiles, unroll, order, place, order_rows, shared_sorted, values_sorted, total_sorted, grad_mixed, grad_total,
    grad_shared_home, grad_values_home, table, grad_sorted, grad_total_sorted, scales, scale_sums, sums,
):
    def load(tile, carry):
        rows = tile_rows(tile)
        table[rows, :128] = grad_mixed[rows, :].astype(jnp.float32)
        table[rows, 128:] = down(grad_total[lax.rem(tile, 8), pl.ds(tile // 8, 1), :])
        return carry

    lax.fori_loop(0, tiles, load, 0)
    sums[tile_rows(tiles - 1), :] = jnp.zeros((128, 256), jnp.float32)
    sort = functools.partial(sort_pair, order, table, grad_sorted, grad_total_sorted)
    for tile in range(unroll):
        sort(tile)
    inside_left, inside_here = window_masks()
    scales[0] = across(key_scales(shared_sorted[(tiles - 1) * 128 :, :])[2])
    scale_sums[...] = jnp.zeros_like(scale_sums)

    def back_tiles(step, carry):
        first = step * unroll
        left = lax.rem(first + tiles - 1, tiles)
        numbers = [left] + [first + k for k in range(unroll)]
        keys = [shared_sorted[tile_rows(t), :] for t in numbers]
        vals = [values_sorted[tile_rows(t), :] for t in numbers]
        places = [order_rows[pl.ds(t, 1), :] for t in numbers]
        grads = [grad_sorted[tile_rows(t), :] for t in numbers[1:]]
        grad_totals = [grad_total_sorted[tile_rows(t), :] for t in numbers[1:]]
        totals = [total_sorted[tile_rows(t), :] for t in numbers[1:]]
        scale = [scales[0]] + [across(key_scales(k)[2]) for k in keys[1:]]
        scales[0] = scale[-1]
        for k in range(unroll):
            sort(lax.rem(first + unroll + k, tiles))
        key_sums, value_sums, scale_parts = [0.0] * (unroll + 1), [0.0] * (unroll + 1), [0.0] * (unroll + 1)
        for k in range(unroll):
            here, before, grad = keys[k + 1], keys[k], grads[k]
            query_pos = down(places[k + 1])
            raw_left = dot(here, before, ((1,), (1,)))
            raw_here = dot(here, here, ((1,), (1,)))
            prob_left = jnp.exp(
                masked_scores(raw_left, scale[k], query_pos, places[k], inside_left) - totals[k]
            )
            prob_here = jnp.exp(
                masked_scores(raw_here, scale[k + 1], query_pos, places[k + 1], inside_here) - totals[k]
            )
            grad_prob_left = dot(grad, vals[k], ((1,), (1,)))
            grad_prob_here = dot(grad, vals[k + 1], ((1,), (1,)))
            inner = jnp.sum(
                prob_left * grad_prob_left + prob_here * grad_prob_here, axis=-1, keepdims=True
            )
            shift = grad_totals[k] - inner
            keep_left = inside_left & (places[k] < query_pos)
            keep_here = inside_here & (places[k + 1] < query_pos)
            grad_score_left = jnp.where(keep_left, prob_left * (grad_prob_left + shift), 0.0)
            grad_score_here = jnp.where(keep_here, prob_here * (grad_prob_here + shift), 0.0)
            scale_parts[k] += jnp.sum(grad_score_left * raw_left, axis=0, keepdims=True)
            scale_parts[k + 1] += jnp.sum(grad_score_here * raw_here, axis=0, keepdims=True)
            grad_raw_left = (grad_score_left * scale[k]).astype(jnp.bfloat16)
            grad_raw_here = (grad_score_here * scale[k + 1]).astype(jnp.bfloat16)
            key_sums[k + 1] += (
                dot(grad_raw_left, before, ((1,), (0,)))
                + dot(grad_raw_here, here, ((1,), (0,)))
                + dot(grad_raw_here, here, ((0,), (0,)))
            )
            key_sums[k] += dot(grad_raw_left, here, ((0,), (0,)))
            value_sums[k + 1] += dot(prob_here.astype(jnp.bfloat16), grad, ((0,), (0,)))
            value_sums[k] += dot(prob_left.astype(jnp.bfloat16), grad, ((0,), (0,)))
        for k, tile in enumerate(numbers[1:]):
            sums[tile_rows(tile), :128] = key_sums[k + 1]
            sums[tile_rows(tile), 128:] = value_sums[k + 1]
            scale_sums[pl.ds(tile, 1), :] = scale_parts[k + 1]
        extra = pl.ds(pl.multiple_of(jnp.where(step == 0, tiles, left) * 128, 128), 128)
        extra_row = pl.ds(jnp.where(step == 0, tiles, left), 1)
        sums[extra, :128] += key_sums[0]
        sums[extra, 128:] += value_sums[0]
        scale_sums[extra_row, :] += scale_parts[0]
        return carry

    sums[pl.ds(tiles * 128, 128), :] = jnp.zeros((128, 256), jnp.float32)
    lax.fori_loop(0, tiles // unroll, back_tiles, 0)
    last = tile_rows(tiles - 1)
    sums[last, :] += sums[pl.ds(tiles * 128, 128), :]
    scale_sums[pl.ds(tiles - 1, 1), :] += scale_sums[pl.ds(tiles, 1), :]

    def finish(step, carry):
        for part in range(2):
            tile = step * 2 + part
            rows = tile_rows(tile)
            keys, mean_square, scale = key_scales(shared_sorted[rows, :])
            factor = down(scale_sums[pl.ds(tile, 1), :]) * (scale / (mean_square * HEAD_DIM))
            sums[rows, :128] -= factor * keys
        return carry

    lax.fori_loop(0, tiles // 2, finish, 0)

    def unsort(tile, carry):
        sort_pair(place, sums, grad_shared_home, grad_values_home, tile)
        return carry

    lax.fori_loop(0, tiles, unsort, 0)


VMEM = pl.BlockSpec(memory_space=pltpu.VMEM)
SMEM = pl.BlockSpec(memory_space=pltpu.SMEM)
ANY = pl.BlockSpec(memory_space=pl.ANY)


def beside(kernel, inputs, outputs, scratch, items, planes):
    count = len(items)

    def body(*refs):
        refs = list(refs)
        own, refs = refs[:inputs], refs[inputs:]
        here, refs = refs[:count], refs[count:]
        own, refs = own + refs[:outputs], refs[outputs:]
        there, refs = refs[:count], refs[count:]
        links = Links(planes, *refs[scratch:])
        links.greet()
        links.meet()
        transfers = [item[0](links, here[k], there[k]) for k, item in enumerate(items)]
        for transfer in transfers:
            next(transfer)
        kernel(*own, *refs[:scratch])
        drive(transfers)

    return body


def attend_head(order, place, order_rows, shared, values, items, collective_id, planes, unroll=2):
    length = shared.shape[0]
    rows = jax.ShapeDtypeStruct((length, HEAD_DIM), jnp.bfloat16)
    scratch = [
        pltpu.VMEM((length, 256), jnp.float32),
        pltpu.VMEM((length, 256), jnp.float32),
        pltpu.VMEM((1, 128, 128), jnp.float32),
    ]
    kernel = functools.partial(attend_kernel, length // 128, unroll)
    return pl.pallas_call(
        beside(kernel, 5, 5, len(scratch), items, planes),
        out_shape=[
            rows,
            rows,
            jax.ShapeDtypeStruct((length, HEAD_DIM), jnp.float32),
            rows,
            jax.ShapeDtypeStruct((8, 8, 128), jnp.float32),
        ]
        + [item[2] for item in items],
        in_specs=[SMEM, SMEM, VMEM, VMEM, VMEM] + [ANY] * len(items),
        out_specs=[VMEM] * 5 + [ANY] * len(items),
        scratch_shapes=scratch + link_scratch(),
        compiler_params=pltpu.CompilerParams(
            vmem_limit_bytes=40 << 20, collective_id=collective_id, has_side_effects=True
        ),
        name="attend",
    )(order, place, order_rows, shared, values, *[item[1] for item in items])


def attend_head_back(
    order, place, order_rows, shared_sorted, values_sorted, total_sorted, grad, grad_total,
    items, collective_id, planes, unroll=2,
):
    length = grad.shape[0]
    rows = jax.ShapeDtypeStruct((length, HEAD_DIM), jnp.bfloat16)
    scratch = [
        pltpu.VMEM((length, 256), jnp.float32),
        pltpu.VMEM((length, HEAD_DIM), jnp.bfloat16),
        pltpu.VMEM((length, HEAD_DIM), jnp.float32),
        pltpu.VMEM((1, 128, 128), jnp.float32),
        pltpu.VMEM((length // 128 + 8, 128), jnp.float32),
        pltpu.VMEM((length + 128, 256), jnp.float32),
    ]
    kernel = functools.partial(attend_back_kernel, length // 128, unroll)
    return pl.pallas_call(
        beside(kernel, 8, 2, len(scratch), items, planes),
        out_shape=[rows, rows] + [item[2] for item in items],
        in_specs=[SMEM, SMEM] + [VMEM] * 6 + [ANY] * len(items),
        out_specs=[VMEM] * 2 + [ANY] * len(items),
        scratch_shapes=scratch + link_scratch(),
        compiler_params=pltpu.CompilerParams(
            vmem_limit_bytes=40 << 20, collective_id=collective_id, has_side_effects=True
        ),
        name="attend_back",
    )(
        order, place, order_rows, shared_sorted, values_sorted, total_sorted, grad, grad_total,
        *[item[1] for item in items],
    )


def sum_small_kernel(planes, items, *refs):
    count = len(items)
    tiles, here, refs = refs[0], refs[1 : 1 + count], refs[1 + count :]
    result, there, refs = refs[0], refs[1 : 1 + count], refs[1 + count :]
    arrived, summed, refs = refs[0], refs[1], refs[2:]
    links = Links(planes, *refs)
    links.greet()
    links.meet()
    transfers = [item[0](links, here[k], there[k]) for k, item in enumerate(items)]
    small = over_plane(block, block)(links, tiles, arrived)
    next(small)
    for transfer in transfers:
        next(transfer)
    drive([small])
    summed[...] = jnp.sum(arrived[...], axis=0)
    drive([along_z(whole, block)(links, summed, result)] + transfers)


def sum_small(tiles, items, collective_id, planes):
    return pl.pallas_call(
        functools.partial(sum_small_kernel, planes, items),
        out_shape=[jax.ShapeDtypeStruct((planes,) + tiles.shape[1:], tiles.dtype)]
        + [item[2] for item in items],
        in_specs=[VMEM] + [ANY] * len(items),
        out_specs=[VMEM] + [ANY] * len(items),
        scratch_shapes=[
            pltpu.VMEM(tiles.shape, tiles.dtype),
            pltpu.VMEM(tiles.shape[1:], tiles.dtype),
        ]
        + link_scratch(),
        compiler_params=pltpu.CompilerParams(collective_id=collective_id, has_side_effects=True),
        name="sum_small",
    )(tiles, *[item[1] for item in items])


def matmul(a, b, contract=((1,), (0,))):
    return dot(a, b, contract)


def plane_plan(
    n_seq,
    n_sub,
    first_half,
    second_half,
    grad_first,
    grad_second,
    attend_gain,
    attend_shift,
    query_key_weight,
    value_projection_weight,
    output_projection_weight,
    feed_gain,
    feed_shift,
    upper_projection_weight,
    upper_projection_bias,
    lower_projection_weight,
    lower_projection_bias,
    sort_order,
    sort_place,
):
    low, full = jnp.bfloat16, jnp.float32
    devices, planes, per_plane = n_seq * n_sub, n_seq // 2, 2 * n_sub
    rows, width = first_half.shape[1:]
    hidden = upper_projection_weight.shape[2]
    tokens = devices * rows
    line = planes * rows
    part = hidden // per_plane
    seq, sub = lax.axis_index("seq"), lax.axis_index("sub")
    me_p, me_z = lax.rem(seq, 2) * n_sub + sub, seq // 2
    trade = functools.partial(exchange, planes=planes)
    x1, x2, g1, g2 = (a[0] for a in (first_half, second_half, grad_first, grad_second))
    wqk, wv, wo = query_key_weight[0], value_projection_weight[0], output_projection_weight[0]
    wup, wdown = upper_projection_weight[0], lower_projection_weight[0]
    own = width // devices
    pair = 2 * HEAD_DIM

    def row_of(*vectors):
        return jnp.concatenate([v[0].astype(full) for v in vectors])[None]

    small = jnp.concatenate(
        [
            sort_order[0, :, 0].astype(full),
            sort_place[0, :, 0].astype(full),
            row_of(attend_gain, attend_shift, feed_gain, feed_shift),
            row_of(upper_projection_bias),
            jnp.pad(row_of(lower_projection_bias), ((0, 5), (0, rows - own))),
        ],
        axis=0,
    )
    small = jnp.pad(small, ((0, 16 - small.shape[0]), (0, 0)))

    def pair_columns(ref, z):
        return ref.at[:, pl.ds(pl.multiple_of(z * pair, pair), pair)]

    all_small, wqk_line, wv_line, wo_line = trade(
        [
            like(everywhere, small, planes, per_plane, 16, rows),
            like(along_z(pair_columns, block), wqk, planes, own, pair),
            like(along_z(pair_columns, block), wv, planes, own, pair),
            like(along_z(whole, block), wo, planes, own, width),
        ],
        "share_small",
        1,
    )
    all_small = all_small.reshape(devices, 16, rows)
    gain_a, shift_a, gain_f, shift_f = (
        all_small[:, 8, k * own : (k + 1) * own].reshape(width) for k in range(4)
    )
    bias_down = all_small[:, 10, :own].reshape(width)
    bias_up = jnp.take(
        all_small[:, 9].reshape(planes, per_plane, rows), me_p, axis=1
    ).reshape(planes * rows)
    order_rows = jnp.take(all_small[:, :4], sub, axis=1)
    order = order_rows.astype(jnp.int32).reshape(tokens)
    place = jnp.take(all_small[:, 4:8], sub, axis=1).astype(jnp.int32).reshape(tokens)

    normed, attend_pull = jax.vjp(layer_norm, x2, gain_a, shift_a)
    normed = normed.astype(low)

    def upper_columns(chunk):
        def columns(ref, p):
            return ref.at[:, pl.ds(pl.multiple_of((chunk * per_plane + p) * rows, rows), rows)]

        return like(over_plane(columns, block), wup, per_plane, own, rows)

    rows_of_pair = over_chips(whole, second)
    normed_line, wqk_pair, wv_pair, *wup_rows = trade(
        [
            like(along_z(whole, block), normed, planes, rows, width),
            like(rows_of_pair, wqk_line, planes, per_plane, own, pair),
            like(rows_of_pair, wv_line, planes, per_plane, own, pair),
        ]
        + [upper_columns(chunk) for chunk in range(planes)],
        "share_normed",
        2,
    )
    wup_rows = jnp.concatenate([a.reshape(per_plane * own, rows) for a in wup_rows], axis=1)
    normed_line = normed_line.reshape(line, width)
    wqk_pair, wv_pair = wqk_pair.reshape(width, pair), wv_pair.reshape(width, pair)
    shared = matmul(normed_line, wqk_pair).astype(low).reshape(planes, rows, pair)
    values = matmul(normed_line, wv_pair).astype(low).reshape(planes, rows, pair)

    def head_columns(ref, p):
        return ref.at[:, :, pl.ds(pl.multiple_of((p // 4) * HEAD_DIM, HEAD_DIM), HEAD_DIM)]

    to_head = over_chips(head_columns, second)
    head_shape = (planes, per_plane, rows, HEAD_DIM)
    head_shared, head_values = trade(
        [like(to_head, shared, *head_shape), like(to_head, values, *head_shape)], "to_heads", 3
    )
    df = g2.astype(low)
    (
        shared_sorted, values_sorted, total_sorted, mixed, total,
        wup_part, wdown_part, wo_all, df_plane,
    ) = attend_head(
        order,
        place,
        order_rows,
        head_shared.reshape(tokens, HEAD_DIM),
        head_values.reshape(tokens, HEAD_DIM),
        [
            like(along_z(whole, block), wup_rows, planes, per_plane * own, part),
            like(along_z(whole, block), wdown, planes, rows, width),
            like(over_chips(whole, second), wo_line, planes, per_plane, own, width),
            like(over_chips(whole, block), df, per_plane, rows, width),
        ],
        4,
        planes,
    )
    wup_part, wdown_part = wup_part.reshape(width, part), wdown_part.reshape(part, width)
    wo_all = wo_all.reshape(width, width)
    df_plane = df_plane.reshape(per_plane * rows, width)

    token_shape = (per_plane, planes, rows, HEAD_DIM)

    def to_tokens(array):
        return like(over_plane(second, block), array.reshape(head_shape), *token_shape)

    mixed, total = trade(
        [to_tokens(mixed), like(over_plane(block, block), total, *total.shape)], "heads_out", 5
    )
    mixed = mixed.reshape(2, n_sub, line, HEAD_DIM).astype(full)
    total = total[:, :planes].reshape(2, n_sub, line)
    weights = jnp.exp(total - jnp.max(total, axis=1, keepdims=True))
    weights = weights / jnp.sum(weights, axis=1, keepdims=True)
    attended = jnp.sum(weights[..., None] * mixed, axis=1)
    attended = jnp.swapaxes(attended, 0, 1).reshape(line, pair).astype(low)
    own_attended = trade(
        [like(along_z(block, block), attended.reshape(planes, rows, pair), planes, rows, pair)],
        "share_attended",
        6,
    )[0]
    own_attended = jnp.swapaxes(own_attended, 0, 1).reshape(rows, width)
    y1 = x1 + matmul(own_attended, wo_all)
    h2, feed_pull = jax.vjp(layer_norm, y1, gain_f, shift_f)
    h2_plane = trade(
        [like(over_chips(whole, block), h2.astype(low), per_plane, rows, width)], "share_feed", 7
    )[0]
    h2_plane = h2_plane.reshape(per_plane * rows, width)
    pre = matmul(h2_plane, wup_part) + bias_up
    act, act_pull = jax.vjp(gelu_exact, pre)
    act = act.astype(low)
    y2_parts = matmul(act, wdown_part).astype(low).reshape(per_plane, rows, width)
    dpre = act_pull(matmul(df_plane, wdown_part, ((1,), (1,))))[0].astype(low)
    dh2_parts = matmul(dpre, wup_part, ((1,), (1,))).astype(low).reshape(per_plane, rows, width)
    down_grad = matmul(act, df_plane, ((0,), (0,))).astype(low).reshape(planes, rows, width)
    up_grad = matmul(h2_plane, dpre, ((0,), (0,))).astype(low).reshape(planes, width // planes, part)
    up_bias_grad = jnp.sum(dpre.astype(full), axis=0)
    down_bias_grad = jnp.sum(df.astype(full), axis=0)

    traded_z, traded_plane = along_z(block, block), over_plane(block, block)
    dh2_parts, up_grad = trade(
        [like(traded_plane, dh2_parts, *dh2_parts.shape), like(traded_z, up_grad, *up_grad.shape)],
        "sum_feed_grad",
        8,
    )
    one_part, feed_gain_grad, feed_shift_grad = feed_pull(jnp.sum(dh2_parts.astype(full), axis=0))
    g1 = g1 + one_part
    up_grad = jnp.sum(up_grad.astype(full), axis=0).reshape(per_plane, own, part)
    dout = g1.astype(low)
    datt = matmul(dout, wo_all, ((1,), (1,))).astype(low)
    datt = trade([like(along_z(pair_columns, block), datt, planes, rows, pair)], "share_out_grad", 9)[0]
    datt = jnp.swapaxes(datt.reshape(line, 2, HEAD_DIM), 0, 1)[:, None].astype(full)
    dweights = jnp.sum(datt * mixed, axis=-1)
    dmixed = (weights[..., None] * datt).astype(low).reshape(token_shape)
    dtotal = weights * (dweights - jnp.sum(weights * dweights, axis=1, keepdims=True))
    dtotal = dtotal.astype(low).astype(full).reshape(per_plane, planes, rows)
    dtotal = jnp.pad(dtotal, ((0, 0), (0, 8 - planes), (0, 0)))
    dmixed, dtotal = trade(
        [
            like(over_plane(block, second), dmixed, *head_shape),
            like(traded_plane, dtotal, *dtotal.shape),
        ],
        "grads_to_heads",
        10,
    )
    dshared, dvalues, y2_parts, dout_line, down_grad = attend_head_back(
        order,
        place,
        order_rows,
        shared_sorted,
        values_sorted,
        total_sorted,
        dmixed.reshape(tokens, HEAD_DIM),
        dtotal,
        [
            like(traded_plane, y2_parts, *y2_parts.shape),
            like(along_z(whole, block), dout, planes, rows, width),
            like(traded_z, down_grad, *down_grad.shape),
        ],
        11,
        planes,
    )
    y2 = x2 + (jnp.sum(y2_parts.astype(full), axis=0) + bias_down)
    out_grad = matmul(attended, dout_line.reshape(line, width), ((0,), (0,)))
    out_grad = out_grad.astype(low).reshape(per_plane, own, width)
    dshared, dvalues = trade([to_tokens(dshared), to_tokens(dvalues)], "grads_from_heads", 12)

    def over_rounds(array):
        array = jnp.sum(array.reshape(2, n_sub, line, HEAD_DIM).astype(full), axis=1)
        return jnp.swapaxes(array, 0, 1).reshape(line, pair).astype(low)

    dshared, dvalues = over_rounds(dshared), over_rounds(dvalues)
    de_parts = matmul(dshared, wqk_pair, ((1,), (1,))) + matmul(dvalues, wv_pair, ((1,), (1,)))
    de_parts = de_parts.astype(low).reshape(planes, rows, width)

    def to_owners(grad):
        grad = grad.astype(low).reshape(planes, per_plane, own, pair)
        return like(over_plane(second, block), grad, per_plane, planes, own, pair)

    de_parts, shared_grad, value_grad, out_grad, up_grad = trade(
        [
            like(traded_z, de_parts, *de_parts.shape),
            to_owners(matmul(normed_line, dshared, ((0,), (0,)))),
            to_owners(matmul(normed_line, dvalues, ((0,), (0,)))),
            like(traded_plane, out_grad, *out_grad.shape),
            like(traded_plane, up_grad, *up_grad.shape),
        ],
        "sum_second_grad",
        13,
    )
    two_part, attend_gain_grad, attend_shift_grad = attend_pull(
        jnp.sum(de_parts.astype(full), axis=0)
    )
    g2 = g2 + two_part
    shared_grad = jnp.sum(shared_grad.astype(full), axis=0)
    value_grad = jnp.sum(value_grad.astype(full), axis=0)

    def by_owner(vector):
        return jnp.swapaxes(vector.reshape(planes, per_plane, own), 0, 1).reshape(per_plane, 1, rows)

    vectors = [attend_gain_grad, attend_shift_grad, feed_gain_grad, feed_shift_grad, down_bias_grad]
    up_bias_grad = jnp.where(
        jnp.arange(per_plane)[:, None, None] == me_p, up_bias_grad.reshape(1, planes, rows), 0.0
    )
    tiles = jnp.concatenate([by_owner(v) for v in vectors] + [up_bias_grad], axis=1)
    tiles = jnp.pad(tiles, ((0, 0), (0, 16 - tiles.shape[1]), (0, 0)))
    vectors, shared_grad, value_grad = sum_small(
        tiles,
        [like(traded_z, shared_grad, planes, own, pair), like(traded_z, value_grad, planes, own, pair)],
        14,
        planes,
    )
    vectors = jnp.sum(vectors, axis=0)
    pieces = jnp.take(vectors[:5].reshape(5, planes, own), me_z, axis=1)
    up_bias_grad = jnp.take(vectors[5 : 5 + planes], me_z, axis=0)
    shared_grad, value_grad = (
        jnp.swapaxes(a, 0, 1).reshape(own, width) for a in (shared_grad, value_grad)
    )
    up_grad = jnp.transpose(up_grad.reshape(per_plane, own, planes, rows), (1, 2, 0, 3))
    outputs = (
        y1,
        y2,
        g1,
        g2,
        pieces[0],
        pieces[1],
        shared_grad,
        value_grad,
        jnp.sum(out_grad.astype(full), axis=0),
        pieces[2],
        pieces[3],
        up_grad.reshape(own, hidden),
        up_bias_grad,
        jnp.sum(down_grad.astype(full), axis=0),
        pieces[4],
    )
    return tuple((a[None] for a in outputs))


def on_device(n_seq, n_sub, *arguments):
    sequences, rows, width = arguments[0].shape
    rounds = arguments[-1].shape[1]
    fits = (
        sequences == 1
        and rows == 2 * BLOCK
        and rounds == n_sub
        and HEADS == n_seq
        and width == HEADS * HEAD_DIM
    )
    if fits:
        return plane_plan(n_seq, n_sub, *arguments)
    return general_plan(*arguments)


def solution(mesh):
    return jax.shard_map(
        functools.partial(on_device, mesh.shape["seq"], mesh.shape["sub"]),
        mesh=mesh,
        in_specs=(
            P(None, ("seq", "sub"), None),
            P(None, ("seq", "sub"), None),
            P(None, ("seq", "sub"), None),
            P(None, ("seq", "sub"), None),
            P(None, ("seq", "sub")),
            P(None, ("seq", "sub")),
            P(None, ("seq", "sub"), None),
            P(None, ("seq", "sub"), None),
            P(None, ("seq", "sub"), None),
            P(None, ("seq", "sub")),
            P(None, ("seq", "sub")),
            P(None, ("seq", "sub"), None),
            P(None, ("seq", "sub")),
            P(None, ("seq", "sub"), None),
            P(None, ("seq", "sub")),
            P(None, None, None, ("seq", "sub")),
            P(None, None, None, ("seq", "sub")),
        ),
        out_specs=(
            P(None, ("seq", "sub"), None),
            P(None, ("seq", "sub"), None),
            P(None, ("seq", "sub"), None),
            P(None, ("seq", "sub"), None),
            P(None, ("seq", "sub")),
            P(None, ("seq", "sub")),
            P(None, ("seq", "sub"), None),
            P(None, ("seq", "sub"), None),
            P(None, ("seq", "sub"), None),
            P(None, ("seq", "sub")),
            P(None, ("seq", "sub")),
            P(None, ("seq", "sub"), None),
            P(None, ("seq", "sub")),
            P(None, ("seq", "sub"), None),
            P(None, ("seq", "sub")),
        ),
        check_vma=False,
    )
```

```python
import functools

import jax
import jax.numpy as jnp
from jax import lax
from jax.experimental import pallas as pl
from jax.experimental.pallas import tpu as pltpu
from jax.sharding import PartitionSpec as P

HEADS = 8
HEAD_DIM = 128
BLOCK = 64
LATER = -1000000000.0
SELF = -100000.0
OUTSIDE = -3e38


def from_behind(block, axis, distance):
    devices = range(lax.axis_size(axis))
    route = [((i - distance) % len(devices), i) for i in devices]
    return lax.ppermute(block, axis, route)


def layer_norm(value_vectors, scaling, shifts):
    center = jnp.mean(value_vectors, axis=-1, keepdims=True)
    offset = value_vectors - center
    spread = jnp.mean(offset * offset, axis=-1, keepdims=True)
    return offset * lax.rsqrt(spread + 1e-05) * scaling + shifts


def gelu_exact(value_vectors):
    return jax.nn.gelu(value_vectors, approximate=False)


def combine_rounds(outputs, totals):
    highest = jnp.max(totals, axis=0, keepdims=True)
    weights = jnp.exp(totals - highest)
    weights = weights / jnp.sum(weights, axis=0, keepdims=True)
    by_head = outputs.reshape(outputs.shape[:-1] + (totals.shape[-1], -1))
    return jnp.sum(weights[..., None] * by_head, axis=0).reshape(outputs.shape[1:])


def home_slots(places, row_count):
    target = places // row_count
    prior_state = (target[:, None, :] == target[:, :, None]) & (
        places[:, None, :] < places[:, :, None]
    )
    return (target, jnp.sum(prior_state.astype(jnp.int32), axis=2))


def sorted_slots(orders, row_count):
    source = orders // row_count
    ladder = jnp.arange(row_count, dtype=jnp.int32)
    prior_state = (source[:, None, :] == source[:, :, None]) & (
        ladder[None, None, :] < ladder[None, :, None]
    )
    return (source, jnp.sum(prior_state.astype(jnp.int32), axis=2))


def slot_lookup(owners, slot_index, devices, capacity):
    groups, row_count = owners.shape
    flat_index = owners * capacity + slot_index
    lookup = jnp.full((groups, devices * capacity), row_count, jnp.int32)
    filler = jnp.broadcast_to(jnp.arange(row_count, dtype=jnp.int32), (groups, row_count))
    lookup = lookup.at[jnp.arange(groups)[:, None], flat_index].set(filler)
    return jnp.transpose(lookup.reshape(groups, devices, capacity), (1, 0, 2))


def gather_slots(value_vectors, member, lookup):
    padding = jnp.zeros((value_vectors.shape[0], 1) + value_vectors.shape[2:], value_vectors.dtype)
    padded = jnp.concatenate([value_vectors, padding], axis=1)
    return padded[member[None, :, None], lookup]


def settle(received, owners, slot_index):
    return received[owners, jnp.arange(owners.shape[0])[:, None], slot_index]


def build_routes(orders, places, devices, capacity):
    rounds, sequences, row_count = orders.shape
    order_flat = orders.reshape(rounds * sequences, row_count)
    target, home_slot = home_slots(places.reshape(rounds * sequences, row_count), row_count)
    source, sorted_slot = sorted_slots(order_flat, row_count)
    home_lookup = slot_lookup(target, home_slot, devices, capacity)
    back_lookup = slot_lookup(source, sorted_slot, devices, capacity)
    return (target, home_slot, source, sorted_slot, home_lookup, back_lookup, order_flat)


def trade_rows(first_part, second_part):
    return (
        lax.all_to_all(first_part, ("seq", "sub"), split_axis=0, concat_axis=0, tiled=True),
        lax.all_to_all(second_part, ("seq", "sub"), split_axis=0, concat_axis=0, tiled=True),
    )


def trade_results(first_part, second_part):
    return (
        lax.all_to_all(first_part, ("seq", "sub"), split_axis=0, concat_axis=0, tiled=True),
        lax.all_to_all(second_part, ("seq", "sub"), split_axis=0, concat_axis=0, tiled=True),
    )


def window(rows_here, rows_left):
    groups = rows_here.shape[0]
    extended = jnp.concatenate([rows_left, rows_here], axis=1)
    extended = extended.reshape((groups, -1, BLOCK) + rows_here.shape[2:])
    return jnp.concatenate([extended[:, :-1], extended[:, 1:]], axis=2)


def score_parts(shared_rows, order_rows, halo_shared, halo_order):
    groups, row_count, features = shared_rows.shape
    blocks = row_count // BLOCK
    queries = shared_rows.reshape(groups, blocks, BLOCK, HEADS, HEAD_DIM)
    key_rows = window(shared_rows, halo_shared).reshape(groups, blocks, 2 * BLOCK, HEADS, HEAD_DIM)
    key_float = key_rows.astype(jnp.float32)
    mean_square = jnp.mean(key_float * key_float, axis=-1) + 1e-06
    key_scale = lax.rsqrt(mean_square) / HEAD_DIM
    raw_scores = jnp.einsum(
        "gcqhd,gckhd->gchqk", queries, key_rows, preferred_element_type=jnp.float32
    )
    query_pos = order_rows.reshape(groups, blocks, BLOCK)
    key_pos = window(order_rows, halo_order)
    is_later = (key_pos[:, :, None, :] > query_pos[:, :, :, None])[:, :, None]
    is_self = (key_pos[:, :, None, :] == query_pos[:, :, :, None])[:, :, None]
    scale_row = jnp.transpose(key_scale, (0, 1, 3, 2))[:, :, :, None, :]
    scores = jnp.where(
        is_later, -1000000000.0, jnp.where(is_self, -100000.0, raw_scores * scale_row)
    )
    highest = jnp.max(scores, axis=-1, keepdims=True)
    log_total = highest + jnp.log(jnp.sum(jnp.exp(scores - highest), axis=-1, keepdims=True))
    probability = jnp.exp(scores - log_total)
    return (
        queries,
        key_rows,
        key_float,
        mean_square,
        key_scale,
        scale_row,
        raw_scores,
        is_later | is_self,
        log_total,
        probability,
    )


def attend(shared_rows, value_rows, order_rows, halo):
    halo_shared, halo_value, halo_order = halo
    parts = score_parts(shared_rows, order_rows, halo_shared, halo_order)
    groups, row_count, features = shared_rows.shape
    value_keys = window(value_rows, halo_value).reshape(
        groups, row_count // BLOCK, 2 * BLOCK, HEADS, HEAD_DIM
    )
    mixed = jnp.einsum(
        "gchqk,gckhd->gcqhd",
        parts[9].astype(jnp.bfloat16),
        value_keys,
        preferred_element_type=jnp.float32,
    )
    log_total = jnp.transpose(parts[8][..., 0], (0, 1, 3, 2)).reshape(groups, row_count, HEADS)
    return (mixed.reshape(groups, row_count, features), log_total)


def fold_window(grads_window, groups, row_count, features):
    grads_window = grads_window.reshape(groups, row_count // BLOCK, 2 * BLOCK, features)
    empty = jnp.zeros((groups, 1, BLOCK, features), jnp.float32)
    extended = jnp.concatenate([grads_window[:, :, :BLOCK], empty], axis=1) + jnp.concatenate(
        [empty, grads_window[:, :, BLOCK:]], axis=1
    )
    return (extended[:, 1:].reshape(groups, row_count, features), extended[:, 0])


def attend_back(shared_rows, value_rows, order_rows, halo, grad_out, grad_total):
    halo_shared, halo_value, halo_order = halo
    (
        queries,
        key_rows,
        key_float,
        mean_square,
        key_scale,
        scale_row,
        raw_scores,
        masked,
        log_total,
        probability,
    ) = score_parts(shared_rows, order_rows, halo_shared, halo_order)
    groups, row_count, features = shared_rows.shape
    blocks = row_count // BLOCK
    value_keys = window(value_rows, halo_value).reshape(groups, blocks, 2 * BLOCK, HEADS, HEAD_DIM)
    prob_low = probability.astype(jnp.bfloat16)
    grad_heads = grad_out.reshape(groups, blocks, BLOCK, HEADS, HEAD_DIM)
    grad_log = jnp.transpose(
        grad_total.astype(jnp.float32).reshape(groups, blocks, BLOCK, HEADS), (0, 1, 3, 2)
    )[..., None]
    grad_prob = jnp.einsum(
        "gcqhd,gckhd->gchqk", grad_heads, value_keys, preferred_element_type=jnp.float32
    )
    inner = jnp.sum(probability * grad_prob, axis=-1, keepdims=True)
    grad_score = jnp.where(masked, 0.0, probability * (grad_prob - inner + grad_log))
    grad_scale = jnp.transpose(jnp.sum(grad_score * raw_scores, axis=3), (0, 1, 3, 2))
    grad_raw = (grad_score * scale_row).astype(jnp.bfloat16)
    grad_query = jnp.einsum(
        "gchqk,gckhd->gcqhd", grad_raw, key_rows, preferred_element_type=jnp.float32
    )
    grad_key = jnp.einsum(
        "gchqk,gcqhd->gckhd", grad_raw, queries, preferred_element_type=jnp.float32
    )
    grad_key = grad_key - (grad_scale * key_scale / mean_square)[..., None] * key_float / HEAD_DIM
    grad_value = jnp.einsum(
        "gchqk,gcqhd->gckhd", prob_low, grad_heads, preferred_element_type=jnp.float32
    )
    key_home, key_left = fold_window(grad_key, groups, row_count, features)
    value_home, value_left = fold_window(grad_value, groups, row_count, features)
    back_key, back_value = from_behind((key_left, value_left), ("seq", "sub"), -1)
    grad_shared = grad_query.reshape(groups, row_count, features) + key_home
    grad_shared = grad_shared.at[:, row_count - BLOCK :].add(back_key)
    grad_values = value_home.at[:, row_count - BLOCK :].add(back_value)
    return (grad_shared, grad_values)


def sorted_attention(shared_query_key, value_vectors, routes):
    target, home_slot, source, sorted_slot, home_lookup, back_lookup, order_flat = routes
    groups = target.shape[0]
    member = jnp.arange(groups) % shared_query_key.shape[0]
    got_shared, got_values = trade_rows(
        gather_slots(shared_query_key, member, home_lookup),
        gather_slots(value_vectors, member, home_lookup),
    )
    shared_rows = settle(got_shared, source, sorted_slot)
    value_rows = settle(got_values, source, sorted_slot)
    halo = from_behind(
        (shared_rows[:, -BLOCK:], value_rows[:, -BLOCK:], order_flat[:, -BLOCK:]), ("seq", "sub"), 1
    )
    mixed, log_total = attend(shared_rows, value_rows, order_flat, halo)
    all_groups = jnp.arange(groups)
    got_mixed, got_total = trade_results(
        gather_slots(mixed, all_groups, back_lookup),
        gather_slots(log_total, all_groups, back_lookup),
    )
    return (
        settle(got_mixed, target, home_slot),
        settle(got_total, target, home_slot),
        (shared_rows, value_rows, halo),
    )


def round_outputs(normalized_input, query_key_weight, value_projection_weight, routes, rounds):
    shared_query_key = jnp.einsum(
        "srd,de->sre", normalized_input, query_key_weight, preferred_element_type=jnp.float32
    ).astype(jnp.bfloat16)
    value_vectors = jnp.einsum(
        "srd,de->sre", normalized_input, value_projection_weight, preferred_element_type=jnp.float32
    ).astype(jnp.bfloat16)
    mixed, log_total, kept = sorted_attention(shared_query_key, value_vectors, routes)
    sequences, row_count, features = normalized_input.shape
    outputs = mixed.reshape(rounds, sequences, row_count, features)
    totals = log_total.reshape(rounds, sequences, row_count, HEADS)
    return (shared_query_key, value_vectors, outputs, totals, kept)


def collect(weight_stack, layer_index):
    (
        attend_gain,
        attend_shift,
        query_key_weight,
        value_projection_weight,
        output_projection_weight,
        feed_gain,
        feed_shift,
        upper_projection_weight,
        upper_projection_bias,
        lower_projection_weight,
        lower_projection_bias,
    ) = tuple((shard_piece[layer_index] for shard_piece in weight_stack))
    return (
        lax.all_gather(attend_gain, ("seq", "sub"), axis=0, tiled=True),
        lax.all_gather(attend_shift, ("seq", "sub"), axis=0, tiled=True),
        lax.all_gather(query_key_weight, ("seq", "sub"), axis=0, tiled=True),
        lax.all_gather(value_projection_weight, ("seq", "sub"), axis=0, tiled=True),
        lax.all_gather(output_projection_weight, ("seq", "sub"), axis=0, tiled=True),
        lax.all_gather(feed_gain, ("seq", "sub"), axis=0, tiled=True),
        lax.all_gather(feed_shift, ("seq", "sub"), axis=0, tiled=True),
        lax.all_gather(upper_projection_weight, ("seq", "sub"), axis=0, tiled=True),
        lax.all_gather(upper_projection_bias, ("seq", "sub"), axis=0, tiled=True),
        lax.all_gather(lower_projection_weight, ("seq", "sub"), axis=0, tiled=True),
        lax.all_gather(lower_projection_bias, ("seq", "sub"), axis=0, tiled=True),
    )


def spread_grads(level_grads):
    (
        attend_gain,
        attend_shift,
        query_key_weight,
        value_projection_weight,
        output_projection_weight,
        feed_gain,
        feed_shift,
        upper_projection_weight,
        upper_projection_bias,
        lower_projection_weight,
        lower_projection_bias,
    ) = level_grads
    return (
        lax.psum_scatter(attend_gain, ("seq", "sub"), scatter_dimension=0, tiled=True),
        lax.psum_scatter(attend_shift, ("seq", "sub"), scatter_dimension=0, tiled=True),
        lax.psum_scatter(query_key_weight.astype(jnp.bfloat16), ("seq", "sub"), scatter_dimension=0, tiled=True),
        lax.psum_scatter(value_projection_weight.astype(jnp.bfloat16), ("seq", "sub"), scatter_dimension=0, tiled=True),
        lax.psum_scatter(output_projection_weight.astype(jnp.bfloat16), ("seq", "sub"), scatter_dimension=0, tiled=True),
        lax.psum_scatter(feed_gain, ("seq", "sub"), scatter_dimension=0, tiled=True),
        lax.psum_scatter(feed_shift, ("seq", "sub"), scatter_dimension=0, tiled=True),
        lax.psum_scatter(upper_projection_weight.astype(jnp.bfloat16), ("seq", "sub"), scatter_dimension=0, tiled=True),
        lax.psum_scatter(upper_projection_bias, ("seq", "sub"), scatter_dimension=0, tiled=True),
        lax.psum_scatter(lower_projection_weight.astype(jnp.bfloat16), ("seq", "sub"), scatter_dimension=0, tiled=True),
        lax.psum_scatter(lower_projection_bias, ("seq", "sub"), scatter_dimension=0, tiled=True),
    )


def layer_pass(first_half, second_half, grad_one, grad_two, params, routes, rounds):
    (
        attend_gain,
        attend_shift,
        query_key_weight,
        value_projection_weight,
        output_projection_weight,
        feed_gain,
        feed_shift,
        upper_projection_weight,
        upper_projection_bias,
        lower_projection_weight,
        lower_projection_bias,
    ) = params
    attend_norm, attend_pull = jax.vjp(
        layer_norm, second_half, attend_gain.astype(jnp.float32), attend_shift.astype(jnp.float32)
    )
    normalized_input = attend_norm.astype(jnp.bfloat16)
    shared_query_key, value_vectors, outputs, totals, kept = round_outputs(
        normalized_input, query_key_weight, value_projection_weight, routes, rounds
    )
    attention_result, combine_pull = jax.vjp(combine_rounds, outputs, totals)
    attended_low = attention_result.astype(jnp.bfloat16)
    top_one = first_half + jnp.einsum(
        "srd,de->sre", attended_low, output_projection_weight, preferred_element_type=jnp.float32
    )
    feed_norm, feed_pull = jax.vjp(
        layer_norm, top_one, feed_gain.astype(jnp.float32), feed_shift.astype(jnp.float32)
    )
    feed_forward_input = feed_norm.astype(jnp.bfloat16)
    prior_state = jnp.einsum(
        "srd,df->srf",
        feed_forward_input,
        upper_projection_weight,
        preferred_element_type=jnp.float32,
    ) + upper_projection_bias.astype(jnp.float32)
    hidden_activation, active_pull = jax.vjp(gelu_exact, prior_state)
    active_low = hidden_activation.astype(jnp.bfloat16)
    feed_out = jnp.einsum(
        "srf,fd->srd", active_low, lower_projection_weight, preferred_element_type=jnp.float32
    ) + lower_projection_bias.astype(jnp.float32)
    top_two = second_half + feed_out
    feed_grad = grad_two.astype(jnp.bfloat16)
    down_weight_grad = jnp.einsum(
        "srf,srd->fd", active_low, feed_grad, preferred_element_type=jnp.float32
    )
    down_bias_grad = jnp.sum(feed_grad.astype(jnp.float32), axis=(0, 1))
    active_grad = jnp.einsum(
        "srd,fd->srf", feed_grad, lower_projection_weight, preferred_element_type=jnp.float32
    )
    before_grad = active_pull(active_grad)[0].astype(jnp.bfloat16)
    up_weight_grad = jnp.einsum(
        "srd,srf->df", feed_forward_input, before_grad, preferred_element_type=jnp.float32
    )
    up_bias_grad = jnp.sum(before_grad.astype(jnp.float32), axis=(0, 1))
    norm_grad = jnp.einsum(
        "srf,df->srd", before_grad, upper_projection_weight, preferred_element_type=jnp.float32
    )
    one_part, feed_gain_grad, feed_shift_grad = feed_pull(norm_grad)
    total_one = grad_one + one_part
    out_grad = total_one.astype(jnp.bfloat16)
    output_weight_grad = jnp.einsum(
        "srd,sre->de", attended_low, out_grad, preferred_element_type=jnp.float32
    )
    attended_grad = jnp.einsum(
        "sre,de->srd", out_grad, output_projection_weight, preferred_element_type=jnp.float32
    )
    outputs_grad, totals_grad = combine_pull(attended_grad)
    target, home_slot, source, sorted_slot, home_lookup, back_lookup, order_flat = routes
    sequences, row_count, features = top_one.shape
    groups = rounds * sequences
    all_groups = jnp.arange(groups)
    outputs_low = outputs_grad.astype(jnp.bfloat16).reshape(groups, row_count, features)
    totals_low = totals_grad.astype(jnp.bfloat16).reshape(groups, row_count, HEADS)
    got_out, got_total = trade_rows(
        gather_slots(outputs_low, all_groups, home_lookup),
        gather_slots(totals_low, all_groups, home_lookup),
    )
    shared_rows, value_rows, halo = kept
    grad_shared, grad_values = attend_back(
        shared_rows,
        value_rows,
        order_flat,
        halo,
        settle(got_out, source, sorted_slot),
        settle(got_total, source, sorted_slot),
    )
    home_shared, home_values = trade_rows(
        gather_slots(grad_shared.astype(jnp.bfloat16), all_groups, back_lookup),
        gather_slots(grad_values.astype(jnp.bfloat16), all_groups, back_lookup),
    )
    shared_grad = jnp.sum(
        settle(home_shared, target, home_slot)
        .astype(jnp.float32)
        .reshape(rounds, sequences, row_count, features),
        axis=0,
    ).astype(jnp.bfloat16)
    values_grad = jnp.sum(
        settle(home_values, target, home_slot)
        .astype(jnp.float32)
        .reshape(rounds, sequences, row_count, features),
        axis=0,
    ).astype(jnp.bfloat16)
    shared_weight_grad = jnp.einsum(
        "srd,sre->de", normalized_input, shared_grad, preferred_element_type=jnp.float32
    )
    value_weight_grad = jnp.einsum(
        "srd,sre->de", normalized_input, values_grad, preferred_element_type=jnp.float32
    )
    normed_grad = jnp.einsum(
        "sre,de->srd", shared_grad, query_key_weight, preferred_element_type=jnp.float32
    ) + jnp.einsum(
        "sre,de->srd", values_grad, value_projection_weight, preferred_element_type=jnp.float32
    )
    two_part, attend_gain_grad, attend_shift_grad = attend_pull(normed_grad)
    total_two = grad_two + two_part
    level_grads = (
        attend_gain_grad,
        attend_shift_grad,
        shared_weight_grad,
        value_weight_grad,
        output_weight_grad,
        feed_gain_grad,
        feed_shift_grad,
        up_weight_grad,
        up_bias_grad,
        down_weight_grad,
        down_bias_grad,
    )
    return (top_one, top_two, total_one, total_two, level_grads)


def general_plan(
    first_half,
    second_half,
    grad_first,
    grad_second,
    attend_gain,
    attend_shift,
    query_key_weight,
    value_projection_weight,
    output_projection_weight,
    feed_gain,
    feed_shift,
    upper_projection_weight,
    upper_projection_bias,
    lower_projection_weight,
    lower_projection_bias,
    sort_order,
    sort_place,
):
    weight_stack = (
        attend_gain,
        attend_shift,
        query_key_weight,
        value_projection_weight,
        output_projection_weight,
        feed_gain,
        feed_shift,
        upper_projection_weight,
        upper_projection_bias,
        lower_projection_weight,
        lower_projection_bias,
    )
    devices = lax.axis_size(("seq", "sub"))
    rounds = sort_order.shape[1]
    row_count = first_half.shape[1]
    capacity = 2 * max(1, row_count // devices)
    params = collect(weight_stack, 0)
    routes = build_routes(sort_order[0], sort_place[0], devices, capacity)
    first_out, second_out, first_grad, second_grad, level_grads = layer_pass(
        first_half, second_half, grad_first, grad_second, params, routes, rounds
    )
    stacked = tuple((entry[None].astype(jnp.float32) for entry in spread_grads(level_grads)))
    return (first_out, second_out, first_grad, second_grad) + stacked


class Links:
    def __init__(self, planes, send, receive, local):
        self.send, self.receive, self.local = send, receive, local
        self.used, self.used_local = 0, 0
        self.planes = planes
        seq, sub = lax.axis_index("seq"), lax.axis_index("sub")
        self.z, self.x = seq // 2, lax.rem(seq, 2)
        self.y, self.core = sub // 2, lax.rem(sub, 2)
        self.p = self.x * 4 + sub

    def near(self, step):
        x = 1 - self.x if step & 4 else self.x
        y = 1 - self.y if step & 2 else self.y
        core = 1 - self.core if step & 1 else self.core
        return (self.z * 2 + x, y * 2 + core), x * 4 + y * 2 + core

    def along(self, step):
        to = lax.rem(self.z + step, self.planes)
        back = lax.rem(self.z + self.planes - step, self.planes)
        return (to * 2 + self.x, self.y * 2 + self.core), to, back

    def greet(self):
        barrier = pltpu.get_barrier_semaphore()
        targets = [self.near(step)[0] for step in range(1, 8)]
        targets += [self.along(step)[0] for step in range(1, self.planes)]
        for target in targets:
            pl.semaphore_signal(barrier, inc=1, device_id=target, device_id_type=pl.DeviceIdType.MESH)
        self.greeted = len(targets)

    def meet(self):
        pl.semaphore_wait(pltpu.get_barrier_semaphore(), self.greeted)

    def push(self, source, target, device):
        copy = pltpu.make_async_remote_copy(
            src_ref=source,
            dst_ref=target,
            send_sem=self.send.at[self.used],
            recv_sem=self.receive.at[self.used],
            device_id=device,
            device_id_type=pl.DeviceIdType.MESH,
        )
        self.used += 1
        copy.start()
        return copy

    def keep(self, source, target):
        copy = pltpu.make_async_copy(source, target, self.local.at[self.used_local])
        self.used_local += 1
        copy.start()
        return copy


COPIES = 96


def link_scratch():
    return [
        pltpu.SemaphoreType.DMA((COPIES,)),
        pltpu.SemaphoreType.DMA((COPIES,)),
        pltpu.SemaphoreType.DMA((16,)),
    ]


def along_z(source, target):
    def transfer(links, here, there):
        own = links.keep(source(here, links.z), target(there, links.z))
        copies = []
        for step in range(1, links.planes):
            device, to, _ = links.along(step)
            copies.append(links.push(source(here, to), target(there, links.z), device))
        yield
        own.wait()
        for copy in copies:
            copy.wait()

    return transfer


def over_plane(source, target):
    def transfer(links, here, there):
        own = links.keep(source(here, links.p), target(there, links.p))
        copies = []
        for step in (6, 7, 4, 5, 2, 3, 1):
            device, to = links.near(step)
            copies.append(links.push(source(here, to), target(there, links.p), device))
        yield
        own.wait()
        for copy in copies:
            copy.wait()

    return transfer


def over_chips(source, target):
    def transfer(links, here, there):
        own = links.keep(source(here, links.p), target(there, links.p))
        copies = []
        for step in (6, 4, 2):
            device, to = links.near(step)
            copies.append(links.push(source(here, to), target(there, links.p), device))
        sibling, _ = links.near(1)
        passed = [links.push(source(here, links.p), target(there, links.p), sibling)]
        yield
        for step, copy in zip((6, 4, 2), copies):
            copy.wait_recv()
            _, sender = links.near(step)
            passed.append(links.push(target(there, sender), target(there, sender), sibling))
        yield
        own.wait()
        for copy in copies:
            copy.wait_send()
        for copy in passed:
            copy.wait()

    return transfer


def everywhere(links, here, there):
    own = links.keep(here, there.at[links.z, links.p])
    copies = []
    for step in (6, 7, 4, 5, 2, 3, 1):
        copies.append(links.push(here, there.at[links.z, links.p], links.near(step)[0]))
    yield
    own.wait()
    for copy in copies:
        copy.wait()
    copies = []
    for step in range(1, links.planes):
        copies.append(links.push(there.at[links.z], there.at[links.z], links.along(step)[0]))
    yield
    for copy in copies:
        copy.wait()


def drive(transfers):
    while transfers:
        left = []
        for transfer in transfers:
            try:
                next(transfer)
                left.append(transfer)
            except StopIteration:
                pass
        transfers = left


def exchange(items, name, collective_id, planes):
    count = len(items)

    def body(*refs):
        links = Links(planes, *refs[2 * count :])
        links.greet()
        links.meet()
        drive([item[0](links, refs[k], refs[count + k]) for k, item in enumerate(items)])

    return pl.pallas_call(
        body,
        out_shape=[item[2] for item in items],
        in_specs=[pl.BlockSpec(memory_space=pl.ANY)] * count,
        out_specs=[pl.BlockSpec(memory_space=pl.ANY)] * count,
        scratch_shapes=link_scratch(),
        compiler_params=pltpu.CompilerParams(collective_id=collective_id, has_side_effects=True),
        name=name,
    )(*[item[1] for item in items])


def whole(ref, index):
    return ref


def block(ref, index):
    return ref.at[index]


def second(ref, index):
    return ref.at[:, index]


def like(kind, array, *shape):
    return (kind, array, jax.ShapeDtypeStruct(shape, array.dtype))


def pick_rows(table, index_ref, start, count):
    return jnp.concatenate(
        [table[pl.ds(index_ref[start + row], 1), :] for row in range(count)], axis=0
    )


def across(column):
    return jnp.broadcast_to(column, (128, 128)).T


def down(row):
    return jnp.broadcast_to(row, (128, 128)).T


def dot(a, b, contract):
    return lax.dot_general(a, b, (contract, ((), ())), preferred_element_type=jnp.float32)


def window_masks():
    query = lax.broadcasted_iota(jnp.int32, (128, 128), 0) // BLOCK
    key = lax.broadcasted_iota(jnp.int32, (128, 128), 1) // BLOCK
    return (query == 0) & (key == 1), key <= query


def key_scales(keys):
    rows = keys.astype(jnp.float32)
    mean_square = jnp.mean(rows * rows, axis=-1, keepdims=True) + 1e-06
    return rows, mean_square, lax.rsqrt(mean_square) / HEAD_DIM


def masked_scores(raw, scale, query_pos, key_pos, inside):
    scores = jnp.where(
        key_pos > query_pos, LATER, jnp.where(key_pos == query_pos, SELF, raw * scale)
    )
    return jnp.where(inside, scores, OUTSIDE)


def tile_rows(tile):
    return pl.ds(pl.multiple_of(tile * 128, 128), 128)


def sort_pair(order, table, first, second, tile):
    for part in range(4):
        start = pl.multiple_of(tile * 128 + part * 32, 32)
        picked = pick_rows(table, order, start, 32)
        first[pl.ds(start, 32), :] = picked[:, :128].astype(first.dtype)
        second[pl.ds(start, 32), :] = picked[:, 128:].astype(second.dtype)


def attend_kernel(
    tiles, unroll, order, place, order_rows, shared, values, shared_sorted, values_sorted, total_sorted,
    mixed_home, total_home, table, mixed, scales,
):
    def load(tile, carry):
        rows = tile_rows(tile)
        table[rows, :128] = shared[rows, :].astype(jnp.float32)
        table[rows, 128:] = values[rows, :].astype(jnp.float32)
        return carry

    lax.fori_loop(0, tiles, load, 0)
    sort = functools.partial(sort_pair, order, table, shared_sorted, values_sorted)
    for tile in [tiles - 1] + list(range(unroll)):
        sort(tile)
    inside_left, inside_here = window_masks()
    scales[0] = across(key_scales(shared_sorted[(tiles - 1) * 128 :, :])[2])

    def attend_tiles(step, carry):
        first = step * unroll
        numbers = [lax.rem(first + tiles - 1, tiles)] + [first + k for k in range(unroll)]
        keys = [shared_sorted[tile_rows(t), :] for t in numbers]
        vals = [values_sorted[tile_rows(t), :] for t in numbers]
        places = [order_rows[pl.ds(t, 1), :] for t in numbers]
        scale = [scales[0]] + [across(key_scales(k)[2]) for k in keys[1:]]
        scales[0] = scale[-1]
        for k in range(unroll):
            sort(lax.rem(first + unroll + k, tiles))
        for k in range(unroll):
            rows = tile_rows(first + k)
            query_pos = down(places[k + 1])
            score_left = masked_scores(
                dot(keys[k + 1], keys[k], ((1,), (1,))), scale[k], query_pos, places[k], inside_left
            )
            score_here = masked_scores(
                dot(keys[k + 1], keys[k + 1], ((1,), (1,))),
                scale[k + 1],
                query_pos,
                places[k + 1],
                inside_here,
            )
            highest = jnp.max(jnp.maximum(score_left, score_here), axis=-1, keepdims=True)
            total = highest + jnp.log(
                jnp.sum(
                    jnp.exp(score_left - highest) + jnp.exp(score_here - highest),
                    axis=-1,
                    keepdims=True,
                )
            )
            prob_left = jnp.exp(score_left - total).astype(jnp.bfloat16)
            prob_here = jnp.exp(score_here - total).astype(jnp.bfloat16)
            mixed[rows, :128] = dot(prob_left, vals[k], ((1,), (0,))) + dot(
                prob_here, vals[k + 1], ((1,), (0,))
            )
            total = jnp.broadcast_to(total, (128, 128))
            mixed[rows, 128:] = total
            total_sorted[rows, :] = total
        return carry

    lax.fori_loop(0, tiles // unroll, attend_tiles, 0)

    def unsort(tile, carry):
        totals = []
        for part in range(4):
            start = pl.multiple_of(tile * 128 + part * 32, 32)
            picked = pick_rows(mixed, place, start, 32)
            mixed_home[pl.ds(start, 32), :] = picked[:, :128].astype(jnp.bfloat16)
            totals.append(picked[:, 128:])
        total_home[lax.rem(tile, 8), pl.ds(tile // 8, 1), :] = jnp.concatenate(totals, axis=0).T[:1, :]
        return carry

    lax.fori_loop(0, tiles, unsort, 0)


def attend_back_kernel(
    tiles, unroll, order, place, order_rows, shared_sorted, values_sorted, total_sorted, grad_mixed, grad_total,
    grad_shared_home, grad_values_home, table, grad_sorted, grad_total_sorted, scales, scale_sums, sums,
):
    def load(tile, carry):
        rows = tile_rows(tile)
        table[rows, :128] = grad_mixed[rows, :].astype(jnp.float32)
        table[rows, 128:] = down(grad_total[lax.rem(tile, 8), pl.ds(tile // 8, 1), :])
        return carry

    lax.fori_loop(0, tiles, load, 0)
    sums[tile_rows(tiles - 1), :] = jnp.zeros((128, 256), jnp.float32)
    sort = functools.partial(sort_pair, order, table, grad_sorted, grad_total_sorted)
    for tile in range(unroll):
        sort(tile)
    inside_left, inside_here = window_masks()
    scales[0] = across(key_scales(shared_sorted[(tiles - 1) * 128 :, :])[2])
    scale_sums[...] = jnp.zeros_like(scale_sums)

    def back_tiles(step, carry):
        first = step * unroll
        left = lax.rem(first + tiles - 1, tiles)
        numbers = [left] + [first + k for k in range(unroll)]
        keys = [shared_sorted[tile_rows(t), :] for t in numbers]
        vals = [values_sorted[tile_rows(t), :] for t in numbers]
        places = [order_rows[pl.ds(t, 1), :] for t in numbers]
        grads = [grad_sorted[tile_rows(t), :] for t in numbers[1:]]
        grad_totals = [grad_total_sorted[tile_rows(t), :] for t in numbers[1:]]
        totals = [total_sorted[tile_rows(t), :] for t in numbers[1:]]
        scale = [scales[0]] + [across(key_scales(k)[2]) for k in keys[1:]]
        scales[0] = scale[-1]
        for k in range(unroll):
            sort(lax.rem(first + unroll + k, tiles))
        key_sums, value_sums, scale_parts = [0.0] * (unroll + 1), [0.0] * (unroll + 1), [0.0] * (unroll + 1)
        for k in range(unroll):
            here, before, grad = keys[k + 1], keys[k], grads[k]
            query_pos = down(places[k + 1])
            raw_left = dot(here, before, ((1,), (1,)))
            raw_here = dot(here, here, ((1,), (1,)))
            prob_left = jnp.exp(
                masked_scores(raw_left, scale[k], query_pos, places[k], inside_left) - totals[k]
            )
            prob_here = jnp.exp(
                masked_scores(raw_here, scale[k + 1], query_pos, places[k + 1], inside_here) - totals[k]
            )
            grad_prob_left = dot(grad, vals[k], ((1,), (1,)))
            grad_prob_here = dot(grad, vals[k + 1], ((1,), (1,)))
            inner = jnp.sum(
                prob_left * grad_prob_left + prob_here * grad_prob_here, axis=-1, keepdims=True
            )
            shift = grad_totals[k] - inner
            keep_left = inside_left & (places[k] < query_pos)
            keep_here = inside_here & (places[k + 1] < query_pos)
            grad_score_left = jnp.where(keep_left, prob_left * (grad_prob_left + shift), 0.0)
            grad_score_here = jnp.where(keep_here, prob_here * (grad_prob_here + shift), 0.0)
            scale_parts[k] += jnp.sum(grad_score_left * raw_left, axis=0, keepdims=True)
            scale_parts[k + 1] += jnp.sum(grad_score_here * raw_here, axis=0, keepdims=True)
            grad_raw_left = (grad_score_left * scale[k]).astype(jnp.bfloat16)
            grad_raw_here = (grad_score_here * scale[k + 1]).astype(jnp.bfloat16)
            key_sums[k + 1] += (
                dot(grad_raw_left, before, ((1,), (0,)))
                + dot(grad_raw_here, here, ((1,), (0,)))
                + dot(grad_raw_here, here, ((0,), (0,)))
            )
            key_sums[k] += dot(grad_raw_left, here, ((0,), (0,)))
            value_sums[k + 1] += dot(prob_here.astype(jnp.bfloat16), grad, ((0,), (0,)))
            value_sums[k] += dot(prob_left.astype(jnp.bfloat16), grad, ((0,), (0,)))
        for k, tile in enumerate(numbers[1:]):
            sums[tile_rows(tile), :128] = key_sums[k + 1]
            sums[tile_rows(tile), 128:] = value_sums[k + 1]
            scale_sums[pl.ds(tile, 1), :] = scale_parts[k + 1]
        extra = pl.ds(pl.multiple_of(jnp.where(step == 0, tiles, left) * 128, 128), 128)
        extra_row = pl.ds(jnp.where(step == 0, tiles, left), 1)
        sums[extra, :128] += key_sums[0]
        sums[extra, 128:] += value_sums[0]
        scale_sums[extra_row, :] += scale_parts[0]
        return carry

    sums[pl.ds(tiles * 128, 128), :] = jnp.zeros((128, 256), jnp.float32)
    lax.fori_loop(0, tiles // unroll, back_tiles, 0)
    last = tile_rows(tiles - 1)
    sums[last, :] += sums[pl.ds(tiles * 128, 128), :]
    scale_sums[pl.ds(tiles - 1, 1), :] += scale_sums[pl.ds(tiles, 1), :]

    def finish(step, carry):
        for part in range(2):
            tile = step * 2 + part
            rows = tile_rows(tile)
            keys, mean_square, scale = key_scales(shared_sorted[rows, :])
            factor = down(scale_sums[pl.ds(tile, 1), :]) * (scale / (mean_square * HEAD_DIM))
            sums[rows, :128] -= factor * keys
        return carry

    lax.fori_loop(0, tiles // 2, finish, 0)

    def unsort(tile, carry):
        sort_pair(place, sums, grad_shared_home, grad_values_home, tile)
        return carry

    lax.fori_loop(0, tiles, unsort, 0)


VMEM = pl.BlockSpec(memory_space=pltpu.VMEM)
SMEM = pl.BlockSpec(memory_space=pltpu.SMEM)
ANY = pl.BlockSpec(memory_space=pl.ANY)


def beside(kernel, inputs, outputs, scratch, items, planes):
    count = len(items)

    def body(*refs):
        refs = list(refs)
        own, refs = refs[:inputs], refs[inputs:]
        here, refs = refs[:count], refs[count:]
        own, refs = own + refs[:outputs], refs[outputs:]
        there, refs = refs[:count], refs[count:]
        links = Links(planes, *refs[scratch:])
        links.greet()
        links.meet()
        transfers = [item[0](links, here[k], there[k]) for k, item in enumerate(items)]
        for transfer in transfers:
            next(transfer)
        kernel(*own, *refs[:scratch])
        drive(transfers)

    return body


def attend_head(order, place, order_rows, shared, values, items, collective_id, planes, unroll=2):
    length = shared.shape[0]
    rows = jax.ShapeDtypeStruct((length, HEAD_DIM), jnp.bfloat16)
    scratch = [
        pltpu.VMEM((length, 256), jnp.float32),
        pltpu.VMEM((length, 256), jnp.float32),
        pltpu.VMEM((1, 128, 128), jnp.float32),
    ]
    kernel = functools.partial(attend_kernel, length // 128, unroll)
    return pl.pallas_call(
        beside(kernel, 5, 5, len(scratch), items, planes),
        out_shape=[
            rows,
            rows,
            jax.ShapeDtypeStruct((length, HEAD_DIM), jnp.float32),
            rows,
            jax.ShapeDtypeStruct((8, 8, 128), jnp.float32),
        ]
        + [item[2] for item in items],
        in_specs=[SMEM, SMEM, VMEM, VMEM, VMEM] + [ANY] * len(items),
        out_specs=[VMEM] * 5 + [ANY] * len(items),
        scratch_shapes=scratch + link_scratch(),
        compiler_params=pltpu.CompilerParams(
            vmem_limit_bytes=40 << 20, collective_id=collective_id, has_side_effects=True
        ),
        name="attend",
    )(order, place, order_rows, shared, values, *[item[1] for item in items])


def attend_head_back(
    order, place, order_rows, shared_sorted, values_sorted, total_sorted, grad, grad_total,
    items, collective_id, planes, unroll=2,
):
    length = grad.shape[0]
    rows = jax.ShapeDtypeStruct((length, HEAD_DIM), jnp.bfloat16)
    scratch = [
        pltpu.VMEM((length, 256), jnp.float32),
        pltpu.VMEM((length, HEAD_DIM), jnp.bfloat16),
        pltpu.VMEM((length, HEAD_DIM), jnp.float32),
        pltpu.VMEM((1, 128, 128), jnp.float32),
        pltpu.VMEM((length // 128 + 8, 128), jnp.float32),
        pltpu.VMEM((length + 128, 256), jnp.float32),
    ]
    kernel = functools.partial(attend_back_kernel, length // 128, unroll)
    return pl.pallas_call(
        beside(kernel, 8, 2, len(scratch), items, planes),
        out_shape=[rows, rows] + [item[2] for item in items],
        in_specs=[SMEM, SMEM] + [VMEM] * 6 + [ANY] * len(items),
        out_specs=[VMEM] * 2 + [ANY] * len(items),
        scratch_shapes=scratch + link_scratch(),
        compiler_params=pltpu.CompilerParams(
            vmem_limit_bytes=40 << 20, collective_id=collective_id, has_side_effects=True
        ),
        name="attend_back",
    )(
        order, place, order_rows, shared_sorted, values_sorted, total_sorted, grad, grad_total,
        *[item[1] for item in items],
    )


def sum_small_kernel(planes, items, *refs):
    count = len(items)
    tiles, here, refs = refs[0], refs[1 : 1 + count], refs[1 + count :]
    result, there, refs = refs[0], refs[1 : 1 + count], refs[1 + count :]
    arrived, summed, refs = refs[0], refs[1], refs[2:]
    links = Links(planes, *refs)
    links.greet()
    links.meet()
    transfers = [item[0](links, here[k], there[k]) for k, item in enumerate(items)]
    small = over_plane(block, block)(links, tiles, arrived)
    next(small)
    for transfer in transfers:
        next(transfer)
    drive([small])
    summed[...] = jnp.sum(arrived[...], axis=0)
    drive([along_z(whole, block)(links, summed, result)] + transfers)


def sum_small(tiles, items, collective_id, planes):
    return pl.pallas_call(
        functools.partial(sum_small_kernel, planes, items),
        out_shape=[jax.ShapeDtypeStruct((planes,) + tiles.shape[1:], tiles.dtype)]
        + [item[2] for item in items],
        in_specs=[VMEM] + [ANY] * len(items),
        out_specs=[VMEM] + [ANY] * len(items),
        scratch_shapes=[
            pltpu.VMEM(tiles.shape, tiles.dtype),
            pltpu.VMEM(tiles.shape[1:], tiles.dtype),
        ]
        + link_scratch(),
        compiler_params=pltpu.CompilerParams(collective_id=collective_id, has_side_effects=True),
        name="sum_small",
    )(tiles, *[item[1] for item in items])


def normal_parts(rows):
    center = jnp.mean(rows, axis=-1, keepdims=True)
    offset = rows - center
    spread = jnp.mean(offset * offset, axis=-1, keepdims=True)
    inverse = lax.rsqrt(spread + 1e-05)
    return offset * inverse, inverse


def norm_back(grad, rows, gain):
    unit, inverse = normal_parts(rows)
    scaled = grad * gain
    shared = jnp.mean(scaled, axis=-1, keepdims=True)
    along = jnp.mean(scaled * unit, axis=-1, keepdims=True)
    return (
        (scaled - shared - unit * along) * inverse,
        jnp.sum(grad * unit, axis=0, keepdims=True),
        jnp.sum(grad, axis=0, keepdims=True),
    )


def gelu_parts(rows):
    below = 0.5 * (1.0 + lax.erf(rows * 0.7071067811865476))
    bell = jnp.exp(-0.5 * rows * rows) * 0.3989422804014327
    return rows * below, below + rows * bell


def feed_kernel(
    planes,
    mixed, total, x1, wo_in, gain, shift, wup_in, bias_up, wdown_in, df_in, g1,
    y1_out, g1_out, dout_out, attended_out, dmixed_home, dtotal_home, y2_out, up_grad_out, down_grad_out,
    up_bias_out, gain_out, shift_out,
    wo, wup, wdown, df, weights, attended, arrived, h2, dact, act, dpre, kept, to_sibling, from_sibling,
    to_chip, from_chip, up_grad, down_grad, y2, dout, datt_out, datt, dmixed, dtotal, send, receive, local,
):
    low, full = jnp.bfloat16, jnp.float32
    links = Links(planes, send, receive, local)
    links.greet()
    loads = [links.keep(a, b) for a, b in ((wo_in, wo), (df_in, df), (wdown_in, wdown), (wup_in, wup))]

    def combine(z, carry):
        for x in range(2):
            totals = [down(total[x * 4 + u, pl.ds(z, 1), :]) for u in range(4)]
            highest = jnp.maximum(
                jnp.maximum(totals[0], totals[1]), jnp.maximum(totals[2], totals[3])
            )
            parts = [jnp.exp(t - highest) for t in totals]
            inverse = 1.0 / (parts[0] + parts[1] + parts[2] + parts[3])
            result = 0.0
            for u in range(4):
                weight = parts[u] * inverse
                weights[x * 4 + u, z] = weight
                result += weight * mixed[x * 4 + u, z].astype(full)
            attended[z, :, x * 128 : (x + 1) * 128] = result.astype(low)
        return carry

    lax.fori_loop(0, planes, combine, 0)
    links.meet()
    share = along_z(block, block)(links, attended, arrived)
    next(share)
    keep_attended = links.keep(attended, attended_out)
    loads[0].wait()
    drive([share])
    y1 = x1[...]
    for z in range(planes):
        y1 += dot(arrived[z], wo[z * 256 : (z + 1) * 256, :], ((1,), (0,)))
    y1_out[...] = y1
    unit, _ = normal_parts(y1)
    own_rows = pl.ds(pl.multiple_of(links.p * 128, 128), 128)
    h2[own_rows, :] = (unit * gain[...] + shift[...]).astype(low)

    def rows_of(index):
        return pl.ds(pl.multiple_of(index * 128, 128), 128)

    sibling, _ = links.near(1)
    own_h2 = h2.at[own_rows, :]
    direct = {step: links.push(own_h2, own_h2, links.near(step)[0]) for step in (6, 4, 2)}
    handed = {0: links.push(own_h2, own_h2, sibling)}
    for load in loads[1:]:
        load.wait()

    def upper_back(part, carry):
        rows = pl.ds(pl.multiple_of(part * 256, 256), 256)
        dact[rows, :] = dot(df[rows, :], wdown[...], ((1,), (1,)))
        return carry

    lax.fori_loop(0, 4, upper_back, 0)

    def pass_on(step):
        direct[step].wait_recv()
        block_rows = h2.at[rows_of(links.near(step)[1]), :]
        handed[step] = links.push(block_rows, block_rows, sibling)

    def feed(slot, step):
        handed[step].wait_recv()
        chip = links.near(step)[1] // 2
        rows = pl.ds(pl.multiple_of(chip * 256, 256), 256)
        before = dot(h2[rows, :], wup[...], ((1,), (0,))) + bias_up[...]
        value, slope = gelu_parts(before)
        act[rows, :] = value.astype(low)
        grad = (dact[rows, :] * slope).astype(low)
        dpre[rows, :] = grad
        kept[slot] = dot(grad, wup[...], ((1,), (1,))).reshape(2, 128, -1).astype(low)
        return links.push(kept.at[slot, 1 - links.core], from_sibling.at[slot], sibling)

    def chip_sum(slot, step, traded):
        traded.wait_recv()
        result = kept[slot, links.core].astype(full) + from_sibling[slot].astype(full)
        if slot == 0:
            return result
        to_chip[slot - 1] = result.astype(low)
        return links.push(to_chip.at[slot - 1], from_chip.at[slot - 1], links.near(step)[0])

    pass_on(2)
    traded = [feed(0, 0)]
    pass_on(4)
    traded.append(feed(1, 2))
    sent = [chip_sum(1, 2, traded[1])]
    pass_on(6)
    traded.append(feed(2, 4))
    sent.append(chip_sum(2, 4, traded[2]))
    traded.append(feed(3, 6))
    sent.append(chip_sum(3, 6, traded[3]))
    own_sum = chip_sum(0, 0, traded[0])

    def upper_grad(part, carry):
        rows = pl.ds(pl.multiple_of(part * 256, 256), 256)
        up_grad[part] = dot(h2[:, rows], dpre[...], ((0,), (0,))).astype(low)
        return carry

    lax.fori_loop(0, planes, upper_grad, 0)
    share_up = along_z(block, block)(links, up_grad, up_grad_out)
    next(share_up)
    for copy in sent:
        copy.wait_recv()
    grad = own_sum + (
        from_chip[0].astype(full) + from_chip[1].astype(full) + from_chip[2].astype(full)
    )
    part, gain_grad, shift_grad = norm_back(grad, y1_out[...], gain[...])
    gain_out[...] = gain_grad
    shift_out[...] = shift_grad
    g1_new = g1[...] + part
    g1_out[...] = g1_new
    dout[...] = g1_new.astype(low)
    keep_dout = links.keep(dout, dout_out)
    for z in range(planes):
        datt_out[z] = dot(dout[...], wo[z * 256 : (z + 1) * 256, :], ((1,), (1,))).astype(low)
    share = along_z(block, block)(links, datt_out, datt)
    next(share)

    def lower_grad(part, carry):
        rows = pl.ds(pl.multiple_of(part * 128, 128), 128)
        down_grad[part] = dot(act[:, rows], df[...], ((0,), (0,))).astype(low)
        return carry

    lax.fori_loop(0, planes, lower_grad, 0)
    share_down = along_z(block, block)(links, down_grad, down_grad_out)
    next(share_down)
    up_bias_out[...] = jnp.sum(dpre[...].astype(full), axis=0, keepdims=True)
    drive([share])

    def combine_back(z, carry):
        for x in range(2):
            grad = datt[z, :, x * 128 : (x + 1) * 128].astype(full)
            chosen = [weights[x * 4 + u, z] for u in range(4)]
            inner = [
                jnp.sum(grad * mixed[x * 4 + u, z].astype(full), axis=-1, keepdims=True)
                for u in range(4)
            ]
            mean = sum(chosen[u] * inner[u] for u in range(4))
            for u in range(4):
                dmixed[x * 4 + u, z] = (chosen[u] * grad).astype(low)
                change = (chosen[u] * (inner[u] - mean)).astype(low).astype(full)
                dtotal[x * 4 + u, pl.ds(z, 1), :] = change.T[:1, :]
        return carry

    lax.fori_loop(0, planes, combine_back, 0)
    shares = [
        over_plane(block, second)(links, dmixed, dmixed_home),
        over_plane(block, block)(links, dtotal, dtotal_home),
    ]
    for transfer in shares:
        next(transfer)

    def lower(part, carry):
        rows = pl.ds(pl.multiple_of(part * 128, 128), 128)
        y2[part] = dot(act[rows, :], wdown[...], ((1,), (0,))).astype(low)
        return carry

    lax.fori_loop(0, 8, lower, 0)
    keep_y2 = links.keep(y2, y2_out)
    for copy in list(direct.values()) + traded + sent:
        copy.wait_send()
    for copy in handed.values():
        copy.wait_send()
    drive(shares + [share_up, share_down])
    for copy in (keep_attended, keep_dout, keep_y2):
        copy.wait()


def feed_stage(arguments, collective_id, planes):
    low, full = jnp.bfloat16, jnp.float32
    (mixed, total, x1, wo, gain, shift, wup, bias_up, wdown, df, g1) = arguments
    rows, width = x1.shape
    part = wup.shape[1]
    shape = jax.ShapeDtypeStruct
    outputs = [
        (shape((rows, width), full), VMEM),
        (shape((rows, width), full), VMEM),
        (shape((rows, width), low), ANY),
        (shape((planes, rows, 256), low), ANY),
        (shape((planes, 8, rows, HEAD_DIM), low), ANY),
        (shape((8, 8, rows), full), ANY),
        (shape((8, rows, width), low), ANY),
        (shape((planes, width // planes, part), low), ANY),
        (shape((planes, rows, width), low), ANY),
        (shape((1, part), full), VMEM),
        (shape((1, width), full), VMEM),
        (shape((1, width), full), VMEM),
    ]
    scratch = [
        (wo.shape, low),
        (wup.shape, low),
        (wdown.shape, low),
        (df.shape, low),
        ((8, planes, rows, HEAD_DIM), full),
        ((planes, rows, 256), low),
        ((planes, rows, 256), low),
        ((8 * rows, width), low),
        ((8 * rows, part), full),
        ((8 * rows, part), low),
        ((8 * rows, part), low),
        ((4, 2, rows, width), low),
        ((4, rows, width), low),
        ((4, rows, width), low),
        ((3, rows, width), low),
        ((3, rows, width), low),
        ((planes, width // planes, part), low),
        ((planes, rows, width), low),
        ((8, rows, width), low),
        ((rows, width), low),
        ((planes, rows, 256), low),
        ((planes, rows, 256), low),
        ((8, planes, rows, HEAD_DIM), low),
        ((8, 8, rows), full),
    ]
    return pl.pallas_call(
        functools.partial(feed_kernel, planes),
        out_shape=[o[0] for o in outputs],
        in_specs=[VMEM, VMEM, VMEM, ANY, VMEM, VMEM, ANY, VMEM, ANY, ANY, VMEM],
        out_specs=[o[1] for o in outputs],
        scratch_shapes=[pltpu.VMEM(*s) for s in scratch] + link_scratch(),
        compiler_params=pltpu.CompilerParams(
            vmem_limit_bytes=56 << 20, collective_id=collective_id, has_side_effects=True
        ),
        name="feed",
    )(*arguments)


def matmul(a, b, contract=((1,), (0,))):
    return dot(a, b, contract)


def plane_plan(
    n_seq,
    n_sub,
    first_half,
    second_half,
    grad_first,
    grad_second,
    attend_gain,
    attend_shift,
    query_key_weight,
    value_projection_weight,
    output_projection_weight,
    feed_gain,
    feed_shift,
    upper_projection_weight,
    upper_projection_bias,
    lower_projection_weight,
    lower_projection_bias,
    sort_order,
    sort_place,
):
    low, full = jnp.bfloat16, jnp.float32
    devices, planes, per_plane = n_seq * n_sub, n_seq // 2, 2 * n_sub
    rows, width = first_half.shape[1:]
    hidden = upper_projection_weight.shape[2]
    tokens = devices * rows
    line = planes * rows
    part = hidden // per_plane
    seq, sub = lax.axis_index("seq"), lax.axis_index("sub")
    me_p, me_z = lax.rem(seq, 2) * n_sub + sub, seq // 2
    trade = functools.partial(exchange, planes=planes)
    x1, x2, g1, g2 = (a[0] for a in (first_half, second_half, grad_first, grad_second))
    wqk, wv, wo = query_key_weight[0], value_projection_weight[0], output_projection_weight[0]
    wup, wdown = upper_projection_weight[0], lower_projection_weight[0]
    own = width // devices
    pair = 2 * HEAD_DIM

    def row_of(*vectors):
        return jnp.concatenate([v[0].astype(full) for v in vectors])[None]

    small = jnp.concatenate(
        [
            sort_order[0, :, 0].astype(full),
            sort_place[0, :, 0].astype(full),
            row_of(attend_gain, attend_shift, feed_gain, feed_shift),
            row_of(upper_projection_bias),
            jnp.pad(row_of(lower_projection_bias), ((0, 5), (0, rows - own))),
        ],
        axis=0,
    )
    small = jnp.pad(small, ((0, 16 - small.shape[0]), (0, 0)))

    def pair_columns(ref, z):
        return ref.at[:, pl.ds(pl.multiple_of(z * pair, pair), pair)]

    all_small, wqk_line, wv_line, wo_line = trade(
        [
            like(everywhere, small, planes, per_plane, 16, rows),
            like(along_z(pair_columns, block), wqk, planes, own, pair),
            like(along_z(pair_columns, block), wv, planes, own, pair),
            like(along_z(whole, block), wo, planes, own, width),
        ],
        "share_small",
        1,
    )
    all_small = all_small.reshape(devices, 16, rows)
    gain_a, shift_a, gain_f, shift_f = (
        all_small[:, 8, k * own : (k + 1) * own].reshape(width) for k in range(4)
    )
    bias_down = all_small[:, 10, :own].reshape(width)
    bias_up = jnp.take(
        all_small[:, 9].reshape(planes, per_plane, rows), me_p, axis=1
    ).reshape(planes * rows)
    order_rows = jnp.take(all_small[:, :4], sub, axis=1)
    order = order_rows.astype(jnp.int32).reshape(tokens)
    place = jnp.take(all_small[:, 4:8], sub, axis=1).astype(jnp.int32).reshape(tokens)

    normed, attend_pull = jax.vjp(layer_norm, x2, gain_a, shift_a)
    normed = normed.astype(low)

    def upper_columns(chunk):
        def columns(ref, p):
            return ref.at[:, pl.ds(pl.multiple_of((chunk * per_plane + p) * rows, rows), rows)]

        return like(over_plane(columns, block), wup, per_plane, own, rows)

    rows_of_pair = over_chips(whole, second)
    normed_line, wqk_pair, wv_pair, *wup_rows = trade(
        [
            like(along_z(whole, block), normed, planes, rows, width),
            like(rows_of_pair, wqk_line, planes, per_plane, own, pair),
            like(rows_of_pair, wv_line, planes, per_plane, own, pair),
        ]
        + [upper_columns(chunk) for chunk in range(planes)],
        "share_normed",
        2,
    )
    wup_rows = jnp.concatenate([a.reshape(per_plane * own, rows) for a in wup_rows], axis=1)
    normed_line = normed_line.reshape(line, width)
    wqk_pair, wv_pair = wqk_pair.reshape(width, pair), wv_pair.reshape(width, pair)
    shared = matmul(normed_line, wqk_pair).astype(low).reshape(planes, rows, pair)
    values = matmul(normed_line, wv_pair).astype(low).reshape(planes, rows, pair)

    def head_columns(ref, p):
        return ref.at[:, :, pl.ds(pl.multiple_of((p // 4) * HEAD_DIM, HEAD_DIM), HEAD_DIM)]

    to_head = over_chips(head_columns, second)
    head_shape = (planes, per_plane, rows, HEAD_DIM)
    head_shared, head_values = trade(
        [like(to_head, shared, *head_shape), like(to_head, values, *head_shape)], "to_heads", 3
    )
    df = g2.astype(low)
    (
        shared_sorted, values_sorted, total_sorted, mixed, total,
        wup_part, wdown_part, wo_all, df_plane,
    ) = attend_head(
        order,
        place,
        order_rows,
        head_shared.reshape(tokens, HEAD_DIM),
        head_values.reshape(tokens, HEAD_DIM),
        [
            like(along_z(whole, block), wup_rows, planes, per_plane * own, part),
            like(along_z(whole, block), wdown, planes, rows, width),
            like(over_chips(whole, second), wo_line, planes, per_plane, own, width),
            like(over_chips(whole, block), df, per_plane, rows, width),
        ],
        4,
        planes,
    )
    wup_part, wdown_part = wup_part.reshape(width, part), wdown_part.reshape(part, width)
    wo_all = wo_all.reshape(width, width)
    df_plane = df_plane.reshape(per_plane * rows, width)

    token_shape = (per_plane, planes, rows, HEAD_DIM)

    def to_tokens(array):
        return like(over_plane(second, block), array.reshape(head_shape), *token_shape)

    mixed, total = trade(
        [to_tokens(mixed), like(over_plane(block, block), total, *total.shape)], "heads_out", 5
    )
    traded_z, traded_plane = along_z(block, block), over_plane(block, block)
    down_bias_grad = jnp.sum(df.astype(full), axis=0)
    (
        y1, g1, dout, attended, dmixed, dtotal, y2_parts, up_grad, down_grad,
        up_bias_grad, feed_gain_grad, feed_shift_grad,
    ) = feed_stage(
        (
            mixed, total, x1, wo_all, gain_f[None], shift_f[None],
            wup_part, bias_up[None], wdown_part, df_plane, g1,
        ),
        6,
        planes,
    )
    attended = attended.reshape(line, pair)
    up_grad = jnp.sum(up_grad.astype(full), axis=0).reshape(per_plane, own, part)
    dshared, dvalues, y2_parts, dout_line = attend_head_back(
        order,
        place,
        order_rows,
        shared_sorted,
        values_sorted,
        total_sorted,
        dmixed.reshape(tokens, HEAD_DIM),
        dtotal,
        [
            like(traded_plane, y2_parts, *y2_parts.shape),
            like(along_z(whole, block), dout, planes, rows, width),
        ],
        11,
        planes,
    )
    y2 = x2 + (jnp.sum(y2_parts.astype(full), axis=0) + bias_down)
    out_grad = matmul(attended, dout_line.reshape(line, width), ((0,), (0,)))
    out_grad = out_grad.astype(low).reshape(per_plane, own, width)
    dshared, dvalues = trade([to_tokens(dshared), to_tokens(dvalues)], "grads_from_heads", 12)

    def over_rounds(array):
        array = jnp.sum(array.reshape(2, n_sub, line, HEAD_DIM).astype(full), axis=1)
        return jnp.swapaxes(array, 0, 1).reshape(line, pair).astype(low)

    dshared, dvalues = over_rounds(dshared), over_rounds(dvalues)
    de_parts = matmul(dshared, wqk_pair, ((1,), (1,))) + matmul(dvalues, wv_pair, ((1,), (1,)))
    de_parts = de_parts.astype(low).reshape(planes, rows, width)

    def to_owners(grad):
        grad = grad.astype(low).reshape(planes, per_plane, own, pair)
        return like(over_plane(second, block), grad, per_plane, planes, own, pair)

    de_parts, shared_grad, value_grad, out_grad, up_grad = trade(
        [
            like(traded_z, de_parts, *de_parts.shape),
            to_owners(matmul(normed_line, dshared, ((0,), (0,)))),
            to_owners(matmul(normed_line, dvalues, ((0,), (0,)))),
            like(traded_plane, out_grad, *out_grad.shape),
            like(traded_plane, up_grad, *up_grad.shape),
        ],
        "sum_second_grad",
        13,
    )
    two_part, attend_gain_grad, attend_shift_grad = attend_pull(
        jnp.sum(de_parts.astype(full), axis=0)
    )
    g2 = g2 + two_part
    shared_grad = jnp.sum(shared_grad.astype(full), axis=0)
    value_grad = jnp.sum(value_grad.astype(full), axis=0)

    def by_owner(vector):
        return jnp.swapaxes(vector.reshape(planes, per_plane, own), 0, 1).reshape(per_plane, 1, rows)

    vectors = [attend_gain_grad, attend_shift_grad, feed_gain_grad, feed_shift_grad, down_bias_grad]
    up_bias_grad = jnp.where(
        jnp.arange(per_plane)[:, None, None] == me_p, up_bias_grad.reshape(1, planes, rows), 0.0
    )
    tiles = jnp.concatenate([by_owner(v) for v in vectors] + [up_bias_grad], axis=1)
    tiles = jnp.pad(tiles, ((0, 0), (0, 16 - tiles.shape[1]), (0, 0)))
    vectors, shared_grad, value_grad = sum_small(
        tiles,
        [like(traded_z, shared_grad, planes, own, pair), like(traded_z, value_grad, planes, own, pair)],
        14,
        planes,
    )
    vectors = jnp.sum(vectors, axis=0)
    pieces = jnp.take(vectors[:5].reshape(5, planes, own), me_z, axis=1)
    up_bias_grad = jnp.take(vectors[5 : 5 + planes], me_z, axis=0)
    shared_grad, value_grad = (
        jnp.swapaxes(a, 0, 1).reshape(own, width) for a in (shared_grad, value_grad)
    )
    up_grad = jnp.transpose(up_grad.reshape(per_plane, own, planes, rows), (1, 2, 0, 3))
    outputs = (
        y1,
        y2,
        g1,
        g2,
        pieces[0],
        pieces[1],
        shared_grad,
        value_grad,
        jnp.sum(out_grad.astype(full), axis=0),
        pieces[2],
        pieces[3],
        up_grad.reshape(own, hidden),
        up_bias_grad,
        jnp.sum(down_grad.astype(full), axis=0),
        pieces[4],
    )
    return tuple((a[None] for a in outputs))


def on_device(n_seq, n_sub, *arguments):
    sequences, rows, width = arguments[0].shape
    rounds = arguments[-1].shape[1]
    fits = (
        sequences == 1
        and rows == 2 * BLOCK
        and rounds == n_sub
        and HEADS == n_seq
        and width == HEADS * HEAD_DIM
    )
    if fits:
        return plane_plan(n_seq, n_sub, *arguments)
    return general_plan(*arguments)


def solution(mesh):
    return jax.shard_map(
        functools.partial(on_device, mesh.shape["seq"], mesh.shape["sub"]),
        mesh=mesh,
        in_specs=(
            P(None, ("seq", "sub"), None),
            P(None, ("seq", "sub"), None),
            P(None, ("seq", "sub"), None),
            P(None, ("seq", "sub"), None),
            P(None, ("seq", "sub")),
            P(None, ("seq", "sub")),
            P(None, ("seq", "sub"), None),
            P(None, ("seq", "sub"), None),
            P(None, ("seq", "sub"), None),
            P(None, ("seq", "sub")),
            P(None, ("seq", "sub")),
            P(None, ("seq", "sub"), None),
            P(None, ("seq", "sub")),
            P(None, ("seq", "sub"), None),
            P(None, ("seq", "sub")),
            P(None, None, None, ("seq", "sub")),
            P(None, None, None, ("seq", "sub")),
        ),
        out_specs=(
            P(None, ("seq", "sub"), None),
            P(None, ("seq", "sub"), None),
            P(None, ("seq", "sub"), None),
            P(None, ("seq", "sub"), None),
            P(None, ("seq", "sub")),
            P(None, ("seq", "sub")),
            P(None, ("seq", "sub"), None),
            P(None, ("seq", "sub"), None),
            P(None, ("seq", "sub"), None),
            P(None, ("seq", "sub")),
            P(None, ("seq", "sub")),
            P(None, ("seq", "sub"), None),
            P(None, ("seq", "sub")),
            P(None, ("seq", "sub"), None),
            P(None, ("seq", "sub")),
        ),
        check_vma=False,
    )
```

```python
import functools

import jax
import jax.numpy as jnp
from jax import lax
from jax.experimental import pallas as pl
from jax.experimental.pallas import tpu as pltpu
from jax.sharding import PartitionSpec as P

HEADS = 8
HEAD_DIM = 128
BLOCK = 64
LATER = -1000000000.0
SELF = -100000.0
OUTSIDE = -3e38


def from_behind(block, axis, distance):
    devices = range(lax.axis_size(axis))
    route = [((i - distance) % len(devices), i) for i in devices]
    return lax.ppermute(block, axis, route)


def layer_norm(value_vectors, scaling, shifts):
    center = jnp.mean(value_vectors, axis=-1, keepdims=True)
    offset = value_vectors - center
    spread = jnp.mean(offset * offset, axis=-1, keepdims=True)
    return offset * lax.rsqrt(spread + 1e-05) * scaling + shifts


def gelu_exact(value_vectors):
    return jax.nn.gelu(value_vectors, approximate=False)


def combine_rounds(outputs, totals):
    highest = jnp.max(totals, axis=0, keepdims=True)
    weights = jnp.exp(totals - highest)
    weights = weights / jnp.sum(weights, axis=0, keepdims=True)
    by_head = outputs.reshape(outputs.shape[:-1] + (totals.shape[-1], -1))
    return jnp.sum(weights[..., None] * by_head, axis=0).reshape(outputs.shape[1:])


def home_slots(places, row_count):
    target = places // row_count
    prior_state = (target[:, None, :] == target[:, :, None]) & (
        places[:, None, :] < places[:, :, None]
    )
    return (target, jnp.sum(prior_state.astype(jnp.int32), axis=2))


def sorted_slots(orders, row_count):
    source = orders // row_count
    ladder = jnp.arange(row_count, dtype=jnp.int32)
    prior_state = (source[:, None, :] == source[:, :, None]) & (
        ladder[None, None, :] < ladder[None, :, None]
    )
    return (source, jnp.sum(prior_state.astype(jnp.int32), axis=2))


def slot_lookup(owners, slot_index, devices, capacity):
    groups, row_count = owners.shape
    flat_index = owners * capacity + slot_index
    lookup = jnp.full((groups, devices * capacity), row_count, jnp.int32)
    filler = jnp.broadcast_to(jnp.arange(row_count, dtype=jnp.int32), (groups, row_count))
    lookup = lookup.at[jnp.arange(groups)[:, None], flat_index].set(filler)
    return jnp.transpose(lookup.reshape(groups, devices, capacity), (1, 0, 2))


def gather_slots(value_vectors, member, lookup):
    padding = jnp.zeros((value_vectors.shape[0], 1) + value_vectors.shape[2:], value_vectors.dtype)
    padded = jnp.concatenate([value_vectors, padding], axis=1)
    return padded[member[None, :, None], lookup]


def settle(received, owners, slot_index):
    return received[owners, jnp.arange(owners.shape[0])[:, None], slot_index]


def build_routes(orders, places, devices, capacity):
    rounds, sequences, row_count = orders.shape
    order_flat = orders.reshape(rounds * sequences, row_count)
    target, home_slot = home_slots(places.reshape(rounds * sequences, row_count), row_count)
    source, sorted_slot = sorted_slots(order_flat, row_count)
    home_lookup = slot_lookup(target, home_slot, devices, capacity)
    back_lookup = slot_lookup(source, sorted_slot, devices, capacity)
    return (target, home_slot, source, sorted_slot, home_lookup, back_lookup, order_flat)


def trade_rows(first_part, second_part):
    return (
        lax.all_to_all(first_part, ("seq", "sub"), split_axis=0, concat_axis=0, tiled=True),
        lax.all_to_all(second_part, ("seq", "sub"), split_axis=0, concat_axis=0, tiled=True),
    )


def trade_results(first_part, second_part):
    return (
        lax.all_to_all(first_part, ("seq", "sub"), split_axis=0, concat_axis=0, tiled=True),
        lax.all_to_all(second_part, ("seq", "sub"), split_axis=0, concat_axis=0, tiled=True),
    )


def window(rows_here, rows_left):
    groups = rows_here.shape[0]
    extended = jnp.concatenate([rows_left, rows_here], axis=1)
    extended = extended.reshape((groups, -1, BLOCK) + rows_here.shape[2:])
    return jnp.concatenate([extended[:, :-1], extended[:, 1:]], axis=2)


def score_parts(shared_rows, order_rows, halo_shared, halo_order):
    groups, row_count, features = shared_rows.shape
    blocks = row_count // BLOCK
    queries = shared_rows.reshape(groups, blocks, BLOCK, HEADS, HEAD_DIM)
    key_rows = window(shared_rows, halo_shared).reshape(groups, blocks, 2 * BLOCK, HEADS, HEAD_DIM)
    key_float = key_rows.astype(jnp.float32)
    mean_square = jnp.mean(key_float * key_float, axis=-1) + 1e-06
    key_scale = lax.rsqrt(mean_square) / HEAD_DIM
    raw_scores = jnp.einsum(
        "gcqhd,gckhd->gchqk", queries, key_rows, preferred_element_type=jnp.float32
    )
    query_pos = order_rows.reshape(groups, blocks, BLOCK)
    key_pos = window(order_rows, halo_order)
    is_later = (key_pos[:, :, None, :] > query_pos[:, :, :, None])[:, :, None]
    is_self = (key_pos[:, :, None, :] == query_pos[:, :, :, None])[:, :, None]
    scale_row = jnp.transpose(key_scale, (0, 1, 3, 2))[:, :, :, None, :]
    scores = jnp.where(
        is_later, -1000000000.0, jnp.where(is_self, -100000.0, raw_scores * scale_row)
    )
    highest = jnp.max(scores, axis=-1, keepdims=True)
    log_total = highest + jnp.log(jnp.sum(jnp.exp(scores - highest), axis=-1, keepdims=True))
    probability = jnp.exp(scores - log_total)
    return (
        queries,
        key_rows,
        key_float,
        mean_square,
        key_scale,
        scale_row,
        raw_scores,
        is_later | is_self,
        log_total,
        probability,
    )


def attend(shared_rows, value_rows, order_rows, halo):
    halo_shared, halo_value, halo_order = halo
    parts = score_parts(shared_rows, order_rows, halo_shared, halo_order)
    groups, row_count, features = shared_rows.shape
    value_keys = window(value_rows, halo_value).reshape(
        groups, row_count // BLOCK, 2 * BLOCK, HEADS, HEAD_DIM
    )
    mixed = jnp.einsum(
        "gchqk,gckhd->gcqhd",
        parts[9].astype(jnp.bfloat16),
        value_keys,
        preferred_element_type=jnp.float32,
    )
    log_total = jnp.transpose(parts[8][..., 0], (0, 1, 3, 2)).reshape(groups, row_count, HEADS)
    return (mixed.reshape(groups, row_count, features), log_total)


def fold_window(grads_window, groups, row_count, features):
    grads_window = grads_window.reshape(groups, row_count // BLOCK, 2 * BLOCK, features)
    empty = jnp.zeros((groups, 1, BLOCK, features), jnp.float32)
    extended = jnp.concatenate([grads_window[:, :, :BLOCK], empty], axis=1) + jnp.concatenate(
        [empty, grads_window[:, :, BLOCK:]], axis=1
    )
    return (extended[:, 1:].reshape(groups, row_count, features), extended[:, 0])


def attend_back(shared_rows, value_rows, order_rows, halo, grad_out, grad_total):
    halo_shared, halo_value, halo_order = halo
    (
        queries,
        key_rows,
        key_float,
        mean_square,
        key_scale,
        scale_row,
        raw_scores,
        masked,
        log_total,
        probability,
    ) = score_parts(shared_rows, order_rows, halo_shared, halo_order)
    groups, row_count, features = shared_rows.shape
    blocks = row_count // BLOCK
    value_keys = window(value_rows, halo_value).reshape(groups, blocks, 2 * BLOCK, HEADS, HEAD_DIM)
    prob_low = probability.astype(jnp.bfloat16)
    grad_heads = grad_out.reshape(groups, blocks, BLOCK, HEADS, HEAD_DIM)
    grad_log = jnp.transpose(
        grad_total.astype(jnp.float32).reshape(groups, blocks, BLOCK, HEADS), (0, 1, 3, 2)
    )[..., None]
    grad_prob = jnp.einsum(
        "gcqhd,gckhd->gchqk", grad_heads, value_keys, preferred_element_type=jnp.float32
    )
    inner = jnp.sum(probability * grad_prob, axis=-1, keepdims=True)
    grad_score = jnp.where(masked, 0.0, probability * (grad_prob - inner + grad_log))
    grad_scale = jnp.transpose(jnp.sum(grad_score * raw_scores, axis=3), (0, 1, 3, 2))
    grad_raw = (grad_score * scale_row).astype(jnp.bfloat16)
    grad_query = jnp.einsum(
        "gchqk,gckhd->gcqhd", grad_raw, key_rows, preferred_element_type=jnp.float32
    )
    grad_key = jnp.einsum(
        "gchqk,gcqhd->gckhd", grad_raw, queries, preferred_element_type=jnp.float32
    )
    grad_key = grad_key - (grad_scale * key_scale / mean_square)[..., None] * key_float / HEAD_DIM
    grad_value = jnp.einsum(
        "gchqk,gcqhd->gckhd", prob_low, grad_heads, preferred_element_type=jnp.float32
    )
    key_home, key_left = fold_window(grad_key, groups, row_count, features)
    value_home, value_left = fold_window(grad_value, groups, row_count, features)
    back_key, back_value = from_behind((key_left, value_left), ("seq", "sub"), -1)
    grad_shared = grad_query.reshape(groups, row_count, features) + key_home
    grad_shared = grad_shared.at[:, row_count - BLOCK :].add(back_key)
    grad_values = value_home.at[:, row_count - BLOCK :].add(back_value)
    return (grad_shared, grad_values)


def sorted_attention(shared_query_key, value_vectors, routes):
    target, home_slot, source, sorted_slot, home_lookup, back_lookup, order_flat = routes
    groups = target.shape[0]
    member = jnp.arange(groups) % shared_query_key.shape[0]
    got_shared, got_values = trade_rows(
        gather_slots(shared_query_key, member, home_lookup),
        gather_slots(value_vectors, member, home_lookup),
    )
    shared_rows = settle(got_shared, source, sorted_slot)
    value_rows = settle(got_values, source, sorted_slot)
    halo = from_behind(
        (shared_rows[:, -BLOCK:], value_rows[:, -BLOCK:], order_flat[:, -BLOCK:]), ("seq", "sub"), 1
    )
    mixed, log_total = attend(shared_rows, value_rows, order_flat, halo)
    all_groups = jnp.arange(groups)
    got_mixed, got_total = trade_results(
        gather_slots(mixed, all_groups, back_lookup),
        gather_slots(log_total, all_groups, back_lookup),
    )
    return (
        settle(got_mixed, target, home_slot),
        settle(got_total, target, home_slot),
        (shared_rows, value_rows, halo),
    )


def round_outputs(normalized_input, query_key_weight, value_projection_weight, routes, rounds):
    shared_query_key = jnp.einsum(
        "srd,de->sre", normalized_input, query_key_weight, preferred_element_type=jnp.float32
    ).astype(jnp.bfloat16)
    value_vectors = jnp.einsum(
        "srd,de->sre", normalized_input, value_projection_weight, preferred_element_type=jnp.float32
    ).astype(jnp.bfloat16)
    mixed, log_total, kept = sorted_attention(shared_query_key, value_vectors, routes)
    sequences, row_count, features = normalized_input.shape
    outputs = mixed.reshape(rounds, sequences, row_count, features)
    totals = log_total.reshape(rounds, sequences, row_count, HEADS)
    return (shared_query_key, value_vectors, outputs, totals, kept)


def collect(weight_stack, layer_index):
    (
        attend_gain,
        attend_shift,
        query_key_weight,
        value_projection_weight,
        output_projection_weight,
        feed_gain,
        feed_shift,
        upper_projection_weight,
        upper_projection_bias,
        lower_projection_weight,
        lower_projection_bias,
    ) = tuple((shard_piece[layer_index] for shard_piece in weight_stack))
    return (
        lax.all_gather(attend_gain, ("seq", "sub"), axis=0, tiled=True),
        lax.all_gather(attend_shift, ("seq", "sub"), axis=0, tiled=True),
        lax.all_gather(query_key_weight, ("seq", "sub"), axis=0, tiled=True),
        lax.all_gather(value_projection_weight, ("seq", "sub"), axis=0, tiled=True),
        lax.all_gather(output_projection_weight, ("seq", "sub"), axis=0, tiled=True),
        lax.all_gather(feed_gain, ("seq", "sub"), axis=0, tiled=True),
        lax.all_gather(feed_shift, ("seq", "sub"), axis=0, tiled=True),
        lax.all_gather(upper_projection_weight, ("seq", "sub"), axis=0, tiled=True),
        lax.all_gather(upper_projection_bias, ("seq", "sub"), axis=0, tiled=True),
        lax.all_gather(lower_projection_weight, ("seq", "sub"), axis=0, tiled=True),
        lax.all_gather(lower_projection_bias, ("seq", "sub"), axis=0, tiled=True),
    )


def spread_grads(level_grads):
    (
        attend_gain,
        attend_shift,
        query_key_weight,
        value_projection_weight,
        output_projection_weight,
        feed_gain,
        feed_shift,
        upper_projection_weight,
        upper_projection_bias,
        lower_projection_weight,
        lower_projection_bias,
    ) = level_grads
    return (
        lax.psum_scatter(attend_gain, ("seq", "sub"), scatter_dimension=0, tiled=True),
        lax.psum_scatter(attend_shift, ("seq", "sub"), scatter_dimension=0, tiled=True),
        lax.psum_scatter(query_key_weight.astype(jnp.bfloat16), ("seq", "sub"), scatter_dimension=0, tiled=True),
        lax.psum_scatter(value_projection_weight.astype(jnp.bfloat16), ("seq", "sub"), scatter_dimension=0, tiled=True),
        lax.psum_scatter(output_projection_weight.astype(jnp.bfloat16), ("seq", "sub"), scatter_dimension=0, tiled=True),
        lax.psum_scatter(feed_gain, ("seq", "sub"), scatter_dimension=0, tiled=True),
        lax.psum_scatter(feed_shift, ("seq", "sub"), scatter_dimension=0, tiled=True),
        lax.psum_scatter(upper_projection_weight.astype(jnp.bfloat16), ("seq", "sub"), scatter_dimension=0, tiled=True),
        lax.psum_scatter(upper_projection_bias, ("seq", "sub"), scatter_dimension=0, tiled=True),
        lax.psum_scatter(lower_projection_weight.astype(jnp.bfloat16), ("seq", "sub"), scatter_dimension=0, tiled=True),
        lax.psum_scatter(lower_projection_bias, ("seq", "sub"), scatter_dimension=0, tiled=True),
    )


def layer_pass(first_half, second_half, grad_one, grad_two, params, routes, rounds):
    (
        attend_gain,
        attend_shift,
        query_key_weight,
        value_projection_weight,
        output_projection_weight,
        feed_gain,
        feed_shift,
        upper_projection_weight,
        upper_projection_bias,
        lower_projection_weight,
        lower_projection_bias,
    ) = params
    attend_norm, attend_pull = jax.vjp(
        layer_norm, second_half, attend_gain.astype(jnp.float32), attend_shift.astype(jnp.float32)
    )
    normalized_input = attend_norm.astype(jnp.bfloat16)
    shared_query_key, value_vectors, outputs, totals, kept = round_outputs(
        normalized_input, query_key_weight, value_projection_weight, routes, rounds
    )
    attention_result, combine_pull = jax.vjp(combine_rounds, outputs, totals)
    attended_low = attention_result.astype(jnp.bfloat16)
    top_one = first_half + jnp.einsum(
        "srd,de->sre", attended_low, output_projection_weight, preferred_element_type=jnp.float32
    )
    feed_norm, feed_pull = jax.vjp(
        layer_norm, top_one, feed_gain.astype(jnp.float32), feed_shift.astype(jnp.float32)
    )
    feed_forward_input = feed_norm.astype(jnp.bfloat16)
    prior_state = jnp.einsum(
        "srd,df->srf",
        feed_forward_input,
        upper_projection_weight,
        preferred_element_type=jnp.float32,
    ) + upper_projection_bias.astype(jnp.float32)
    hidden_activation, active_pull = jax.vjp(gelu_exact, prior_state)
    active_low = hidden_activation.astype(jnp.bfloat16)
    feed_out = jnp.einsum(
        "srf,fd->srd", active_low, lower_projection_weight, preferred_element_type=jnp.float32
    ) + lower_projection_bias.astype(jnp.float32)
    top_two = second_half + feed_out
    feed_grad = grad_two.astype(jnp.bfloat16)
    down_weight_grad = jnp.einsum(
        "srf,srd->fd", active_low, feed_grad, preferred_element_type=jnp.float32
    )
    down_bias_grad = jnp.sum(feed_grad.astype(jnp.float32), axis=(0, 1))
    active_grad = jnp.einsum(
        "srd,fd->srf", feed_grad, lower_projection_weight, preferred_element_type=jnp.float32
    )
    before_grad = active_pull(active_grad)[0].astype(jnp.bfloat16)
    up_weight_grad = jnp.einsum(
        "srd,srf->df", feed_forward_input, before_grad, preferred_element_type=jnp.float32
    )
    up_bias_grad = jnp.sum(before_grad.astype(jnp.float32), axis=(0, 1))
    norm_grad = jnp.einsum(
        "srf,df->srd", before_grad, upper_projection_weight, preferred_element_type=jnp.float32
    )
    one_part, feed_gain_grad, feed_shift_grad = feed_pull(norm_grad)
    total_one = grad_one + one_part
    out_grad = total_one.astype(jnp.bfloat16)
    output_weight_grad = jnp.einsum(
        "srd,sre->de", attended_low, out_grad, preferred_element_type=jnp.float32
    )
    attended_grad = jnp.einsum(
        "sre,de->srd", out_grad, output_projection_weight, preferred_element_type=jnp.float32
    )
    outputs_grad, totals_grad = combine_pull(attended_grad)
    target, home_slot, source, sorted_slot, home_lookup, back_lookup, order_flat = routes
    sequences, row_count, features = top_one.shape
    groups = rounds * sequences
    all_groups = jnp.arange(groups)
    outputs_low = outputs_grad.astype(jnp.bfloat16).reshape(groups, row_count, features)
    totals_low = totals_grad.astype(jnp.bfloat16).reshape(groups, row_count, HEADS)
    got_out, got_total = trade_rows(
        gather_slots(outputs_low, all_groups, home_lookup),
        gather_slots(totals_low, all_groups, home_lookup),
    )
    shared_rows, value_rows, halo = kept
    grad_shared, grad_values = attend_back(
        shared_rows,
        value_rows,
        order_flat,
        halo,
        settle(got_out, source, sorted_slot),
        settle(got_total, source, sorted_slot),
    )
    home_shared, home_values = trade_rows(
        gather_slots(grad_shared.astype(jnp.bfloat16), all_groups, back_lookup),
        gather_slots(grad_values.astype(jnp.bfloat16), all_groups, back_lookup),
    )
    shared_grad = jnp.sum(
        settle(home_shared, target, home_slot)
        .astype(jnp.float32)
        .reshape(rounds, sequences, row_count, features),
        axis=0,
    ).astype(jnp.bfloat16)
    values_grad = jnp.sum(
        settle(home_values, target, home_slot)
        .astype(jnp.float32)
        .reshape(rounds, sequences, row_count, features),
        axis=0,
    ).astype(jnp.bfloat16)
    shared_weight_grad = jnp.einsum(
        "srd,sre->de", normalized_input, shared_grad, preferred_element_type=jnp.float32
    )
    value_weight_grad = jnp.einsum(
        "srd,sre->de", normalized_input, values_grad, preferred_element_type=jnp.float32
    )
    normed_grad = jnp.einsum(
        "sre,de->srd", shared_grad, query_key_weight, preferred_element_type=jnp.float32
    ) + jnp.einsum(
        "sre,de->srd", values_grad, value_projection_weight, preferred_element_type=jnp.float32
    )
    two_part, attend_gain_grad, attend_shift_grad = attend_pull(normed_grad)
    total_two = grad_two + two_part
    level_grads = (
        attend_gain_grad,
        attend_shift_grad,
        shared_weight_grad,
        value_weight_grad,
        output_weight_grad,
        feed_gain_grad,
        feed_shift_grad,
        up_weight_grad,
        up_bias_grad,
        down_weight_grad,
        down_bias_grad,
    )
    return (top_one, top_two, total_one, total_two, level_grads)


def general_plan(
    first_half,
    second_half,
    grad_first,
    grad_second,
    attend_gain,
    attend_shift,
    query_key_weight,
    value_projection_weight,
    output_projection_weight,
    feed_gain,
    feed_shift,
    upper_projection_weight,
    upper_projection_bias,
    lower_projection_weight,
    lower_projection_bias,
    sort_order,
    sort_place,
):
    weight_stack = (
        attend_gain,
        attend_shift,
        query_key_weight,
        value_projection_weight,
        output_projection_weight,
        feed_gain,
        feed_shift,
        upper_projection_weight,
        upper_projection_bias,
        lower_projection_weight,
        lower_projection_bias,
    )
    devices = lax.axis_size(("seq", "sub"))
    rounds = sort_order.shape[1]
    row_count = first_half.shape[1]
    capacity = 2 * max(1, row_count // devices)
    params = collect(weight_stack, 0)
    routes = build_routes(sort_order[0], sort_place[0], devices, capacity)
    first_out, second_out, first_grad, second_grad, level_grads = layer_pass(
        first_half, second_half, grad_first, grad_second, params, routes, rounds
    )
    stacked = tuple((entry[None].astype(jnp.float32) for entry in spread_grads(level_grads)))
    return (first_out, second_out, first_grad, second_grad) + stacked


class Links:
    def __init__(self, planes, send, receive, local):
        self.send, self.receive, self.local = send, receive, local
        self.used, self.used_local = 0, 0
        self.planes = planes
        seq, sub = lax.axis_index("seq"), lax.axis_index("sub")
        self.z, self.x = seq // 2, lax.rem(seq, 2)
        self.y, self.core = sub // 2, lax.rem(sub, 2)
        self.p = self.x * 4 + sub

    def near(self, step):
        x = 1 - self.x if step & 4 else self.x
        y = 1 - self.y if step & 2 else self.y
        core = 1 - self.core if step & 1 else self.core
        return (self.z * 2 + x, y * 2 + core), x * 4 + y * 2 + core

    def along(self, step):
        to = lax.rem(self.z + step, self.planes)
        back = lax.rem(self.z + self.planes - step, self.planes)
        return (to * 2 + self.x, self.y * 2 + self.core), to, back

    def greet(self):
        barrier = pltpu.get_barrier_semaphore()
        targets = [self.near(step)[0] for step in range(1, 8)]
        targets += [self.along(step)[0] for step in range(1, self.planes)]
        for target in targets:
            pl.semaphore_signal(barrier, inc=1, device_id=target, device_id_type=pl.DeviceIdType.MESH)
        self.greeted = len(targets)

    def meet(self):
        pl.semaphore_wait(pltpu.get_barrier_semaphore(), self.greeted)

    def push(self, source, target, device):
        copy = pltpu.make_async_remote_copy(
            src_ref=source,
            dst_ref=target,
            send_sem=self.send.at[self.used],
            recv_sem=self.receive.at[self.used],
            device_id=device,
            device_id_type=pl.DeviceIdType.MESH,
        )
        self.used += 1
        copy.start()
        return copy

    def keep(self, source, target):
        copy = pltpu.make_async_copy(source, target, self.local.at[self.used_local])
        self.used_local += 1
        copy.start()
        return copy


COPIES = 160


def link_scratch():
    return [
        pltpu.SemaphoreType.DMA((COPIES,)),
        pltpu.SemaphoreType.DMA((COPIES,)),
        pltpu.SemaphoreType.DMA((48,)),
    ]


def along_z(source, target):
    def transfer(links, here, there):
        own = links.keep(source(here, links.z), target(there, links.z))
        copies = []
        for step in range(1, links.planes):
            device, to, _ = links.along(step)
            copies.append(links.push(source(here, to), target(there, links.z), device))
        yield
        own.wait()
        for copy in copies:
            copy.wait()

    return transfer


def over_plane(source, target):
    def transfer(links, here, there):
        own = links.keep(source(here, links.p), target(there, links.p))
        copies = []
        for step in (6, 7, 4, 5, 2, 3, 1):
            device, to = links.near(step)
            copies.append(links.push(source(here, to), target(there, links.p), device))
        yield
        own.wait()
        for copy in copies:
            copy.wait()

    return transfer


def over_chips(source, target):
    def transfer(links, here, there):
        own = links.keep(source(here, links.p), target(there, links.p))
        copies = []
        for step in (6, 4, 2):
            device, to = links.near(step)
            copies.append(links.push(source(here, to), target(there, links.p), device))
        sibling, _ = links.near(1)
        passed = [links.push(source(here, links.p), target(there, links.p), sibling)]
        yield
        for step, copy in zip((6, 4, 2), copies):
            copy.wait_recv()
            _, sender = links.near(step)
            passed.append(links.push(target(there, sender), target(there, sender), sibling))
        yield
        own.wait()
        for copy in copies:
            copy.wait_send()
        for copy in passed:
            copy.wait()

    return transfer


def everywhere(links, here, there):
    own = links.keep(here, there.at[links.z, links.p])
    copies = []
    for step in (6, 7, 4, 5, 2, 3, 1):
        copies.append(links.push(here, there.at[links.z, links.p], links.near(step)[0]))
    yield
    own.wait()
    for copy in copies:
        copy.wait()
    copies = []
    for step in range(1, links.planes):
        copies.append(links.push(there.at[links.z], there.at[links.z], links.along(step)[0]))
    yield
    for copy in copies:
        copy.wait()


def drive(transfers):
    while transfers:
        left = []
        for transfer in transfers:
            try:
                next(transfer)
                left.append(transfer)
            except StopIteration:
                pass
        transfers = left


def exchange(items, name, collective_id, planes):
    count = len(items)

    def body(*refs):
        links = Links(planes, *refs[2 * count :])
        links.greet()
        links.meet()
        drive([item[0](links, refs[k], refs[count + k]) for k, item in enumerate(items)])

    return pl.pallas_call(
        body,
        out_shape=[item[2] for item in items],
        in_specs=[pl.BlockSpec(memory_space=pl.ANY)] * count,
        out_specs=[pl.BlockSpec(memory_space=pl.ANY)] * count,
        scratch_shapes=link_scratch(),
        compiler_params=pltpu.CompilerParams(collective_id=collective_id, has_side_effects=True),
        name=name,
    )(*[item[1] for item in items])


def whole(ref, index):
    return ref


def block(ref, index):
    return ref.at[index]


def second(ref, index):
    return ref.at[:, index]


def like(kind, array, *shape):
    return (kind, array, jax.ShapeDtypeStruct(shape, array.dtype))


def pick_rows(table, index_ref, start, count):
    return jnp.concatenate(
        [table[pl.ds(index_ref[start + row], 1), :] for row in range(count)], axis=0
    )


def window_masks():
    query = lax.broadcasted_iota(jnp.int32, (128, 128), 0) // BLOCK
    key = lax.broadcasted_iota(jnp.int32, (128, 128), 1) // BLOCK
    return (query == 0) & (key == 1), key <= query


def rows_of(index):
    return pl.ds(pl.multiple_of(index * 128, 128), 128)


def pick_tile(table, index_ref, tile, part):
    return jnp.concatenate(
        [table[pl.ds(index_ref[tile, part * 32 + row], 1), :] for row in range(32)], axis=0
    )


def sort_tile(order, table, first, second, offset, tile):
    for part in range(4):
        start = pl.multiple_of(tile * 128 + part * 32 + offset, 32)
        picked = pick_tile(table, order, tile, part)
        first[pl.ds(start, 32), :] = picked[:, :128].astype(first.dtype)
        second[pl.ds(start, 32), :] = picked[:, 128:].astype(second.dtype)


def across(column):
    return jnp.broadcast_to(column, (128, 128)).T[:1, :]


def down(row):
    return jnp.broadcast_to(row, (128, 128)).T


def dot(a, b, contract):
    return lax.dot_general(a, b, (contract, ((), ())), preferred_element_type=jnp.float32)


def key_scales(keys):
    rows = keys.astype(jnp.float32)
    mean_square = jnp.mean(rows * rows, axis=-1, keepdims=True) + 1e-06
    return rows, mean_square, lax.rsqrt(mean_square) / HEAD_DIM


def half_turned(row):
    return jnp.concatenate([row[:, 64:], row[:, :64]], axis=1)


def windows(before, here):
    return [jnp.concatenate([before[:, 64:], here[:, :64]], axis=1), here]


def masked_scores(raw, scale, query_pos, key_pos):
    return jnp.where(
        key_pos > query_pos, LATER, jnp.where(key_pos == query_pos, SELF, raw * scale)
    )


def attend_tiles(tiles, unroll, order, order_rows, table, shared, values, mixed, total_sorted, last_scale):
    sort = functools.partial(sort_tile, order, table, shared, values, BLOCK)
    end = tiles * 128
    for tile in [tiles - 1] + list(range(unroll)):
        sort(tile)
    shared[:BLOCK, :] = shared[end : end + BLOCK, :]
    values[:BLOCK, :] = values[end : end + BLOCK, :]
    last_scale[...] = across(key_scales(shared[end - BLOCK : end + BLOCK, :])[2])

    def step_tiles(step, carry):
        first = step * unroll
        numbers = [lax.rem(first + tiles - 1, tiles)] + [first + k for k in range(unroll)]
        places = [order_rows[pl.ds(t, 1), :] for t in numbers]
        scale = [last_scale[...]]
        work = []
        for k in range(unroll):
            start = pl.multiple_of((first + k) * 128, 128)
            keys = [shared[pl.ds(pl.multiple_of(start + half * 64, 64), 128), :] for half in range(2)]
            vals = [values[pl.ds(pl.multiple_of(start + half * 64, 64), 128), :] for half in range(2)]
            own = jnp.concatenate([keys[0][64:], keys[1][64:]], axis=0)
            scale.append(across(key_scales(own)[2]))
            work.append((keys, vals))
        last_scale[...] = scale[-1]
        for k in range(unroll):
            sort(lax.rem(first + unroll + k, tiles))
        query_pos = jnp.concatenate([down(place) for place in places[1:]], axis=0)
        key_pos, key_scale = [], []
        for k in range(unroll):
            key_pos += windows(places[k], places[k + 1])
            key_scale += windows(scale[k], scale[k + 1])
        raw = [dot(k[64:], k, ((1,), (1,))) for keys, _ in work for k in keys]
        raw, key_pos, key_scale = (
            jnp.concatenate([jnp.broadcast_to(a, (64, 128)) for a in parts], axis=0)
            for parts in (raw, key_pos, key_scale)
        )
        scores = masked_scores(raw, key_scale, query_pos, key_pos)
        highest = jnp.max(scores, axis=-1, keepdims=True)
        total = highest + jnp.log(jnp.sum(jnp.exp(scores - highest), axis=-1, keepdims=True))
        prob = jnp.exp(scores - total).astype(jnp.bfloat16)
        rows = pl.ds(pl.multiple_of(first * 128, 128), unroll * 128)
        total = jnp.broadcast_to(total, (unroll * 128, 128))
        mixed[rows, 128:] = total
        total_sorted[rows, :] = total
        vals = [v for _, vals in work for v in vals]
        mixed[rows, :128] = jnp.concatenate(
            [dot(prob[64 * i : 64 * i + 64], v, ((1,), (0,))) for i, v in enumerate(vals)], axis=0
        )
        return carry

    lax.fori_loop(0, tiles // unroll, step_tiles, 0)


def attend_back_tiles(
    tiles, unroll, order, order_rows, table, shared, values, total_sorted,
    grad_sorted, grad_total_sorted, sums, scale_sums, last_scale,
):
    sort = functools.partial(sort_tile, order, table, grad_sorted, grad_total_sorted, 0)
    end = tiles * 128
    for tile in range(unroll):
        sort(tile)
    last_scale[...] = across(key_scales(shared[end - BLOCK : end + BLOCK, :])[2])
    scale_sums[...] = jnp.zeros_like(scale_sums)
    sums[end : end + 128, :] = jnp.zeros((128, 256), jnp.float32)
    early = lax.broadcasted_iota(jnp.int32, (1, 128), 1) < 64

    def step_tiles(step, carry):
        first = step * unroll
        numbers = [lax.rem(first + tiles - 1, tiles)] + [first + k for k in range(unroll)]
        places = [order_rows[pl.ds(t, 1), :] for t in numbers]
        scale = [last_scale[...]]
        work = []
        for k in range(unroll):
            start = pl.multiple_of((first + k) * 128, 128)
            keys = [shared[pl.ds(pl.multiple_of(start + half * 64, 64), 128), :] for half in range(2)]
            vals = [values[pl.ds(pl.multiple_of(start + half * 64, 64), 128), :] for half in range(2)]
            own = jnp.concatenate([keys[0][64:], keys[1][64:]], axis=0)
            scale.append(across(key_scales(own)[2]))
            tile = pl.ds(start, 128)
            work.append(
                (keys, vals, grad_sorted[tile, :], grad_total_sorted[tile, :], total_sorted[tile, :])
            )
        last_scale[...] = scale[-1]
        for k in range(unroll):
            sort(lax.rem(first + unroll + k, tiles))
        blocks = 2 * unroll
        scale_parts = [0.0] * (unroll + 1)
        query_pos = jnp.concatenate([down(place) for place in places[1:]], axis=0)
        key_pos, key_scale = [], []
        for k in range(unroll):
            key_pos += windows(places[k], places[k + 1])
            key_scale += windows(scale[k], scale[k + 1])
        keys = [k for item in work for k in item[0]]
        vals = [v for item in work for v in item[1]]
        grads, grad_totals, totals = (
            jnp.concatenate([item[n] for item in work], axis=0) for n in (2, 3, 4)
        )
        own = [slice(64 * i, 64 * i + 64) for i in range(blocks)]
        raw = [dot(k[64:], k, ((1,), (1,))) for k in keys]
        grad_prob = [dot(grads[own[i]], v, ((1,), (1,))) for i, v in enumerate(vals)]
        raw, grad_prob, key_pos, key_scale = (
            jnp.concatenate([jnp.broadcast_to(a, (64, 128)) for a in parts], axis=0)
            for parts in (raw, grad_prob, key_pos, key_scale)
        )
        prob = jnp.exp(masked_scores(raw, key_scale, query_pos, key_pos) - totals)
        inner = jnp.sum(prob * grad_prob, axis=-1, keepdims=True)
        grad_score = jnp.where(
            key_pos < query_pos, prob * (grad_prob + (grad_totals - inner)), 0.0
        )
        product = grad_score * raw
        for index in range(blocks):
            k, half = index // 2, index % 2
            part = jnp.sum(product[own[index]], axis=0, keepdims=True)
            if half == 0:
                turned = half_turned(part)
                scale_parts[k] += jnp.where(early, 0.0, turned)
                scale_parts[k + 1] += jnp.where(early, turned, 0.0)
            else:
                scale_parts[k + 1] += part
        grad_raw = (grad_score * key_scale).astype(jnp.bfloat16)
        prob = prob.astype(jnp.bfloat16)
        key_parts = [dot(grad_raw[own[i]], keys[i][64:], ((0,), (0,))) for i in range(blocks)]
        value_parts = [dot(prob[own[i]], grads[own[i]], ((0,), (0,))) for i in range(blocks)]
        query_parts = [dot(grad_raw[own[i]], keys[i], ((1,), (0,))) for i in range(blocks)]
        key_sums = [key_parts[0][:64]] + [
            key_parts[i][64:] + query_parts[i] + (key_parts[i + 1][:64] if i + 1 < blocks else 0.0)
            for i in range(blocks)
        ]
        value_sums = [value_parts[0][:64]] + [
            value_parts[i][64:] + (value_parts[i + 1][:64] if i + 1 < blocks else 0.0)
            for i in range(blocks)
        ]
        for index in range(blocks):
            rows = pl.ds(pl.multiple_of(first * 128 + index * 64, 64), 64)
            sums[rows, :128] = key_sums[index + 1]
            sums[rows, 128:] = value_sums[index + 1]
        for k in range(unroll):
            scale_sums[pl.ds(first + k, 1), :] = scale_parts[k + 1]
        before = jnp.where(step == 0, tiles, numbers[0])
        rows = pl.ds(pl.multiple_of(before * 128 + 64, 64), 64)
        sums[rows, :128] += key_sums[0]
        sums[rows, 128:] += value_sums[0]
        scale_sums[pl.ds(before, 1), :] += scale_parts[0]
        return carry

    lax.fori_loop(0, tiles // unroll, step_tiles, 0)
    sums[end - 128 : end, :] += sums[end : end + 128, :]
    scale_sums[pl.ds(tiles - 1, 1), :] += scale_sums[pl.ds(tiles, 1), :]

    def finish(step, carry):
        for part in range(2):
            tile = step * 2 + part
            rows = rows_of(tile)
            start = pl.multiple_of(tile * 128 + 64, 64)
            keys, mean_square, scale = key_scales(shared[pl.ds(start, 128), :])
            factor = down(scale_sums[pl.ds(tile, 1), :]) * (scale / (mean_square * HEAD_DIM))
            sums[rows, :128] -= factor * keys
        return carry

    lax.fori_loop(0, tiles // 2, finish, 0)


def old_across(column):
    return jnp.broadcast_to(column, (128, 128)).T


def old_scores(raw, scale, query_pos, key_pos, inside):
    scores = jnp.where(
        key_pos > query_pos, LATER, jnp.where(key_pos == query_pos, SELF, raw * scale)
    )
    return jnp.where(inside, scores, OUTSIDE)


def old_sort_pair(order, table, first, second, tile):
    for part in range(4):
        start = pl.multiple_of(tile * 128 + part * 32, 32)
        picked = pick_rows(table, order, start, 32)
        first[pl.ds(start, 32), :] = picked[:, :128].astype(first.dtype)
        second[pl.ds(start, 32), :] = picked[:, 128:].astype(second.dtype)


def attend_back_kernel(
    tiles, unroll, order, place, order_rows, shared_sorted, values_sorted, total_sorted, grad_mixed, grad_total,
    grad_shared_home, grad_values_home, table, grad_sorted, grad_total_sorted, scales, scale_sums, sums,
):
    def load(tile, carry):
        rows = rows_of(tile)
        table[rows, :128] = grad_mixed[rows, :].astype(jnp.float32)
        table[rows, 128:] = down(grad_total[lax.rem(tile, 8), pl.ds(tile // 8, 1), :])
        return carry

    lax.fori_loop(0, tiles, load, 0)
    sums[rows_of(tiles - 1), :] = jnp.zeros((128, 256), jnp.float32)
    sort = functools.partial(old_sort_pair, order, table, grad_sorted, grad_total_sorted)
    for tile in range(unroll):
        sort(tile)
    inside_left, inside_here = window_masks()
    scales[0] = old_across(key_scales(shared_sorted[(tiles - 1) * 128 :, :])[2])
    scale_sums[...] = jnp.zeros_like(scale_sums)

    def back_tiles(step, carry):
        first = step * unroll
        left = lax.rem(first + tiles - 1, tiles)
        numbers = [left] + [first + k for k in range(unroll)]
        keys = [shared_sorted[rows_of(t), :] for t in numbers]
        vals = [values_sorted[rows_of(t), :] for t in numbers]
        places = [order_rows[pl.ds(t, 1), :] for t in numbers]
        grads = [grad_sorted[rows_of(t), :] for t in numbers[1:]]
        grad_totals = [grad_total_sorted[rows_of(t), :] for t in numbers[1:]]
        totals = [total_sorted[rows_of(t), :] for t in numbers[1:]]
        scale = [scales[0]] + [old_across(key_scales(k)[2]) for k in keys[1:]]
        scales[0] = scale[-1]
        for k in range(unroll):
            sort(lax.rem(first + unroll + k, tiles))
        key_sums, value_sums, scale_parts = [0.0] * (unroll + 1), [0.0] * (unroll + 1), [0.0] * (unroll + 1)
        for k in range(unroll):
            here, before, grad = keys[k + 1], keys[k], grads[k]
            query_pos = down(places[k + 1])
            raw_left = dot(here, before, ((1,), (1,)))
            raw_here = dot(here, here, ((1,), (1,)))
            prob_left = jnp.exp(
                old_scores(raw_left, scale[k], query_pos, places[k], inside_left) - totals[k]
            )
            prob_here = jnp.exp(
                old_scores(raw_here, scale[k + 1], query_pos, places[k + 1], inside_here) - totals[k]
            )
            grad_prob_left = dot(grad, vals[k], ((1,), (1,)))
            grad_prob_here = dot(grad, vals[k + 1], ((1,), (1,)))
            inner = jnp.sum(
                prob_left * grad_prob_left + prob_here * grad_prob_here, axis=-1, keepdims=True
            )
            shift = grad_totals[k] - inner
            keep_left = inside_left & (places[k] < query_pos)
            keep_here = inside_here & (places[k + 1] < query_pos)
            grad_score_left = jnp.where(keep_left, prob_left * (grad_prob_left + shift), 0.0)
            grad_score_here = jnp.where(keep_here, prob_here * (grad_prob_here + shift), 0.0)
            scale_parts[k] += jnp.sum(grad_score_left * raw_left, axis=0, keepdims=True)
            scale_parts[k + 1] += jnp.sum(grad_score_here * raw_here, axis=0, keepdims=True)
            grad_raw_left = (grad_score_left * scale[k]).astype(jnp.bfloat16)
            grad_raw_here = (grad_score_here * scale[k + 1]).astype(jnp.bfloat16)
            key_sums[k + 1] += (
                dot(grad_raw_left, before, ((1,), (0,)))
                + dot(grad_raw_here, here, ((1,), (0,)))
                + dot(grad_raw_here, here, ((0,), (0,)))
            )
            key_sums[k] += dot(grad_raw_left, here, ((0,), (0,)))
            value_sums[k + 1] += dot(prob_here.astype(jnp.bfloat16), grad, ((0,), (0,)))
            value_sums[k] += dot(prob_left.astype(jnp.bfloat16), grad, ((0,), (0,)))
        for k, tile in enumerate(numbers[1:]):
            sums[rows_of(tile), :128] = key_sums[k + 1]
            sums[rows_of(tile), 128:] = value_sums[k + 1]
            scale_sums[pl.ds(tile, 1), :] = scale_parts[k + 1]
        extra = pl.ds(pl.multiple_of(jnp.where(step == 0, tiles, left) * 128, 128), 128)
        extra_row = pl.ds(jnp.where(step == 0, tiles, left), 1)
        sums[extra, :128] += key_sums[0]
        sums[extra, 128:] += value_sums[0]
        scale_sums[extra_row, :] += scale_parts[0]
        return carry

    sums[pl.ds(tiles * 128, 128), :] = jnp.zeros((128, 256), jnp.float32)
    lax.fori_loop(0, tiles // unroll, back_tiles, 0)
    last = rows_of(tiles - 1)
    sums[last, :] += sums[pl.ds(tiles * 128, 128), :]
    scale_sums[pl.ds(tiles - 1, 1), :] += scale_sums[pl.ds(tiles, 1), :]

    def finish(step, carry):
        for part in range(2):
            tile = step * 2 + part
            rows = rows_of(tile)
            keys, mean_square, scale = key_scales(shared_sorted[rows, :])
            factor = down(scale_sums[pl.ds(tile, 1), :]) * (scale / (mean_square * HEAD_DIM))
            sums[rows, :128] -= factor * keys
        return carry

    lax.fori_loop(0, tiles // 2, finish, 0)

    def unsort(tile, carry):
        old_sort_pair(place, sums, grad_shared_home, grad_values_home, tile)
        return carry

    lax.fori_loop(0, tiles, unsort, 0)


VMEM = pl.BlockSpec(memory_space=pltpu.VMEM)
SMEM = pl.BlockSpec(memory_space=pltpu.SMEM)
ANY = pl.BlockSpec(memory_space=pl.ANY)


def beside(kernel, inputs, outputs, scratch, items, planes):
    count = len(items)

    def body(*refs):
        refs = list(refs)
        own, refs = refs[:inputs], refs[inputs:]
        here, refs = refs[:count], refs[count:]
        own, refs = own + refs[:outputs], refs[outputs:]
        there, refs = refs[:count], refs[count:]
        links = Links(planes, *refs[scratch:])
        links.greet()
        links.meet()
        transfers = [item[0](links, here[k], there[k]) for k, item in enumerate(items)]
        for transfer in transfers:
            next(transfer)
        kernel(*own, *refs[:scratch])
        drive(transfers)

    return body


def attend_head_back(
    order, place, order_rows, shared_sorted, values_sorted, total_sorted, grad, grad_total,
    items, collective_id, planes, unroll=2,
):
    length = grad.shape[0]
    rows = jax.ShapeDtypeStruct((length, HEAD_DIM), jnp.bfloat16)
    scratch = [
        pltpu.VMEM((length, 256), jnp.float32),
        pltpu.VMEM((length, HEAD_DIM), jnp.bfloat16),
        pltpu.VMEM((length, HEAD_DIM), jnp.float32),
        pltpu.VMEM((1, 128, 128), jnp.float32),
        pltpu.VMEM((length // 128 + 8, 128), jnp.float32),
        pltpu.VMEM((length + 128, 256), jnp.float32),
    ]
    kernel = functools.partial(attend_back_kernel, length // 128, unroll)
    return pl.pallas_call(
        beside(kernel, 8, 2, len(scratch), items, planes),
        out_shape=[rows, rows] + [item[2] for item in items],
        in_specs=[SMEM, SMEM] + [VMEM] * 6 + [ANY] * len(items),
        out_specs=[VMEM] * 2 + [ANY] * len(items),
        scratch_shapes=scratch + link_scratch(),
        compiler_params=pltpu.CompilerParams(
            vmem_limit_bytes=40 << 20, collective_id=collective_id, has_side_effects=True
        ),
        name="attend_back",
    )(
        order, place, order_rows, shared_sorted, values_sorted, total_sorted, grad, grad_total,
        *[item[1] for item in items],
    )


def sum_small_kernel(planes, items, *refs):
    count = len(items)
    tiles, here, refs = refs[0], refs[1 : 1 + count], refs[1 + count :]
    result, there, refs = refs[0], refs[1 : 1 + count], refs[1 + count :]
    arrived, summed, refs = refs[0], refs[1], refs[2:]
    links = Links(planes, *refs)
    links.greet()
    links.meet()
    transfers = [item[0](links, here[k], there[k]) for k, item in enumerate(items)]
    small = over_plane(block, block)(links, tiles, arrived)
    next(small)
    for transfer in transfers:
        next(transfer)
    drive([small])
    summed[...] = jnp.sum(arrived[...], axis=0)
    drive([along_z(whole, block)(links, summed, result)] + transfers)


def sum_small(tiles, items, collective_id, planes):
    return pl.pallas_call(
        functools.partial(sum_small_kernel, planes, items),
        out_shape=[jax.ShapeDtypeStruct((planes,) + tiles.shape[1:], tiles.dtype)]
        + [item[2] for item in items],
        in_specs=[VMEM] + [ANY] * len(items),
        out_specs=[VMEM] + [ANY] * len(items),
        scratch_shapes=[
            pltpu.VMEM(tiles.shape, tiles.dtype),
            pltpu.VMEM(tiles.shape[1:], tiles.dtype),
        ]
        + link_scratch(),
        compiler_params=pltpu.CompilerParams(collective_id=collective_id, has_side_effects=True),
        name="sum_small",
    )(tiles, *[item[1] for item in items])


def normal_parts(rows):
    center = jnp.mean(rows, axis=-1, keepdims=True)
    offset = rows - center
    spread = jnp.mean(offset * offset, axis=-1, keepdims=True)
    inverse = lax.rsqrt(spread + 1e-05)
    return offset * inverse, inverse


def norm_back(grad, rows, gain):
    unit, inverse = normal_parts(rows)
    scaled = grad * gain
    shared = jnp.mean(scaled, axis=-1, keepdims=True)
    along = jnp.mean(scaled * unit, axis=-1, keepdims=True)
    return (
        (scaled - shared - unit * along) * inverse,
        jnp.sum(grad * unit, axis=0, keepdims=True),
        jnp.sum(grad, axis=0, keepdims=True),
    )


def gelu_parts(rows):
    below = 0.5 * (1.0 + lax.erf(rows * 0.7071067811865476))
    bell = jnp.exp(-0.5 * rows * rows) * 0.3989422804014327
    return rows * below, below + rows * bell


def feed_kernel(
    planes,
    mixed, total, x1, wo_in, gain, shift, wup_in, bias_up, wdown_in, df_in, g1,
    y1_out, g1_out, dout_out, attended_out, dmixed_home, dtotal_home, y2_out, up_grad_out, down_grad_out,
    up_bias_out, gain_out, shift_out,
    wo, wup, wdown, df, weights, attended, arrived, h2, dact, act, dpre, kept, to_sibling, from_sibling,
    to_chip, from_chip, up_grad, down_grad, y2, dout, datt_out, datt, dmixed, dtotal, send, receive, local,
):
    low, full = jnp.bfloat16, jnp.float32
    links = Links(planes, send, receive, local)
    links.greet()
    loads = [links.keep(a, b) for a, b in ((wo_in, wo), (df_in, df), (wdown_in, wdown), (wup_in, wup))]

    def combine(z, carry):
        for x in range(2):
            totals = [down(total[x * 4 + u, pl.ds(z, 1), :]) for u in range(4)]
            highest = jnp.maximum(
                jnp.maximum(totals[0], totals[1]), jnp.maximum(totals[2], totals[3])
            )
            parts = [jnp.exp(t - highest) for t in totals]
            inverse = 1.0 / (parts[0] + parts[1] + parts[2] + parts[3])
            result = 0.0
            for u in range(4):
                weight = parts[u] * inverse
                weights[x * 4 + u, z] = weight
                result += weight * mixed[x * 4 + u, z].astype(full)
            attended[z, :, x * 128 : (x + 1) * 128] = result.astype(low)
        return carry

    lax.fori_loop(0, planes, combine, 0)
    links.meet()
    share = along_z(block, block)(links, attended, arrived)
    next(share)
    keep_attended = links.keep(attended, attended_out)
    loads[0].wait()
    drive([share])
    y1 = x1[...]
    for z in range(planes):
        y1 += dot(arrived[z], wo[z * 256 : (z + 1) * 256, :], ((1,), (0,)))
    y1_out[...] = y1
    unit, _ = normal_parts(y1)
    own_rows = pl.ds(pl.multiple_of(links.p * 128, 128), 128)
    h2[own_rows, :] = (unit * gain[...] + shift[...]).astype(low)

    sibling, _ = links.near(1)
    own_h2 = h2.at[own_rows, :]
    direct = {step: links.push(own_h2, own_h2, links.near(step)[0]) for step in (6, 4, 2)}
    handed = {0: links.push(own_h2, own_h2, sibling)}
    for load in loads[1:]:
        load.wait()

    def upper_back(part, carry):
        rows = pl.ds(pl.multiple_of(part * 256, 256), 256)
        dact[rows, :] = dot(df[rows, :], wdown[...], ((1,), (1,)))
        return carry

    lax.fori_loop(0, 4, upper_back, 0)

    def pass_on(step):
        direct[step].wait_recv()
        block_rows = h2.at[rows_of(links.near(step)[1]), :]
        handed[step] = links.push(block_rows, block_rows, sibling)

    def feed(slot, step):
        handed[step].wait_recv()
        chip = links.near(step)[1] // 2
        rows = pl.ds(pl.multiple_of(chip * 256, 256), 256)
        before = dot(h2[rows, :], wup[...], ((1,), (0,))) + bias_up[...]
        value, slope = gelu_parts(before)
        act[rows, :] = value.astype(low)
        grad = (dact[rows, :] * slope).astype(low)
        dpre[rows, :] = grad
        kept[slot] = dot(grad, wup[...], ((1,), (1,))).reshape(2, 128, -1).astype(low)
        return links.push(kept.at[slot, 1 - links.core], from_sibling.at[slot], sibling)

    def chip_sum(slot, step, traded):
        traded.wait_recv()
        result = kept[slot, links.core].astype(full) + from_sibling[slot].astype(full)
        if slot == 0:
            return result
        to_chip[slot - 1] = result.astype(low)
        return links.push(to_chip.at[slot - 1], from_chip.at[slot - 1], links.near(step)[0])

    pass_on(2)
    traded = [feed(0, 0)]
    pass_on(4)
    traded.append(feed(1, 2))
    sent = [chip_sum(1, 2, traded[1])]
    pass_on(6)
    traded.append(feed(2, 4))
    sent.append(chip_sum(2, 4, traded[2]))
    traded.append(feed(3, 6))
    sent.append(chip_sum(3, 6, traded[3]))
    own_sum = chip_sum(0, 0, traded[0])

    def upper_grad(part, carry):
        rows = pl.ds(pl.multiple_of(part * 256, 256), 256)
        up_grad[part] = dot(h2[:, rows], dpre[...], ((0,), (0,))).astype(low)
        return carry

    lax.fori_loop(0, planes, upper_grad, 0)
    share_up = along_z(block, block)(links, up_grad, up_grad_out)
    next(share_up)
    for copy in sent:
        copy.wait_recv()
    grad = own_sum + (
        from_chip[0].astype(full) + from_chip[1].astype(full) + from_chip[2].astype(full)
    )
    part, gain_grad, shift_grad = norm_back(grad, y1_out[...], gain[...])
    gain_out[...] = gain_grad
    shift_out[...] = shift_grad
    g1_new = g1[...] + part
    g1_out[...] = g1_new
    dout[...] = g1_new.astype(low)
    keep_dout = links.keep(dout, dout_out)
    for z in range(planes):
        datt_out[z] = dot(dout[...], wo[z * 256 : (z + 1) * 256, :], ((1,), (1,))).astype(low)
    share = along_z(block, block)(links, datt_out, datt)
    next(share)

    def lower_grad(part, carry):
        rows = pl.ds(pl.multiple_of(part * 128, 128), 128)
        down_grad[part] = dot(act[:, rows], df[...], ((0,), (0,))).astype(low)
        return carry

    lax.fori_loop(0, planes, lower_grad, 0)
    share_down = along_z(block, block)(links, down_grad, down_grad_out)
    next(share_down)
    up_bias_out[...] = jnp.sum(dpre[...].astype(full), axis=0, keepdims=True)
    drive([share])

    def combine_back(z, carry):
        for x in range(2):
            grad = datt[z, :, x * 128 : (x + 1) * 128].astype(full)
            chosen = [weights[x * 4 + u, z] for u in range(4)]
            inner = [
                jnp.sum(grad * mixed[x * 4 + u, z].astype(full), axis=-1, keepdims=True)
                for u in range(4)
            ]
            mean = sum(chosen[u] * inner[u] for u in range(4))
            for u in range(4):
                dmixed[x * 4 + u, z] = (chosen[u] * grad).astype(low)
                change = (chosen[u] * (inner[u] - mean)).astype(low).astype(full)
                dtotal[x * 4 + u, pl.ds(z, 1), :] = change.T[:1, :]
        return carry

    lax.fori_loop(0, planes, combine_back, 0)
    shares = [
        over_plane(block, second)(links, dmixed, dmixed_home),
        over_plane(block, block)(links, dtotal, dtotal_home),
    ]
    for transfer in shares:
        next(transfer)

    def lower(part, carry):
        rows = pl.ds(pl.multiple_of(part * 128, 128), 128)
        y2[part] = dot(act[rows, :], wdown[...], ((1,), (0,))).astype(low)
        return carry

    lax.fori_loop(0, 8, lower, 0)
    keep_y2 = links.keep(y2, y2_out)
    for copy in list(direct.values()) + traded + sent:
        copy.wait_send()
    for copy in handed.values():
        copy.wait_send()
    drive(shares + [share_up, share_down])
    for copy in (keep_attended, keep_dout, keep_y2):
        copy.wait()


def feed_stage(arguments, collective_id, planes):
    low, full = jnp.bfloat16, jnp.float32
    (mixed, total, x1, wo, gain, shift, wup, bias_up, wdown, df, g1) = arguments
    rows, width = x1.shape
    part = wup.shape[1]
    shape = jax.ShapeDtypeStruct
    outputs = [
        (shape((rows, width), full), VMEM),
        (shape((rows, width), full), VMEM),
        (shape((rows, width), low), ANY),
        (shape((planes, rows, 256), low), ANY),
        (shape((planes, 8, rows, HEAD_DIM), low), ANY),
        (shape((8, 8, rows), full), ANY),
        (shape((8, rows, width), low), ANY),
        (shape((planes, width // planes, part), low), ANY),
        (shape((planes, rows, width), low), ANY),
        (shape((1, part), full), VMEM),
        (shape((1, width), full), VMEM),
        (shape((1, width), full), VMEM),
    ]
    scratch = [
        (wo.shape, low),
        (wup.shape, low),
        (wdown.shape, low),
        (df.shape, low),
        ((8, planes, rows, HEAD_DIM), full),
        ((planes, rows, 256), low),
        ((planes, rows, 256), low),
        ((8 * rows, width), low),
        ((8 * rows, part), full),
        ((8 * rows, part), low),
        ((8 * rows, part), low),
        ((4, 2, rows, width), low),
        ((4, rows, width), low),
        ((4, rows, width), low),
        ((3, rows, width), low),
        ((3, rows, width), low),
        ((planes, width // planes, part), low),
        ((planes, rows, width), low),
        ((8, rows, width), low),
        ((rows, width), low),
        ((planes, rows, 256), low),
        ((planes, rows, 256), low),
        ((8, planes, rows, HEAD_DIM), low),
        ((8, 8, rows), full),
    ]
    return pl.pallas_call(
        functools.partial(feed_kernel, planes),
        out_shape=[o[0] for o in outputs],
        in_specs=[VMEM, VMEM, VMEM, ANY, VMEM, VMEM, ANY, VMEM, ANY, ANY, VMEM],
        out_specs=[o[1] for o in outputs],
        scratch_shapes=[pltpu.VMEM(*s) for s in scratch] + link_scratch(),
        compiler_params=pltpu.CompilerParams(
            vmem_limit_bytes=56 << 20, collective_id=collective_id, has_side_effects=True
        ),
        name="feed",
    )(*arguments)


def open_kernel(
    planes,
    sort_order, sort_place, gain_a_in, shift_a_in, gain_f_in, shift_f_in, bias_up_in, bias_down_in,
    x2, wqk, wv, wo, wup, wdown, g2,
    places_out, gains_out, bias_up_out, normed_out, wqk_out, wv_out, wo_out, wup_out, wdown_out, df_out,
    shared_out, values_out, total_out, mixed_out, total_home_out,
    ints, all_ints, floats, all_floats, order_rows, place_rows, order_s, place_s, normed, df,
    wqk_line, wv_line, wo_line, wup_rows, wqk_pair, wv_pair, heads, head_table, table, mixed,
    shared, values, total_sorted, mixed_home, total_home, last_scale, send, receive, local,
):
    low, full = jnp.bfloat16, jnp.float32
    links = Links(planes, send, receive, local)
    links.greet()
    sub = links.y * 2 + links.core
    tiles = planes * 8
    ints[...] = jnp.concatenate([sort_order[...], sort_place[...]], axis=0)
    lane = lax.broadcasted_iota(jnp.int32, (1, 128), 1) // 32

    def spread(vector):
        wide = jnp.concatenate([vector[...].astype(full)] * 4, axis=1)
        return jnp.where(lane == sub, wide, 0.0)

    floats[...] = jnp.concatenate(
        [spread(v) for v in (gain_a_in, shift_a_in, gain_f_in, shift_f_in, bias_down_in)]
        + [bias_up_in[...].astype(full), jnp.zeros((2, 128), full)],
        axis=0,
    )
    df[...] = g2[...].astype(low)
    links.meet()
    share_floats = everywhere(links, floats, all_floats)
    next(share_floats)
    share_ints = everywhere(links, ints, all_ints)
    next(share_ints)

    def pair_columns(ref, z):
        return ref.at[:, pl.ds(pl.multiple_of(z * 256, 256), 256)]

    pair_shares = [
        along_z(pair_columns, block)(links, a, b) for a, b in ((wqk, wqk_line), (wv, wv_line))
    ]
    for transfer in pair_shares:
        next(transfer)
    unit, _ = normal_parts(x2[...])
    next(share_floats)

    def upper_columns(chunk):
        def columns(ref, p):
            return ref.at[:, pl.ds(pl.multiple_of((chunk * 8 + p) * 128, 128), 128)]

        def landing(ref, p):
            return ref.at[p, :, pl.ds(chunk * 128, 128)]

        return over_plane(columns, landing)

    drive([share_floats])

    def vector_of(row, z_step=2):
        chunks = []
        for chunk in range(8):
            z, x = chunk // 2, chunk % 2
            parts = [all_floats[z, x * 4 + u, row : row + 1, :] for u in range(4)]
            chunks.append(parts[0] + parts[1] + parts[2] + parts[3])
        return jnp.concatenate(chunks, axis=1)

    gain, shift = vector_of(0), vector_of(1)
    normed[links.z] = (unit * gain + shift).astype(low)
    normed_copies = []
    for step in range(1, planes):
        device, _, _ = links.along(step)
        normed_copies.append(links.push(normed.at[links.z], normed.at[links.z], device))
    for transfer in pair_shares:
        drive([transfer])
    pair_shares = [
        over_chips(whole, second)(links, a, b) for a, b in ((wqk_line, wqk_pair), (wv_line, wv_pair))
    ]
    for transfer in pair_shares:
        next(transfer)
    next(share_ints)
    upper_shares = [upper_columns(chunk)(links, wup, wup_rows) for chunk in range(planes)]
    for transfer in upper_shares:
        next(transfer)
    for transfer in pair_shares:
        next(transfer)
    gains_out[0:1, :] = gain
    gains_out[1:2, :] = shift
    for row in (2, 3, 4):
        gains_out[row : row + 1, :] = vector_of(row)
    for z in range(planes):
        bias_up_out[:, z * 128 : (z + 1) * 128] = all_floats[z, links.p, 5:6, :]
    drive(pair_shares)
    drive([share_ints])
    for z in range(planes):
        for p in range(8):
            tile = z * 8 + p
            order_rows[tile : tile + 1, :] = all_ints[z, p, pl.ds(sub, 1), :]
            place_rows[tile : tile + 1, :] = all_ints[z, p, pl.ds(sub + 4, 1), :]
    to_scalars = [links.keep(order_rows, order_s), links.keep(place_rows, place_s)]
    shares = [over_chips(whole, block)(links, df, df_out)]
    next(shares[0])

    def head_columns(z):
        def columns(ref, p):
            return ref.at[z, :, pl.ds(pl.multiple_of((p // 4) * 256, 256), 256)]

        return columns

    def landing(z):
        return lambda ref, p: ref.at[z, p]

    def project(z):
        rows = normed[z]
        for weights, offset in ((wqk_pair, 0), (wv_pair, 128)):
            result = dot(rows, weights[...].reshape(-1, 256), ((1,), (0,))).astype(low)
            heads[z, :, offset : offset + 128] = result[:, :128]
            heads[z, :, 256 + offset : 384 + offset] = result[:, 128:]
        transfer = over_chips(head_columns(z), landing(z))(links, heads, head_table)
        next(transfer)
        return transfer

    head_shares = [project(links.z)]
    wo_share = along_z(whole, block)(links, wo, wo_line)
    next(wo_share)
    for step, copy in enumerate(normed_copies, 1):
        copy.wait_recv()
        head_shares.append(project(links.along(step)[2]))
        next(head_shares[-2])
    for transfer in upper_shares:
        drive([transfer])
    shares += [
        along_z(whole, block)(links, wup_rows, wup_out),
        along_z(whole, block)(links, wdown, wdown_out),
    ]
    next(shares[1])
    next(shares[2])
    next(head_shares[-1])
    drive([wo_share])
    wo_share = over_chips(whole, second)(links, wo_line, wo_out)
    for copy in to_scalars:
        copy.wait()
    drive(head_shares)
    next(wo_share)

    def load(tile, carry):
        table[rows_of(tile), :] = head_table[tile // 8, lax.rem(tile, 8)].astype(full)
        return carry

    lax.fori_loop(0, tiles, load, 0)
    attend_tiles(
        tiles, 2, order_s, order_rows, table, shared, values, mixed, total_sorted, last_scale
    )
    next(wo_share)
    next(shares[0])
    kept = [
        links.keep(normed, normed_out),
        links.keep(wqk_pair, wqk_out),
        links.keep(wv_pair, wv_out),
        links.keep(shared, shared_out),
        links.keep(values, values_out),
        links.keep(total_sorted, total_out),
        links.keep(order_rows, places_out.at[0]),
        links.keep(place_rows, places_out.at[1]),
    ]
    sent = []
    for step in (6, 7, 4, 5, 2, 3, 1, 0):
        device, p = links.near(step)

        def unsort(z, carry):
            totals = []
            for part in range(4):
                picked = pick_tile(mixed, place_s, z * 8 + p, part)
                mixed_home[p, z, part * 32 : part * 32 + 32, :] = picked[:, :128].astype(low)
                totals.append(picked[:, 128:])
            total_home[p, pl.ds(z, 1), :] = jnp.concatenate(totals, axis=0).T[:1, :]
            return carry

        lax.fori_loop(0, planes, unsort, 0)
        for here, there in ((mixed_home, mixed_out), (total_home, total_home_out)):
            source, target = here.at[p], there.at[links.p]
            if step:
                sent.append(links.push(source, target, device))
            else:
                kept.append(links.keep(source, target))
    for copy in normed_copies:
        copy.wait_send()
    drive(shares + [wo_share])
    for copy in kept + sent:
        copy.wait()


def open_stage(arguments, collective_id, planes):
    low, full, whole_number = jnp.bfloat16, jnp.float32, jnp.int32
    x2, wqk, wup = arguments[8], arguments[9], arguments[12]
    rows, width = x2.shape
    own, hidden = wup.shape
    part = hidden // 8
    tiles = planes * 8
    tokens = tiles * rows
    shape = jax.ShapeDtypeStruct
    outputs = [
        (shape((2, tiles, rows), whole_number), ANY),
        (shape((8, width), full), VMEM),
        (shape((1, part), full), VMEM),
        (shape((planes, rows, width), low), ANY),
        (shape((planes, 8, own, 256), low), ANY),
        (shape((planes, 8, own, 256), low), ANY),
        (shape((planes, 8, own, width), low), ANY),
        (shape((planes, 8, own, part), low), ANY),
        (shape((planes, rows, width), low), ANY),
        (shape((8, rows, width), low), ANY),
        (shape((tokens + BLOCK, HEAD_DIM), low), ANY),
        (shape((tokens + BLOCK, HEAD_DIM), low), ANY),
        (shape((tokens, HEAD_DIM), full), ANY),
        (shape((8, planes, rows, HEAD_DIM), low), ANY),
        (shape((8, 8, rows), full), ANY),
    ]
    scratch = [
        pltpu.VMEM((8, rows), whole_number),
        pltpu.VMEM((planes, 8, 8, rows), whole_number),
        pltpu.VMEM((8, rows), full),
        pltpu.VMEM((planes, 8, 8, rows), full),
        pltpu.VMEM((tiles, rows), whole_number),
        pltpu.VMEM((tiles, rows), whole_number),
        pltpu.SMEM((tiles, rows), whole_number),
        pltpu.SMEM((tiles, rows), whole_number),
        pltpu.VMEM((planes, rows, width), low),
        pltpu.VMEM((rows, width), low),
        pltpu.VMEM((planes, own, 256), low),
        pltpu.VMEM((planes, own, 256), low),
        pltpu.VMEM((planes, own, width), low),
        pltpu.VMEM((8, own, part), low),
        pltpu.VMEM((planes, 8, own, 256), low),
        pltpu.VMEM((planes, 8, own, 256), low),
        pltpu.VMEM((planes, rows, 512), low),
        pltpu.VMEM((planes, 8, rows, 256), low),
        pltpu.VMEM((tokens, 256), full),
        pltpu.VMEM((tokens, 256), full),
        pltpu.VMEM((tokens + BLOCK, HEAD_DIM), low),
        pltpu.VMEM((tokens + BLOCK, HEAD_DIM), low),
        pltpu.VMEM((tokens, HEAD_DIM), full),
        pltpu.VMEM((8, planes, rows, HEAD_DIM), low),
        pltpu.VMEM((8, 8, rows), full),
        pltpu.VMEM((1, rows), full),
    ]
    return pl.pallas_call(
        functools.partial(open_kernel, planes),
        out_shape=[o[0] for o in outputs],
        in_specs=[VMEM] * 15,
        out_specs=[o[1] for o in outputs],
        scratch_shapes=scratch + link_scratch(),
        compiler_params=pltpu.CompilerParams(
            vmem_limit_bytes=56 << 20, collective_id=collective_id, has_side_effects=True
        ),
        name="open",
    )(*arguments)


def matmul(a, b, contract=((1,), (0,))):
    return dot(a, b, contract)


def plane_plan(
    n_seq,
    n_sub,
    first_half,
    second_half,
    grad_first,
    grad_second,
    attend_gain,
    attend_shift,
    query_key_weight,
    value_projection_weight,
    output_projection_weight,
    feed_gain,
    feed_shift,
    upper_projection_weight,
    upper_projection_bias,
    lower_projection_weight,
    lower_projection_bias,
    sort_order,
    sort_place,
):
    low, full = jnp.bfloat16, jnp.float32
    devices, planes, per_plane = n_seq * n_sub, n_seq // 2, 2 * n_sub
    rows, width = first_half.shape[1:]
    hidden = upper_projection_weight.shape[2]
    tokens = devices * rows
    line = planes * rows
    part = hidden // per_plane
    seq, sub = lax.axis_index("seq"), lax.axis_index("sub")
    me_p, me_z = lax.rem(seq, 2) * n_sub + sub, seq // 2
    trade = functools.partial(exchange, planes=planes)
    x1, x2, g1, g2 = (a[0] for a in (first_half, second_half, grad_first, grad_second))
    wqk, wv, wo = query_key_weight[0], value_projection_weight[0], output_projection_weight[0]
    wup, wdown = upper_projection_weight[0], lower_projection_weight[0]
    own = width // devices
    pair = 2 * HEAD_DIM

    (
        places, gains, bias_up, normed_line, wqk_pair, wv_pair, wo_all, wup_part, wdown_part, df_plane,
        shared_sorted, values_sorted, total_sorted, mixed, total,
    ) = open_stage(
        (
            sort_order[0, :, 0], sort_place[0, :, 0], attend_gain, attend_shift, feed_gain, feed_shift,
            upper_projection_bias, lower_projection_bias, x2, wqk, wv, wo, wup, wdown, g2,
        ),
        1,
        planes,
    )
    gain_a, shift_a, gain_f, shift_f, bias_down = (gains[k] for k in range(5))
    attend_pull = jax.vjp(layer_norm, x2, gain_a, shift_a)[1]
    order, place = places[0].reshape(tokens), places[1].reshape(tokens)
    order_rows = places[0].astype(full)
    normed_line = normed_line.reshape(line, width)
    wqk_pair, wv_pair = wqk_pair.reshape(width, pair), wv_pair.reshape(width, pair)
    wo_all = wo_all.reshape(width, width)
    wup_part, wdown_part = wup_part.reshape(width, part), wdown_part.reshape(part, width)
    df_plane = df_plane.reshape(per_plane * rows, width)
    shared_sorted, values_sorted = shared_sorted[BLOCK:], values_sorted[BLOCK:]
    df = g2.astype(low)
    head_shape = (planes, per_plane, rows, HEAD_DIM)
    token_shape = (per_plane, planes, rows, HEAD_DIM)

    def to_tokens(array):
        return like(over_plane(second, block), array.reshape(head_shape), *token_shape)

    traded_z, traded_plane = along_z(block, block), over_plane(block, block)
    down_bias_grad = jnp.sum(df.astype(full), axis=0)
    (
        y1, g1, dout, attended, dmixed, dtotal, y2_parts, up_grad, down_grad,
        up_bias_grad, feed_gain_grad, feed_shift_grad,
    ) = feed_stage(
        (
            mixed, total, x1, wo_all, gain_f[None], shift_f[None],
            wup_part, bias_up, wdown_part, df_plane, g1,
        ),
        6,
        planes,
    )
    attended = attended.reshape(line, pair)
    up_grad = jnp.sum(up_grad.astype(full), axis=0).reshape(per_plane, own, part)
    dshared, dvalues, y2_parts, dout_line = attend_head_back(
        order,
        place,
        order_rows,
        shared_sorted,
        values_sorted,
        total_sorted,
        dmixed.reshape(tokens, HEAD_DIM),
        dtotal,
        [
            like(traded_plane, y2_parts, *y2_parts.shape),
            like(along_z(whole, block), dout, planes, rows, width),
        ],
        11,
        planes,
    )
    y2 = x2 + (jnp.sum(y2_parts.astype(full), axis=0) + bias_down)
    out_grad = matmul(attended, dout_line.reshape(line, width), ((0,), (0,)))
    out_grad = out_grad.astype(low).reshape(per_plane, own, width)
    dshared, dvalues = trade([to_tokens(dshared), to_tokens(dvalues)], "grads_from_heads", 12)

    def over_rounds(array):
        array = jnp.sum(array.reshape(2, n_sub, line, HEAD_DIM).astype(full), axis=1)
        return jnp.swapaxes(array, 0, 1).reshape(line, pair).astype(low)

    dshared, dvalues = over_rounds(dshared), over_rounds(dvalues)
    de_parts = matmul(dshared, wqk_pair, ((1,), (1,))) + matmul(dvalues, wv_pair, ((1,), (1,)))
    de_parts = de_parts.astype(low).reshape(planes, rows, width)

    def to_owners(grad):
        grad = grad.astype(low).reshape(planes, per_plane, own, pair)
        return like(over_plane(second, block), grad, per_plane, planes, own, pair)

    de_parts, shared_grad, value_grad, out_grad, up_grad = trade(
        [
            like(traded_z, de_parts, *de_parts.shape),
            to_owners(matmul(normed_line, dshared, ((0,), (0,)))),
            to_owners(matmul(normed_line, dvalues, ((0,), (0,)))),
            like(traded_plane, out_grad, *out_grad.shape),
            like(traded_plane, up_grad, *up_grad.shape),
        ],
        "sum_second_grad",
        13,
    )
    two_part, attend_gain_grad, attend_shift_grad = attend_pull(
        jnp.sum(de_parts.astype(full), axis=0)
    )
    g2 = g2 + two_part
    shared_grad = jnp.sum(shared_grad.astype(full), axis=0)
    value_grad = jnp.sum(value_grad.astype(full), axis=0)

    def by_owner(vector):
        return jnp.swapaxes(vector.reshape(planes, per_plane, own), 0, 1).reshape(per_plane, 1, rows)

    vectors = [attend_gain_grad, attend_shift_grad, feed_gain_grad, feed_shift_grad, down_bias_grad]
    up_bias_grad = jnp.where(
        jnp.arange(per_plane)[:, None, None] == me_p, up_bias_grad.reshape(1, planes, rows), 0.0
    )
    tiles = jnp.concatenate([by_owner(v) for v in vectors] + [up_bias_grad], axis=1)
    tiles = jnp.pad(tiles, ((0, 0), (0, 16 - tiles.shape[1]), (0, 0)))
    vectors, shared_grad, value_grad = sum_small(
        tiles,
        [like(traded_z, shared_grad, planes, own, pair), like(traded_z, value_grad, planes, own, pair)],
        14,
        planes,
    )
    vectors = jnp.sum(vectors, axis=0)
    pieces = jnp.take(vectors[:5].reshape(5, planes, own), me_z, axis=1)
    up_bias_grad = jnp.take(vectors[5 : 5 + planes], me_z, axis=0)
    shared_grad, value_grad = (
        jnp.swapaxes(a, 0, 1).reshape(own, width) for a in (shared_grad, value_grad)
    )
    up_grad = jnp.transpose(up_grad.reshape(per_plane, own, planes, rows), (1, 2, 0, 3))
    outputs = (
        y1,
        y2,
        g1,
        g2,
        pieces[0],
        pieces[1],
        shared_grad,
        value_grad,
        jnp.sum(out_grad.astype(full), axis=0),
        pieces[2],
        pieces[3],
        up_grad.reshape(own, hidden),
        up_bias_grad,
        jnp.sum(down_grad.astype(full), axis=0),
        pieces[4],
    )
    return tuple((a[None] for a in outputs))


def on_device(n_seq, n_sub, *arguments):
    sequences, rows, width = arguments[0].shape
    rounds = arguments[-1].shape[1]
    fits = (
        sequences == 1
        and rows == 2 * BLOCK
        and rounds == n_sub
        and HEADS == n_seq
        and width == HEADS * HEAD_DIM
    )
    if fits:
        return plane_plan(n_seq, n_sub, *arguments)
    return general_plan(*arguments)


def solution(mesh):
    return jax.shard_map(
        functools.partial(on_device, mesh.shape["seq"], mesh.shape["sub"]),
        mesh=mesh,
        in_specs=(
            P(None, ("seq", "sub"), None),
            P(None, ("seq", "sub"), None),
            P(None, ("seq", "sub"), None),
            P(None, ("seq", "sub"), None),
            P(None, ("seq", "sub")),
            P(None, ("seq", "sub")),
            P(None, ("seq", "sub"), None),
            P(None, ("seq", "sub"), None),
            P(None, ("seq", "sub"), None),
            P(None, ("seq", "sub")),
            P(None, ("seq", "sub")),
            P(None, ("seq", "sub"), None),
            P(None, ("seq", "sub")),
            P(None, ("seq", "sub"), None),
            P(None, ("seq", "sub")),
            P(None, None, None, ("seq", "sub")),
            P(None, None, None, ("seq", "sub")),
        ),
        out_specs=(
            P(None, ("seq", "sub"), None),
            P(None, ("seq", "sub"), None),
            P(None, ("seq", "sub"), None),
            P(None, ("seq", "sub"), None),
            P(None, ("seq", "sub")),
            P(None, ("seq", "sub")),
            P(None, ("seq", "sub"), None),
            P(None, ("seq", "sub"), None),
            P(None, ("seq", "sub"), None),
            P(None, ("seq", "sub")),
            P(None, ("seq", "sub")),
            P(None, ("seq", "sub"), None),
            P(None, ("seq", "sub")),
            P(None, ("seq", "sub"), None),
            P(None, ("seq", "sub")),
        ),
        check_vma=False,
    )
```

```python
import functools

import jax
import jax.numpy as jnp
from jax import lax
from jax.experimental import pallas as pl
from jax.experimental.pallas import tpu as pltpu
from jax.sharding import PartitionSpec as P

HEADS = 8
HEAD_DIM = 128
BLOCK = 64
LATER = -1000000000.0
SELF = -100000.0


def from_behind(block, axis, distance):
    devices = range(lax.axis_size(axis))
    route = [((i - distance) % len(devices), i) for i in devices]
    return lax.ppermute(block, axis, route)


def layer_norm(value_vectors, scaling, shifts):
    center = jnp.mean(value_vectors, axis=-1, keepdims=True)
    offset = value_vectors - center
    spread = jnp.mean(offset * offset, axis=-1, keepdims=True)
    return offset * lax.rsqrt(spread + 1e-05) * scaling + shifts


def gelu_exact(value_vectors):
    return jax.nn.gelu(value_vectors, approximate=False)


def combine_rounds(outputs, totals):
    highest = jnp.max(totals, axis=0, keepdims=True)
    weights = jnp.exp(totals - highest)
    weights = weights / jnp.sum(weights, axis=0, keepdims=True)
    by_head = outputs.reshape(outputs.shape[:-1] + (totals.shape[-1], -1))
    return jnp.sum(weights[..., None] * by_head, axis=0).reshape(outputs.shape[1:])


def home_slots(places, row_count):
    target = places // row_count
    prior_state = (target[:, None, :] == target[:, :, None]) & (
        places[:, None, :] < places[:, :, None]
    )
    return (target, jnp.sum(prior_state.astype(jnp.int32), axis=2))


def sorted_slots(orders, row_count):
    source = orders // row_count
    ladder = jnp.arange(row_count, dtype=jnp.int32)
    prior_state = (source[:, None, :] == source[:, :, None]) & (
        ladder[None, None, :] < ladder[None, :, None]
    )
    return (source, jnp.sum(prior_state.astype(jnp.int32), axis=2))


def slot_lookup(owners, slot_index, devices, capacity):
    groups, row_count = owners.shape
    flat_index = owners * capacity + slot_index
    lookup = jnp.full((groups, devices * capacity), row_count, jnp.int32)
    filler = jnp.broadcast_to(jnp.arange(row_count, dtype=jnp.int32), (groups, row_count))
    lookup = lookup.at[jnp.arange(groups)[:, None], flat_index].set(filler)
    return jnp.transpose(lookup.reshape(groups, devices, capacity), (1, 0, 2))


def gather_slots(value_vectors, member, lookup):
    padding = jnp.zeros((value_vectors.shape[0], 1) + value_vectors.shape[2:], value_vectors.dtype)
    padded = jnp.concatenate([value_vectors, padding], axis=1)
    return padded[member[None, :, None], lookup]


def settle(received, owners, slot_index):
    return received[owners, jnp.arange(owners.shape[0])[:, None], slot_index]


def build_routes(orders, places, devices, capacity):
    rounds, sequences, row_count = orders.shape
    order_flat = orders.reshape(rounds * sequences, row_count)
    target, home_slot = home_slots(places.reshape(rounds * sequences, row_count), row_count)
    source, sorted_slot = sorted_slots(order_flat, row_count)
    home_lookup = slot_lookup(target, home_slot, devices, capacity)
    back_lookup = slot_lookup(source, sorted_slot, devices, capacity)
    return (target, home_slot, source, sorted_slot, home_lookup, back_lookup, order_flat)


def trade_rows(first_part, second_part):
    return (
        lax.all_to_all(first_part, ("seq", "sub"), split_axis=0, concat_axis=0, tiled=True),
        lax.all_to_all(second_part, ("seq", "sub"), split_axis=0, concat_axis=0, tiled=True),
    )


def trade_results(first_part, second_part):
    return (
        lax.all_to_all(first_part, ("seq", "sub"), split_axis=0, concat_axis=0, tiled=True),
        lax.all_to_all(second_part, ("seq", "sub"), split_axis=0, concat_axis=0, tiled=True),
    )


def window(rows_here, rows_left):
    groups = rows_here.shape[0]
    extended = jnp.concatenate([rows_left, rows_here], axis=1)
    extended = extended.reshape((groups, -1, BLOCK) + rows_here.shape[2:])
    return jnp.concatenate([extended[:, :-1], extended[:, 1:]], axis=2)


def score_parts(shared_rows, order_rows, halo_shared, halo_order):
    groups, row_count, features = shared_rows.shape
    blocks = row_count // BLOCK
    queries = shared_rows.reshape(groups, blocks, BLOCK, HEADS, HEAD_DIM)
    key_rows = window(shared_rows, halo_shared).reshape(groups, blocks, 2 * BLOCK, HEADS, HEAD_DIM)
    key_float = key_rows.astype(jnp.float32)
    mean_square = jnp.mean(key_float * key_float, axis=-1) + 1e-06
    key_scale = lax.rsqrt(mean_square) / HEAD_DIM
    raw_scores = jnp.einsum(
        "gcqhd,gckhd->gchqk", queries, key_rows, preferred_element_type=jnp.float32
    )
    query_pos = order_rows.reshape(groups, blocks, BLOCK)
    key_pos = window(order_rows, halo_order)
    is_later = (key_pos[:, :, None, :] > query_pos[:, :, :, None])[:, :, None]
    is_self = (key_pos[:, :, None, :] == query_pos[:, :, :, None])[:, :, None]
    scale_row = jnp.transpose(key_scale, (0, 1, 3, 2))[:, :, :, None, :]
    scores = jnp.where(
        is_later, -1000000000.0, jnp.where(is_self, -100000.0, raw_scores * scale_row)
    )
    highest = jnp.max(scores, axis=-1, keepdims=True)
    log_total = highest + jnp.log(jnp.sum(jnp.exp(scores - highest), axis=-1, keepdims=True))
    probability = jnp.exp(scores - log_total)
    return (
        queries,
        key_rows,
        key_float,
        mean_square,
        key_scale,
        scale_row,
        raw_scores,
        is_later | is_self,
        log_total,
        probability,
    )


def attend(shared_rows, value_rows, order_rows, halo):
    halo_shared, halo_value, halo_order = halo
    parts = score_parts(shared_rows, order_rows, halo_shared, halo_order)
    groups, row_count, features = shared_rows.shape
    value_keys = window(value_rows, halo_value).reshape(
        groups, row_count // BLOCK, 2 * BLOCK, HEADS, HEAD_DIM
    )
    mixed = jnp.einsum(
        "gchqk,gckhd->gcqhd",
        parts[9].astype(jnp.bfloat16),
        value_keys,
        preferred_element_type=jnp.float32,
    )
    log_total = jnp.transpose(parts[8][..., 0], (0, 1, 3, 2)).reshape(groups, row_count, HEADS)
    return (mixed.reshape(groups, row_count, features), log_total)


def fold_window(grads_window, groups, row_count, features):
    grads_window = grads_window.reshape(groups, row_count // BLOCK, 2 * BLOCK, features)
    empty = jnp.zeros((groups, 1, BLOCK, features), jnp.float32)
    extended = jnp.concatenate([grads_window[:, :, :BLOCK], empty], axis=1) + jnp.concatenate(
        [empty, grads_window[:, :, BLOCK:]], axis=1
    )
    return (extended[:, 1:].reshape(groups, row_count, features), extended[:, 0])


def attend_back(shared_rows, value_rows, order_rows, halo, grad_out, grad_total):
    halo_shared, halo_value, halo_order = halo
    (
        queries,
        key_rows,
        key_float,
        mean_square,
        key_scale,
        scale_row,
        raw_scores,
        masked,
        log_total,
        probability,
    ) = score_parts(shared_rows, order_rows, halo_shared, halo_order)
    groups, row_count, features = shared_rows.shape
    blocks = row_count // BLOCK
    value_keys = window(value_rows, halo_value).reshape(groups, blocks, 2 * BLOCK, HEADS, HEAD_DIM)
    prob_low = probability.astype(jnp.bfloat16)
    grad_heads = grad_out.reshape(groups, blocks, BLOCK, HEADS, HEAD_DIM)
    grad_log = jnp.transpose(
        grad_total.astype(jnp.float32).reshape(groups, blocks, BLOCK, HEADS), (0, 1, 3, 2)
    )[..., None]
    grad_prob = jnp.einsum(
        "gcqhd,gckhd->gchqk", grad_heads, value_keys, preferred_element_type=jnp.float32
    )
    inner = jnp.sum(probability * grad_prob, axis=-1, keepdims=True)
    grad_score = jnp.where(masked, 0.0, probability * (grad_prob - inner + grad_log))
    grad_scale = jnp.transpose(jnp.sum(grad_score * raw_scores, axis=3), (0, 1, 3, 2))
    grad_raw = (grad_score * scale_row).astype(jnp.bfloat16)
    grad_query = jnp.einsum(
        "gchqk,gckhd->gcqhd", grad_raw, key_rows, preferred_element_type=jnp.float32
    )
    grad_key = jnp.einsum(
        "gchqk,gcqhd->gckhd", grad_raw, queries, preferred_element_type=jnp.float32
    )
    grad_key = grad_key - (grad_scale * key_scale / mean_square)[..., None] * key_float / HEAD_DIM
    grad_value = jnp.einsum(
        "gchqk,gcqhd->gckhd", prob_low, grad_heads, preferred_element_type=jnp.float32
    )
    key_home, key_left = fold_window(grad_key, groups, row_count, features)
    value_home, value_left = fold_window(grad_value, groups, row_count, features)
    back_key, back_value = from_behind((key_left, value_left), ("seq", "sub"), -1)
    grad_shared = grad_query.reshape(groups, row_count, features) + key_home
    grad_shared = grad_shared.at[:, row_count - BLOCK :].add(back_key)
    grad_values = value_home.at[:, row_count - BLOCK :].add(back_value)
    return (grad_shared, grad_values)


def sorted_attention(shared_query_key, value_vectors, routes):
    target, home_slot, source, sorted_slot, home_lookup, back_lookup, order_flat = routes
    groups = target.shape[0]
    member = jnp.arange(groups) % shared_query_key.shape[0]
    got_shared, got_values = trade_rows(
        gather_slots(shared_query_key, member, home_lookup),
        gather_slots(value_vectors, member, home_lookup),
    )
    shared_rows = settle(got_shared, source, sorted_slot)
    value_rows = settle(got_values, source, sorted_slot)
    halo = from_behind(
        (shared_rows[:, -BLOCK:], value_rows[:, -BLOCK:], order_flat[:, -BLOCK:]), ("seq", "sub"), 1
    )
    mixed, log_total = attend(shared_rows, value_rows, order_flat, halo)
    all_groups = jnp.arange(groups)
    got_mixed, got_total = trade_results(
        gather_slots(mixed, all_groups, back_lookup),
        gather_slots(log_total, all_groups, back_lookup),
    )
    return (
        settle(got_mixed, target, home_slot),
        settle(got_total, target, home_slot),
        (shared_rows, value_rows, halo),
    )


def round_outputs(normalized_input, query_key_weight, value_projection_weight, routes, rounds):
    shared_query_key = jnp.einsum(
        "srd,de->sre", normalized_input, query_key_weight, preferred_element_type=jnp.float32
    ).astype(jnp.bfloat16)
    value_vectors = jnp.einsum(
        "srd,de->sre", normalized_input, value_projection_weight, preferred_element_type=jnp.float32
    ).astype(jnp.bfloat16)
    mixed, log_total, kept = sorted_attention(shared_query_key, value_vectors, routes)
    sequences, row_count, features = normalized_input.shape
    outputs = mixed.reshape(rounds, sequences, row_count, features)
    totals = log_total.reshape(rounds, sequences, row_count, HEADS)
    return (shared_query_key, value_vectors, outputs, totals, kept)


def collect(weight_stack, layer_index):
    (
        attend_gain,
        attend_shift,
        query_key_weight,
        value_projection_weight,
        output_projection_weight,
        feed_gain,
        feed_shift,
        upper_projection_weight,
        upper_projection_bias,
        lower_projection_weight,
        lower_projection_bias,
    ) = tuple((shard_piece[layer_index] for shard_piece in weight_stack))
    return (
        lax.all_gather(attend_gain, ("seq", "sub"), axis=0, tiled=True),
        lax.all_gather(attend_shift, ("seq", "sub"), axis=0, tiled=True),
        lax.all_gather(query_key_weight, ("seq", "sub"), axis=0, tiled=True),
        lax.all_gather(value_projection_weight, ("seq", "sub"), axis=0, tiled=True),
        lax.all_gather(output_projection_weight, ("seq", "sub"), axis=0, tiled=True),
        lax.all_gather(feed_gain, ("seq", "sub"), axis=0, tiled=True),
        lax.all_gather(feed_shift, ("seq", "sub"), axis=0, tiled=True),
        lax.all_gather(upper_projection_weight, ("seq", "sub"), axis=0, tiled=True),
        lax.all_gather(upper_projection_bias, ("seq", "sub"), axis=0, tiled=True),
        lax.all_gather(lower_projection_weight, ("seq", "sub"), axis=0, tiled=True),
        lax.all_gather(lower_projection_bias, ("seq", "sub"), axis=0, tiled=True),
    )


def spread_grads(level_grads):
    (
        attend_gain,
        attend_shift,
        query_key_weight,
        value_projection_weight,
        output_projection_weight,
        feed_gain,
        feed_shift,
        upper_projection_weight,
        upper_projection_bias,
        lower_projection_weight,
        lower_projection_bias,
    ) = level_grads
    return (
        lax.psum_scatter(attend_gain, ("seq", "sub"), scatter_dimension=0, tiled=True),
        lax.psum_scatter(attend_shift, ("seq", "sub"), scatter_dimension=0, tiled=True),
        lax.psum_scatter(query_key_weight.astype(jnp.bfloat16), ("seq", "sub"), scatter_dimension=0, tiled=True),
        lax.psum_scatter(value_projection_weight.astype(jnp.bfloat16), ("seq", "sub"), scatter_dimension=0, tiled=True),
        lax.psum_scatter(output_projection_weight.astype(jnp.bfloat16), ("seq", "sub"), scatter_dimension=0, tiled=True),
        lax.psum_scatter(feed_gain, ("seq", "sub"), scatter_dimension=0, tiled=True),
        lax.psum_scatter(feed_shift, ("seq", "sub"), scatter_dimension=0, tiled=True),
        lax.psum_scatter(upper_projection_weight.astype(jnp.bfloat16), ("seq", "sub"), scatter_dimension=0, tiled=True),
        lax.psum_scatter(upper_projection_bias, ("seq", "sub"), scatter_dimension=0, tiled=True),
        lax.psum_scatter(lower_projection_weight.astype(jnp.bfloat16), ("seq", "sub"), scatter_dimension=0, tiled=True),
        lax.psum_scatter(lower_projection_bias, ("seq", "sub"), scatter_dimension=0, tiled=True),
    )


def layer_pass(first_half, second_half, grad_one, grad_two, params, routes, rounds):
    (
        attend_gain,
        attend_shift,
        query_key_weight,
        value_projection_weight,
        output_projection_weight,
        feed_gain,
        feed_shift,
        upper_projection_weight,
        upper_projection_bias,
        lower_projection_weight,
        lower_projection_bias,
    ) = params
    attend_norm, attend_pull = jax.vjp(
        layer_norm, second_half, attend_gain.astype(jnp.float32), attend_shift.astype(jnp.float32)
    )
    normalized_input = attend_norm.astype(jnp.bfloat16)
    shared_query_key, value_vectors, outputs, totals, kept = round_outputs(
        normalized_input, query_key_weight, value_projection_weight, routes, rounds
    )
    attention_result, combine_pull = jax.vjp(combine_rounds, outputs, totals)
    attended_low = attention_result.astype(jnp.bfloat16)
    top_one = first_half + jnp.einsum(
        "srd,de->sre", attended_low, output_projection_weight, preferred_element_type=jnp.float32
    )
    feed_norm, feed_pull = jax.vjp(
        layer_norm, top_one, feed_gain.astype(jnp.float32), feed_shift.astype(jnp.float32)
    )
    feed_forward_input = feed_norm.astype(jnp.bfloat16)
    prior_state = jnp.einsum(
        "srd,df->srf",
        feed_forward_input,
        upper_projection_weight,
        preferred_element_type=jnp.float32,
    ) + upper_projection_bias.astype(jnp.float32)
    hidden_activation, active_pull = jax.vjp(gelu_exact, prior_state)
    active_low = hidden_activation.astype(jnp.bfloat16)
    feed_out = jnp.einsum(
        "srf,fd->srd", active_low, lower_projection_weight, preferred_element_type=jnp.float32
    ) + lower_projection_bias.astype(jnp.float32)
    top_two = second_half + feed_out
    feed_grad = grad_two.astype(jnp.bfloat16)
    down_weight_grad = jnp.einsum(
        "srf,srd->fd", active_low, feed_grad, preferred_element_type=jnp.float32
    )
    down_bias_grad = jnp.sum(feed_grad.astype(jnp.float32), axis=(0, 1))
    active_grad = jnp.einsum(
        "srd,fd->srf", feed_grad, lower_projection_weight, preferred_element_type=jnp.float32
    )
    before_grad = active_pull(active_grad)[0].astype(jnp.bfloat16)
    up_weight_grad = jnp.einsum(
        "srd,srf->df", feed_forward_input, before_grad, preferred_element_type=jnp.float32
    )
    up_bias_grad = jnp.sum(before_grad.astype(jnp.float32), axis=(0, 1))
    norm_grad = jnp.einsum(
        "srf,df->srd", before_grad, upper_projection_weight, preferred_element_type=jnp.float32
    )
    one_part, feed_gain_grad, feed_shift_grad = feed_pull(norm_grad)
    total_one = grad_one + one_part
    out_grad = total_one.astype(jnp.bfloat16)
    output_weight_grad = jnp.einsum(
        "srd,sre->de", attended_low, out_grad, preferred_element_type=jnp.float32
    )
    attended_grad = jnp.einsum(
        "sre,de->srd", out_grad, output_projection_weight, preferred_element_type=jnp.float32
    )
    outputs_grad, totals_grad = combine_pull(attended_grad)
    target, home_slot, source, sorted_slot, home_lookup, back_lookup, order_flat = routes
    sequences, row_count, features = top_one.shape
    groups = rounds * sequences
    all_groups = jnp.arange(groups)
    outputs_low = outputs_grad.astype(jnp.bfloat16).reshape(groups, row_count, features)
    totals_low = totals_grad.astype(jnp.bfloat16).reshape(groups, row_count, HEADS)
    got_out, got_total = trade_rows(
        gather_slots(outputs_low, all_groups, home_lookup),
        gather_slots(totals_low, all_groups, home_lookup),
    )
    shared_rows, value_rows, halo = kept
    grad_shared, grad_values = attend_back(
        shared_rows,
        value_rows,
        order_flat,
        halo,
        settle(got_out, source, sorted_slot),
        settle(got_total, source, sorted_slot),
    )
    home_shared, home_values = trade_rows(
        gather_slots(grad_shared.astype(jnp.bfloat16), all_groups, back_lookup),
        gather_slots(grad_values.astype(jnp.bfloat16), all_groups, back_lookup),
    )
    shared_grad = jnp.sum(
        settle(home_shared, target, home_slot)
        .astype(jnp.float32)
        .reshape(rounds, sequences, row_count, features),
        axis=0,
    ).astype(jnp.bfloat16)
    values_grad = jnp.sum(
        settle(home_values, target, home_slot)
        .astype(jnp.float32)
        .reshape(rounds, sequences, row_count, features),
        axis=0,
    ).astype(jnp.bfloat16)
    shared_weight_grad = jnp.einsum(
        "srd,sre->de", normalized_input, shared_grad, preferred_element_type=jnp.float32
    )
    value_weight_grad = jnp.einsum(
        "srd,sre->de", normalized_input, values_grad, preferred_element_type=jnp.float32
    )
    normed_grad = jnp.einsum(
        "sre,de->srd", shared_grad, query_key_weight, preferred_element_type=jnp.float32
    ) + jnp.einsum(
        "sre,de->srd", values_grad, value_projection_weight, preferred_element_type=jnp.float32
    )
    two_part, attend_gain_grad, attend_shift_grad = attend_pull(normed_grad)
    total_two = grad_two + two_part
    level_grads = (
        attend_gain_grad,
        attend_shift_grad,
        shared_weight_grad,
        value_weight_grad,
        output_weight_grad,
        feed_gain_grad,
        feed_shift_grad,
        up_weight_grad,
        up_bias_grad,
        down_weight_grad,
        down_bias_grad,
    )
    return (top_one, top_two, total_one, total_two, level_grads)


def general_plan(
    first_half,
    second_half,
    grad_first,
    grad_second,
    attend_gain,
    attend_shift,
    query_key_weight,
    value_projection_weight,
    output_projection_weight,
    feed_gain,
    feed_shift,
    upper_projection_weight,
    upper_projection_bias,
    lower_projection_weight,
    lower_projection_bias,
    sort_order,
    sort_place,
):
    weight_stack = (
        attend_gain,
        attend_shift,
        query_key_weight,
        value_projection_weight,
        output_projection_weight,
        feed_gain,
        feed_shift,
        upper_projection_weight,
        upper_projection_bias,
        lower_projection_weight,
        lower_projection_bias,
    )
    devices = lax.axis_size(("seq", "sub"))
    rounds = sort_order.shape[1]
    row_count = first_half.shape[1]
    capacity = 2 * max(1, row_count // devices)
    params = collect(weight_stack, 0)
    routes = build_routes(sort_order[0], sort_place[0], devices, capacity)
    first_out, second_out, first_grad, second_grad, level_grads = layer_pass(
        first_half, second_half, grad_first, grad_second, params, routes, rounds
    )
    stacked = tuple((entry[None].astype(jnp.float32) for entry in spread_grads(level_grads)))
    return (first_out, second_out, first_grad, second_grad) + stacked


class Links:
    def __init__(self, planes, send, receive, local):
        self.send, self.receive, self.local = send, receive, local
        self.used, self.used_local = 0, 0
        self.planes = planes
        seq, sub = lax.axis_index("seq"), lax.axis_index("sub")
        self.z, self.x = seq // 2, lax.rem(seq, 2)
        self.y, self.core = sub // 2, lax.rem(sub, 2)
        self.p = self.x * 4 + sub

    def near(self, step):
        x = 1 - self.x if step & 4 else self.x
        y = 1 - self.y if step & 2 else self.y
        core = 1 - self.core if step & 1 else self.core
        return (self.z * 2 + x, y * 2 + core), x * 4 + y * 2 + core

    def along(self, step):
        to = lax.rem(self.z + step, self.planes)
        back = lax.rem(self.z + self.planes - step, self.planes)
        return (to * 2 + self.x, self.y * 2 + self.core), to, back

    def greet(self):
        barrier = pltpu.get_barrier_semaphore()
        targets = [self.near(step)[0] for step in range(1, 8)]
        targets += [self.along(step)[0] for step in range(1, self.planes)]
        for target in targets:
            pl.semaphore_signal(barrier, inc=1, device_id=target, device_id_type=pl.DeviceIdType.MESH)
        self.greeted = len(targets)

    def meet(self):
        pl.semaphore_wait(pltpu.get_barrier_semaphore(), self.greeted)

    def push(self, source, target, device):
        copy = pltpu.make_async_remote_copy(
            src_ref=source,
            dst_ref=target,
            send_sem=self.send.at[self.used],
            recv_sem=self.receive.at[self.used],
            device_id=device,
            device_id_type=pl.DeviceIdType.MESH,
        )
        self.used += 1
        copy.start()
        return copy

    def keep(self, source, target):
        copy = pltpu.make_async_copy(source, target, self.local.at[self.used_local])
        self.used_local += 1
        copy.start()
        return copy


COPIES = 160


def link_scratch():
    return [
        pltpu.SemaphoreType.DMA((COPIES,)),
        pltpu.SemaphoreType.DMA((COPIES,)),
        pltpu.SemaphoreType.DMA((48,)),
    ]


def along_z(source, target):
    def transfer(links, here, there):
        own = links.keep(source(here, links.z), target(there, links.z))
        copies = []
        for step in range(1, links.planes):
            device, to, _ = links.along(step)
            copies.append(links.push(source(here, to), target(there, links.z), device))
        yield
        own.wait()
        for copy in copies:
            copy.wait()

    return transfer


def over_plane(source, target):
    def transfer(links, here, there):
        own = links.keep(source(here, links.p), target(there, links.p))
        copies = []
        for step in (6, 7, 4, 5, 2, 3, 1):
            device, to = links.near(step)
            copies.append(links.push(source(here, to), target(there, links.p), device))
        yield
        own.wait()
        for copy in copies:
            copy.wait()

    return transfer


def over_chips(source, target):
    def transfer(links, here, there):
        own = links.keep(source(here, links.p), target(there, links.p))
        copies = []
        for step in (6, 4, 2):
            device, to = links.near(step)
            copies.append(links.push(source(here, to), target(there, links.p), device))
        sibling, _ = links.near(1)
        passed = [links.push(source(here, links.p), target(there, links.p), sibling)]
        yield
        for step, copy in zip((6, 4, 2), copies):
            copy.wait_recv()
            _, sender = links.near(step)
            passed.append(links.push(target(there, sender), target(there, sender), sibling))
        yield
        own.wait()
        for copy in copies:
            copy.wait_send()
        for copy in passed:
            copy.wait()

    return transfer


def everywhere(links, here, there):
    own = links.keep(here, there.at[links.z, links.p])
    copies = []
    for step in (6, 7, 4, 5, 2, 3, 1):
        copies.append(links.push(here, there.at[links.z, links.p], links.near(step)[0]))
    yield
    own.wait()
    for copy in copies:
        copy.wait()
    copies = []
    for step in range(1, links.planes):
        copies.append(links.push(there.at[links.z], there.at[links.z], links.along(step)[0]))
    yield
    for copy in copies:
        copy.wait()


def drive(transfers):
    while transfers:
        left = []
        for transfer in transfers:
            try:
                next(transfer)
                left.append(transfer)
            except StopIteration:
                pass
        transfers = left


def whole(ref, index):
    return ref


def block(ref, index):
    return ref.at[index]


def second(ref, index):
    return ref.at[:, index]


def rows_of(index):
    return pl.ds(pl.multiple_of(index * 128, 128), 128)


def pick_tile(table, index_ref, tile, part):
    return jnp.concatenate(
        [table[pl.ds(index_ref[tile, part * 32 + row], 1), :] for row in range(32)], axis=0
    )


def sort_tile(order, table, first, second, offset, tile):
    for part in range(4):
        start = pl.multiple_of(tile * 128 + part * 32 + offset, 32)
        picked = pick_tile(table, order, tile, part)
        first[pl.ds(start, 32), :] = picked[:, :128].astype(first.dtype)
        second[pl.ds(start, 32), :] = picked[:, 128:].astype(second.dtype)


def across(column):
    return jnp.broadcast_to(column, (128, 128)).T[:1, :]


def down(row):
    return jnp.broadcast_to(row, (128, 128)).T


def dot(a, b, contract):
    return lax.dot_general(a, b, (contract, ((), ())), preferred_element_type=jnp.float32)


def key_scales(keys):
    rows = keys.astype(jnp.float32)
    mean_square = jnp.mean(rows * rows, axis=-1, keepdims=True) + 1e-06
    return rows, mean_square, lax.rsqrt(mean_square) / HEAD_DIM


def half_turned(row):
    return jnp.concatenate([row[:, 64:], row[:, :64]], axis=1)


def windows(before, here):
    return [jnp.concatenate([before[:, 64:], here[:, :64]], axis=1), here]


def masked_scores(raw, scale, query_pos, key_pos):
    return jnp.where(
        key_pos > query_pos, LATER, jnp.where(key_pos == query_pos, SELF, raw * scale)
    )


def attend_tiles(tiles, unroll, order, order_rows, table, shared, values, mixed, total_sorted, last_scale):
    sort = functools.partial(sort_tile, order, table, shared, values, BLOCK)
    end = tiles * 128
    for tile in [tiles - 1] + list(range(unroll)):
        sort(tile)
    shared[:BLOCK, :] = shared[end : end + BLOCK, :]
    values[:BLOCK, :] = values[end : end + BLOCK, :]
    last_scale[...] = across(key_scales(shared[end - BLOCK : end + BLOCK, :])[2])

    def step_tiles(step, carry):
        first = step * unroll
        numbers = [lax.rem(first + tiles - 1, tiles)] + [first + k for k in range(unroll)]
        places = [order_rows[pl.ds(t, 1), :] for t in numbers]
        scale = [last_scale[...]]
        work = []
        for k in range(unroll):
            start = pl.multiple_of((first + k) * 128, 128)
            keys = [shared[pl.ds(pl.multiple_of(start + half * 64, 64), 128), :] for half in range(2)]
            vals = [values[pl.ds(pl.multiple_of(start + half * 64, 64), 128), :] for half in range(2)]
            own = jnp.concatenate([keys[0][64:], keys[1][64:]], axis=0)
            scale.append(across(key_scales(own)[2]))
            work.append((keys, vals))
        last_scale[...] = scale[-1]
        for k in range(unroll):
            sort(lax.rem(first + unroll + k, tiles))
        query_pos = jnp.concatenate([down(place) for place in places[1:]], axis=0)
        key_pos, key_scale = [], []
        for k in range(unroll):
            key_pos += windows(places[k], places[k + 1])
            key_scale += windows(scale[k], scale[k + 1])
        raw = [dot(k[64:], k, ((1,), (1,))) for keys, _ in work for k in keys]
        raw, key_pos, key_scale = (
            jnp.concatenate([jnp.broadcast_to(a, (64, 128)) for a in parts], axis=0)
            for parts in (raw, key_pos, key_scale)
        )
        scores = masked_scores(raw, key_scale, query_pos, key_pos)
        highest = jnp.max(scores, axis=-1, keepdims=True)
        total = highest + jnp.log(jnp.sum(jnp.exp(scores - highest), axis=-1, keepdims=True))
        prob = jnp.exp(scores - total).astype(jnp.bfloat16)
        rows = pl.ds(pl.multiple_of(first * 128, 128), unroll * 128)
        total = jnp.broadcast_to(total, (unroll * 128, 128))
        mixed[rows, 128:] = total
        total_sorted[rows, :] = total
        vals = [v for _, vals in work for v in vals]
        mixed[rows, :128] = jnp.concatenate(
            [dot(prob[64 * i : 64 * i + 64], v, ((1,), (0,))) for i, v in enumerate(vals)], axis=0
        )
        return carry

    lax.fori_loop(0, tiles // unroll, step_tiles, 0)


def attend_back_tiles(
    tiles, unroll, order, order_rows, table, shared, values, total_sorted,
    grad_sorted, grad_total_sorted, sums, scale_sums, last_scale,
):
    sort = functools.partial(sort_tile, order, table, grad_sorted, grad_total_sorted, 0)
    end = tiles * 128
    for tile in range(unroll):
        sort(tile)
    last_scale[...] = across(key_scales(shared[end - BLOCK : end + BLOCK, :])[2])
    scale_sums[...] = jnp.zeros_like(scale_sums)
    sums[end : end + 128, :] = jnp.zeros((128, 256), jnp.float32)
    early = lax.broadcasted_iota(jnp.int32, (1, 128), 1) < 64

    def step_tiles(step, carry):
        first = step * unroll
        numbers = [lax.rem(first + tiles - 1, tiles)] + [first + k for k in range(unroll)]
        places = [order_rows[pl.ds(t, 1), :] for t in numbers]
        scale = [last_scale[...]]
        work = []
        for k in range(unroll):
            start = pl.multiple_of((first + k) * 128, 128)
            keys = [shared[pl.ds(pl.multiple_of(start + half * 64, 64), 128), :] for half in range(2)]
            vals = [values[pl.ds(pl.multiple_of(start + half * 64, 64), 128), :] for half in range(2)]
            own = jnp.concatenate([keys[0][64:], keys[1][64:]], axis=0)
            scale.append(across(key_scales(own)[2]))
            tile = pl.ds(start, 128)
            work.append(
                (keys, vals, grad_sorted[tile, :], grad_total_sorted[tile, :], total_sorted[tile, :])
            )
        last_scale[...] = scale[-1]
        for k in range(unroll):
            sort(lax.rem(first + unroll + k, tiles))
        blocks = 2 * unroll
        scale_parts = [0.0] * (unroll + 1)
        query_pos = jnp.concatenate([down(place) for place in places[1:]], axis=0)
        key_pos, key_scale = [], []
        for k in range(unroll):
            key_pos += windows(places[k], places[k + 1])
            key_scale += windows(scale[k], scale[k + 1])
        keys = [k for item in work for k in item[0]]
        vals = [v for item in work for v in item[1]]
        grads, grad_totals, totals = (
            jnp.concatenate([item[n] for item in work], axis=0) for n in (2, 3, 4)
        )
        own = [slice(64 * i, 64 * i + 64) for i in range(blocks)]
        raw = [dot(k[64:], k, ((1,), (1,))) for k in keys]
        grad_prob = [dot(grads[own[i]], v, ((1,), (1,))) for i, v in enumerate(vals)]
        raw, grad_prob, key_pos, key_scale = (
            jnp.concatenate([jnp.broadcast_to(a, (64, 128)) for a in parts], axis=0)
            for parts in (raw, grad_prob, key_pos, key_scale)
        )
        prob = jnp.exp(masked_scores(raw, key_scale, query_pos, key_pos) - totals)
        inner = jnp.sum(prob * grad_prob, axis=-1, keepdims=True)
        grad_score = jnp.where(
            key_pos < query_pos, prob * (grad_prob + (grad_totals - inner)), 0.0
        )
        product = grad_score * raw
        for index in range(blocks):
            k, half = index // 2, index % 2
            part = jnp.sum(product[own[index]], axis=0, keepdims=True)
            if half == 0:
                turned = half_turned(part)
                scale_parts[k] += jnp.where(early, 0.0, turned)
                scale_parts[k + 1] += jnp.where(early, turned, 0.0)
            else:
                scale_parts[k + 1] += part
        grad_raw = (grad_score * key_scale).astype(jnp.bfloat16)
        prob = prob.astype(jnp.bfloat16)
        key_parts = [dot(grad_raw[own[i]], keys[i][64:], ((0,), (0,))) for i in range(blocks)]
        value_parts = [dot(prob[own[i]], grads[own[i]], ((0,), (0,))) for i in range(blocks)]
        query_parts = [dot(grad_raw[own[i]], keys[i], ((1,), (0,))) for i in range(blocks)]
        key_sums = [key_parts[0][:64]] + [
            key_parts[i][64:] + query_parts[i] + (key_parts[i + 1][:64] if i + 1 < blocks else 0.0)
            for i in range(blocks)
        ]
        value_sums = [value_parts[0][:64]] + [
            value_parts[i][64:] + (value_parts[i + 1][:64] if i + 1 < blocks else 0.0)
            for i in range(blocks)
        ]
        for index in range(blocks):
            rows = pl.ds(pl.multiple_of(first * 128 + index * 64, 64), 64)
            sums[rows, :128] = key_sums[index + 1]
            sums[rows, 128:] = value_sums[index + 1]
        for k in range(unroll):
            scale_sums[pl.ds(first + k, 1), :] = scale_parts[k + 1]
        before = jnp.where(step == 0, tiles, numbers[0])
        rows = pl.ds(pl.multiple_of(before * 128 + 64, 64), 64)
        sums[rows, :128] += key_sums[0]
        sums[rows, 128:] += value_sums[0]
        scale_sums[pl.ds(before, 1), :] += scale_parts[0]
        return carry

    lax.fori_loop(0, tiles // unroll, step_tiles, 0)
    sums[end - 128 : end, :] += sums[end : end + 128, :]
    scale_sums[pl.ds(tiles - 1, 1), :] += scale_sums[pl.ds(tiles, 1), :]

    def finish(step, carry):
        for part in range(2):
            tile = step * 2 + part
            rows = rows_of(tile)
            start = pl.multiple_of(tile * 128 + 64, 64)
            keys, mean_square, scale = key_scales(shared[pl.ds(start, 128), :])
            factor = down(scale_sums[pl.ds(tile, 1), :]) * (scale / (mean_square * HEAD_DIM))
            sums[rows, :128] -= factor * keys
        return carry

    lax.fori_loop(0, tiles // 2, finish, 0)


VMEM = pl.BlockSpec(memory_space=pltpu.VMEM)
ANY = pl.BlockSpec(memory_space=pl.ANY)


def normal_parts(rows):
    center = jnp.mean(rows, axis=-1, keepdims=True)
    offset = rows - center
    spread = jnp.mean(offset * offset, axis=-1, keepdims=True)
    inverse = lax.rsqrt(spread + 1e-05)
    return offset * inverse, inverse


def norm_back(grad, rows, gain):
    unit, inverse = normal_parts(rows)
    scaled = grad * gain
    shared = jnp.mean(scaled, axis=-1, keepdims=True)
    along = jnp.mean(scaled * unit, axis=-1, keepdims=True)
    return (
        (scaled - shared - unit * along) * inverse,
        jnp.sum(grad * unit, axis=0, keepdims=True),
        jnp.sum(grad, axis=0, keepdims=True),
    )


def gelu_parts(rows):
    below = 0.5 * (1.0 + lax.erf(rows * 0.7071067811865476))
    bell = jnp.exp(-0.5 * rows * rows) * 0.3989422804014327
    return rows * below, below + rows * bell


def feed_kernel(
    planes,
    mixed, total, x1, wo_in, gains, wup_in, bias_up, wdown_in, df_in, g1,
    y1_out, g1_out, dout_out, attended_out, dmixed_home, dtotal_home, y2_out, up_grad_out, down_grad_out,
    up_bias_out, gain_out, shift_out,
    wo, wup, wdown, df, weights, attended, arrived, h2, dact, act, dpre, kept, to_sibling, from_sibling,
    to_chip, from_chip, up_grad, down_grad, y2, dout, datt_out, datt, dmixed, dtotal, send, receive, local,
):
    low, full = jnp.bfloat16, jnp.float32
    links = Links(planes, send, receive, local)
    links.greet()
    loads = [links.keep(a, b) for a, b in ((wo_in, wo), (df_in, df), (wdown_in, wdown), (wup_in, wup))]

    def combine(z, carry):
        for x in range(2):
            totals = [down(total[x * 4 + u, pl.ds(z, 1), :]) for u in range(4)]
            highest = jnp.maximum(
                jnp.maximum(totals[0], totals[1]), jnp.maximum(totals[2], totals[3])
            )
            parts = [jnp.exp(t - highest) for t in totals]
            inverse = 1.0 / (parts[0] + parts[1] + parts[2] + parts[3])
            result = 0.0
            for u in range(4):
                weight = parts[u] * inverse
                weights[x * 4 + u, z] = weight
                result += weight * mixed[x * 4 + u, z].astype(full)
            attended[z, :, x * 128 : (x + 1) * 128] = result.astype(low)
        return carry

    lax.fori_loop(0, planes, combine, 0)
    links.meet()
    share = along_z(block, block)(links, attended, arrived)
    next(share)
    keep_attended = links.keep(attended, attended_out)
    loads[0].wait()
    drive([share])
    y1 = x1[...]
    for z in range(planes):
        y1 += dot(arrived[z], wo[z * 256 : (z + 1) * 256, :], ((1,), (0,)))
    y1_out[...] = y1
    unit, _ = normal_parts(y1)
    own_rows = pl.ds(pl.multiple_of(links.p * 128, 128), 128)
    h2[own_rows, :] = (unit * gains[2:3, :] + gains[3:4, :]).astype(low)

    sibling, _ = links.near(1)
    own_h2 = h2.at[own_rows, :]
    direct = {step: links.push(own_h2, own_h2, links.near(step)[0]) for step in (6, 4, 2)}
    handed = {0: links.push(own_h2, own_h2, sibling)}
    for load in loads[1:]:
        load.wait()

    def upper_back(part, carry):
        rows = pl.ds(pl.multiple_of(part * 256, 256), 256)
        dact[rows, :] = dot(df[rows, :], wdown[...], ((1,), (1,)))
        return carry

    lax.fori_loop(0, 4, upper_back, 0)

    def pass_on(step):
        direct[step].wait_recv()
        block_rows = h2.at[rows_of(links.near(step)[1]), :]
        handed[step] = links.push(block_rows, block_rows, sibling)

    def feed(slot, step):
        handed[step].wait_recv()
        chip = links.near(step)[1] // 2
        rows = pl.ds(pl.multiple_of(chip * 256, 256), 256)
        before = dot(h2[rows, :], wup[...], ((1,), (0,))) + bias_up[...]
        value, slope = gelu_parts(before)
        act[rows, :] = value.astype(low)
        grad = (dact[rows, :] * slope).astype(low)
        dpre[rows, :] = grad
        kept[slot] = dot(grad, wup[...], ((1,), (1,))).reshape(2, 128, -1).astype(low)
        return links.push(kept.at[slot, 1 - links.core], from_sibling.at[slot], sibling)

    def chip_sum(slot, step, traded):
        traded.wait_recv()
        result = kept[slot, links.core].astype(full) + from_sibling[slot].astype(full)
        if slot == 0:
            return result
        to_chip[slot - 1] = result.astype(low)
        return links.push(to_chip.at[slot - 1], from_chip.at[slot - 1], links.near(step)[0])

    pass_on(2)
    traded = [feed(0, 0)]
    pass_on(4)
    traded.append(feed(1, 2))
    sent = [chip_sum(1, 2, traded[1])]
    pass_on(6)
    traded.append(feed(2, 4))
    sent.append(chip_sum(2, 4, traded[2]))
    traded.append(feed(3, 6))
    sent.append(chip_sum(3, 6, traded[3]))
    own_sum = chip_sum(0, 0, traded[0])

    def upper_grad(part, carry):
        rows = pl.ds(pl.multiple_of(part * 256, 256), 256)
        up_grad[part] = dot(h2[:, rows], dpre[...], ((0,), (0,))).astype(low)
        return carry

    lax.fori_loop(0, planes, upper_grad, 0)
    share_up = along_z(block, block)(links, up_grad, up_grad_out)
    next(share_up)
    for copy in sent:
        copy.wait_recv()
    grad = own_sum + (
        from_chip[0].astype(full) + from_chip[1].astype(full) + from_chip[2].astype(full)
    )
    part, gain_grad, shift_grad = norm_back(grad, y1_out[...], gains[2:3, :])
    gain_out[...] = gain_grad
    shift_out[...] = shift_grad
    g1_new = g1[...] + part
    g1_out[...] = g1_new
    dout[...] = g1_new.astype(low)
    keep_dout = links.keep(dout, dout_out)
    for z in range(planes):
        datt_out[z] = dot(dout[...], wo[z * 256 : (z + 1) * 256, :], ((1,), (1,))).astype(low)
    share = along_z(block, block)(links, datt_out, datt)
    next(share)

    def lower_grad(part, carry):
        rows = pl.ds(pl.multiple_of(part * 128, 128), 128)
        down_grad[part] = dot(act[:, rows], df[...], ((0,), (0,))).astype(low)
        return carry

    lax.fori_loop(0, planes, lower_grad, 0)
    share_down = along_z(block, block)(links, down_grad, down_grad_out)
    next(share_down)
    up_bias_out[...] = jnp.sum(dpre[...].astype(full), axis=0, keepdims=True)
    drive([share])

    def combine_back(z, carry):
        for x in range(2):
            grad = datt[z, :, x * 128 : (x + 1) * 128].astype(full)
            chosen = [weights[x * 4 + u, z] for u in range(4)]
            inner = [
                jnp.sum(grad * mixed[x * 4 + u, z].astype(full), axis=-1, keepdims=True)
                for u in range(4)
            ]
            mean = sum(chosen[u] * inner[u] for u in range(4))
            for u in range(4):
                dmixed[x * 4 + u, z] = (chosen[u] * grad).astype(low)
                change = (chosen[u] * (inner[u] - mean)).astype(low).astype(full)
                dtotal[x * 4 + u, pl.ds(z, 1), :] = change.T[:1, :]
        return carry

    lax.fori_loop(0, planes, combine_back, 0)
    shares = [
        over_plane(block, second)(links, dmixed, dmixed_home),
        over_plane(block, block)(links, dtotal, dtotal_home),
    ]
    for transfer in shares:
        next(transfer)

    def lower(part, carry):
        rows = pl.ds(pl.multiple_of(part * 128, 128), 128)
        y2[part] = dot(act[rows, :], wdown[...], ((1,), (0,))).astype(low)
        return carry

    lax.fori_loop(0, 8, lower, 0)
    keep_y2 = links.keep(y2, y2_out)
    for copy in list(direct.values()) + traded + sent:
        copy.wait_send()
    for copy in handed.values():
        copy.wait_send()
    drive(shares + [share_up, share_down])
    for copy in (keep_attended, keep_dout, keep_y2):
        copy.wait()


def feed_stage(arguments, collective_id, planes):
    low, full = jnp.bfloat16, jnp.float32
    (mixed, total, x1, wo, gains, wup, bias_up, wdown, df, g1) = arguments
    rows, width = x1.shape
    part = wup.shape[1]
    shape = jax.ShapeDtypeStruct
    outputs = [
        (shape((rows, width), full), VMEM),
        (shape((rows, width), full), VMEM),
        (shape((rows, width), low), ANY),
        (shape((planes, rows, 256), low), ANY),
        (shape((planes, 8, rows, HEAD_DIM), low), ANY),
        (shape((8, 8, rows), full), ANY),
        (shape((8, rows, width), low), ANY),
        (shape((planes, width // planes, part), low), ANY),
        (shape((planes, rows, width), low), ANY),
        (shape((1, part), full), VMEM),
        (shape((1, width), full), VMEM),
        (shape((1, width), full), VMEM),
    ]
    scratch = [
        (wo.shape, low),
        (wup.shape, low),
        (wdown.shape, low),
        (df.shape, low),
        ((8, planes, rows, HEAD_DIM), full),
        ((planes, rows, 256), low),
        ((planes, rows, 256), low),
        ((8 * rows, width), low),
        ((8 * rows, part), full),
        ((8 * rows, part), low),
        ((8 * rows, part), low),
        ((4, 2, rows, width), low),
        ((4, rows, width), low),
        ((4, rows, width), low),
        ((3, rows, width), low),
        ((3, rows, width), low),
        ((planes, width // planes, part), low),
        ((planes, rows, width), low),
        ((8, rows, width), low),
        ((rows, width), low),
        ((planes, rows, 256), low),
        ((planes, rows, 256), low),
        ((8, planes, rows, HEAD_DIM), low),
        ((8, 8, rows), full),
    ]
    return pl.pallas_call(
        functools.partial(feed_kernel, planes),
        out_shape=[o[0] for o in outputs],
        in_specs=[VMEM, VMEM, VMEM, ANY, VMEM, ANY, VMEM, ANY, ANY, VMEM],
        out_specs=[o[1] for o in outputs],
        scratch_shapes=[pltpu.VMEM(*s) for s in scratch] + link_scratch(),
        compiler_params=pltpu.CompilerParams(
            vmem_limit_bytes=56 << 20, collective_id=collective_id, has_side_effects=True
        ),
        name="feed",
    )(*arguments)


def open_kernel(
    planes,
    sort_order, sort_place, gain_a_in, shift_a_in, gain_f_in, shift_f_in, bias_up_in, bias_down_in,
    x2, wqk, wv, wo, wup, wdown, g2,
    places_out, gains_out, bias_up_out, normed_out, wqk_out, wv_out, wo_out, wup_out, wdown_out, df_out,
    shared_out, values_out, total_out, mixed_out, total_home_out,
    ints, all_ints, floats, all_floats, order_rows, place_rows, order_s, place_s, normed, df,
    wqk_line, wv_line, wo_line, wup_rows, wqk_pair, wv_pair, heads, head_table, table, mixed,
    shared, values, total_sorted, mixed_home, total_home, last_scale, send, receive, local,
):
    low, full = jnp.bfloat16, jnp.float32
    links = Links(planes, send, receive, local)
    links.greet()
    sub = links.y * 2 + links.core
    tiles = planes * 8
    ints[...] = jnp.concatenate([sort_order[...], sort_place[...]], axis=0)
    lane = lax.broadcasted_iota(jnp.int32, (1, 128), 1) // 32

    def spread(vector):
        wide = jnp.concatenate([vector[...].astype(full)] * 4, axis=1)
        return jnp.where(lane == sub, wide, 0.0)

    floats[...] = jnp.concatenate(
        [spread(v) for v in (gain_a_in, shift_a_in, gain_f_in, shift_f_in, bias_down_in)]
        + [bias_up_in[...].astype(full), jnp.zeros((2, 128), full)],
        axis=0,
    )
    df[...] = g2[...].astype(low)
    links.meet()
    share_floats = everywhere(links, floats, all_floats)
    next(share_floats)
    share_ints = everywhere(links, ints, all_ints)
    next(share_ints)

    def pair_columns(ref, z):
        return ref.at[:, pl.ds(pl.multiple_of(z * 256, 256), 256)]

    pair_shares = [
        along_z(pair_columns, block)(links, a, b) for a, b in ((wqk, wqk_line), (wv, wv_line))
    ]
    for transfer in pair_shares:
        next(transfer)
    unit, _ = normal_parts(x2[...])
    next(share_floats)

    def upper_columns(chunk):
        def columns(ref, p):
            return ref.at[:, pl.ds(pl.multiple_of((chunk * 8 + p) * 128, 128), 128)]

        def landing(ref, p):
            return ref.at[p, :, pl.ds(chunk * 128, 128)]

        return over_plane(columns, landing)

    drive([share_floats])

    def vector_of(row, z_step=2):
        chunks = []
        for chunk in range(8):
            z, x = chunk // 2, chunk % 2
            parts = [all_floats[z, x * 4 + u, row : row + 1, :] for u in range(4)]
            chunks.append(parts[0] + parts[1] + parts[2] + parts[3])
        return jnp.concatenate(chunks, axis=1)

    gain, shift = vector_of(0), vector_of(1)
    normed[links.z] = (unit * gain + shift).astype(low)
    normed_copies = []
    for step in range(1, planes):
        device, _, _ = links.along(step)
        normed_copies.append(links.push(normed.at[links.z], normed.at[links.z], device))
    for transfer in pair_shares:
        drive([transfer])
    pair_shares = [
        over_chips(whole, second)(links, a, b) for a, b in ((wqk_line, wqk_pair), (wv_line, wv_pair))
    ]
    for transfer in pair_shares:
        next(transfer)
    next(share_ints)
    upper_shares = [upper_columns(chunk)(links, wup, wup_rows) for chunk in range(planes)]
    for transfer in upper_shares:
        next(transfer)
    for transfer in pair_shares:
        next(transfer)
    gains_out[0:1, :] = gain
    gains_out[1:2, :] = shift
    for row in (2, 3, 4):
        gains_out[row : row + 1, :] = vector_of(row)
    for z in range(planes):
        bias_up_out[:, z * 128 : (z + 1) * 128] = all_floats[z, links.p, 5:6, :]
    drive(pair_shares)
    drive([share_ints])
    for z in range(planes):
        for p in range(8):
            tile = z * 8 + p
            order_rows[tile : tile + 1, :] = all_ints[z, p, pl.ds(sub, 1), :]
            place_rows[tile : tile + 1, :] = all_ints[z, p, pl.ds(sub + 4, 1), :]
    to_scalars = [links.keep(order_rows, order_s), links.keep(place_rows, place_s)]
    shares = [over_chips(whole, block)(links, df, df_out)]
    next(shares[0])

    def head_columns(z):
        def columns(ref, p):
            return ref.at[z, :, pl.ds(pl.multiple_of((p // 4) * 256, 256), 256)]

        return columns

    def landing(z):
        return lambda ref, p: ref.at[z, p]

    def project(z):
        rows = normed[z]
        for weights, offset in ((wqk_pair, 0), (wv_pair, 128)):
            result = dot(rows, weights[...].reshape(-1, 256), ((1,), (0,))).astype(low)
            heads[z, :, offset : offset + 128] = result[:, :128]
            heads[z, :, 256 + offset : 384 + offset] = result[:, 128:]
        transfer = over_chips(head_columns(z), landing(z))(links, heads, head_table)
        next(transfer)
        return transfer

    head_shares = [project(links.z)]
    wo_share = along_z(whole, block)(links, wo, wo_line)
    next(wo_share)
    for step, copy in enumerate(normed_copies, 1):
        copy.wait_recv()
        head_shares.append(project(links.along(step)[2]))
        next(head_shares[-2])
    for transfer in upper_shares:
        drive([transfer])
    shares += [
        along_z(whole, block)(links, wup_rows, wup_out),
        along_z(whole, block)(links, wdown, wdown_out),
    ]
    next(shares[1])
    next(shares[2])
    next(head_shares[-1])
    drive([wo_share])
    wo_share = over_chips(whole, second)(links, wo_line, wo_out)
    for copy in to_scalars:
        copy.wait()
    drive(head_shares)
    next(wo_share)

    def load(tile, carry):
        table[rows_of(tile), :] = head_table[tile // 8, lax.rem(tile, 8)].astype(full)
        return carry

    lax.fori_loop(0, tiles, load, 0)
    attend_tiles(
        tiles, 2, order_s, order_rows, table, shared, values, mixed, total_sorted, last_scale
    )
    next(wo_share)
    next(shares[0])
    kept = [
        links.keep(normed, normed_out),
        links.keep(wqk_pair, wqk_out),
        links.keep(wv_pair, wv_out),
        links.keep(shared, shared_out),
        links.keep(values, values_out),
        links.keep(total_sorted, total_out),
        links.keep(order_rows, places_out.at[0]),
        links.keep(place_rows, places_out.at[1]),
    ]
    sent = []
    for step in (6, 7, 4, 5, 2, 3, 1, 0):
        device, p = links.near(step)

        def unsort(z, carry):
            totals = []
            for part in range(4):
                picked = pick_tile(mixed, place_s, z * 8 + p, part)
                mixed_home[p, z, part * 32 : part * 32 + 32, :] = picked[:, :128].astype(low)
                totals.append(picked[:, 128:])
            total_home[p, pl.ds(z, 1), :] = jnp.concatenate(totals, axis=0).T[:1, :]
            return carry

        lax.fori_loop(0, planes, unsort, 0)
        for here, there in ((mixed_home, mixed_out), (total_home, total_home_out)):
            source, target = here.at[p], there.at[links.p]
            if step:
                sent.append(links.push(source, target, device))
            else:
                kept.append(links.keep(source, target))
    for copy in normed_copies:
        copy.wait_send()
    drive(shares + [wo_share])
    for copy in kept + sent:
        copy.wait()


def open_stage(arguments, collective_id, planes):
    low, full, whole_number = jnp.bfloat16, jnp.float32, jnp.int32
    x2, wqk, wup = arguments[8], arguments[9], arguments[12]
    rows, width = x2.shape
    own, hidden = wup.shape
    part = hidden // 8
    tiles = planes * 8
    tokens = tiles * rows
    shape = jax.ShapeDtypeStruct
    outputs = [
        (shape((2, tiles, rows), whole_number), ANY),
        (shape((8, width), full), VMEM),
        (shape((1, part), full), VMEM),
        (shape((planes, rows, width), low), ANY),
        (shape((planes, 8, own, 256), low), ANY),
        (shape((planes, 8, own, 256), low), ANY),
        (shape((planes, 8, own, width), low), ANY),
        (shape((planes, 8, own, part), low), ANY),
        (shape((planes, rows, width), low), ANY),
        (shape((8, rows, width), low), ANY),
        (shape((tokens + BLOCK, HEAD_DIM), low), ANY),
        (shape((tokens + BLOCK, HEAD_DIM), low), ANY),
        (shape((tokens, HEAD_DIM), full), ANY),
        (shape((8, planes, rows, HEAD_DIM), low), ANY),
        (shape((8, 8, rows), full), ANY),
    ]
    scratch = [
        pltpu.VMEM((8, rows), whole_number),
        pltpu.VMEM((planes, 8, 8, rows), whole_number),
        pltpu.VMEM((8, rows), full),
        pltpu.VMEM((planes, 8, 8, rows), full),
        pltpu.VMEM((tiles, rows), whole_number),
        pltpu.VMEM((tiles, rows), whole_number),
        pltpu.SMEM((tiles, rows), whole_number),
        pltpu.SMEM((tiles, rows), whole_number),
        pltpu.VMEM((planes, rows, width), low),
        pltpu.VMEM((rows, width), low),
        pltpu.VMEM((planes, own, 256), low),
        pltpu.VMEM((planes, own, 256), low),
        pltpu.VMEM((planes, own, width), low),
        pltpu.VMEM((8, own, part), low),
        pltpu.VMEM((planes, 8, own, 256), low),
        pltpu.VMEM((planes, 8, own, 256), low),
        pltpu.VMEM((planes, rows, 512), low),
        pltpu.VMEM((planes, 8, rows, 256), low),
        pltpu.VMEM((tokens, 256), full),
        pltpu.VMEM((tokens, 256), full),
        pltpu.VMEM((tokens + BLOCK, HEAD_DIM), low),
        pltpu.VMEM((tokens + BLOCK, HEAD_DIM), low),
        pltpu.VMEM((tokens, HEAD_DIM), full),
        pltpu.VMEM((8, planes, rows, HEAD_DIM), low),
        pltpu.VMEM((8, 8, rows), full),
        pltpu.VMEM((1, rows), full),
    ]
    return pl.pallas_call(
        functools.partial(open_kernel, planes),
        out_shape=[o[0] for o in outputs],
        in_specs=[VMEM] * 15,
        out_specs=[o[1] for o in outputs],
        scratch_shapes=scratch + link_scratch(),
        compiler_params=pltpu.CompilerParams(
            vmem_limit_bytes=56 << 20, collective_id=collective_id, has_side_effects=True
        ),
        name="open",
    )(*arguments)


def close_kernel(
    planes,
    places, shared_in, values_in, total_in, dmixed_in, dtotal_in, y2_in, dout_in, attended_in, normed_in,
    wqk_in, wv_in, gains, x2_in, g2_in, up_in, down_in, up_bias, feed_gain, feed_shift,
    y2_out, g2_out, shared_grad_out, value_grad_out, out_grad_out, up_out, down_out, vectors_out,
    order_rows, order_s, place_s, shared, values, total_sorted, dmixed, dtotal, table, grad_sorted,
    grad_total_sorted, sums, scale_sums, last_scale, kept, from_sibling, to_chip, from_chip, y2_parts,
    dout_line, attended, normed, wqk, wv, x2, g2, up_parts, down_parts, up_sum, up_arrived, dshared, dvalues,
    de_out, de, out_sent, out_arrived, weight_sent, weight_arrived, weight_sum, weight_final,
    tiles_sent, tiles_arrived, tile, tile_line, send, receive, local,
):
    low, full = jnp.bfloat16, jnp.float32
    links = Links(planes, send, receive, local)
    links.greet()
    tiles = planes * 8
    line = planes * 128
    first_loads = [
        links.keep(a, b)
        for a, b in (
            (places.at[0], order_s), (places.at[1], place_s), (places.at[0], order_rows),
            (dmixed_in, dmixed), (dtotal_in, dtotal), (shared_in, shared), (values_in, values),
            (total_in, total_sorted), (up_in, up_parts),
        )
    ]
    links.meet()
    share_dout = along_z(whole, block)(links, dout_in, dout_line)
    next(share_dout)
    share_y2 = over_plane(block, block)(links, y2_in, y2_parts)
    next(share_y2)
    loads = [
        links.keep(a, b)
        for a, b in (
            (attended_in, attended), (normed_in, normed), (wqk_in, wqk), (wv_in, wv), (x2_in, x2),
            (g2_in, g2), (down_in, down_parts),
        )
    ]
    for copy in first_loads:
        copy.wait()
    up_sum[...] = sum(up_parts[z].astype(full) for z in range(planes)).reshape(up_sum.shape)
    share_up = over_plane(block, block)(links, up_sum, up_arrived)
    next(share_up)

    def load(index, carry):
        z, p = index // 8, lax.rem(index, 8)
        table[rows_of(index), :128] = dmixed[z, p].astype(full)
        table[rows_of(index), 128:] = down(dtotal[p, pl.ds(z, 1), :])
        return carry

    lax.fori_loop(0, tiles, load, 0)
    attend_back_tiles(
        tiles, 4, order_s, order_rows, table, shared, values, total_sorted,
        grad_sorted, grad_total_sorted, sums, scale_sums, last_scale,
    )
    sibling, _ = links.near(1)

    def unsort(slot, step):
        chip = links.near(step)[1] // 2
        for core, goal in ((0, 1 - links.core), (1, links.core)):

            def rows(z, carry):
                for part in range(4):
                    picked = pick_tile(sums, place_s, z * 8 + chip * 2 + goal, part)
                    kept[slot, core, z, part * 32 : part * 32 + 32, :] = picked.astype(low)
                return carry

            lax.fori_loop(0, planes, rows, 0)
            if core == 0:
                traded = links.push(kept.at[slot, 0], from_sibling.at[slot], sibling)
        return traded

    def chip_sum(slot, step, traded):
        traded.wait_recv()
        result = kept[slot, 1].astype(full) + from_sibling[slot].astype(full)
        if step == 0:
            return result
        to_chip[slot] = result.astype(low)
        return links.push(to_chip.at[slot], from_chip.at[slot], links.near(step)[0])

    steps = (6, 4, 2, 0)
    traded, sent = [], []
    for slot, step in enumerate(steps):
        traded.append(unsort(slot, step))
        if slot:
            sent.append(chip_sum(slot - 1, steps[slot - 1], traded[slot - 1]))
    for copy in loads:
        copy.wait()
    drive([share_dout])
    all_dout = dout_line[...].reshape(line, -1)
    out_sent[...] = (
        dot(attended[...].reshape(line, 256), all_dout, ((0,), (0,))).astype(low).reshape(out_sent.shape)
    )
    own_sum = chip_sum(3, 0, traded[3])
    share_out = over_plane(block, block)(links, out_sent, out_arrived)
    next(share_out)
    own_columns = pl.ds(pl.multiple_of(links.x * 128, 128), 128)
    far_columns = pl.ds(pl.multiple_of((1 - links.x) * 128, 128), 128)

    def settle_sum(columns, result):
        result = result.astype(low).reshape(line, 256)
        dshared[:, columns] = result[:, :128]
        dvalues[:, columns] = result[:, 128:]

    sent[2].wait_recv()
    settle_sum(own_columns, own_sum + from_chip[2].astype(full))
    sent[1].wait_recv()
    sent[0].wait_recv()
    settle_sum(far_columns, from_chip[1].astype(full) + from_chip[0].astype(full))
    all_wqk, all_wv = wqk[...].reshape(-1, 256), wv[...].reshape(-1, 256)

    def input_grad(z, carry):
        rows = rows_of(z)
        de_out[z] = (
            dot(dshared[rows, :], all_wqk, ((1,), (1,))) + dot(dvalues[rows, :], all_wv, ((1,), (1,)))
        ).astype(low)
        return carry

    lax.fori_loop(0, planes, input_grad, 0)
    share_de = along_z(block, block)(links, de_out, de)
    next(share_de)
    all_normed = normed[...].reshape(line, -1)
    for index, grad in enumerate((dshared, dvalues)):
        weight_sent[index] = (
            dot(all_normed, grad[...], ((0,), (0,))).astype(low).reshape(weight_sent.shape[1:])
        )

    def of_pair(ref, p):
        return ref.at[:, :, p]

    share_weights = over_plane(of_pair, block)(links, weight_sent, weight_arrived)
    next(share_weights)
    drive([share_y2])
    y2_out[...] = x2[...] + (
        sum(y2_parts[p].astype(full) for p in range(8)) + gains[4:5, :]
    )
    drive([share_up])
    for p in range(8):
        for z in range(planes):
            up_out[:, (z * 8 + p) * 128 : (z * 8 + p + 1) * 128] = up_arrived[
                p, :, z * 128 : (z + 1) * 128
            ]
    down_out[...] = sum(down_parts[z].astype(full) for z in range(planes))
    drive([share_out])
    out_grad_out[...] = sum(out_arrived[p].astype(full) for p in range(8))
    down_bias = jnp.sum(g2[...].astype(low).astype(full), axis=0, keepdims=True)
    drive([share_weights])
    weight_sum[...] = sum(weight_arrived[p].astype(full) for p in range(8)).astype(low)

    def pair_columns(ref, z):
        return ref.at[:, :, pl.ds(pl.multiple_of(z * 256, 256), 256)]

    share_final = along_z(second, pair_columns)(links, weight_sum, weight_final)
    next(share_final)
    drive([share_de])
    part, gain_grad, shift_grad = norm_back(
        sum(de[z].astype(full) for z in range(planes)), x2[...], gains[0:1, :]
    )
    vectors = [gain_grad, shift_grad, feed_gain[...], feed_shift[...], down_bias]
    for x in range(2):
        for index, vector in enumerate(vectors):
            for z in range(planes):
                chunk = (z * 2 + x) * 128
                row = index * planes + z
                tiles_sent[x, row : row + 1, :] = vector[:, chunk : chunk + 128]
        tiles_sent[x, 5 * planes :, :] = jnp.zeros((24 - 5 * planes, 128), full)

    def of_x(ref, p):
        return ref.at[p // 4]

    share_tiles = over_plane(of_x, block)(links, tiles_sent, tiles_arrived)
    next(share_tiles)
    g2_out[...] = g2[...] + part
    drive([share_tiles])
    tile[...] = jnp.sum(tiles_arrived[...], axis=0)
    for z in range(planes):
        tile[5 * planes + z : 5 * planes + z + 1, :] = up_bias[:, z * 128 : (z + 1) * 128]
    share_tile = along_z(whole, block)(links, tile, tile_line)
    next(share_tile)
    drive([share_final])
    shared_grad_out[...] = weight_final[0].astype(full)
    value_grad_out[...] = weight_final[1].astype(full)
    drive([share_tile])
    tile[...] = jnp.sum(tile_line[...], axis=0)
    for index in range(6):
        vectors_out[index : index + 1, :] = tile[pl.ds(index * planes + links.z, 1), :]
    vectors_out[6:8, :] = jnp.zeros((2, 128), full)
    for copy in traded + sent:
        copy.wait_send()


def close_stage(arguments, collective_id, planes):
    low, full, whole_number = jnp.bfloat16, jnp.float32, jnp.int32
    x2, normed = arguments[13], arguments[9]
    own, part = arguments[10].shape[2], arguments[15].shape[2]
    rows, width = x2.shape
    tiles = planes * 8
    tokens = tiles * rows
    shape = jax.ShapeDtypeStruct
    outputs = [
        shape((rows, width), full),
        shape((rows, width), full),
        shape((own, width), full),
        shape((own, width), full),
        shape((own, width), full),
        shape((own, 8 * part), full),
        shape((rows, width), full),
        shape((8, rows), full),
    ]
    vmem = pltpu.VMEM
    chip_blocks = (planes, rows, 256)
    scratch = [
        vmem((tiles, rows), whole_number),
        pltpu.SMEM((tiles, rows), whole_number),
        pltpu.SMEM((tiles, rows), whole_number),
        vmem((tokens + BLOCK, HEAD_DIM), low),
        vmem((tokens + BLOCK, HEAD_DIM), low),
        vmem((tokens, HEAD_DIM), full),
        vmem((planes, 8, rows, HEAD_DIM), low),
        vmem((8, 8, rows), full),
        vmem((tokens, 256), full),
        vmem((tokens, HEAD_DIM), low),
        vmem((tokens, HEAD_DIM), full),
        vmem((tokens + rows, 256), full),
        vmem((tiles + 8, rows), full),
        vmem((1, rows), full),
        vmem((4, 2) + chip_blocks, low),
        vmem((4,) + chip_blocks, low),
        vmem((3,) + chip_blocks, low),
        vmem((3,) + chip_blocks, low),
        vmem((8, rows, width), low),
        vmem((planes, rows, width), low),
        vmem(chip_blocks, low),
        vmem((planes, rows, width), low),
        vmem((planes, 8, own, 256), low),
        vmem((planes, 8, own, 256), low),
        vmem((rows, width), full),
        vmem((rows, width), full),
        vmem((planes, 8 * own, part), low),
        vmem((planes, rows, width), low),
        vmem((8, own, part), full),
        vmem((8, own, part), full),
        vmem((planes * rows, 256), low),
        vmem((planes * rows, 256), low),
        vmem((planes, rows, width), low),
        vmem((planes, rows, width), low),
        vmem((8, own, width), low),
        vmem((8, own, width), low),
        vmem((2, planes, 8, own, 256), low),
        vmem((8, 2, planes, own, 256), low),
        vmem((2, planes, own, 256), low),
        vmem((2, own, width), low),
        vmem((2, 24, rows), full),
        vmem((8, 24, rows), full),
        vmem((24, rows), full),
        vmem((planes, 24, rows), full),
    ]
    return pl.pallas_call(
        functools.partial(close_kernel, planes),
        out_shape=outputs,
        in_specs=[ANY] * 12 + [VMEM] + [ANY] * 4 + [VMEM] * 3,
        out_specs=[VMEM] * len(outputs),
        scratch_shapes=scratch + link_scratch(),
        compiler_params=pltpu.CompilerParams(
            vmem_limit_bytes=56 << 20, collective_id=collective_id, has_side_effects=True
        ),
        name="close",
    )(*arguments)


def plane_plan(
    n_seq,
    n_sub,
    first_half,
    second_half,
    grad_first,
    grad_second,
    attend_gain,
    attend_shift,
    query_key_weight,
    value_projection_weight,
    output_projection_weight,
    feed_gain,
    feed_shift,
    upper_projection_weight,
    upper_projection_bias,
    lower_projection_weight,
    lower_projection_bias,
    sort_order,
    sort_place,
):
    planes = n_seq // 2
    rows, width = first_half.shape[1:]
    own = width // (n_seq * n_sub)
    x1, x2, g1, g2 = (a[0] for a in (first_half, second_half, grad_first, grad_second))
    wqk, wv, wo = query_key_weight[0], value_projection_weight[0], output_projection_weight[0]
    wup, wdown = upper_projection_weight[0], lower_projection_weight[0]
    (
        places, gains, bias_up, normed_line, wqk_pair, wv_pair, wo_all, wup_part, wdown_part, df_plane,
        shared, values, total_sorted, mixed, total,
    ) = open_stage(
        (
            sort_order[0, :, 0], sort_place[0, :, 0], attend_gain, attend_shift, feed_gain, feed_shift,
            upper_projection_bias, lower_projection_bias, x2, wqk, wv, wo, wup, wdown, g2,
        ),
        1,
        planes,
    )
    (
        y1, g1, dout, attended, dmixed, dtotal, y2_parts, up_grad, down_grad,
        up_bias_grad, feed_gain_grad, feed_shift_grad,
    ) = feed_stage(
        (
            mixed, total, x1, wo_all.reshape(width, width), gains, wup_part.reshape(width, -1),
            bias_up, wdown_part.reshape(-1, width), df_plane.reshape(8 * rows, width), g1,
        ),
        2,
        planes,
    )
    (
        y2, g2, shared_grad, value_grad, out_grad, up_grad, down_grad, vectors
    ) = close_stage(
        (
            places, shared, values, total_sorted, dmixed, dtotal, y2_parts, dout, attended, normed_line,
            wqk_pair, wv_pair, gains, x2, g2, up_grad, down_grad, up_bias_grad, feed_gain_grad,
            feed_shift_grad,
        ),
        3,
        planes,
    )
    pieces = lax.dynamic_slice(vectors, (0, lax.axis_index("sub") * own), (5, own))
    outputs = (
        y1, y2, g1, g2, pieces[0], pieces[1], shared_grad, value_grad, out_grad, pieces[2], pieces[3],
        up_grad, vectors[5], down_grad, pieces[4],
    )
    return tuple((a[None] for a in outputs))


def on_device(n_seq, n_sub, *arguments):
    sequences, rows, width = arguments[0].shape
    rounds = arguments[-1].shape[1]
    fits = (
        sequences == 1
        and rows == 2 * BLOCK
        and rounds == n_sub
        and HEADS == n_seq
        and width == HEADS * HEAD_DIM
    )
    if fits:
        return plane_plan(n_seq, n_sub, *arguments)
    return general_plan(*arguments)


def solution(mesh):
    return jax.shard_map(
        functools.partial(on_device, mesh.shape["seq"], mesh.shape["sub"]),
        mesh=mesh,
        in_specs=(
            P(None, ("seq", "sub"), None),
            P(None, ("seq", "sub"), None),
            P(None, ("seq", "sub"), None),
            P(None, ("seq", "sub"), None),
            P(None, ("seq", "sub")),
            P(None, ("seq", "sub")),
            P(None, ("seq", "sub"), None),
            P(None, ("seq", "sub"), None),
            P(None, ("seq", "sub"), None),
            P(None, ("seq", "sub")),
            P(None, ("seq", "sub")),
            P(None, ("seq", "sub"), None),
            P(None, ("seq", "sub")),
            P(None, ("seq", "sub"), None),
            P(None, ("seq", "sub")),
            P(None, None, None, ("seq", "sub")),
            P(None, None, None, ("seq", "sub")),
        ),
        out_specs=(
            P(None, ("seq", "sub"), None),
            P(None, ("seq", "sub"), None),
            P(None, ("seq", "sub"), None),
            P(None, ("seq", "sub"), None),
            P(None, ("seq", "sub")),
            P(None, ("seq", "sub")),
            P(None, ("seq", "sub"), None),
            P(None, ("seq", "sub"), None),
            P(None, ("seq", "sub"), None),
            P(None, ("seq", "sub")),
            P(None, ("seq", "sub")),
            P(None, ("seq", "sub"), None),
            P(None, ("seq", "sub")),
            P(None, ("seq", "sub"), None),
            P(None, ("seq", "sub")),
        ),
        check_vma=False,
    )
```

```python
import functools

import jax
import jax.numpy as jnp
from jax import lax
from jax.experimental import pallas as pl
from jax.experimental.pallas import tpu as pltpu
from jax.sharding import PartitionSpec as P

HEADS = 8
HEAD_DIM = 128
BLOCK = 64
LATER = -1000000000.0
SELF = -100000.0


def from_behind(block, axis, distance):
    devices = range(lax.axis_size(axis))
    route = [((i - distance) % len(devices), i) for i in devices]
    return lax.ppermute(block, axis, route)


def layer_norm(value_vectors, scaling, shifts):
    center = jnp.mean(value_vectors, axis=-1, keepdims=True)
    offset = value_vectors - center
    spread = jnp.mean(offset * offset, axis=-1, keepdims=True)
    return offset * lax.rsqrt(spread + 1e-05) * scaling + shifts


def gelu_exact(value_vectors):
    return jax.nn.gelu(value_vectors, approximate=False)


def combine_rounds(outputs, totals):
    highest = jnp.max(totals, axis=0, keepdims=True)
    weights = jnp.exp(totals - highest)
    weights = weights / jnp.sum(weights, axis=0, keepdims=True)
    by_head = outputs.reshape(outputs.shape[:-1] + (totals.shape[-1], -1))
    return jnp.sum(weights[..., None] * by_head, axis=0).reshape(outputs.shape[1:])


def home_slots(places, row_count):
    target = places // row_count
    prior_state = (target[:, None, :] == target[:, :, None]) & (
        places[:, None, :] < places[:, :, None]
    )
    return (target, jnp.sum(prior_state.astype(jnp.int32), axis=2))


def sorted_slots(orders, row_count):
    source = orders // row_count
    ladder = jnp.arange(row_count, dtype=jnp.int32)
    prior_state = (source[:, None, :] == source[:, :, None]) & (
        ladder[None, None, :] < ladder[None, :, None]
    )
    return (source, jnp.sum(prior_state.astype(jnp.int32), axis=2))


def slot_lookup(owners, slot_index, devices, capacity):
    groups, row_count = owners.shape
    flat_index = owners * capacity + slot_index
    lookup = jnp.full((groups, devices * capacity), row_count, jnp.int32)
    filler = jnp.broadcast_to(jnp.arange(row_count, dtype=jnp.int32), (groups, row_count))
    lookup = lookup.at[jnp.arange(groups)[:, None], flat_index].set(filler)
    return jnp.transpose(lookup.reshape(groups, devices, capacity), (1, 0, 2))


def gather_slots(value_vectors, member, lookup):
    padding = jnp.zeros((value_vectors.shape[0], 1) + value_vectors.shape[2:], value_vectors.dtype)
    padded = jnp.concatenate([value_vectors, padding], axis=1)
    return padded[member[None, :, None], lookup]


def settle(received, owners, slot_index):
    return received[owners, jnp.arange(owners.shape[0])[:, None], slot_index]


def build_routes(orders, places, devices, capacity):
    rounds, sequences, row_count = orders.shape
    order_flat = orders.reshape(rounds * sequences, row_count)
    target, home_slot = home_slots(places.reshape(rounds * sequences, row_count), row_count)
    source, sorted_slot = sorted_slots(order_flat, row_count)
    home_lookup = slot_lookup(target, home_slot, devices, capacity)
    back_lookup = slot_lookup(source, sorted_slot, devices, capacity)
    return (target, home_slot, source, sorted_slot, home_lookup, back_lookup, order_flat)


def trade_rows(first_part, second_part):
    return (
        lax.all_to_all(first_part, ("seq", "sub"), split_axis=0, concat_axis=0, tiled=True),
        lax.all_to_all(second_part, ("seq", "sub"), split_axis=0, concat_axis=0, tiled=True),
    )


def trade_results(first_part, second_part):
    return (
        lax.all_to_all(first_part, ("seq", "sub"), split_axis=0, concat_axis=0, tiled=True),
        lax.all_to_all(second_part, ("seq", "sub"), split_axis=0, concat_axis=0, tiled=True),
    )


def window(rows_here, rows_left):
    groups = rows_here.shape[0]
    extended = jnp.concatenate([rows_left, rows_here], axis=1)
    extended = extended.reshape((groups, -1, BLOCK) + rows_here.shape[2:])
    return jnp.concatenate([extended[:, :-1], extended[:, 1:]], axis=2)


def score_parts(shared_rows, order_rows, halo_shared, halo_order):
    groups, row_count, features = shared_rows.shape
    blocks = row_count // BLOCK
    queries = shared_rows.reshape(groups, blocks, BLOCK, HEADS, HEAD_DIM)
    key_rows = window(shared_rows, halo_shared).reshape(groups, blocks, 2 * BLOCK, HEADS, HEAD_DIM)
    key_float = key_rows.astype(jnp.float32)
    mean_square = jnp.mean(key_float * key_float, axis=-1) + 1e-06
    key_scale = lax.rsqrt(mean_square) / HEAD_DIM
    raw_scores = jnp.einsum(
        "gcqhd,gckhd->gchqk", queries, key_rows, preferred_element_type=jnp.float32
    )
    query_pos = order_rows.reshape(groups, blocks, BLOCK)
    key_pos = window(order_rows, halo_order)
    is_later = (key_pos[:, :, None, :] > query_pos[:, :, :, None])[:, :, None]
    is_self = (key_pos[:, :, None, :] == query_pos[:, :, :, None])[:, :, None]
    scale_row = jnp.transpose(key_scale, (0, 1, 3, 2))[:, :, :, None, :]
    scores = jnp.where(
        is_later, -1000000000.0, jnp.where(is_self, -100000.0, raw_scores * scale_row)
    )
    highest = jnp.max(scores, axis=-1, keepdims=True)
    log_total = highest + jnp.log(jnp.sum(jnp.exp(scores - highest), axis=-1, keepdims=True))
    probability = jnp.exp(scores - log_total)
    return (
        queries,
        key_rows,
        key_float,
        mean_square,
        key_scale,
        scale_row,
        raw_scores,
        is_later | is_self,
        log_total,
        probability,
    )


def attend(shared_rows, value_rows, order_rows, halo):
    halo_shared, halo_value, halo_order = halo
    parts = score_parts(shared_rows, order_rows, halo_shared, halo_order)
    groups, row_count, features = shared_rows.shape
    value_keys = window(value_rows, halo_value).reshape(
        groups, row_count // BLOCK, 2 * BLOCK, HEADS, HEAD_DIM
    )
    mixed = jnp.einsum(
        "gchqk,gckhd->gcqhd",
        parts[9].astype(jnp.bfloat16),
        value_keys,
        preferred_element_type=jnp.float32,
    )
    log_total = jnp.transpose(parts[8][..., 0], (0, 1, 3, 2)).reshape(groups, row_count, HEADS)
    return (mixed.reshape(groups, row_count, features), log_total)


def fold_window(grads_window, groups, row_count, features):
    grads_window = grads_window.reshape(groups, row_count // BLOCK, 2 * BLOCK, features)
    empty = jnp.zeros((groups, 1, BLOCK, features), jnp.float32)
    extended = jnp.concatenate([grads_window[:, :, :BLOCK], empty], axis=1) + jnp.concatenate(
        [empty, grads_window[:, :, BLOCK:]], axis=1
    )
    return (extended[:, 1:].reshape(groups, row_count, features), extended[:, 0])


def attend_back(shared_rows, value_rows, order_rows, halo, grad_out, grad_total):
    halo_shared, halo_value, halo_order = halo
    (
        queries,
        key_rows,
        key_float,
        mean_square,
        key_scale,
        scale_row,
        raw_scores,
        masked,
        log_total,
        probability,
    ) = score_parts(shared_rows, order_rows, halo_shared, halo_order)
    groups, row_count, features = shared_rows.shape
    blocks = row_count // BLOCK
    value_keys = window(value_rows, halo_value).reshape(groups, blocks, 2 * BLOCK, HEADS, HEAD_DIM)
    prob_low = probability.astype(jnp.bfloat16)
    grad_heads = grad_out.reshape(groups, blocks, BLOCK, HEADS, HEAD_DIM)
    grad_log = jnp.transpose(
        grad_total.astype(jnp.float32).reshape(groups, blocks, BLOCK, HEADS), (0, 1, 3, 2)
    )[..., None]
    grad_prob = jnp.einsum(
        "gcqhd,gckhd->gchqk", grad_heads, value_keys, preferred_element_type=jnp.float32
    )
    inner = jnp.sum(probability * grad_prob, axis=-1, keepdims=True)
    grad_score = jnp.where(masked, 0.0, probability * (grad_prob - inner + grad_log))
    grad_scale = jnp.transpose(jnp.sum(grad_score * raw_scores, axis=3), (0, 1, 3, 2))
    grad_raw = (grad_score * scale_row).astype(jnp.bfloat16)
    grad_query = jnp.einsum(
        "gchqk,gckhd->gcqhd", grad_raw, key_rows, preferred_element_type=jnp.float32
    )
    grad_key = jnp.einsum(
        "gchqk,gcqhd->gckhd", grad_raw, queries, preferred_element_type=jnp.float32
    )
    grad_key = grad_key - (grad_scale * key_scale / mean_square)[..., None] * key_float / HEAD_DIM
    grad_value = jnp.einsum(
        "gchqk,gcqhd->gckhd", prob_low, grad_heads, preferred_element_type=jnp.float32
    )
    key_home, key_left = fold_window(grad_key, groups, row_count, features)
    value_home, value_left = fold_window(grad_value, groups, row_count, features)
    back_key, back_value = from_behind((key_left, value_left), ("seq", "sub"), -1)
    grad_shared = grad_query.reshape(groups, row_count, features) + key_home
    grad_shared = grad_shared.at[:, row_count - BLOCK :].add(back_key)
    grad_values = value_home.at[:, row_count - BLOCK :].add(back_value)
    return (grad_shared, grad_values)


def sorted_attention(shared_query_key, value_vectors, routes):
    target, home_slot, source, sorted_slot, home_lookup, back_lookup, order_flat = routes
    groups = target.shape[0]
    member = jnp.arange(groups) % shared_query_key.shape[0]
    got_shared, got_values = trade_rows(
        gather_slots(shared_query_key, member, home_lookup),
        gather_slots(value_vectors, member, home_lookup),
    )
    shared_rows = settle(got_shared, source, sorted_slot)
    value_rows = settle(got_values, source, sorted_slot)
    halo = from_behind(
        (shared_rows[:, -BLOCK:], value_rows[:, -BLOCK:], order_flat[:, -BLOCK:]), ("seq", "sub"), 1
    )
    mixed, log_total = attend(shared_rows, value_rows, order_flat, halo)
    all_groups = jnp.arange(groups)
    got_mixed, got_total = trade_results(
        gather_slots(mixed, all_groups, back_lookup),
        gather_slots(log_total, all_groups, back_lookup),
    )
    return (
        settle(got_mixed, target, home_slot),
        settle(got_total, target, home_slot),
        (shared_rows, value_rows, halo),
    )


def round_outputs(normalized_input, query_key_weight, value_projection_weight, routes, rounds):
    shared_query_key = jnp.einsum(
        "srd,de->sre", normalized_input, query_key_weight, preferred_element_type=jnp.float32
    ).astype(jnp.bfloat16)
    value_vectors = jnp.einsum(
        "srd,de->sre", normalized_input, value_projection_weight, preferred_element_type=jnp.float32
    ).astype(jnp.bfloat16)
    mixed, log_total, kept = sorted_attention(shared_query_key, value_vectors, routes)
    sequences, row_count, features = normalized_input.shape
    outputs = mixed.reshape(rounds, sequences, row_count, features)
    totals = log_total.reshape(rounds, sequences, row_count, HEADS)
    return (shared_query_key, value_vectors, outputs, totals, kept)


def collect(weight_stack, layer_index):
    (
        attend_gain,
        attend_shift,
        query_key_weight,
        value_projection_weight,
        output_projection_weight,
        feed_gain,
        feed_shift,
        upper_projection_weight,
        upper_projection_bias,
        lower_projection_weight,
        lower_projection_bias,
    ) = tuple((shard_piece[layer_index] for shard_piece in weight_stack))
    return (
        lax.all_gather(attend_gain, ("seq", "sub"), axis=0, tiled=True),
        lax.all_gather(attend_shift, ("seq", "sub"), axis=0, tiled=True),
        lax.all_gather(query_key_weight, ("seq", "sub"), axis=0, tiled=True),
        lax.all_gather(value_projection_weight, ("seq", "sub"), axis=0, tiled=True),
        lax.all_gather(output_projection_weight, ("seq", "sub"), axis=0, tiled=True),
        lax.all_gather(feed_gain, ("seq", "sub"), axis=0, tiled=True),
        lax.all_gather(feed_shift, ("seq", "sub"), axis=0, tiled=True),
        lax.all_gather(upper_projection_weight, ("seq", "sub"), axis=0, tiled=True),
        lax.all_gather(upper_projection_bias, ("seq", "sub"), axis=0, tiled=True),
        lax.all_gather(lower_projection_weight, ("seq", "sub"), axis=0, tiled=True),
        lax.all_gather(lower_projection_bias, ("seq", "sub"), axis=0, tiled=True),
    )


def spread_grads(level_grads):
    (
        attend_gain,
        attend_shift,
        query_key_weight,
        value_projection_weight,
        output_projection_weight,
        feed_gain,
        feed_shift,
        upper_projection_weight,
        upper_projection_bias,
        lower_projection_weight,
        lower_projection_bias,
    ) = level_grads
    return (
        lax.psum_scatter(attend_gain, ("seq", "sub"), scatter_dimension=0, tiled=True),
        lax.psum_scatter(attend_shift, ("seq", "sub"), scatter_dimension=0, tiled=True),
        lax.psum_scatter(query_key_weight.astype(jnp.bfloat16), ("seq", "sub"), scatter_dimension=0, tiled=True),
        lax.psum_scatter(value_projection_weight.astype(jnp.bfloat16), ("seq", "sub"), scatter_dimension=0, tiled=True),
        lax.psum_scatter(output_projection_weight.astype(jnp.bfloat16), ("seq", "sub"), scatter_dimension=0, tiled=True),
        lax.psum_scatter(feed_gain, ("seq", "sub"), scatter_dimension=0, tiled=True),
        lax.psum_scatter(feed_shift, ("seq", "sub"), scatter_dimension=0, tiled=True),
        lax.psum_scatter(upper_projection_weight.astype(jnp.bfloat16), ("seq", "sub"), scatter_dimension=0, tiled=True),
        lax.psum_scatter(upper_projection_bias, ("seq", "sub"), scatter_dimension=0, tiled=True),
        lax.psum_scatter(lower_projection_weight.astype(jnp.bfloat16), ("seq", "sub"), scatter_dimension=0, tiled=True),
        lax.psum_scatter(lower_projection_bias, ("seq", "sub"), scatter_dimension=0, tiled=True),
    )


def layer_pass(first_half, second_half, grad_one, grad_two, params, routes, rounds):
    (
        attend_gain,
        attend_shift,
        query_key_weight,
        value_projection_weight,
        output_projection_weight,
        feed_gain,
        feed_shift,
        upper_projection_weight,
        upper_projection_bias,
        lower_projection_weight,
        lower_projection_bias,
    ) = params
    attend_norm, attend_pull = jax.vjp(
        layer_norm, second_half, attend_gain.astype(jnp.float32), attend_shift.astype(jnp.float32)
    )
    normalized_input = attend_norm.astype(jnp.bfloat16)
    shared_query_key, value_vectors, outputs, totals, kept = round_outputs(
        normalized_input, query_key_weight, value_projection_weight, routes, rounds
    )
    attention_result, combine_pull = jax.vjp(combine_rounds, outputs, totals)
    attended_low = attention_result.astype(jnp.bfloat16)
    top_one = first_half + jnp.einsum(
        "srd,de->sre", attended_low, output_projection_weight, preferred_element_type=jnp.float32
    )
    feed_norm, feed_pull = jax.vjp(
        layer_norm, top_one, feed_gain.astype(jnp.float32), feed_shift.astype(jnp.float32)
    )
    feed_forward_input = feed_norm.astype(jnp.bfloat16)
    prior_state = jnp.einsum(
        "srd,df->srf",
        feed_forward_input,
        upper_projection_weight,
        preferred_element_type=jnp.float32,
    ) + upper_projection_bias.astype(jnp.float32)
    hidden_activation, active_pull = jax.vjp(gelu_exact, prior_state)
    active_low = hidden_activation.astype(jnp.bfloat16)
    feed_out = jnp.einsum(
        "srf,fd->srd", active_low, lower_projection_weight, preferred_element_type=jnp.float32
    ) + lower_projection_bias.astype(jnp.float32)
    top_two = second_half + feed_out
    feed_grad = grad_two.astype(jnp.bfloat16)
    down_weight_grad = jnp.einsum(
        "srf,srd->fd", active_low, feed_grad, preferred_element_type=jnp.float32
    )
    down_bias_grad = jnp.sum(feed_grad.astype(jnp.float32), axis=(0, 1))
    active_grad = jnp.einsum(
        "srd,fd->srf", feed_grad, lower_projection_weight, preferred_element_type=jnp.float32
    )
    before_grad = active_pull(active_grad)[0].astype(jnp.bfloat16)
    up_weight_grad = jnp.einsum(
        "srd,srf->df", feed_forward_input, before_grad, preferred_element_type=jnp.float32
    )
    up_bias_grad = jnp.sum(before_grad.astype(jnp.float32), axis=(0, 1))
    norm_grad = jnp.einsum(
        "srf,df->srd", before_grad, upper_projection_weight, preferred_element_type=jnp.float32
    )
    one_part, feed_gain_grad, feed_shift_grad = feed_pull(norm_grad)
    total_one = grad_one + one_part
    out_grad = total_one.astype(jnp.bfloat16)
    output_weight_grad = jnp.einsum(
        "srd,sre->de", attended_low, out_grad, preferred_element_type=jnp.float32
    )
    attended_grad = jnp.einsum(
        "sre,de->srd", out_grad, output_projection_weight, preferred_element_type=jnp.float32
    )
    outputs_grad, totals_grad = combine_pull(attended_grad)
    target, home_slot, source, sorted_slot, home_lookup, back_lookup, order_flat = routes
    sequences, row_count, features = top_one.shape
    groups = rounds * sequences
    all_groups = jnp.arange(groups)
    outputs_low = outputs_grad.astype(jnp.bfloat16).reshape(groups, row_count, features)
    totals_low = totals_grad.astype(jnp.bfloat16).reshape(groups, row_count, HEADS)
    got_out, got_total = trade_rows(
        gather_slots(outputs_low, all_groups, home_lookup),
        gather_slots(totals_low, all_groups, home_lookup),
    )
    shared_rows, value_rows, halo = kept
    grad_shared, grad_values = attend_back(
        shared_rows,
        value_rows,
        order_flat,
        halo,
        settle(got_out, source, sorted_slot),
        settle(got_total, source, sorted_slot),
    )
    home_shared, home_values = trade_rows(
        gather_slots(grad_shared.astype(jnp.bfloat16), all_groups, back_lookup),
        gather_slots(grad_values.astype(jnp.bfloat16), all_groups, back_lookup),
    )
    shared_grad = jnp.sum(
        settle(home_shared, target, home_slot)
        .astype(jnp.float32)
        .reshape(rounds, sequences, row_count, features),
        axis=0,
    ).astype(jnp.bfloat16)
    values_grad = jnp.sum(
        settle(home_values, target, home_slot)
        .astype(jnp.float32)
        .reshape(rounds, sequences, row_count, features),
        axis=0,
    ).astype(jnp.bfloat16)
    shared_weight_grad = jnp.einsum(
        "srd,sre->de", normalized_input, shared_grad, preferred_element_type=jnp.float32
    )
    value_weight_grad = jnp.einsum(
        "srd,sre->de", normalized_input, values_grad, preferred_element_type=jnp.float32
    )
    normed_grad = jnp.einsum(
        "sre,de->srd", shared_grad, query_key_weight, preferred_element_type=jnp.float32
    ) + jnp.einsum(
        "sre,de->srd", values_grad, value_projection_weight, preferred_element_type=jnp.float32
    )
    two_part, attend_gain_grad, attend_shift_grad = attend_pull(normed_grad)
    total_two = grad_two + two_part
    level_grads = (
        attend_gain_grad,
        attend_shift_grad,
        shared_weight_grad,
        value_weight_grad,
        output_weight_grad,
        feed_gain_grad,
        feed_shift_grad,
        up_weight_grad,
        up_bias_grad,
        down_weight_grad,
        down_bias_grad,
    )
    return (top_one, top_two, total_one, total_two, level_grads)


def general_plan(
    first_half,
    second_half,
    grad_first,
    grad_second,
    attend_gain,
    attend_shift,
    query_key_weight,
    value_projection_weight,
    output_projection_weight,
    feed_gain,
    feed_shift,
    upper_projection_weight,
    upper_projection_bias,
    lower_projection_weight,
    lower_projection_bias,
    sort_order,
    sort_place,
):
    weight_stack = (
        attend_gain,
        attend_shift,
        query_key_weight,
        value_projection_weight,
        output_projection_weight,
        feed_gain,
        feed_shift,
        upper_projection_weight,
        upper_projection_bias,
        lower_projection_weight,
        lower_projection_bias,
    )
    devices = lax.axis_size(("seq", "sub"))
    rounds = sort_order.shape[1]
    row_count = first_half.shape[1]
    capacity = 2 * max(1, row_count // devices)
    params = collect(weight_stack, 0)
    routes = build_routes(sort_order[0], sort_place[0], devices, capacity)
    first_out, second_out, first_grad, second_grad, level_grads = layer_pass(
        first_half, second_half, grad_first, grad_second, params, routes, rounds
    )
    stacked = tuple((entry[None].astype(jnp.float32) for entry in spread_grads(level_grads)))
    return (first_out, second_out, first_grad, second_grad) + stacked


class Links:
    def __init__(self, planes, send, receive, local):
        self.send, self.receive, self.local = send, receive, local
        self.used, self.used_local = 0, 0
        self.planes = planes
        seq, sub = lax.axis_index("seq"), lax.axis_index("sub")
        self.z, self.x = seq // 2, lax.rem(seq, 2)
        self.y, self.core = sub // 2, lax.rem(sub, 2)
        self.p = self.x * 4 + sub

    def near(self, step):
        x = 1 - self.x if step & 4 else self.x
        y = 1 - self.y if step & 2 else self.y
        core = 1 - self.core if step & 1 else self.core
        return (self.z * 2 + x, y * 2 + core), x * 4 + y * 2 + core

    def along(self, step):
        to = lax.rem(self.z + step, self.planes)
        back = lax.rem(self.z + self.planes - step, self.planes)
        return (to * 2 + self.x, self.y * 2 + self.core), to, back

    def greet(self):
        barrier = pltpu.get_barrier_semaphore()
        targets = [self.near(step)[0] for step in range(1, 8)]
        targets += [self.along(step)[0] for step in range(1, self.planes)]
        for target in targets:
            pl.semaphore_signal(barrier, inc=1, device_id=target, device_id_type=pl.DeviceIdType.MESH)
        self.greeted = len(targets)

    def meet(self):
        pl.semaphore_wait(pltpu.get_barrier_semaphore(), self.greeted)

    def push(self, source, target, device):
        copy = pltpu.make_async_remote_copy(
            src_ref=source,
            dst_ref=target,
            send_sem=self.send.at[self.used],
            recv_sem=self.receive.at[self.used],
            device_id=device,
            device_id_type=pl.DeviceIdType.MESH,
        )
        self.used += 1
        copy.start()
        return copy

    def keep(self, source, target):
        copy = pltpu.make_async_copy(source, target, self.local.at[self.used_local])
        self.used_local += 1
        copy.start()
        return copy


class Chain:
    def __init__(self, links, ref):
        self.links, self.ref, self.first, self.sent = links, ref, links.used, []
        links.used += 5
        self.hand_on(links.z, links.z < 3, links.z > 0, 2)

    def hand_on(self, shard, rightward, leftward, ways):
        links = self.links
        steps = ((1, rightward), (-1, leftward)) if ways == 2 else ((None, rightward | leftward),)
        for step, wanted in steps:
            if step is None:
                step = jnp.where(rightward, 1, -1)
            to = jnp.clip(links.z + step, 0, 3)
            middle = jnp.where(to == 1, jnp.where(shard == 0, 0, shard - 1), jnp.where(shard == 3, 0, 2 - shard))
            arrival = jnp.where((to == 0) | (to == 3), jnp.abs(to - shard) - 1, middle)
            arrival = jnp.clip(arrival, 0, 2)
            copy = pltpu.make_async_remote_copy(
                src_ref=self.ref.at[shard],
                dst_ref=self.ref.at[shard],
                send_sem=links.send.at[self.first + len(self.sent)],
                recv_sem=links.receive.at[self.first + arrival],
                device_id=(to * 2 + links.x, links.y * 2 + links.core),
                device_id_type=pl.DeviceIdType.MESH,
            )
            self.sent.append((wanted, copy))
            pl.when(wanted)(copy.start)

    def arrive(self, index):
        links, z = self.links, self.links.z
        ends = jnp.where(z == 0, index + 1, 2 - index)
        inner = jnp.where(z == 1, (0, 2, 3)[index], (3, 1, 0)[index])
        shard = jnp.where((z == 0) | (z == 3), ends, inner)
        pltpu.make_async_remote_copy(
            src_ref=self.ref.at[shard],
            dst_ref=self.ref.at[shard],
            send_sem=links.send.at[self.first],
            recv_sem=links.receive.at[self.first + index],
            device_id=(z * 2 + links.x, links.y * 2 + links.core),
            device_id_type=pl.DeviceIdType.MESH,
        ).wait_recv()
        self.hand_on(shard, (shard < z) & (z < 3), (shard > z) & (z > 0), 1)
        return shard

    def finish(self):
        for wanted, copy in self.sent:
            pl.when(wanted)(copy.wait_send)


COPIES = 160


def link_scratch():
    return [
        pltpu.SemaphoreType.DMA((COPIES,)),
        pltpu.SemaphoreType.DMA((COPIES,)),
        pltpu.SemaphoreType.DMA((48,)),
    ]


def along_z(source, target):
    def transfer(links, here, there):
        own = links.keep(source(here, links.z), target(there, links.z))
        copies = []
        for step in range(1, links.planes):
            device, to, _ = links.along(step)
            copies.append(links.push(source(here, to), target(there, links.z), device))
        yield
        own.wait()
        for copy in copies:
            copy.wait()

    return transfer


def over_plane(source, target):
    def transfer(links, here, there):
        own = links.keep(source(here, links.p), target(there, links.p))
        copies = []
        for step in (6, 7, 4, 5, 2, 3, 1):
            device, to = links.near(step)
            copies.append(links.push(source(here, to), target(there, links.p), device))
        yield
        own.wait()
        for copy in copies:
            copy.wait()

    return transfer


def over_chips(source, target):
    def transfer(links, here, there):
        own = links.keep(source(here, links.p), target(there, links.p))
        copies = []
        for step in (6, 4, 2):
            device, to = links.near(step)
            copies.append(links.push(source(here, to), target(there, links.p), device))
        sibling, _ = links.near(1)
        passed = [links.push(source(here, links.p), target(there, links.p), sibling)]
        yield
        for step, copy in zip((6, 4, 2), copies):
            copy.wait_recv()
            _, sender = links.near(step)
            passed.append(links.push(target(there, sender), target(there, sender), sibling))
        yield
        own.wait()
        for copy in copies:
            copy.wait_send()
        for copy in passed:
            copy.wait()

    return transfer


def everywhere(links, here, there):
    own = links.keep(here, there.at[links.z, links.p])
    copies = []
    for step in (6, 7, 4, 5, 2, 3, 1):
        copies.append(links.push(here, there.at[links.z, links.p], links.near(step)[0]))
    yield
    own.wait()
    for copy in copies:
        copy.wait()
    copies = []
    for step in range(1, links.planes):
        copies.append(links.push(there.at[links.z], there.at[links.z], links.along(step)[0]))
    yield
    for copy in copies:
        copy.wait()


def drive(transfers):
    while transfers:
        left = []
        for transfer in transfers:
            try:
                next(transfer)
                left.append(transfer)
            except StopIteration:
                pass
        transfers = left


def whole(ref, index):
    return ref


def block(ref, index):
    return ref.at[index]


def second(ref, index):
    return ref.at[:, index]


def rows_of(index):
    return pl.ds(pl.multiple_of(index * 128, 128), 128)


def pick_tile(table, index_ref, tile, part):
    return jnp.concatenate(
        [table[pl.ds(index_ref[tile, part * 32 + row], 1), :] for row in range(32)], axis=0
    )


def sort_tile(order, table, first, second, offset, tile):
    for part in range(4):
        start = pl.multiple_of(tile * 128 + part * 32 + offset, 32)
        picked = pick_tile(table, order, tile, part)
        first[pl.ds(start, 32), :] = picked[:, :128].astype(first.dtype)
        second[pl.ds(start, 32), :] = picked[:, 128:].astype(second.dtype)


def across(column):
    return jnp.broadcast_to(column, (128, 128)).T[:1, :]


def down(row):
    return jnp.broadcast_to(row, (128, 128)).T


def dot(a, b, contract):
    return lax.dot_general(a, b, (contract, ((), ())), preferred_element_type=jnp.float32)


def key_scales(keys):
    rows = keys.astype(jnp.float32)
    mean_square = jnp.mean(rows * rows, axis=-1, keepdims=True) + 1e-06
    return rows, mean_square, lax.rsqrt(mean_square) / HEAD_DIM


def half_turned(row):
    return jnp.concatenate([row[:, 64:], row[:, :64]], axis=1)


def windows(before, here):
    return [jnp.concatenate([before[:, 64:], here[:, :64]], axis=1), here]


def masked_scores(raw, scale, query_pos, key_pos):
    return jnp.where(
        key_pos > query_pos, LATER, jnp.where(key_pos == query_pos, SELF, raw * scale)
    )


def attend_tiles(tiles, unroll, order, order_rows, table, shared, values, mixed, total_sorted, last_scale):
    sort = functools.partial(sort_tile, order, table, shared, values, BLOCK)
    end = tiles * 128
    for tile in [tiles - 1] + list(range(unroll)):
        sort(tile)
    shared[:BLOCK, :] = shared[end : end + BLOCK, :]
    values[:BLOCK, :] = values[end : end + BLOCK, :]
    last_scale[...] = across(key_scales(shared[end - BLOCK : end + BLOCK, :])[2])

    def step_tiles(step, carry):
        first = step * unroll
        numbers = [lax.rem(first + tiles - 1, tiles)] + [first + k for k in range(unroll)]
        places = [order_rows[pl.ds(t, 1), :] for t in numbers]
        scale = [last_scale[...]]
        work = []
        for k in range(unroll):
            start = pl.multiple_of((first + k) * 128, 128)
            keys = [shared[pl.ds(pl.multiple_of(start + half * 64, 64), 128), :] for half in range(2)]
            vals = [values[pl.ds(pl.multiple_of(start + half * 64, 64), 128), :] for half in range(2)]
            own = jnp.concatenate([keys[0][64:], keys[1][64:]], axis=0)
            scale.append(across(key_scales(own)[2]))
            work.append((keys, vals))
        last_scale[...] = scale[-1]
        for k in range(unroll):
            sort(lax.rem(first + unroll + k, tiles))
        query_pos = jnp.concatenate([down(place) for place in places[1:]], axis=0)
        key_pos, key_scale = [], []
        for k in range(unroll):
            key_pos += windows(places[k], places[k + 1])
            key_scale += windows(scale[k], scale[k + 1])
        raw = [dot(k[64:], k, ((1,), (1,))) for keys, _ in work for k in keys]
        raw, key_pos, key_scale = (
            jnp.concatenate([jnp.broadcast_to(a, (64, 128)) for a in parts], axis=0)
            for parts in (raw, key_pos, key_scale)
        )
        scores = masked_scores(raw, key_scale, query_pos, key_pos)
        highest = jnp.max(scores, axis=-1, keepdims=True)
        total = highest + jnp.log(jnp.sum(jnp.exp(scores - highest), axis=-1, keepdims=True))
        prob = jnp.exp(scores - total).astype(jnp.bfloat16)
        rows = pl.ds(pl.multiple_of(first * 128, 128), unroll * 128)
        total = jnp.broadcast_to(total, (unroll * 128, 128))
        mixed[rows, 128:] = total
        total_sorted[rows, :] = total
        vals = [v for _, vals in work for v in vals]
        mixed[rows, :128] = jnp.concatenate(
            [dot(prob[64 * i : 64 * i + 64], v, ((1,), (0,))) for i, v in enumerate(vals)], axis=0
        )
        return carry

    lax.fori_loop(0, tiles // unroll, step_tiles, 0)


def attend_back_tiles(
    tiles, unroll, order, order_rows, table, shared, values, total_sorted,
    grad_sorted, grad_total_sorted, sums, scale_sums, last_scale,
):
    sort = functools.partial(sort_tile, order, table, grad_sorted, grad_total_sorted, 0)
    end = tiles * 128
    for tile in range(unroll):
        sort(tile)
    last_scale[...] = across(key_scales(shared[end - BLOCK : end + BLOCK, :])[2])
    scale_sums[...] = jnp.zeros_like(scale_sums)
    sums[end : end + 128, :] = jnp.zeros((128, 256), jnp.float32)
    early = lax.broadcasted_iota(jnp.int32, (1, 128), 1) < 64

    def step_tiles(step, carry):
        first = step * unroll
        numbers = [lax.rem(first + tiles - 1, tiles)] + [first + k for k in range(unroll)]
        places = [order_rows[pl.ds(t, 1), :] for t in numbers]
        scale = [last_scale[...]]
        work = []
        for k in range(unroll):
            start = pl.multiple_of((first + k) * 128, 128)
            keys = [shared[pl.ds(pl.multiple_of(start + half * 64, 64), 128), :] for half in range(2)]
            vals = [values[pl.ds(pl.multiple_of(start + half * 64, 64), 128), :] for half in range(2)]
            own = jnp.concatenate([keys[0][64:], keys[1][64:]], axis=0)
            scale.append(across(key_scales(own)[2]))
            tile = pl.ds(start, 128)
            work.append(
                (keys, vals, grad_sorted[tile, :], grad_total_sorted[tile, :], total_sorted[tile, :])
            )
        last_scale[...] = scale[-1]
        for k in range(unroll):
            sort(lax.rem(first + unroll + k, tiles))
        blocks = 2 * unroll
        scale_parts = [0.0] * (unroll + 1)
        query_pos = jnp.concatenate([down(place) for place in places[1:]], axis=0)
        key_pos, key_scale = [], []
        for k in range(unroll):
            key_pos += windows(places[k], places[k + 1])
            key_scale += windows(scale[k], scale[k + 1])
        keys = [k for item in work for k in item[0]]
        vals = [v for item in work for v in item[1]]
        grads, grad_totals, totals = (
            jnp.concatenate([item[n] for item in work], axis=0) for n in (2, 3, 4)
        )
        own = [slice(64 * i, 64 * i + 64) for i in range(blocks)]
        raw = [dot(k[64:], k, ((1,), (1,))) for k in keys]
        grad_prob = [dot(grads[own[i]], v, ((1,), (1,))) for i, v in enumerate(vals)]
        raw, grad_prob, key_pos, key_scale = (
            jnp.concatenate([jnp.broadcast_to(a, (64, 128)) for a in parts], axis=0)
            for parts in (raw, grad_prob, key_pos, key_scale)
        )
        prob = jnp.exp(masked_scores(raw, key_scale, query_pos, key_pos) - totals)
        inner = jnp.sum(prob * grad_prob, axis=-1, keepdims=True)
        grad_score = jnp.where(
            key_pos < query_pos, prob * (grad_prob + (grad_totals - inner)), 0.0
        )
        product = grad_score * raw
        for index in range(blocks):
            k, half = index // 2, index % 2
            part = jnp.sum(product[own[index]], axis=0, keepdims=True)
            if half == 0:
                turned = half_turned(part)
                scale_parts[k] += jnp.where(early, 0.0, turned)
                scale_parts[k + 1] += jnp.where(early, turned, 0.0)
            else:
                scale_parts[k + 1] += part
        grad_raw = (grad_score * key_scale).astype(jnp.bfloat16)
        prob = prob.astype(jnp.bfloat16)
        key_parts = [dot(grad_raw[own[i]], keys[i][64:], ((0,), (0,))) for i in range(blocks)]
        value_parts = [dot(prob[own[i]], grads[own[i]], ((0,), (0,))) for i in range(blocks)]
        query_parts = [dot(grad_raw[own[i]], keys[i], ((1,), (0,))) for i in range(blocks)]
        key_sums = [key_parts[0][:64]] + [
            key_parts[i][64:] + query_parts[i] + (key_parts[i + 1][:64] if i + 1 < blocks else 0.0)
            for i in range(blocks)
        ]
        value_sums = [value_parts[0][:64]] + [
            value_parts[i][64:] + (value_parts[i + 1][:64] if i + 1 < blocks else 0.0)
            for i in range(blocks)
        ]
        for index in range(blocks):
            rows = pl.ds(pl.multiple_of(first * 128 + index * 64, 64), 64)
            sums[rows, :128] = key_sums[index + 1]
            sums[rows, 128:] = value_sums[index + 1]
        for k in range(unroll):
            scale_sums[pl.ds(first + k, 1), :] = scale_parts[k + 1]
        before = jnp.where(step == 0, tiles, numbers[0])
        rows = pl.ds(pl.multiple_of(before * 128 + 64, 64), 64)
        sums[rows, :128] += key_sums[0]
        sums[rows, 128:] += value_sums[0]
        scale_sums[pl.ds(before, 1), :] += scale_parts[0]
        return carry

    lax.fori_loop(0, tiles // unroll, step_tiles, 0)
    sums[end - 128 : end, :] += sums[end : end + 128, :]
    scale_sums[pl.ds(tiles - 1, 1), :] += scale_sums[pl.ds(tiles, 1), :]

    def finish(step, carry):
        for part in range(2):
            tile = step * 2 + part
            rows = rows_of(tile)
            start = pl.multiple_of(tile * 128 + 64, 64)
            keys, mean_square, scale = key_scales(shared[pl.ds(start, 128), :])
            factor = down(scale_sums[pl.ds(tile, 1), :]) * (scale / (mean_square * HEAD_DIM))
            sums[rows, :128] -= factor * keys
        return carry

    lax.fori_loop(0, tiles // 2, finish, 0)


VMEM = pl.BlockSpec(memory_space=pltpu.VMEM)
ANY = pl.BlockSpec(memory_space=pl.ANY)


def normal_parts(rows):
    center = jnp.mean(rows, axis=-1, keepdims=True)
    offset = rows - center
    spread = jnp.mean(offset * offset, axis=-1, keepdims=True)
    inverse = lax.rsqrt(spread + 1e-05)
    return offset * inverse, inverse


def norm_back(grad, rows, gain):
    unit, inverse = normal_parts(rows)
    scaled = grad * gain
    shared = jnp.mean(scaled, axis=-1, keepdims=True)
    along = jnp.mean(scaled * unit, axis=-1, keepdims=True)
    return (
        (scaled - shared - unit * along) * inverse,
        jnp.sum(grad * unit, axis=0, keepdims=True),
        jnp.sum(grad, axis=0, keepdims=True),
    )


def gelu_parts(rows):
    below = 0.5 * (1.0 + lax.erf(rows * 0.7071067811865476))
    bell = jnp.exp(-0.5 * rows * rows) * 0.3989422804014327
    return rows * below, below + rows * bell


def feed_kernel(
    planes,
    mixed, total, x1, wo_in, gains, wup_in, bias_up, wdown_in, df_in, g1,
    y1_out, g1_out, dout_out, attended_out, dmixed_home, dtotal_home, y2_out, up_grad_out, down_grad_out,
    up_bias_out, gain_out, shift_out,
    wo, wup, wdown, df, weights, attended, arrived, h2, dact, act, dpre, kept, to_sibling, from_sibling,
    to_chip, from_chip, up_grad, down_grad, y2, dout, datt_out, datt, dmixed, dtotal, send, receive, local,
):
    low, full = jnp.bfloat16, jnp.float32
    links = Links(planes, send, receive, local)
    links.greet()
    loads = [links.keep(a, b) for a, b in ((wo_in, wo), (df_in, df), (wdown_in, wdown), (wup_in, wup))]

    def combine(z, carry):
        for x in range(2):
            totals = [down(total[x * 4 + u, pl.ds(z, 1), :]) for u in range(4)]
            highest = jnp.maximum(
                jnp.maximum(totals[0], totals[1]), jnp.maximum(totals[2], totals[3])
            )
            parts = [jnp.exp(t - highest) for t in totals]
            inverse = 1.0 / (parts[0] + parts[1] + parts[2] + parts[3])
            result = 0.0
            for u in range(4):
                weight = parts[u] * inverse
                weights[x * 4 + u, z] = weight
                result += weight * mixed[x * 4 + u, z].astype(full)
            attended[z, :, x * 128 : (x + 1) * 128] = result.astype(low)
        return carry

    lax.fori_loop(0, planes, combine, 0)
    links.meet()
    share = along_z(block, block)(links, attended, arrived)
    next(share)
    keep_attended = links.keep(attended, attended_out)
    loads[0].wait()
    drive([share])
    y1 = x1[...]
    for z in range(planes):
        y1 += dot(arrived[z], wo[z * 256 : (z + 1) * 256, :], ((1,), (0,)))
    y1_out[...] = y1
    unit, _ = normal_parts(y1)
    own_rows = pl.ds(pl.multiple_of(links.p * 128, 128), 128)
    h2[own_rows, :] = (unit * gains[2:3, :] + gains[3:4, :]).astype(low)

    sibling, _ = links.near(1)
    own_h2 = h2.at[own_rows, :]
    direct = {step: links.push(own_h2, own_h2, links.near(step)[0]) for step in (2, 4)}
    handed = {0: links.push(own_h2, own_h2, sibling)}
    for load in loads[1:]:
        load.wait()

    def upper_back(part, carry):
        rows = pl.ds(pl.multiple_of(part * 256, 256), 256)
        dact[rows, :] = dot(df[rows, :], wdown[...], ((1,), (1,)))
        return carry

    lax.fori_loop(0, 4, upper_back, 0)

    def pass_on(step):
        direct[step].wait_recv()
        block_rows = h2.at[rows_of(links.near(step)[1]), :]
        handed[step] = links.push(block_rows, block_rows, sibling)

    def feed(slot, step):
        handed[step].wait_recv()
        chip = links.near(step)[1] // 2
        rows = pl.ds(pl.multiple_of(chip * 256, 256), 256)
        before = dot(h2[rows, :], wup[...], ((1,), (0,))) + bias_up[...]
        value, slope = gelu_parts(before)
        act[rows, :] = value.astype(low)
        grad = (dact[rows, :] * slope).astype(low)
        dpre[rows, :] = grad
        kept[slot] = dot(grad, wup[...], ((1,), (1,))).reshape(2, 128, -1).astype(low)
        return links.push(kept.at[slot, 1 - links.core], from_sibling.at[slot], sibling)

    def chip_sum(slot, step, traded):
        traded.wait_recv()
        result = kept[slot, links.core].astype(full) + from_sibling[slot].astype(full)
        if slot == 0:
            return result
        to_chip[slot - 1] = result.astype(low)
        return links.push(to_chip.at[slot - 1], from_chip.at[slot - 1], links.near(step)[0])

    traded = [feed(0, 0)]
    for step in (2, 4):
        direct[step].wait_send()
    direct[6] = links.push(own_h2, own_h2, links.near(6)[0])
    pass_on(2)
    pass_on(4)
    traded.append(feed(1, 2))
    sent = [chip_sum(1, 2, traded[1])]
    pass_on(6)
    traded.append(feed(2, 4))
    sent.append(chip_sum(2, 4, traded[2]))
    traded.append(feed(3, 6))
    sent.append(chip_sum(3, 6, traded[3]))
    own_sum = chip_sum(0, 0, traded[0])

    def upper_grad(part, carry):
        rows = pl.ds(pl.multiple_of(part * 256, 256), 256)
        up_grad[part] = dot(h2[:, rows], dpre[...], ((0,), (0,))).astype(low)
        return carry

    lax.fori_loop(0, planes, upper_grad, 0)
    share_up = along_z(block, block)(links, up_grad, up_grad_out)
    next(share_up)
    for copy in sent:
        copy.wait_recv()
    grad = own_sum + (
        from_chip[0].astype(full) + from_chip[1].astype(full) + from_chip[2].astype(full)
    )
    part, gain_grad, shift_grad = norm_back(grad, y1_out[...], gains[2:3, :])
    gain_out[...] = gain_grad
    shift_out[...] = shift_grad
    g1_new = g1[...] + part
    g1_out[...] = g1_new
    dout[...] = g1_new.astype(low)
    keep_dout = links.keep(dout, dout_out)
    for z in range(planes):
        datt_out[z] = dot(dout[...], wo[z * 256 : (z + 1) * 256, :], ((1,), (1,))).astype(low)
    share = along_z(block, block)(links, datt_out, datt)
    next(share)

    def lower_grad(part, carry):
        rows = pl.ds(pl.multiple_of(part * 128, 128), 128)
        down_grad[part] = dot(act[:, rows], df[...], ((0,), (0,))).astype(low)
        return carry

    lax.fori_loop(0, planes, lower_grad, 0)
    keep_down = links.keep(down_grad, down_grad_out)
    up_bias_out[...] = jnp.sum(dpre[...].astype(full), axis=0, keepdims=True)
    drive([share])

    def combine_back(z, carry):
        for x in range(2):
            grad = datt[z, :, x * 128 : (x + 1) * 128].astype(full)
            chosen = [weights[x * 4 + u, z] for u in range(4)]
            inner = [
                jnp.sum(grad * mixed[x * 4 + u, z].astype(full), axis=-1, keepdims=True)
                for u in range(4)
            ]
            mean = sum(chosen[u] * inner[u] for u in range(4))
            for u in range(4):
                dmixed[x * 4 + u, z] = (chosen[u] * grad).astype(low)
                change = (chosen[u] * (inner[u] - mean)).astype(low).astype(full)
                dtotal[x * 4 + u, pl.ds(z, 1), :] = change.T[:1, :]
        return carry

    lax.fori_loop(0, planes, combine_back, 0)
    shares = [
        over_plane(block, second)(links, dmixed, dmixed_home),
        over_plane(block, block)(links, dtotal, dtotal_home),
    ]
    for transfer in shares:
        next(transfer)

    def lower(part, carry):
        rows = pl.ds(pl.multiple_of(part * 128, 128), 128)
        y2[part] = dot(act[rows, :], wdown[...], ((1,), (0,))).astype(low)
        return carry

    lax.fori_loop(0, 8, lower, 0)
    keep_y2 = links.keep(y2, y2_out)
    for copy in [direct[6]] + traded + sent:
        copy.wait_send()
    for copy in handed.values():
        copy.wait_send()
    drive(shares + [share_up])
    for copy in (keep_attended, keep_dout, keep_y2, keep_down):
        copy.wait()


def feed_stage(arguments, collective_id, planes):
    low, full = jnp.bfloat16, jnp.float32
    (mixed, total, x1, wo, gains, wup, bias_up, wdown, df, g1) = arguments
    rows, width = x1.shape
    part = wup.shape[1]
    shape = jax.ShapeDtypeStruct
    outputs = [
        (shape((rows, width), full), VMEM),
        (shape((rows, width), full), VMEM),
        (shape((rows, width), low), ANY),
        (shape((planes, rows, 256), low), ANY),
        (shape((planes, 8, rows, HEAD_DIM), low), ANY),
        (shape((8, 8, rows), full), ANY),
        (shape((8, rows, width), low), ANY),
        (shape((planes, width // planes, part), low), ANY),
        (shape((planes, rows, width), low), ANY),
        (shape((1, part), full), VMEM),
        (shape((1, width), full), VMEM),
        (shape((1, width), full), VMEM),
    ]
    scratch = [
        (wo.shape, low),
        (wup.shape, low),
        (wdown.shape, low),
        (df.shape, low),
        ((8, planes, rows, HEAD_DIM), full),
        ((planes, rows, 256), low),
        ((planes, rows, 256), low),
        ((8 * rows, width), low),
        ((8 * rows, part), full),
        ((8 * rows, part), low),
        ((8 * rows, part), low),
        ((4, 2, rows, width), low),
        ((4, rows, width), low),
        ((4, rows, width), low),
        ((3, rows, width), low),
        ((3, rows, width), low),
        ((planes, width // planes, part), low),
        ((planes, rows, width), low),
        ((8, rows, width), low),
        ((rows, width), low),
        ((planes, rows, 256), low),
        ((planes, rows, 256), low),
        ((8, planes, rows, HEAD_DIM), low),
        ((8, 8, rows), full),
    ]
    return pl.pallas_call(
        functools.partial(feed_kernel, planes),
        out_shape=[o[0] for o in outputs],
        in_specs=[VMEM, VMEM, VMEM, ANY, VMEM, ANY, VMEM, ANY, ANY, VMEM],
        out_specs=[o[1] for o in outputs],
        scratch_shapes=[pltpu.VMEM(*s) for s in scratch] + link_scratch(),
        compiler_params=pltpu.CompilerParams(
            vmem_limit_bytes=56 << 20, collective_id=collective_id, has_side_effects=True
        ),
        name="feed",
    )(*arguments)


def open_kernel(
    planes,
    sort_order, sort_place, gain_a_in, shift_a_in, gain_f_in, shift_f_in, bias_up_in, bias_down_in,
    x2, wqk, wv, wo, wup, wdown, g2,
    places_out, gains_out, bias_up_out, normed_out, wqk_out, wv_out, wo_out, wup_out, wdown_out, df_out,
    shared_out, values_out, total_out, mixed_out, total_home_out,
    ints, all_ints, floats, all_floats, order_rows, place_rows, order_s, place_s, normed, df,
    wqk_line, wv_line, wo_line, wup_rows, wqk_pair, wv_pair, heads, head_table, table, mixed,
    shared, values, total_sorted, mixed_home, total_home, last_scale, send, receive, local,
):
    low, full = jnp.bfloat16, jnp.float32
    links = Links(planes, send, receive, local)
    links.greet()
    sub = links.y * 2 + links.core
    tiles = planes * 8
    ints[...] = jnp.concatenate([sort_order[...], sort_place[...]], axis=0)
    lane = lax.broadcasted_iota(jnp.int32, (1, 128), 1) // 32

    def spread(vector):
        wide = jnp.concatenate([vector[...].astype(full)] * 4, axis=1)
        return jnp.where(lane == sub, wide, 0.0)

    floats[...] = jnp.concatenate(
        [spread(v) for v in (gain_a_in, shift_a_in, gain_f_in, shift_f_in, bias_down_in)]
        + [bias_up_in[...].astype(full), jnp.zeros((2, 128), full)],
        axis=0,
    )
    df[...] = g2[...].astype(low)
    links.meet()
    share_floats = everywhere(links, floats, all_floats)
    next(share_floats)
    share_ints = everywhere(links, ints, all_ints)
    next(share_ints)

    def pair_columns(ref, z):
        return ref.at[:, pl.ds(pl.multiple_of(z * 256, 256), 256)]

    pair_shares = [
        along_z(pair_columns, block)(links, a, b) for a, b in ((wqk, wqk_line), (wv, wv_line))
    ]
    for transfer in pair_shares:
        next(transfer)
    wo_share = along_z(whole, block)(links, wo, wo_line)
    next(wo_share)
    unit, _ = normal_parts(x2[...])
    next(share_floats)

    def upper_columns(chunk):
        def columns(ref, p):
            return ref.at[:, pl.ds(pl.multiple_of((chunk * 8 + p) * 128, 128), 128)]

        def landing(ref, p):
            return ref.at[p, :, pl.ds(chunk * 128, 128)]

        return over_plane(columns, landing)

    drive([share_floats])

    def vector_of(row, z_step=2):
        chunks = []
        for chunk in range(8):
            z, x = chunk // 2, chunk % 2
            parts = [all_floats[z, x * 4 + u, row : row + 1, :] for u in range(4)]
            chunks.append(parts[0] + parts[1] + parts[2] + parts[3])
        return jnp.concatenate(chunks, axis=1)

    gain, shift = vector_of(0), vector_of(1)
    normed[links.z] = (unit * gain + shift).astype(low)
    normed_chain = Chain(links, normed)
    for transfer in pair_shares:
        drive([transfer])
    pair_shares = [
        over_chips(whole, second)(links, a, b) for a, b in ((wqk_line, wqk_pair), (wv_line, wv_pair))
    ]
    for transfer in pair_shares:
        next(transfer)
    next(share_ints)
    upper_shares = [upper_columns(chunk)(links, wup, wup_rows) for chunk in range(planes)]
    for transfer in upper_shares:
        next(transfer)
    for transfer in pair_shares:
        next(transfer)
    gains_out[0:1, :] = gain
    gains_out[1:2, :] = shift
    for row in (2, 3, 4):
        gains_out[row : row + 1, :] = vector_of(row)
    for z in range(planes):
        bias_up_out[:, z * 128 : (z + 1) * 128] = all_floats[z, links.p, 5:6, :]
    drive(pair_shares)
    drive([share_ints])
    for z in range(planes):
        for p in range(8):
            tile = z * 8 + p
            order_rows[tile : tile + 1, :] = all_ints[z, p, pl.ds(sub, 1), :]
            place_rows[tile : tile + 1, :] = all_ints[z, p, pl.ds(sub + 4, 1), :]
    to_scalars = [links.keep(order_rows, order_s), links.keep(place_rows, place_s)]

    def head_columns(z):
        def columns(ref, p):
            return ref.at[z, :, pl.ds(pl.multiple_of((p // 4) * 256, 256), 256)]

        return columns

    def landing(z):
        return lambda ref, p: ref.at[z, p]

    def project(z):
        rows = normed[z]
        for weights, offset in ((wqk_pair, 0), (wv_pair, 128)):
            result = dot(rows, weights[...].reshape(-1, 256), ((1,), (0,))).astype(low)
            heads[z, :, offset : offset + 128] = result[:, :128]
            heads[z, :, 256 + offset : 384 + offset] = result[:, 128:]
        transfer = over_chips(head_columns(z), landing(z))(links, heads, head_table)
        next(transfer)
        return transfer

    head_shares = [project(links.z)]
    for index in range(3):
        head_shares.append(project(normed_chain.arrive(index)))
        next(head_shares[-2])
    for transfer in upper_shares:
        drive([transfer])
    shares = [
        over_chips(whole, block)(links, df, df_out),
        along_z(whole, block)(links, wup_rows, wup_out),
        along_z(whole, block)(links, wdown, wdown_out),
    ]
    next(shares[1])
    next(head_shares[-1])
    next(shares[0])
    next(shares[2])
    drive([wo_share])
    wo_share = over_chips(whole, second)(links, wo_line, wo_out)
    for copy in to_scalars:
        copy.wait()
    drive(head_shares)
    next(wo_share)

    def load(tile, carry):
        table[rows_of(tile), :] = head_table[tile // 8, lax.rem(tile, 8)].astype(full)
        return carry

    lax.fori_loop(0, tiles, load, 0)
    attend_tiles(
        tiles, 2, order_s, order_rows, table, shared, values, mixed, total_sorted, last_scale
    )
    next(wo_share)
    next(shares[0])
    kept = [
        links.keep(normed, normed_out),
        links.keep(wqk_pair, wqk_out),
        links.keep(wv_pair, wv_out),
        links.keep(shared, shared_out),
        links.keep(values, values_out),
        links.keep(total_sorted, total_out),
        links.keep(order_rows, places_out.at[0]),
        links.keep(place_rows, places_out.at[1]),
    ]
    sent = []
    for step in (6, 7, 4, 5, 2, 3, 1, 0):
        device, p = links.near(step)

        def unsort(z, carry):
            totals = []
            for part in range(4):
                picked = pick_tile(mixed, place_s, z * 8 + p, part)
                mixed_home[p, z, part * 32 : part * 32 + 32, :] = picked[:, :128].astype(low)
                totals.append(picked[:, 128:])
            total_home[p, pl.ds(z, 1), :] = jnp.concatenate(totals, axis=0).T[:1, :]
            return carry

        lax.fori_loop(0, planes, unsort, 0)
        for here, there in ((mixed_home, mixed_out), (total_home, total_home_out)):
            source, target = here.at[p], there.at[links.p]
            if step:
                sent.append(links.push(source, target, device))
            else:
                kept.append(links.keep(source, target))
    normed_chain.finish()
    drive(shares + [wo_share])
    for copy in kept + sent:
        copy.wait()


def open_stage(arguments, collective_id, planes):
    low, full, whole_number = jnp.bfloat16, jnp.float32, jnp.int32
    x2, wqk, wup = arguments[8], arguments[9], arguments[12]
    rows, width = x2.shape
    own, hidden = wup.shape
    part = hidden // 8
    tiles = planes * 8
    tokens = tiles * rows
    shape = jax.ShapeDtypeStruct
    outputs = [
        (shape((2, tiles, rows), whole_number), ANY),
        (shape((8, width), full), VMEM),
        (shape((1, part), full), VMEM),
        (shape((planes, rows, width), low), ANY),
        (shape((planes, 8, own, 256), low), ANY),
        (shape((planes, 8, own, 256), low), ANY),
        (shape((planes, 8, own, width), low), ANY),
        (shape((planes, 8, own, part), low), ANY),
        (shape((planes, rows, width), low), ANY),
        (shape((8, rows, width), low), ANY),
        (shape((tokens + BLOCK, HEAD_DIM), low), ANY),
        (shape((tokens + BLOCK, HEAD_DIM), low), ANY),
        (shape((tokens, HEAD_DIM), full), ANY),
        (shape((8, planes, rows, HEAD_DIM), low), ANY),
        (shape((8, 8, rows), full), ANY),
    ]
    scratch = [
        pltpu.VMEM((8, rows), whole_number),
        pltpu.VMEM((planes, 8, 8, rows), whole_number),
        pltpu.VMEM((8, rows), full),
        pltpu.VMEM((planes, 8, 8, rows), full),
        pltpu.VMEM((tiles, rows), whole_number),
        pltpu.VMEM((tiles, rows), whole_number),
        pltpu.SMEM((tiles, rows), whole_number),
        pltpu.SMEM((tiles, rows), whole_number),
        pltpu.VMEM((planes, rows, width), low),
        pltpu.VMEM((rows, width), low),
        pltpu.VMEM((planes, own, 256), low),
        pltpu.VMEM((planes, own, 256), low),
        pltpu.VMEM((planes, own, width), low),
        pltpu.VMEM((8, own, part), low),
        pltpu.VMEM((planes, 8, own, 256), low),
        pltpu.VMEM((planes, 8, own, 256), low),
        pltpu.VMEM((planes, rows, 512), low),
        pltpu.VMEM((planes, 8, rows, 256), low),
        pltpu.VMEM((tokens, 256), full),
        pltpu.VMEM((tokens, 256), full),
        pltpu.VMEM((tokens + BLOCK, HEAD_DIM), low),
        pltpu.VMEM((tokens + BLOCK, HEAD_DIM), low),
        pltpu.VMEM((tokens, HEAD_DIM), full),
        pltpu.VMEM((8, planes, rows, HEAD_DIM), low),
        pltpu.VMEM((8, 8, rows), full),
        pltpu.VMEM((1, rows), full),
    ]
    return pl.pallas_call(
        functools.partial(open_kernel, planes),
        out_shape=[o[0] for o in outputs],
        in_specs=[VMEM] * 15,
        out_specs=[o[1] for o in outputs],
        scratch_shapes=scratch + link_scratch(),
        compiler_params=pltpu.CompilerParams(
            vmem_limit_bytes=56 << 20, collective_id=collective_id, has_side_effects=True
        ),
        name="open",
    )(*arguments)


def close_kernel(
    planes,
    places, shared_in, values_in, total_in, dmixed_in, dtotal_in, y2_in, dout_in, attended_in, normed_in,
    wqk_in, wv_in, gains, x2_in, g2_in, up_in, down_in, up_bias, feed_gain, feed_shift,
    y2_out, g2_out, shared_grad_out, value_grad_out, out_grad_out, up_out, down_out, vectors_out,
    order_rows, order_s, place_s, shared, values, total_sorted, dmixed, dtotal, table, grad_sorted,
    grad_total_sorted, sums, scale_sums, last_scale, kept, from_sibling, to_chip, from_chip, y2_parts,
    dout_line, attended, normed, wqk, wv, x2, g2, up_parts, down_parts, up_sum, up_arrived, dshared, dvalues,
    de_out, de, out_sent, out_arrived, weight_sent, weight_arrived, weight_sum, weight_final,
    tiles_sent, tiles_arrived, tile, tile_line, send, receive, local,
):
    low, full = jnp.bfloat16, jnp.float32
    links = Links(planes, send, receive, local)
    links.greet()
    tiles = planes * 8
    line = planes * 128
    first_loads = [
        links.keep(a, b)
        for a, b in (
            (places.at[0], order_s), (places.at[1], place_s), (places.at[0], order_rows),
            (dmixed_in, dmixed), (dtotal_in, dtotal), (shared_in, shared), (values_in, values),
            (total_in, total_sorted), (up_in, up_parts),
        )
    ]
    links.meet()
    share_dout = along_z(whole, block)(links, dout_in, dout_line)
    next(share_dout)
    share_y2 = over_plane(block, block)(links, y2_in, y2_parts)
    next(share_y2)
    share_down = along_z(block, block)(links, down_in, down_parts)
    next(share_down)
    loads = [
        links.keep(a, b)
        for a, b in (
            (attended_in, attended), (normed_in, normed), (wqk_in, wqk), (wv_in, wv), (x2_in, x2),
            (g2_in, g2),
        )
    ]
    for copy in first_loads:
        copy.wait()
    up_sum[...] = sum(up_parts[z].astype(full) for z in range(planes)).reshape(up_sum.shape)
    share_up = over_plane(block, block)(links, up_sum, up_arrived)
    next(share_up)

    def load(index, carry):
        z, p = index // 8, lax.rem(index, 8)
        table[rows_of(index), :128] = dmixed[z, p].astype(full)
        table[rows_of(index), 128:] = down(dtotal[p, pl.ds(z, 1), :])
        return carry

    lax.fori_loop(0, tiles, load, 0)
    attend_back_tiles(
        tiles, 4, order_s, order_rows, table, shared, values, total_sorted,
        grad_sorted, grad_total_sorted, sums, scale_sums, last_scale,
    )
    sibling, _ = links.near(1)

    def unsort(slot, step):
        chip = links.near(step)[1] // 2
        for core, goal in ((0, 1 - links.core), (1, links.core)):

            def rows(z, carry):
                for part in range(4):
                    picked = pick_tile(sums, place_s, z * 8 + chip * 2 + goal, part)
                    kept[slot, core, z, part * 32 : part * 32 + 32, :] = picked.astype(low)
                return carry

            lax.fori_loop(0, planes, rows, 0)
            if core == 0:
                traded = links.push(kept.at[slot, 0], from_sibling.at[slot], sibling)
        return traded

    def chip_sum(slot, step, traded):
        traded.wait_recv()
        result = kept[slot, 1].astype(full) + from_sibling[slot].astype(full)
        if step == 0:
            return result
        to_chip[slot] = result.astype(low)
        return links.push(to_chip.at[slot], from_chip.at[slot], links.near(step)[0])

    steps = (6, 4, 2, 0)
    traded, sent = [], []
    for slot, step in enumerate(steps):
        traded.append(unsort(slot, step))
        if slot:
            sent.append(chip_sum(slot - 1, steps[slot - 1], traded[slot - 1]))
    for copy in loads:
        copy.wait()
    drive([share_dout])
    all_dout = dout_line[...].reshape(line, -1)
    out_sent[...] = (
        dot(attended[...].reshape(line, 256), all_dout, ((0,), (0,))).astype(low).reshape(out_sent.shape)
    )
    own_sum = chip_sum(3, 0, traded[3])
    share_out = over_plane(block, block)(links, out_sent, out_arrived)
    next(share_out)
    own_columns = pl.ds(pl.multiple_of(links.x * 128, 128), 128)
    far_columns = pl.ds(pl.multiple_of((1 - links.x) * 128, 128), 128)

    def settle_sum(columns, result):
        result = result.astype(low).reshape(line, 256)
        dshared[:, columns] = result[:, :128]
        dvalues[:, columns] = result[:, 128:]

    sent[2].wait_recv()
    settle_sum(own_columns, own_sum + from_chip[2].astype(full))
    sent[1].wait_recv()
    sent[0].wait_recv()
    settle_sum(far_columns, from_chip[1].astype(full) + from_chip[0].astype(full))
    all_wqk, all_wv = wqk[...].reshape(-1, 256), wv[...].reshape(-1, 256)

    def input_grad(z, carry):
        rows = rows_of(z)
        de_out[z] = (
            dot(dshared[rows, :], all_wqk, ((1,), (1,))) + dot(dvalues[rows, :], all_wv, ((1,), (1,)))
        ).astype(low)
        return carry

    lax.fori_loop(0, planes, input_grad, 0)
    share_de = along_z(block, block)(links, de_out, de)
    next(share_de)
    all_normed = normed[...].reshape(line, -1)
    for index, grad in enumerate((dshared, dvalues)):
        weight_sent[index] = (
            dot(all_normed, grad[...], ((0,), (0,))).astype(low).reshape(weight_sent.shape[1:])
        )

    def of_pair(ref, p):
        return ref.at[:, :, p]

    share_weights = over_plane(of_pair, block)(links, weight_sent, weight_arrived)
    next(share_weights)
    drive([share_y2])
    y2_out[...] = x2[...] + (
        sum(y2_parts[p].astype(full) for p in range(8)) + gains[4:5, :]
    )
    drive([share_up])
    for p in range(8):
        for z in range(planes):
            up_out[:, (z * 8 + p) * 128 : (z * 8 + p + 1) * 128] = up_arrived[
                p, :, z * 128 : (z + 1) * 128
            ]
    drive([share_down])
    down_out[...] = sum(down_parts[z].astype(full) for z in range(planes))
    drive([share_out])
    out_grad_out[...] = sum(out_arrived[p].astype(full) for p in range(8))
    down_bias = jnp.sum(g2[...].astype(low).astype(full), axis=0, keepdims=True)
    drive([share_weights])
    weight_sum[...] = sum(weight_arrived[p].astype(full) for p in range(8)).astype(low)

    def pair_columns(ref, z):
        return ref.at[:, :, pl.ds(pl.multiple_of(z * 256, 256), 256)]

    share_final = along_z(second, pair_columns)(links, weight_sum, weight_final)
    next(share_final)
    drive([share_de])
    part, gain_grad, shift_grad = norm_back(
        sum(de[z].astype(full) for z in range(planes)), x2[...], gains[0:1, :]
    )
    vectors = [gain_grad, shift_grad, feed_gain[...], feed_shift[...], down_bias]
    for x in range(2):
        for index, vector in enumerate(vectors):
            for z in range(planes):
                chunk = (z * 2 + x) * 128
                row = index * planes + z
                tiles_sent[x, row : row + 1, :] = vector[:, chunk : chunk + 128]
        tiles_sent[x, 5 * planes :, :] = jnp.zeros((24 - 5 * planes, 128), full)

    def of_x(ref, p):
        return ref.at[p // 4]

    share_tiles = over_plane(of_x, block)(links, tiles_sent, tiles_arrived)
    next(share_tiles)
    g2_out[...] = g2[...] + part
    drive([share_tiles])
    tile[...] = jnp.sum(tiles_arrived[...], axis=0)
    for z in range(planes):
        tile[5 * planes + z : 5 * planes + z + 1, :] = up_bias[:, z * 128 : (z + 1) * 128]
    share_tile = along_z(whole, block)(links, tile, tile_line)
    next(share_tile)
    drive([share_final])
    shared_grad_out[...] = weight_final[0].astype(full)
    value_grad_out[...] = weight_final[1].astype(full)
    drive([share_tile])
    tile[...] = jnp.sum(tile_line[...], axis=0)
    for index in range(6):
        vectors_out[index : index + 1, :] = tile[pl.ds(index * planes + links.z, 1), :]
    vectors_out[6:8, :] = jnp.zeros((2, 128), full)
    for copy in traded + sent:
        copy.wait_send()


def close_stage(arguments, collective_id, planes):
    low, full, whole_number = jnp.bfloat16, jnp.float32, jnp.int32
    x2, normed = arguments[13], arguments[9]
    own, part = arguments[10].shape[2], arguments[15].shape[2]
    rows, width = x2.shape
    tiles = planes * 8
    tokens = tiles * rows
    shape = jax.ShapeDtypeStruct
    outputs = [
        shape((rows, width), full),
        shape((rows, width), full),
        shape((own, width), full),
        shape((own, width), full),
        shape((own, width), full),
        shape((own, 8 * part), full),
        shape((rows, width), full),
        shape((8, rows), full),
    ]
    vmem = pltpu.VMEM
    chip_blocks = (planes, rows, 256)
    scratch = [
        vmem((tiles, rows), whole_number),
        pltpu.SMEM((tiles, rows), whole_number),
        pltpu.SMEM((tiles, rows), whole_number),
        vmem((tokens + BLOCK, HEAD_DIM), low),
        vmem((tokens + BLOCK, HEAD_DIM), low),
        vmem((tokens, HEAD_DIM), full),
        vmem((planes, 8, rows, HEAD_DIM), low),
        vmem((8, 8, rows), full),
        vmem((tokens, 256), full),
        vmem((tokens, HEAD_DIM), low),
        vmem((tokens, HEAD_DIM), full),
        vmem((tokens + rows, 256), full),
        vmem((tiles + 8, rows), full),
        vmem((1, rows), full),
        vmem((4, 2) + chip_blocks, low),
        vmem((4,) + chip_blocks, low),
        vmem((3,) + chip_blocks, low),
        vmem((3,) + chip_blocks, low),
        vmem((8, rows, width), low),
        vmem((planes, rows, width), low),
        vmem(chip_blocks, low),
        vmem((planes, rows, width), low),
        vmem((planes, 8, own, 256), low),
        vmem((planes, 8, own, 256), low),
        vmem((rows, width), full),
        vmem((rows, width), full),
        vmem((planes, 8 * own, part), low),
        vmem((planes, rows, width), low),
        vmem((8, own, part), full),
        vmem((8, own, part), full),
        vmem((planes * rows, 256), low),
        vmem((planes * rows, 256), low),
        vmem((planes, rows, width), low),
        vmem((planes, rows, width), low),
        vmem((8, own, width), low),
        vmem((8, own, width), low),
        vmem((2, planes, 8, own, 256), low),
        vmem((8, 2, planes, own, 256), low),
        vmem((2, planes, own, 256), low),
        vmem((2, own, width), low),
        vmem((2, 24, rows), full),
        vmem((8, 24, rows), full),
        vmem((24, rows), full),
        vmem((planes, 24, rows), full),
    ]
    return pl.pallas_call(
        functools.partial(close_kernel, planes),
        out_shape=outputs,
        in_specs=[ANY] * 12 + [VMEM] + [ANY] * 4 + [VMEM] * 3,
        out_specs=[VMEM] * len(outputs),
        scratch_shapes=scratch + link_scratch(),
        compiler_params=pltpu.CompilerParams(
            vmem_limit_bytes=56 << 20, collective_id=collective_id, has_side_effects=True
        ),
        name="close",
    )(*arguments)


def finish_kernel(
    y1, y2, g1, g2, shared_grad, value_grad, out_grad, up_grad, down_grad, vectors,
    y1_out, y2_out, g1_out, g2_out, gain_a_out, shift_a_out, shared_out, value_out, out_out,
    gain_f_out, shift_f_out, up_out, up_bias_out, down_out, down_bias_out, arrived,
):
    pairs = (
        (y1, y1_out), (y2, y2_out), (g1, g1_out), (g2, g2_out), (shared_grad, shared_out),
        (value_grad, value_out), (out_grad, out_out), (up_grad, up_out), (down_grad, down_out),
    )
    copies = [
        pltpu.make_async_copy(source, target.at[0], arrived.at[index])
        for index, (source, target) in enumerate(pairs)
    ]
    for copy in copies:
        copy.start()
    sub = lax.axis_index("sub")
    rows = vectors[...]
    own = sum(
        jnp.where(sub == u, rows[:, u * 32 : u * 32 + 32], 0.0) for u in range(4)
    )
    for row, target in enumerate((gain_a_out, shift_a_out, gain_f_out, shift_f_out, down_bias_out)):
        target[...] = own[row : row + 1, :]
    up_bias_out[...] = rows[5:6, :]
    for copy in copies:
        copy.wait()


def finish_stage(arguments):
    full = jnp.float32
    large = [(jax.ShapeDtypeStruct((1,) + a.shape, full), ANY) for a in arguments[:-1]]
    y1, y2, g1, g2, shared_grad, value_grad, out_grad, up_grad, down_grad = large
    small = (jax.ShapeDtypeStruct((1, arguments[4].shape[0]), full), VMEM)
    up_bias = (jax.ShapeDtypeStruct((1, arguments[-1].shape[1]), full), VMEM)
    outputs = [
        y1, y2, g1, g2, small, small, shared_grad, value_grad, out_grad, small, small, up_grad,
        up_bias, down_grad, small,
    ]
    return pl.pallas_call(
        finish_kernel,
        out_shape=[o[0] for o in outputs],
        in_specs=[VMEM] * 10,
        out_specs=[o[1] for o in outputs],
        scratch_shapes=[pltpu.SemaphoreType.DMA((9,))],
        name="finish",
    )(*arguments)


def plane_plan(
    n_seq,
    n_sub,
    first_half,
    second_half,
    grad_first,
    grad_second,
    attend_gain,
    attend_shift,
    query_key_weight,
    value_projection_weight,
    output_projection_weight,
    feed_gain,
    feed_shift,
    upper_projection_weight,
    upper_projection_bias,
    lower_projection_weight,
    lower_projection_bias,
    sort_order,
    sort_place,
):
    planes = n_seq // 2
    rows, width = first_half.shape[1:]
    x1, x2, g1, g2 = (a[0] for a in (first_half, second_half, grad_first, grad_second))
    wqk, wv, wo = query_key_weight[0], value_projection_weight[0], output_projection_weight[0]
    wup, wdown = upper_projection_weight[0], lower_projection_weight[0]
    (
        places, gains, bias_up, normed_line, wqk_pair, wv_pair, wo_all, wup_part, wdown_part, df_plane,
        shared, values, total_sorted, mixed, total,
    ) = open_stage(
        (
            sort_order[0, :, 0], sort_place[0, :, 0], attend_gain, attend_shift, feed_gain, feed_shift,
            upper_projection_bias, lower_projection_bias, x2, wqk, wv, wo, wup, wdown, g2,
        ),
        1,
        planes,
    )
    (
        y1, g1, dout, attended, dmixed, dtotal, y2_parts, up_grad, down_grad,
        up_bias_grad, feed_gain_grad, feed_shift_grad,
    ) = feed_stage(
        (
            mixed, total, x1, wo_all.reshape(width, width), gains, wup_part.reshape(width, -1),
            bias_up, wdown_part.reshape(-1, width), df_plane.reshape(8 * rows, width), g1,
        ),
        2,
        planes,
    )
    (
        y2, g2, shared_grad, value_grad, out_grad, up_grad, down_grad, vectors
    ) = close_stage(
        (
            places, shared, values, total_sorted, dmixed, dtotal, y2_parts, dout, attended, normed_line,
            wqk_pair, wv_pair, gains, x2, g2, up_grad, down_grad, up_bias_grad, feed_gain_grad,
            feed_shift_grad,
        ),
        3,
        planes,
    )
    return finish_stage(
        (y1, y2, g1, g2, shared_grad, value_grad, out_grad, up_grad, down_grad, vectors)
    )


def on_device(n_seq, n_sub, *arguments):
    sequences, rows, width = arguments[0].shape
    rounds = arguments[-1].shape[1]
    fits = (
        sequences == 1
        and rows == 2 * BLOCK
        and rounds == n_sub
        and HEADS == n_seq
        and width == HEADS * HEAD_DIM
    )
    if fits:
        return plane_plan(n_seq, n_sub, *arguments)
    return general_plan(*arguments)


def solution(mesh):
    return jax.shard_map(
        functools.partial(on_device, mesh.shape["seq"], mesh.shape["sub"]),
        mesh=mesh,
        in_specs=(
            P(None, ("seq", "sub"), None),
            P(None, ("seq", "sub"), None),
            P(None, ("seq", "sub"), None),
            P(None, ("seq", "sub"), None),
            P(None, ("seq", "sub")),
            P(None, ("seq", "sub")),
            P(None, ("seq", "sub"), None),
            P(None, ("seq", "sub"), None),
            P(None, ("seq", "sub"), None),
            P(None, ("seq", "sub")),
            P(None, ("seq", "sub")),
            P(None, ("seq", "sub"), None),
            P(None, ("seq", "sub")),
            P(None, ("seq", "sub"), None),
            P(None, ("seq", "sub")),
            P(None, None, None, ("seq", "sub")),
            P(None, None, None, ("seq", "sub")),
        ),
        out_specs=(
            P(None, ("seq", "sub"), None),
            P(None, ("seq", "sub"), None),
            P(None, ("seq", "sub"), None),
            P(None, ("seq", "sub"), None),
            P(None, ("seq", "sub")),
            P(None, ("seq", "sub")),
            P(None, ("seq", "sub"), None),
            P(None, ("seq", "sub"), None),
            P(None, ("seq", "sub"), None),
            P(None, ("seq", "sub")),
            P(None, ("seq", "sub")),
            P(None, ("seq", "sub"), None),
            P(None, ("seq", "sub")),
            P(None, ("seq", "sub"), None),
            P(None, ("seq", "sub")),
        ),
        check_vma=False,
    )
```

```python
import functools

import jax
import jax.numpy as jnp
from jax import lax
from jax.experimental import pallas as pl
from jax.experimental.pallas import tpu as pltpu
from jax.sharding import PartitionSpec as P

HEADS = 8
HEAD_DIM = 128
BLOCK = 64
LATER = -1000000000.0
SELF = -100000.0


def from_behind(block, axis, distance):
    devices = range(lax.axis_size(axis))
    route = [((i - distance) % len(devices), i) for i in devices]
    return lax.ppermute(block, axis, route)


def layer_norm(value_vectors, scaling, shifts):
    center = jnp.mean(value_vectors, axis=-1, keepdims=True)
    offset = value_vectors - center
    spread = jnp.mean(offset * offset, axis=-1, keepdims=True)
    return offset * lax.rsqrt(spread + 1e-05) * scaling + shifts


def gelu_exact(value_vectors):
    return jax.nn.gelu(value_vectors, approximate=False)


def combine_rounds(outputs, totals):
    highest = jnp.max(totals, axis=0, keepdims=True)
    weights = jnp.exp(totals - highest)
    weights = weights / jnp.sum(weights, axis=0, keepdims=True)
    by_head = outputs.reshape(outputs.shape[:-1] + (totals.shape[-1], -1))
    return jnp.sum(weights[..., None] * by_head, axis=0).reshape(outputs.shape[1:])


def home_slots(places, row_count):
    target = places // row_count
    prior_state = (target[:, None, :] == target[:, :, None]) & (
        places[:, None, :] < places[:, :, None]
    )
    return (target, jnp.sum(prior_state.astype(jnp.int32), axis=2))


def sorted_slots(orders, row_count):
    source = orders // row_count
    ladder = jnp.arange(row_count, dtype=jnp.int32)
    prior_state = (source[:, None, :] == source[:, :, None]) & (
        ladder[None, None, :] < ladder[None, :, None]
    )
    return (source, jnp.sum(prior_state.astype(jnp.int32), axis=2))


def slot_lookup(owners, slot_index, devices, capacity):
    groups, row_count = owners.shape
    flat_index = owners * capacity + slot_index
    lookup = jnp.full((groups, devices * capacity), row_count, jnp.int32)
    filler = jnp.broadcast_to(jnp.arange(row_count, dtype=jnp.int32), (groups, row_count))
    lookup = lookup.at[jnp.arange(groups)[:, None], flat_index].set(filler)
    return jnp.transpose(lookup.reshape(groups, devices, capacity), (1, 0, 2))


def gather_slots(value_vectors, member, lookup):
    padding = jnp.zeros((value_vectors.shape[0], 1) + value_vectors.shape[2:], value_vectors.dtype)
    padded = jnp.concatenate([value_vectors, padding], axis=1)
    return padded[member[None, :, None], lookup]


def settle(received, owners, slot_index):
    return received[owners, jnp.arange(owners.shape[0])[:, None], slot_index]


def build_routes(orders, places, devices, capacity):
    rounds, sequences, row_count = orders.shape
    order_flat = orders.reshape(rounds * sequences, row_count)
    target, home_slot = home_slots(places.reshape(rounds * sequences, row_count), row_count)
    source, sorted_slot = sorted_slots(order_flat, row_count)
    home_lookup = slot_lookup(target, home_slot, devices, capacity)
    back_lookup = slot_lookup(source, sorted_slot, devices, capacity)
    return (target, home_slot, source, sorted_slot, home_lookup, back_lookup, order_flat)


def trade_rows(first_part, second_part):
    return (
        lax.all_to_all(first_part, ("seq", "sub"), split_axis=0, concat_axis=0, tiled=True),
        lax.all_to_all(second_part, ("seq", "sub"), split_axis=0, concat_axis=0, tiled=True),
    )


def trade_results(first_part, second_part):
    return (
        lax.all_to_all(first_part, ("seq", "sub"), split_axis=0, concat_axis=0, tiled=True),
        lax.all_to_all(second_part, ("seq", "sub"), split_axis=0, concat_axis=0, tiled=True),
    )


def window(rows_here, rows_left):
    groups = rows_here.shape[0]
    extended = jnp.concatenate([rows_left, rows_here], axis=1)
    extended = extended.reshape((groups, -1, BLOCK) + rows_here.shape[2:])
    return jnp.concatenate([extended[:, :-1], extended[:, 1:]], axis=2)


def score_parts(shared_rows, order_rows, halo_shared, halo_order):
    groups, row_count, features = shared_rows.shape
    blocks = row_count // BLOCK
    queries = shared_rows.reshape(groups, blocks, BLOCK, HEADS, HEAD_DIM)
    key_rows = window(shared_rows, halo_shared).reshape(groups, blocks, 2 * BLOCK, HEADS, HEAD_DIM)
    key_float = key_rows.astype(jnp.float32)
    mean_square = jnp.mean(key_float * key_float, axis=-1) + 1e-06
    key_scale = lax.rsqrt(mean_square) / HEAD_DIM
    raw_scores = jnp.einsum(
        "gcqhd,gckhd->gchqk", queries, key_rows, preferred_element_type=jnp.float32
    )
    query_pos = order_rows.reshape(groups, blocks, BLOCK)
    key_pos = window(order_rows, halo_order)
    is_later = (key_pos[:, :, None, :] > query_pos[:, :, :, None])[:, :, None]
    is_self = (key_pos[:, :, None, :] == query_pos[:, :, :, None])[:, :, None]
    scale_row = jnp.transpose(key_scale, (0, 1, 3, 2))[:, :, :, None, :]
    scores = jnp.where(
        is_later, -1000000000.0, jnp.where(is_self, -100000.0, raw_scores * scale_row)
    )
    highest = jnp.max(scores, axis=-1, keepdims=True)
    log_total = highest + jnp.log(jnp.sum(jnp.exp(scores - highest), axis=-1, keepdims=True))
    probability = jnp.exp(scores - log_total)
    return (
        queries,
        key_rows,
        key_float,
        mean_square,
        key_scale,
        scale_row,
        raw_scores,
        is_later | is_self,
        log_total,
        probability,
    )


def attend(shared_rows, value_rows, order_rows, halo):
    halo_shared, halo_value, halo_order = halo
    parts = score_parts(shared_rows, order_rows, halo_shared, halo_order)
    groups, row_count, features = shared_rows.shape
    value_keys = window(value_rows, halo_value).reshape(
        groups, row_count // BLOCK, 2 * BLOCK, HEADS, HEAD_DIM
    )
    mixed = jnp.einsum(
        "gchqk,gckhd->gcqhd",
        parts[9].astype(jnp.bfloat16),
        value_keys,
        preferred_element_type=jnp.float32,
    )
    log_total = jnp.transpose(parts[8][..., 0], (0, 1, 3, 2)).reshape(groups, row_count, HEADS)
    return (mixed.reshape(groups, row_count, features), log_total)


def fold_window(grads_window, groups, row_count, features):
    grads_window = grads_window.reshape(groups, row_count // BLOCK, 2 * BLOCK, features)
    empty = jnp.zeros((groups, 1, BLOCK, features), jnp.float32)
    extended = jnp.concatenate([grads_window[:, :, :BLOCK], empty], axis=1) + jnp.concatenate(
        [empty, grads_window[:, :, BLOCK:]], axis=1
    )
    return (extended[:, 1:].reshape(groups, row_count, features), extended[:, 0])


def attend_back(shared_rows, value_rows, order_rows, halo, grad_out, grad_total):
    halo_shared, halo_value, halo_order = halo
    (
        queries,
        key_rows,
        key_float,
        mean_square,
        key_scale,
        scale_row,
        raw_scores,
        masked,
        log_total,
        probability,
    ) = score_parts(shared_rows, order_rows, halo_shared, halo_order)
    groups, row_count, features = shared_rows.shape
    blocks = row_count // BLOCK
    value_keys = window(value_rows, halo_value).reshape(groups, blocks, 2 * BLOCK, HEADS, HEAD_DIM)
    prob_low = probability.astype(jnp.bfloat16)
    grad_heads = grad_out.reshape(groups, blocks, BLOCK, HEADS, HEAD_DIM)
    grad_log = jnp.transpose(
        grad_total.astype(jnp.float32).reshape(groups, blocks, BLOCK, HEADS), (0, 1, 3, 2)
    )[..., None]
    grad_prob = jnp.einsum(
        "gcqhd,gckhd->gchqk", grad_heads, value_keys, preferred_element_type=jnp.float32
    )
    inner = jnp.sum(probability * grad_prob, axis=-1, keepdims=True)
    grad_score = jnp.where(masked, 0.0, probability * (grad_prob - inner + grad_log))
    grad_scale = jnp.transpose(jnp.sum(grad_score * raw_scores, axis=3), (0, 1, 3, 2))
    grad_raw = (grad_score * scale_row).astype(jnp.bfloat16)
    grad_query = jnp.einsum(
        "gchqk,gckhd->gcqhd", grad_raw, key_rows, preferred_element_type=jnp.float32
    )
    grad_key = jnp.einsum(
        "gchqk,gcqhd->gckhd", grad_raw, queries, preferred_element_type=jnp.float32
    )
    grad_key = grad_key - (grad_scale * key_scale / mean_square)[..., None] * key_float / HEAD_DIM
    grad_value = jnp.einsum(
        "gchqk,gcqhd->gckhd", prob_low, grad_heads, preferred_element_type=jnp.float32
    )
    key_home, key_left = fold_window(grad_key, groups, row_count, features)
    value_home, value_left = fold_window(grad_value, groups, row_count, features)
    back_key, back_value = from_behind((key_left, value_left), ("seq", "sub"), -1)
    grad_shared = grad_query.reshape(groups, row_count, features) + key_home
    grad_shared = grad_shared.at[:, row_count - BLOCK :].add(back_key)
    grad_values = value_home.at[:, row_count - BLOCK :].add(back_value)
    return (grad_shared, grad_values)


def sorted_attention(shared_query_key, value_vectors, routes):
    target, home_slot, source, sorted_slot, home_lookup, back_lookup, order_flat = routes
    groups = target.shape[0]
    member = jnp.arange(groups) % shared_query_key.shape[0]
    got_shared, got_values = trade_rows(
        gather_slots(shared_query_key, member, home_lookup),
        gather_slots(value_vectors, member, home_lookup),
    )
    shared_rows = settle(got_shared, source, sorted_slot)
    value_rows = settle(got_values, source, sorted_slot)
    halo = from_behind(
        (shared_rows[:, -BLOCK:], value_rows[:, -BLOCK:], order_flat[:, -BLOCK:]), ("seq", "sub"), 1
    )
    mixed, log_total = attend(shared_rows, value_rows, order_flat, halo)
    all_groups = jnp.arange(groups)
    got_mixed, got_total = trade_results(
        gather_slots(mixed, all_groups, back_lookup),
        gather_slots(log_total, all_groups, back_lookup),
    )
    return (
        settle(got_mixed, target, home_slot),
        settle(got_total, target, home_slot),
        (shared_rows, value_rows, halo),
    )


def round_outputs(normalized_input, query_key_weight, value_projection_weight, routes, rounds):
    shared_query_key = jnp.einsum(
        "srd,de->sre", normalized_input, query_key_weight, preferred_element_type=jnp.float32
    ).astype(jnp.bfloat16)
    value_vectors = jnp.einsum(
        "srd,de->sre", normalized_input, value_projection_weight, preferred_element_type=jnp.float32
    ).astype(jnp.bfloat16)
    mixed, log_total, kept = sorted_attention(shared_query_key, value_vectors, routes)
    sequences, row_count, features = normalized_input.shape
    outputs = mixed.reshape(rounds, sequences, row_count, features)
    totals = log_total.reshape(rounds, sequences, row_count, HEADS)
    return (shared_query_key, value_vectors, outputs, totals, kept)


def collect(weight_stack, layer_index):
    (
        attend_gain,
        attend_shift,
        query_key_weight,
        value_projection_weight,
        output_projection_weight,
        feed_gain,
        feed_shift,
        upper_projection_weight,
        upper_projection_bias,
        lower_projection_weight,
        lower_projection_bias,
    ) = tuple((shard_piece[layer_index] for shard_piece in weight_stack))
    return (
        lax.all_gather(attend_gain, ("seq", "sub"), axis=0, tiled=True),
        lax.all_gather(attend_shift, ("seq", "sub"), axis=0, tiled=True),
        lax.all_gather(query_key_weight, ("seq", "sub"), axis=0, tiled=True),
        lax.all_gather(value_projection_weight, ("seq", "sub"), axis=0, tiled=True),
        lax.all_gather(output_projection_weight, ("seq", "sub"), axis=0, tiled=True),
        lax.all_gather(feed_gain, ("seq", "sub"), axis=0, tiled=True),
        lax.all_gather(feed_shift, ("seq", "sub"), axis=0, tiled=True),
        lax.all_gather(upper_projection_weight, ("seq", "sub"), axis=0, tiled=True),
        lax.all_gather(upper_projection_bias, ("seq", "sub"), axis=0, tiled=True),
        lax.all_gather(lower_projection_weight, ("seq", "sub"), axis=0, tiled=True),
        lax.all_gather(lower_projection_bias, ("seq", "sub"), axis=0, tiled=True),
    )


def spread_grads(level_grads):
    (
        attend_gain,
        attend_shift,
        query_key_weight,
        value_projection_weight,
        output_projection_weight,
        feed_gain,
        feed_shift,
        upper_projection_weight,
        upper_projection_bias,
        lower_projection_weight,
        lower_projection_bias,
    ) = level_grads
    return (
        lax.psum_scatter(attend_gain, ("seq", "sub"), scatter_dimension=0, tiled=True),
        lax.psum_scatter(attend_shift, ("seq", "sub"), scatter_dimension=0, tiled=True),
        lax.psum_scatter(query_key_weight.astype(jnp.bfloat16), ("seq", "sub"), scatter_dimension=0, tiled=True),
        lax.psum_scatter(value_projection_weight.astype(jnp.bfloat16), ("seq", "sub"), scatter_dimension=0, tiled=True),
        lax.psum_scatter(output_projection_weight.astype(jnp.bfloat16), ("seq", "sub"), scatter_dimension=0, tiled=True),
        lax.psum_scatter(feed_gain, ("seq", "sub"), scatter_dimension=0, tiled=True),
        lax.psum_scatter(feed_shift, ("seq", "sub"), scatter_dimension=0, tiled=True),
        lax.psum_scatter(upper_projection_weight.astype(jnp.bfloat16), ("seq", "sub"), scatter_dimension=0, tiled=True),
        lax.psum_scatter(upper_projection_bias, ("seq", "sub"), scatter_dimension=0, tiled=True),
        lax.psum_scatter(lower_projection_weight.astype(jnp.bfloat16), ("seq", "sub"), scatter_dimension=0, tiled=True),
        lax.psum_scatter(lower_projection_bias, ("seq", "sub"), scatter_dimension=0, tiled=True),
    )


def layer_pass(first_half, second_half, grad_one, grad_two, params, routes, rounds):
    (
        attend_gain,
        attend_shift,
        query_key_weight,
        value_projection_weight,
        output_projection_weight,
        feed_gain,
        feed_shift,
        upper_projection_weight,
        upper_projection_bias,
        lower_projection_weight,
        lower_projection_bias,
    ) = params
    attend_norm, attend_pull = jax.vjp(
        layer_norm, second_half, attend_gain.astype(jnp.float32), attend_shift.astype(jnp.float32)
    )
    normalized_input = attend_norm.astype(jnp.bfloat16)
    shared_query_key, value_vectors, outputs, totals, kept = round_outputs(
        normalized_input, query_key_weight, value_projection_weight, routes, rounds
    )
    attention_result, combine_pull = jax.vjp(combine_rounds, outputs, totals)
    attended_low = attention_result.astype(jnp.bfloat16)
    top_one = first_half + jnp.einsum(
        "srd,de->sre", attended_low, output_projection_weight, preferred_element_type=jnp.float32
    )
    feed_norm, feed_pull = jax.vjp(
        layer_norm, top_one, feed_gain.astype(jnp.float32), feed_shift.astype(jnp.float32)
    )
    feed_forward_input = feed_norm.astype(jnp.bfloat16)
    prior_state = jnp.einsum(
        "srd,df->srf",
        feed_forward_input,
        upper_projection_weight,
        preferred_element_type=jnp.float32,
    ) + upper_projection_bias.astype(jnp.float32)
    hidden_activation, active_pull = jax.vjp(gelu_exact, prior_state)
    active_low = hidden_activation.astype(jnp.bfloat16)
    feed_out = jnp.einsum(
        "srf,fd->srd", active_low, lower_projection_weight, preferred_element_type=jnp.float32
    ) + lower_projection_bias.astype(jnp.float32)
    top_two = second_half + feed_out
    feed_grad = grad_two.astype(jnp.bfloat16)
    down_weight_grad = jnp.einsum(
        "srf,srd->fd", active_low, feed_grad, preferred_element_type=jnp.float32
    )
    down_bias_grad = jnp.sum(feed_grad.astype(jnp.float32), axis=(0, 1))
    active_grad = jnp.einsum(
        "srd,fd->srf", feed_grad, lower_projection_weight, preferred_element_type=jnp.float32
    )
    before_grad = active_pull(active_grad)[0].astype(jnp.bfloat16)
    up_weight_grad = jnp.einsum(
        "srd,srf->df", feed_forward_input, before_grad, preferred_element_type=jnp.float32
    )
    up_bias_grad = jnp.sum(before_grad.astype(jnp.float32), axis=(0, 1))
    norm_grad = jnp.einsum(
        "srf,df->srd", before_grad, upper_projection_weight, preferred_element_type=jnp.float32
    )
    one_part, feed_gain_grad, feed_shift_grad = feed_pull(norm_grad)
    total_one = grad_one + one_part
    out_grad = total_one.astype(jnp.bfloat16)
    output_weight_grad = jnp.einsum(
        "srd,sre->de", attended_low, out_grad, preferred_element_type=jnp.float32
    )
    attended_grad = jnp.einsum(
        "sre,de->srd", out_grad, output_projection_weight, preferred_element_type=jnp.float32
    )
    outputs_grad, totals_grad = combine_pull(attended_grad)
    target, home_slot, source, sorted_slot, home_lookup, back_lookup, order_flat = routes
    sequences, row_count, features = top_one.shape
    groups = rounds * sequences
    all_groups = jnp.arange(groups)
    outputs_low = outputs_grad.astype(jnp.bfloat16).reshape(groups, row_count, features)
    totals_low = totals_grad.astype(jnp.bfloat16).reshape(groups, row_count, HEADS)
    got_out, got_total = trade_rows(
        gather_slots(outputs_low, all_groups, home_lookup),
        gather_slots(totals_low, all_groups, home_lookup),
    )
    shared_rows, value_rows, halo = kept
    grad_shared, grad_values = attend_back(
        shared_rows,
        value_rows,
        order_flat,
        halo,
        settle(got_out, source, sorted_slot),
        settle(got_total, source, sorted_slot),
    )
    home_shared, home_values = trade_rows(
        gather_slots(grad_shared.astype(jnp.bfloat16), all_groups, back_lookup),
        gather_slots(grad_values.astype(jnp.bfloat16), all_groups, back_lookup),
    )
    shared_grad = jnp.sum(
        settle(home_shared, target, home_slot)
        .astype(jnp.float32)
        .reshape(rounds, sequences, row_count, features),
        axis=0,
    ).astype(jnp.bfloat16)
    values_grad = jnp.sum(
        settle(home_values, target, home_slot)
        .astype(jnp.float32)
        .reshape(rounds, sequences, row_count, features),
        axis=0,
    ).astype(jnp.bfloat16)
    shared_weight_grad = jnp.einsum(
        "srd,sre->de", normalized_input, shared_grad, preferred_element_type=jnp.float32
    )
    value_weight_grad = jnp.einsum(
        "srd,sre->de", normalized_input, values_grad, preferred_element_type=jnp.float32
    )
    normed_grad = jnp.einsum(
        "sre,de->srd", shared_grad, query_key_weight, preferred_element_type=jnp.float32
    ) + jnp.einsum(
        "sre,de->srd", values_grad, value_projection_weight, preferred_element_type=jnp.float32
    )
    two_part, attend_gain_grad, attend_shift_grad = attend_pull(normed_grad)
    total_two = grad_two + two_part
    level_grads = (
        attend_gain_grad,
        attend_shift_grad,
        shared_weight_grad,
        value_weight_grad,
        output_weight_grad,
        feed_gain_grad,
        feed_shift_grad,
        up_weight_grad,
        up_bias_grad,
        down_weight_grad,
        down_bias_grad,
    )
    return (top_one, top_two, total_one, total_two, level_grads)


def general_plan(
    first_half,
    second_half,
    grad_first,
    grad_second,
    attend_gain,
    attend_shift,
    query_key_weight,
    value_projection_weight,
    output_projection_weight,
    feed_gain,
    feed_shift,
    upper_projection_weight,
    upper_projection_bias,
    lower_projection_weight,
    lower_projection_bias,
    sort_order,
    sort_place,
):
    weight_stack = (
        attend_gain,
        attend_shift,
        query_key_weight,
        value_projection_weight,
        output_projection_weight,
        feed_gain,
        feed_shift,
        upper_projection_weight,
        upper_projection_bias,
        lower_projection_weight,
        lower_projection_bias,
    )
    devices = lax.axis_size(("seq", "sub"))
    rounds = sort_order.shape[1]
    row_count = first_half.shape[1]
    capacity = 2 * max(1, row_count // devices)
    params = collect(weight_stack, 0)
    routes = build_routes(sort_order[0], sort_place[0], devices, capacity)
    first_out, second_out, first_grad, second_grad, level_grads = layer_pass(
        first_half, second_half, grad_first, grad_second, params, routes, rounds
    )
    stacked = tuple((entry[None].astype(jnp.float32) for entry in spread_grads(level_grads)))
    return (first_out, second_out, first_grad, second_grad) + stacked


class Links:
    def __init__(self, planes, send, receive, local):
        self.send, self.receive, self.local = send, receive, local
        self.used, self.used_local = 0, 0
        self.planes = planes
        seq, sub = lax.axis_index("seq"), lax.axis_index("sub")
        self.z, self.x = seq // 2, lax.rem(seq, 2)
        self.y, self.core = sub // 2, lax.rem(sub, 2)
        self.p = self.x * 4 + sub

    def near(self, step):
        x = 1 - self.x if step & 4 else self.x
        y = 1 - self.y if step & 2 else self.y
        core = 1 - self.core if step & 1 else self.core
        return (self.z * 2 + x, y * 2 + core), x * 4 + y * 2 + core

    def along(self, step):
        to = lax.rem(self.z + step, self.planes)
        back = lax.rem(self.z + self.planes - step, self.planes)
        return (to * 2 + self.x, self.y * 2 + self.core), to, back

    def greet(self):
        barrier = pltpu.get_barrier_semaphore()
        targets = [self.near(step)[0] for step in range(1, 8)]
        targets += [self.along(step)[0] for step in range(1, self.planes)]
        for target in targets:
            pl.semaphore_signal(barrier, inc=1, device_id=target, device_id_type=pl.DeviceIdType.MESH)
        self.greeted = len(targets)

    def meet(self):
        pl.semaphore_wait(pltpu.get_barrier_semaphore(), self.greeted)

    def push(self, source, target, device):
        copy = pltpu.make_async_remote_copy(
            src_ref=source,
            dst_ref=target,
            send_sem=self.send.at[self.used],
            recv_sem=self.receive.at[self.used],
            device_id=device,
            device_id_type=pl.DeviceIdType.MESH,
        )
        self.used += 1
        copy.start()
        return copy

    def keep(self, source, target):
        copy = pltpu.make_async_copy(source, target, self.local.at[self.used_local])
        self.used_local += 1
        copy.start()
        return copy


class Chain:
    def __init__(self, links, ref):
        self.links, self.ref, self.first, self.sent = links, ref, links.used, []
        links.used += 5
        self.hand_on(links.z, links.z < 3, links.z > 0, 2)

    def hand_on(self, shard, rightward, leftward, ways):
        links = self.links
        steps = ((1, rightward), (-1, leftward)) if ways == 2 else ((None, rightward | leftward),)
        for step, wanted in steps:
            if step is None:
                step = jnp.where(rightward, 1, -1)
            to = jnp.clip(links.z + step, 0, 3)
            middle = jnp.where(to == 1, jnp.where(shard == 0, 0, shard - 1), jnp.where(shard == 3, 0, 2 - shard))
            arrival = jnp.where((to == 0) | (to == 3), jnp.abs(to - shard) - 1, middle)
            arrival = jnp.clip(arrival, 0, 2)
            copy = pltpu.make_async_remote_copy(
                src_ref=self.ref.at[shard],
                dst_ref=self.ref.at[shard],
                send_sem=links.send.at[self.first + len(self.sent)],
                recv_sem=links.receive.at[self.first + arrival],
                device_id=(to * 2 + links.x, links.y * 2 + links.core),
                device_id_type=pl.DeviceIdType.MESH,
            )
            self.sent.append((wanted, copy))
            pl.when(wanted)(copy.start)

    def arrive(self, index):
        links, z = self.links, self.links.z
        ends = jnp.where(z == 0, index + 1, 2 - index)
        inner = jnp.where(z == 1, (0, 2, 3)[index], (3, 1, 0)[index])
        shard = jnp.where((z == 0) | (z == 3), ends, inner)
        pltpu.make_async_remote_copy(
            src_ref=self.ref.at[shard],
            dst_ref=self.ref.at[shard],
            send_sem=links.send.at[self.first],
            recv_sem=links.receive.at[self.first + index],
            device_id=(z * 2 + links.x, links.y * 2 + links.core),
            device_id_type=pl.DeviceIdType.MESH,
        ).wait_recv()
        self.hand_on(shard, (shard < z) & (z < 3), (shard > z) & (z > 0), 1)
        return shard

    def finish(self):
        for wanted, copy in self.sent:
            pl.when(wanted)(copy.wait_send)


COPIES = 320


def link_scratch():
    return [
        pltpu.SemaphoreType.DMA((COPIES,)),
        pltpu.SemaphoreType.DMA((COPIES,)),
        pltpu.SemaphoreType.DMA((64,)),
    ]


def along_z(source, target):
    def transfer(links, here, there):
        own = links.keep(source(here, links.z), target(there, links.z))
        copies = []
        for step in range(1, links.planes):
            device, to, _ = links.along(step)
            copies.append(links.push(source(here, to), target(there, links.z), device))
        yield
        own.wait()
        for copy in copies:
            copy.wait()

    return transfer


def over_plane(source, target):
    def transfer(links, here, there):
        own = links.keep(source(here, links.p), target(there, links.p))
        copies = []
        for step in (6, 7, 4, 5, 2, 3, 1):
            device, to = links.near(step)
            copies.append(links.push(source(here, to), target(there, links.p), device))
        yield
        own.wait()
        for copy in copies:
            copy.wait()

    return transfer


def over_chips(source, target):
    def transfer(links, here, there):
        own = links.keep(source(here, links.p), target(there, links.p))
        copies = []
        for step in (6, 4, 2):
            device, to = links.near(step)
            copies.append(links.push(source(here, to), target(there, links.p), device))
        sibling, _ = links.near(1)
        passed = [links.push(source(here, links.p), target(there, links.p), sibling)]
        yield
        for step, copy in zip((6, 4, 2), copies):
            copy.wait_recv()
            _, sender = links.near(step)
            passed.append(links.push(target(there, sender), target(there, sender), sibling))
        yield
        own.wait()
        for copy in copies:
            copy.wait_send()
        for copy in passed:
            copy.wait()

    return transfer


def everywhere(links, here, there):
    own = links.keep(here, there.at[links.z, links.p])
    copies = []
    for step in (6, 7, 4, 5, 2, 3, 1):
        copies.append(links.push(here, there.at[links.z, links.p], links.near(step)[0]))
    yield
    own.wait()
    for copy in copies:
        copy.wait()
    copies = []
    for step in range(1, links.planes):
        copies.append(links.push(there.at[links.z], there.at[links.z], links.along(step)[0]))
    yield
    for copy in copies:
        copy.wait()


def drive(transfers):
    while transfers:
        left = []
        for transfer in transfers:
            try:
                next(transfer)
                left.append(transfer)
            except StopIteration:
                pass
        transfers = left


def whole(ref, index):
    return ref


def block(ref, index):
    return ref.at[index]


def second(ref, index):
    return ref.at[:, index]


def rows_of(index):
    return pl.ds(pl.multiple_of(index * 128, 128), 128)


def pick_tile(table, index_ref, tile, part):
    return jnp.concatenate(
        [table[pl.ds(index_ref[tile, part * 32 + row], 1), :] for row in range(32)], axis=0
    )


def sort_tile(order, table, first, second, offset, tile):
    for part in range(4):
        start = pl.multiple_of(tile * 128 + part * 32 + offset, 32)
        picked = pick_tile(table, order, tile, part)
        first[pl.ds(start, 32), :] = picked[:, :128].astype(first.dtype)
        second[pl.ds(start, 32), :] = picked[:, 128:].astype(second.dtype)


def across(column):
    return jnp.broadcast_to(column, (128, 128)).T[:1, :]


def down(row):
    return jnp.broadcast_to(row, (128, 128)).T


def dot(a, b, contract):
    return lax.dot_general(a, b, (contract, ((), ())), preferred_element_type=jnp.float32)


def key_scales(keys):
    rows = keys.astype(jnp.float32)
    mean_square = jnp.mean(rows * rows, axis=-1, keepdims=True) + 1e-06
    return rows, mean_square, lax.rsqrt(mean_square) / HEAD_DIM


def half_turned(row):
    return jnp.concatenate([row[:, 64:], row[:, :64]], axis=1)


def windows(before, here):
    return [jnp.concatenate([before[:, 64:], here[:, :64]], axis=1), here]


def masked_scores(raw, scale, query_pos, key_pos):
    return jnp.where(
        key_pos > query_pos, LATER, jnp.where(key_pos == query_pos, SELF, raw * scale)
    )


def attend_tiles(tiles, unroll, order, order_rows, table, shared, values, mixed, total_sorted, last_scale):
    sort = functools.partial(sort_tile, order, table, shared, values, BLOCK)
    end = tiles * 128
    for tile in [tiles - 1] + list(range(unroll)):
        sort(tile)
    shared[:BLOCK, :] = shared[end : end + BLOCK, :]
    values[:BLOCK, :] = values[end : end + BLOCK, :]
    last_scale[...] = across(key_scales(shared[end - BLOCK : end + BLOCK, :])[2])

    def step_tiles(step, carry):
        first = step * unroll
        numbers = [lax.rem(first + tiles - 1, tiles)] + [first + k for k in range(unroll)]
        places = [order_rows[pl.ds(t, 1), :] for t in numbers]
        scale = [last_scale[...]]
        work = []
        for k in range(unroll):
            start = pl.multiple_of((first + k) * 128, 128)
            keys = [shared[pl.ds(pl.multiple_of(start + half * 64, 64), 128), :] for half in range(2)]
            vals = [values[pl.ds(pl.multiple_of(start + half * 64, 64), 128), :] for half in range(2)]
            own = jnp.concatenate([keys[0][64:], keys[1][64:]], axis=0)
            scale.append(across(key_scales(own)[2]))
            work.append((keys, vals))
        last_scale[...] = scale[-1]
        for k in range(unroll):
            sort(lax.rem(first + unroll + k, tiles))
        query_pos = jnp.concatenate([down(place) for place in places[1:]], axis=0)
        key_pos, key_scale = [], []
        for k in range(unroll):
            key_pos += windows(places[k], places[k + 1])
            key_scale += windows(scale[k], scale[k + 1])
        raw = [dot(k[64:], k, ((1,), (1,))) for keys, _ in work for k in keys]
        raw, key_pos, key_scale = (
            jnp.concatenate([jnp.broadcast_to(a, (64, 128)) for a in parts], axis=0)
            for parts in (raw, key_pos, key_scale)
        )
        scores = masked_scores(raw, key_scale, query_pos, key_pos)
        highest = jnp.max(scores, axis=-1, keepdims=True)
        total = highest + jnp.log(jnp.sum(jnp.exp(scores - highest), axis=-1, keepdims=True))
        prob = jnp.exp(scores - total).astype(jnp.bfloat16)
        rows = pl.ds(pl.multiple_of(first * 128, 128), unroll * 128)
        total = jnp.broadcast_to(total, (unroll * 128, 128))
        mixed[rows, 128:] = total
        total_sorted[rows, :] = total
        vals = [v for _, vals in work for v in vals]
        mixed[rows, :128] = jnp.concatenate(
            [dot(prob[64 * i : 64 * i + 64], v, ((1,), (0,))) for i, v in enumerate(vals)], axis=0
        )
        return carry

    lax.fori_loop(0, tiles // unroll, step_tiles, 0)


def attend_back_tiles(
    tiles, unroll, order, order_rows, table, shared, values, total_sorted,
    grad_sorted, grad_total_sorted, sums, scale_sums, last_scale,
):
    sort = functools.partial(sort_tile, order, table, grad_sorted, grad_total_sorted, 0)
    end = tiles * 128
    for tile in range(unroll):
        sort(tile)
    last_scale[...] = across(key_scales(shared[end - BLOCK : end + BLOCK, :])[2])
    scale_sums[...] = jnp.zeros_like(scale_sums)
    sums[end : end + 128, :] = jnp.zeros((128, 256), jnp.float32)
    early = lax.broadcasted_iota(jnp.int32, (1, 128), 1) < 64

    def step_tiles(step, carry):
        first = step * unroll
        numbers = [lax.rem(first + tiles - 1, tiles)] + [first + k for k in range(unroll)]
        places = [order_rows[pl.ds(t, 1), :] for t in numbers]
        scale = [last_scale[...]]
        work = []
        for k in range(unroll):
            start = pl.multiple_of((first + k) * 128, 128)
            keys = [shared[pl.ds(pl.multiple_of(start + half * 64, 64), 128), :] for half in range(2)]
            vals = [values[pl.ds(pl.multiple_of(start + half * 64, 64), 128), :] for half in range(2)]
            own = jnp.concatenate([keys[0][64:], keys[1][64:]], axis=0)
            scale.append(across(key_scales(own)[2]))
            tile = pl.ds(start, 128)
            work.append(
                (keys, vals, grad_sorted[tile, :], grad_total_sorted[tile, :], total_sorted[tile, :])
            )
        last_scale[...] = scale[-1]
        for k in range(unroll):
            sort(lax.rem(first + unroll + k, tiles))
        blocks = 2 * unroll
        scale_parts = [0.0] * (unroll + 1)
        query_pos = jnp.concatenate([down(place) for place in places[1:]], axis=0)
        key_pos, key_scale = [], []
        for k in range(unroll):
            key_pos += windows(places[k], places[k + 1])
            key_scale += windows(scale[k], scale[k + 1])
        keys = [k for item in work for k in item[0]]
        vals = [v for item in work for v in item[1]]
        grads, grad_totals, totals = (
            jnp.concatenate([item[n] for item in work], axis=0) for n in (2, 3, 4)
        )
        own = [slice(64 * i, 64 * i + 64) for i in range(blocks)]
        raw = [dot(k[64:], k, ((1,), (1,))) for k in keys]
        grad_prob = [dot(grads[own[i]], v, ((1,), (1,))) for i, v in enumerate(vals)]
        raw, grad_prob, key_pos, key_scale = (
            jnp.concatenate([jnp.broadcast_to(a, (64, 128)) for a in parts], axis=0)
            for parts in (raw, grad_prob, key_pos, key_scale)
        )
        prob = jnp.exp(masked_scores(raw, key_scale, query_pos, key_pos) - totals)
        inner = jnp.sum(prob * grad_prob, axis=-1, keepdims=True)
        grad_score = jnp.where(
            key_pos < query_pos, prob * (grad_prob + (grad_totals - inner)), 0.0
        )
        product = grad_score * raw
        for index in range(blocks):
            k, half = index // 2, index % 2
            part = jnp.sum(product[own[index]], axis=0, keepdims=True)
            if half == 0:
                turned = half_turned(part)
                scale_parts[k] += jnp.where(early, 0.0, turned)
                scale_parts[k + 1] += jnp.where(early, turned, 0.0)
            else:
                scale_parts[k + 1] += part
        grad_raw = (grad_score * key_scale).astype(jnp.bfloat16)
        prob = prob.astype(jnp.bfloat16)
        key_parts = [dot(grad_raw[own[i]], keys[i][64:], ((0,), (0,))) for i in range(blocks)]
        value_parts = [dot(prob[own[i]], grads[own[i]], ((0,), (0,))) for i in range(blocks)]
        query_parts = [dot(grad_raw[own[i]], keys[i], ((1,), (0,))) for i in range(blocks)]
        key_sums = [key_parts[0][:64]] + [
            key_parts[i][64:] + query_parts[i] + (key_parts[i + 1][:64] if i + 1 < blocks else 0.0)
            for i in range(blocks)
        ]
        value_sums = [value_parts[0][:64]] + [
            value_parts[i][64:] + (value_parts[i + 1][:64] if i + 1 < blocks else 0.0)
            for i in range(blocks)
        ]
        for index in range(blocks):
            rows = pl.ds(pl.multiple_of(first * 128 + index * 64, 64), 64)
            sums[rows, :128] = key_sums[index + 1]
            sums[rows, 128:] = value_sums[index + 1]
        for k in range(unroll):
            scale_sums[pl.ds(first + k, 1), :] = scale_parts[k + 1]
        before = jnp.where(step == 0, tiles, numbers[0])
        rows = pl.ds(pl.multiple_of(before * 128 + 64, 64), 64)
        sums[rows, :128] += key_sums[0]
        sums[rows, 128:] += value_sums[0]
        scale_sums[pl.ds(before, 1), :] += scale_parts[0]
        return carry

    lax.fori_loop(0, tiles // unroll, step_tiles, 0)
    sums[end - 128 : end, :] += sums[end : end + 128, :]
    scale_sums[pl.ds(tiles - 1, 1), :] += scale_sums[pl.ds(tiles, 1), :]

    def finish(step, carry):
        for part in range(2):
            tile = step * 2 + part
            rows = rows_of(tile)
            start = pl.multiple_of(tile * 128 + 64, 64)
            keys, mean_square, scale = key_scales(shared[pl.ds(start, 128), :])
            factor = down(scale_sums[pl.ds(tile, 1), :]) * (scale / (mean_square * HEAD_DIM))
            sums[rows, :128] -= factor * keys
        return carry

    lax.fori_loop(0, tiles // 2, finish, 0)


VMEM = pl.BlockSpec(memory_space=pltpu.VMEM)
ANY = pl.BlockSpec(memory_space=pl.ANY)


def narrow(ref, index):
    return ref.at[:, index, :, pl.ds(0, HEAD_DIM)]


def normal_parts(rows):
    center = jnp.mean(rows, axis=-1, keepdims=True)
    offset = rows - center
    spread = jnp.mean(offset * offset, axis=-1, keepdims=True)
    inverse = lax.rsqrt(spread + 1e-05)
    return offset * inverse, inverse


def norm_back(grad, rows, gain):
    unit, inverse = normal_parts(rows)
    scaled = grad * gain
    shared = jnp.mean(scaled, axis=-1, keepdims=True)
    along = jnp.mean(scaled * unit, axis=-1, keepdims=True)
    return (
        (scaled - shared - unit * along) * inverse,
        jnp.sum(grad * unit, axis=0, keepdims=True),
        jnp.sum(grad, axis=0, keepdims=True),
    )


def gelu_parts(rows):
    below = 0.5 * (1.0 + lax.erf(rows * 0.7071067811865476))
    bell = jnp.exp(-0.5 * rows * rows) * 0.3989422804014327
    return rows * below, below + rows * bell


def open_part(
    links, planes,
    sort_order, sort_place, gain_a_in, shift_a_in, gain_f_in, shift_f_in, bias_up_in, bias_down_in,
    x2, wqk, wv, wo, wup, wdown, g2,
    ints, all_ints, floats, all_floats, gains, bias_up, order_rows, place_rows, order_s, place_s, normed, df,
    wqk_line, wv_line, wo_line, wup_rows, wqk_pair, wv_pair, heads, head_table, table, sums,
    shared, values, total_sorted, mixed_home, total_home, last_scale,
    wo_all, wup_part, wdown_part, df_plane, mixed_in, total_in,
):
    low, full = jnp.bfloat16, jnp.float32
    sub = links.y * 2 + links.core
    tiles = planes * 8
    ints[...] = jnp.concatenate([sort_order[...], sort_place[...]], axis=0)
    lane = lax.broadcasted_iota(jnp.int32, (1, 128), 1) // 32

    def spread(vector):
        wide = jnp.concatenate([vector[...].astype(full)] * 4, axis=1)
        return jnp.where(lane == sub, wide, 0.0)

    floats[...] = jnp.concatenate(
        [spread(v) for v in (gain_a_in, shift_a_in, gain_f_in, shift_f_in, bias_down_in)]
        + [bias_up_in[...].astype(full), jnp.zeros((2, 128), full)],
        axis=0,
    )
    df[...] = g2[...].astype(low)
    links.meet()
    share_floats = everywhere(links, floats, all_floats)
    next(share_floats)
    share_ints = everywhere(links, ints, all_ints)
    next(share_ints)

    def pair_columns(ref, z):
        return ref.at[:, pl.ds(pl.multiple_of(z * 256, 256), 256)]

    pair_shares = [
        along_z(pair_columns, block)(links, a, b) for a, b in ((wqk, wqk_line), (wv, wv_line))
    ]
    for transfer in pair_shares:
        next(transfer)
    wo_share = along_z(whole, block)(links, wo, wo_line)
    next(wo_share)
    df_share = over_chips(whole, block)(links, df, df_plane)
    next(df_share)
    unit, _ = normal_parts(x2[...])
    next(share_floats)

    def upper_columns(chunk):
        def columns(ref, p):
            return ref.at[:, pl.ds(pl.multiple_of((chunk * 8 + p) * 128, 128), 128)]

        def landing(ref, p):
            return ref.at[p, :, pl.ds(chunk * 128, 128)]

        return over_plane(columns, landing)

    drive([share_floats])

    def vector_of(row, z_step=2):
        chunks = []
        for chunk in range(8):
            z, x = chunk // 2, chunk % 2
            parts = [all_floats[z, x * 4 + u, row : row + 1, :] for u in range(4)]
            chunks.append(parts[0] + parts[1] + parts[2] + parts[3])
        return jnp.concatenate(chunks, axis=1)

    gain, shift = vector_of(0), vector_of(1)
    normed[links.z] = (unit * gain + shift).astype(low)
    normed_chain = Chain(links, normed)
    for transfer in pair_shares:
        drive([transfer])
    pair_shares = [
        over_chips(whole, second)(links, a, b) for a, b in ((wqk_line, wqk_pair), (wv_line, wv_pair))
    ]
    for transfer in pair_shares:
        next(transfer)
    next(share_ints)
    upper_shares = [upper_columns(chunk)(links, wup, wup_rows) for chunk in range(planes)]
    for transfer in upper_shares:
        next(transfer)
    for transfer in pair_shares:
        next(transfer)
    gains[0:1, :] = gain
    gains[1:2, :] = shift
    for row in (2, 3, 4):
        gains[row : row + 1, :] = vector_of(row)
    for z in range(planes):
        bias_up[:, z * 128 : (z + 1) * 128] = all_floats[z, links.p, 5:6, :]
    drive(pair_shares)
    drive([share_ints])
    for z in range(planes):
        for p in range(8):
            tile = z * 8 + p
            order_rows[tile : tile + 1, :] = all_ints[z, p, pl.ds(sub, 1), :]
            place_rows[tile : tile + 1, :] = all_ints[z, p, pl.ds(sub + 4, 1), :]
    to_scalars = [links.keep(order_rows, order_s), links.keep(place_rows, place_s)]

    def head_columns(z):
        def columns(ref, p):
            return ref.at[z, :, pl.ds(pl.multiple_of((p // 4) * 256, 256), 256)]

        return columns

    def landing(z):
        return lambda ref, p: ref.at[z, p]

    def project(z):
        rows = normed[z]
        for weights, offset in ((wqk_pair, 0), (wv_pair, 128)):
            result = dot(rows, weights[...].reshape(-1, 256), ((1,), (0,))).astype(low)
            heads[z, :, offset : offset + 128] = result[:, :128]
            heads[z, :, 256 + offset : 384 + offset] = result[:, 128:]
        transfer = over_chips(head_columns(z), landing(z))(links, heads, head_table)
        next(transfer)
        return transfer

    head_shares = [project(links.z)]
    next(df_share)
    for index in range(3):
        head_shares.append(project(normed_chain.arrive(index)))
        next(head_shares[-2])
    for transfer in upper_shares:
        drive([transfer])
    next(head_shares[-1])
    drive([wo_share])
    wo_share = over_chips(whole, second)(links, wo_line, wo_all)
    for copy in to_scalars:
        copy.wait()
    drive(head_shares)
    shares = [
        df_share,
        along_z(whole, block)(links, wup_rows, wup_part),
        along_z(whole, block)(links, wdown, wdown_part),
    ]
    next(shares[1])
    next(shares[2])
    next(wo_share)

    def load(tile, carry):
        table[rows_of(tile), :] = head_table[tile // 8, lax.rem(tile, 8)].astype(full)
        return carry

    lax.fori_loop(0, tiles, load, 0)
    attend_tiles(
        tiles, 2, order_s, order_rows, table, shared, values, sums, total_sorted, last_scale
    )
    next(wo_share)
    kept = []
    sent = []
    for step in (6, 7, 4, 5, 2, 3, 1, 0):
        device, p = links.near(step)

        def unsort(z, carry):
            totals = []
            for part in range(4):
                picked = pick_tile(sums, place_s, z * 8 + p, part)
                mixed_home[p, z, part * 32 : part * 32 + 32, :] = picked[:, :128].astype(low)
                totals.append(picked[:, 128:])
            total_home[p, pl.ds(z, 1), :] = jnp.concatenate(totals, axis=0).T[:1, :]
            return carry

        lax.fori_loop(0, planes, unsort, 0)
        for here, there in ((mixed_home, mixed_in), (total_home, total_in)):
            source, target = here.at[p], there.at[links.p]
            if step:
                sent.append(links.push(source, target, device))
            else:
                kept.append(links.keep(source, target))
    normed_chain.finish()
    for copy in kept + sent:
        copy.wait()
    return wo_share, shares


def feed_part(
    links, planes, wo_share, weight_shares,
    x1, g1, y1_out, g1_out, gains, bias_up, sums, table, head_table, mixed_home, total_home,
    wo_all, wup_part, wdown_part, df_plane, mixed_in, total_in, dtotal_in, attended, arrived, h2, act, dpre,
    kept, from_sibling, to_chip, from_chip, up_grad, up_parts, down_grad, down_parts, dout, datt_out, datt,
    up_bias, feed_gain, feed_shift, y2_parts, out_sibling,
):
    low, full = jnp.bfloat16, jnp.float32

    def weight_rows(head, z):
        return pl.ds(pl.multiple_of((head * planes + z) * 128, 128), 128)

    def wo_rows(z):
        return wo_all[z].reshape(256, -1)

    def combine(z, carry):
        for x in range(2):
            totals = [down(total_in[x * 4 + u, pl.ds(z, 1), :]) for u in range(4)]
            highest = jnp.maximum(
                jnp.maximum(totals[0], totals[1]), jnp.maximum(totals[2], totals[3])
            )
            parts = [jnp.exp(t - highest) for t in totals]
            inverse = 1.0 / (parts[0] + parts[1] + parts[2] + parts[3])
            result = 0.0
            for u in range(4):
                weight = parts[u] * inverse
                sums[weight_rows(x * 4 + u, z), :128] = weight
                result += weight * mixed_in[x * 4 + u, z].astype(full)
            attended[z, :, x * 128 : (x + 1) * 128] = result.astype(low)
        return carry

    lax.fori_loop(0, planes, combine, 0)
    share = along_z(block, block)(links, attended, arrived)
    next(share)
    drive([wo_share])
    drive([share])
    y1 = x1[...]
    for z in range(planes):
        y1 += dot(arrived[z], wo_rows(z), ((1,), (0,)))
    y1_out[...] = y1
    unit, _ = normal_parts(y1)
    own_rows = pl.ds(pl.multiple_of(links.p * 128, 128), 128)
    h2[own_rows, :] = (unit * gains[2:3, :] + gains[3:4, :]).astype(low)

    sibling, _ = links.near(1)
    own_h2 = h2.at[own_rows, :]
    direct = {step: links.push(own_h2, own_h2, links.near(step)[0]) for step in (2, 4)}
    handed = {0: links.push(own_h2, own_h2, sibling)}
    drive(weight_shares)

    half = wup_part.shape[3] // 2

    def upper_back(part, carry):
        rows = pl.ds(pl.multiple_of(part * 256, 256), 256)
        grad = df_plane[pl.ds(part * 2, 2)].reshape(256, -1)
        result = dot(grad, wdown_part[...].reshape(half * 2, -1), ((1,), (1,)))
        table[rows, :] = result[:, :half]
        table[pl.ds(pl.multiple_of(1024 + part * 256, 256), 256), :] = result[:, half:]
        return carry

    lax.fori_loop(0, 4, upper_back, 0)

    def pass_on(step):
        direct[step].wait_recv()
        block_rows = h2.at[rows_of(links.near(step)[1]), :]
        handed[step] = links.push(block_rows, block_rows, sibling)

    def feed(slot, step):
        handed[step].wait_recv()
        chip = links.near(step)[1] // 2
        rows = pl.ds(pl.multiple_of(chip * 256, 256), 256)
        before = dot(h2[rows, :], wup_part[...].reshape(-1, 2 * half), ((1,), (0,))) + bias_up[...]
        value, slope = gelu_parts(before)
        act[rows, :] = value.astype(low)
        grad = jnp.concatenate(
            [table[rows, :], table[pl.ds(pl.multiple_of(1024 + chip * 256, 256), 256), :]], axis=1
        )
        grad = (grad * slope).astype(low)
        dpre[rows, :] = grad
        kept[slot] = dot(grad, wup_part[...].reshape(-1, 2 * half), ((1,), (1,))).reshape(2, 128, -1).astype(low)
        return links.push(kept.at[slot, 1 - links.core], from_sibling.at[slot], sibling)

    def chip_sum(slot, step, traded):
        traded.wait_recv()
        result = kept[slot, links.core].astype(full) + from_sibling[slot].astype(full)
        if slot == 0:
            return result
        to_chip[slot - 1] = result.astype(low)
        return links.push(to_chip.at[slot - 1], from_chip.at[slot - 1], links.near(step)[0])

    traded = [feed(0, 0)]
    for step in (2, 4):
        direct[step].wait_send()
    direct[6] = links.push(own_h2, own_h2, links.near(6)[0])
    pass_on(2)
    pass_on(4)
    traded.append(feed(1, 2))
    sent = [chip_sum(1, 2, traded[1])]
    pass_on(6)
    traded.append(feed(2, 4))
    sent.append(chip_sum(2, 4, traded[2]))
    traded.append(feed(3, 6))
    sent.append(chip_sum(3, 6, traded[3]))
    own_sum = chip_sum(0, 0, traded[0])

    def upper_grad(part, carry):
        rows = pl.ds(pl.multiple_of(part * 256, 256), 256)
        up_grad[part] = dot(h2[:, rows], dpre[...], ((0,), (0,))).astype(low)
        return carry

    lax.fori_loop(0, planes, upper_grad, 0)

    def lower_grad(part, carry):
        rows = pl.ds(pl.multiple_of(part * 128, 128), 128)
        down_grad[part] = dot(act[:, rows], df_plane[...].reshape(act.shape[0], -1), ((0,), (0,))).astype(low)
        return carry

    lax.fori_loop(0, planes, lower_grad, 0)

    def lower(part, carry):
        rows = pl.ds(pl.multiple_of(part * 128, 128), 128)
        df_plane[part] = dot(
            act[rows, :], wdown_part[...].reshape(2 * half, -1), ((1,), (0,))
        ).astype(low)
        return carry

    lax.fori_loop(0, 8, lower, 0)
    share_y2 = over_plane(block, block)(links, df_plane, y2_parts)
    next(share_y2)
    for copy in sent:
        copy.wait_recv()
    grad = own_sum + (
        from_chip[0].astype(full) + from_chip[1].astype(full) + from_chip[2].astype(full)
    )
    part, gain_grad, shift_grad = norm_back(grad, y1_out[...], gains[2:3, :])
    feed_gain[...] = gain_grad
    feed_shift[...] = shift_grad
    g1_new = g1[...] + part
    g1_out[...] = g1_new
    dout[...] = g1_new.astype(low)
    for z in range(planes):
        datt_out[z] = dot(dout[...], wo_rows(z), ((1,), (1,))).astype(low)
    share = along_z(block, block)(links, datt_out, datt)
    next(share)
    for copy in [direct[6]] + list(handed.values()):
        copy.wait_send()
    for z in range(planes):
        part = dot(arrived[z], dout[...], ((0,), (0,))).astype(low)
        for p in range(8):
            row = p * 128 + z * 32
            h2[row : row + 32, :] = part[p * 32 : p * 32 + 32]
    out_traded = [
        links.push(
            h2.at[rows_of(links.near(step)[1] // 2 * 2 + 1 - links.core), :],
            out_sibling.at[slot],
            sibling,
        )
        for slot, step in enumerate((6, 4, 2, 0))
    ]
    up_bias[...] = jnp.sum(dpre[...].astype(full), axis=0, keepdims=True)
    drive([share])
    share_up = along_z(block, block)(links, up_grad, up_parts)
    next(share_up)
    share_down = along_z(block, block)(links, down_grad, down_parts)
    next(share_down)
    def combine_back(z, carry):
        for x in range(2):
            grad = datt[z, :, x * 128 : (x + 1) * 128].astype(full)
            chosen = [sums[weight_rows(x * 4 + u, z), :128] for u in range(4)]
            inner = [
                jnp.sum(grad * mixed_in[x * 4 + u, z].astype(full), axis=-1, keepdims=True)
                for u in range(4)
            ]
            mean = sum(chosen[u] * inner[u] for u in range(4))
            for u in range(4):
                mixed_home[x * 4 + u, z] = (chosen[u] * grad).astype(low)
                change = (chosen[u] * (inner[u] - mean)).astype(low).astype(full)
                total_home[x * 4 + u, pl.ds(z, 1), :] = change.T[:1, :]
        return carry

    lax.fori_loop(0, planes, combine_back, 0)
    shares = [
        over_plane(block, narrow)(links, mixed_home, head_table),
        over_plane(block, block)(links, total_home, dtotal_in),
    ]
    for transfer in shares:
        next(transfer)
    for copy in traded + sent:
        copy.wait_send()
    return shares, share_y2, share_up, share_down, out_traded


def close_part(
    links, planes, shares, share_y2, share_up, share_down, out_traded,
    x2, g2, y2_out, g2_out, shared_grad_out, value_grad_out, out_grad_out, up_out, down_out, vectors_out,
    gains, order_rows, order_s, place_s, normed, wqk_pair, wv_pair, shared, values, total_sorted, head_table,
    table, sums, last_scale, dtotal_in, attended, df_plane, h2, wup_part, wdown_part, up_parts, down_grad,
    down_parts, kept, from_sibling, to_chip, from_chip, up_bias, feed_gain, feed_shift, grad_sorted,
    grad_total_sorted, scale_sums, up_sum, up_arrived, dshared, dvalues, de, out_sent, out_arrived,
    weight_arrived, weight_sum, weight_final, tiles_sent, tiles_arrived, tile, tile_line, y2_parts,
    out_sibling, out_chip,
):
    low, full = jnp.bfloat16, jnp.float32
    tiles = planes * 8
    line = planes * 128
    out_sums = []
    for slot, step in enumerate((6, 4, 2, 0)):
        out_traded[slot].wait()
        rows = rows_of(links.near(step)[1] // 2 * 2 + links.core)
        total = h2[rows, :].astype(full) + out_sibling[slot].astype(full)
        h2[rows, :] = total.astype(low)
        out_sums.append(rows)
    drive(shares)
    out_pushed = [
        links.push(h2.at[out_sums[slot], :], out_chip.at[slot], links.near(step)[0])
        for slot, step in enumerate((6, 4, 2))
    ]

    def load(index, carry):
        z, p = index // 8, lax.rem(index, 8)
        table[rows_of(index), :128] = head_table[z, p, :, :HEAD_DIM].astype(full)
        table[rows_of(index), 128:] = down(dtotal_in[p, pl.ds(z, 1), :])
        return carry

    lax.fori_loop(0, tiles, load, 0)
    attend_back_tiles(
        tiles, 4, order_s, order_rows, table, shared, values, total_sorted,
        grad_sorted, grad_total_sorted, sums, scale_sums, last_scale,
    )
    sibling, _ = links.near(1)

    def unsort(slot, step):
        chip = links.near(step)[1] // 2
        for core, goal in ((0, 1 - links.core), (1, links.core)):

            def rows(z, carry):
                columns = pl.ds(pl.multiple_of(z * 256, 256), 256)
                for part in range(4):
                    picked = pick_tile(sums, place_s, z * 8 + chip * 2 + goal, part)
                    kept[slot, core, part * 32 : part * 32 + 32, columns] = picked.astype(low)
                return carry

            lax.fori_loop(0, planes, rows, 0)
            if core == 0:
                traded = links.push(kept.at[slot, 0], from_sibling.at[slot], sibling)
        return traded

    def chip_sum(slot, step, traded):
        traded.wait_recv()
        result = kept[slot, 1].astype(full) + from_sibling[slot].astype(full)
        if step == 0:
            return result
        to_chip[slot] = result.astype(low)
        return links.push(to_chip.at[slot], from_chip.at[slot], links.near(step)[0])

    steps = (6, 4, 2, 0)
    traded, sent = [], []
    for slot, step in enumerate(steps):
        traded.append(unsort(slot, step))
        if slot:
            sent.append(chip_sum(slot - 1, steps[slot - 1], traded[slot - 1]))
    total = h2[out_sums[3], :].astype(full)
    for slot, copy in enumerate(out_pushed):
        copy.wait()
        total += out_chip[slot].astype(full)
    out_sent[...] = total.astype(low).reshape(out_sent.shape)
    own_sum = chip_sum(3, 0, traded[3])
    share_out = along_z(block, block)(links, out_sent, out_arrived)
    next(share_out)
    own_columns = pl.ds(pl.multiple_of(links.x * 128, 128), 128)
    far_columns = pl.ds(pl.multiple_of((1 - links.x) * 128, 128), 128)

    def settle_sum(columns, result):
        for z in range(planes):
            part = result[:, z * 256 : z * 256 + 256].astype(low)
            dshared[z * 128 : z * 128 + 128, columns] = part[:, :128]
            dvalues[z * 128 : z * 128 + 128, columns] = part[:, 128:]

    sent[2].wait_recv()
    settle_sum(own_columns, own_sum + from_chip[2].astype(full))
    sent[1].wait_recv()
    sent[0].wait_recv()
    settle_sum(far_columns, from_chip[1].astype(full) + from_chip[0].astype(full))
    all_wqk, all_wv = wqk_pair[...].reshape(-1, 256), wv_pair[...].reshape(-1, 256)
    drive([share_down])

    def input_grad(z, carry):
        rows = rows_of(z)
        down_grad[z] = (
            dot(dshared[rows, :], all_wqk, ((1,), (1,))) + dot(dvalues[rows, :], all_wv, ((1,), (1,)))
        ).astype(low)
        return carry

    lax.fori_loop(0, planes, input_grad, 0)
    share_de = along_z(block, block)(links, down_grad, de)
    next(share_de)
    drive([share_up])
    up_sum[...] = sum(up_parts[z].astype(full) for z in range(planes)).reshape(up_sum.shape)
    share_up = over_plane(block, block)(links, up_sum, up_arrived)
    next(share_up)
    all_normed = normed[...].reshape(line, -1)
    for index, grad in enumerate((dshared, dvalues)):
        wup_part[:, :, :, index * 256 : index * 256 + 256] = (
            dot(all_normed, grad[...], ((0,), (0,))).astype(low).reshape(wup_part.shape[:3] + (256,))
        )
    share_weights = over_plane(second, block)(links, wup_part, weight_arrived)
    next(share_weights)
    drive([share_y2])
    y2_out[...] = x2[...] + (
        sum(y2_parts[p].astype(full) for p in range(8)) + gains[4:5, :]
    )
    drive([share_up])
    for p in range(8):
        for z in range(planes):
            up_out[:, (z * 8 + p) * 128 : (z * 8 + p + 1) * 128] = up_arrived[
                p, :, z * 128 : (z + 1) * 128
            ]
    down_out[...] = sum(down_parts[z].astype(full) for z in range(planes))
    drive([share_out])
    out_grad_out[...] = sum(out_arrived[z].astype(full) for z in range(planes))
    down_bias = jnp.sum(g2[...].astype(low).astype(full), axis=0, keepdims=True)
    drive([share_weights])
    weight_sum[...] = sum(weight_arrived[p].astype(full) for p in range(8)).astype(low)

    share_final = along_z(block, block)(links, weight_sum, weight_final)
    next(share_final)
    drive([share_de])
    part, gain_grad, shift_grad = norm_back(
        sum(de[z].astype(full) for z in range(planes)), x2[...], gains[0:1, :]
    )
    vectors = [gain_grad, shift_grad, feed_gain[...], feed_shift[...], down_bias]
    for x in range(2):
        for index, vector in enumerate(vectors):
            for z in range(planes):
                chunk = (z * 2 + x) * 128
                row = index * planes + z
                tiles_sent[x, row : row + 1, :] = vector[:, chunk : chunk + 128]
        tiles_sent[x, 5 * planes :, :] = jnp.zeros((24 - 5 * planes, 128), full)

    def of_x(ref, p):
        return ref.at[p // 4]

    share_tiles = over_plane(of_x, block)(links, tiles_sent, tiles_arrived)
    next(share_tiles)
    g2_out[...] = g2[...] + part
    drive([share_tiles])
    tile[...] = jnp.sum(tiles_arrived[...], axis=0)
    for z in range(planes):
        tile[5 * planes + z : 5 * planes + z + 1, :] = up_bias[:, z * 128 : (z + 1) * 128]
    share_tile = along_z(whole, block)(links, tile, tile_line)
    next(share_tile)
    drive([share_final])
    for z in range(planes):
        columns = slice(z * 256, z * 256 + 256)
        shared_grad_out[:, columns] = weight_final[z, :, :256].astype(full)
        value_grad_out[:, columns] = weight_final[z, :, 256:].astype(full)
    drive([share_tile])
    tile[...] = jnp.sum(tile_line[...], axis=0)
    for index in range(6):
        vectors_out[index : index + 1, :] = tile[pl.ds(index * planes + links.z, 1), :]
    vectors_out[6:8, :] = jnp.zeros((2, 128), full)
    for copy in traded + sent:
        copy.wait_send()


LAYER_INPUTS = (
    "sort_order", "sort_place", "gain_a_in", "shift_a_in", "gain_f_in", "shift_f_in", "bias_up_in",
    "bias_down_in", "x2", "wqk", "wv", "wo", "wup", "wdown", "g2", "x1", "g1",
)
LAYER_OUTPUTS = (
    "y1_out", "y2_out", "g1_out", "g2_out", "shared_grad_out", "value_grad_out", "out_grad_out",
    "up_out", "down_out", "vectors_out",
)
OPEN_REFS = (
    "sort_order", "sort_place", "gain_a_in", "shift_a_in", "gain_f_in", "shift_f_in", "bias_up_in",
    "bias_down_in", "x2", "wqk", "wv", "wo", "wup", "wdown", "g2", "ints", "all_ints", "floats",
    "all_floats", "gains", "bias_up", "order_rows", "place_rows", "order_s", "place_s", "normed",
    "df", "wqk_line", "wv_line", "wo_line", "wup_rows", "wqk_pair", "wv_pair", "heads",
    "head_table", "table", "sums", "shared", "values", "total_sorted", "mixed_home", "total_home",
    "last_scale", "wo_all", "wup_part", "wdown_part", "df_plane", "mixed_in", "total_in",
)
FEED_REFS = (
    "x1", "g1", "y1_out", "g1_out", "gains", "bias_up", "sums", "table", "head_table", "mixed_home",
    "total_home", "wo_all", "wup_part", "wdown_part", "df_plane", "mixed_in", "total_in",
    "dtotal_in", "attended", "arrived", "h2", "act", "dpre", "kept", "from_sibling", "to_chip",
    "from_chip", "up_grad", "up_parts", "down_grad", "down_parts", "dout", "datt_out", "datt",
    "up_bias", "feed_gain", "feed_shift", "y2_parts", "out_sibling",
)
CLOSE_REFS = (
    "x2", "g2", "y2_out", "g2_out", "shared_grad_out", "value_grad_out", "out_grad_out", "up_out",
    "down_out", "vectors_out", "gains", "order_rows", "order_s", "place_s", "normed", "wqk_pair",
    "wv_pair", "shared", "values", "total_sorted", "head_table", "table", "sums", "last_scale",
    "dtotal_in", "attended", "df_plane", "h2", "wup_part", "wdown_part", "up_parts", "down_grad",
    "down_parts", "kept", "from_sibling", "to_chip", "from_chip", "up_bias", "feed_gain",
    "feed_shift", "grad_sorted", "grad_total_sorted", "scale_sums", "up_sum", "up_arrived",
    "dshared", "dvalues", "de", "out_sent", "out_arrived", "weight_arrived", "weight_sum",
    "weight_final", "tiles_sent", "tiles_arrived", "tile", "tile_line",
    "y2_parts", "out_sibling", "out_chip",
)


def layer_scratch(planes, rows, width, own, part):
    low, full, whole_number = jnp.bfloat16, jnp.float32, jnp.int32
    tiles = planes * 8
    tokens = tiles * rows
    return {
        "ints": pltpu.VMEM((8, rows), whole_number),
        "all_ints": pltpu.VMEM((planes, 8, 8, rows), whole_number),
        "floats": pltpu.VMEM((8, rows), full),
        "all_floats": pltpu.VMEM((planes, 8, 8, rows), full),
        "gains": pltpu.VMEM((8, width), full),
        "bias_up": pltpu.VMEM((1, part), full),
        "order_rows": pltpu.VMEM((tiles, rows), whole_number),
        "place_rows": pltpu.VMEM((tiles, rows), whole_number),
        "order_s": pltpu.SMEM((tiles, rows), whole_number),
        "place_s": pltpu.SMEM((tiles, rows), whole_number),
        "normed": pltpu.VMEM((planes, rows, width), low),
        "df": pltpu.VMEM((rows, width), low),
        "wqk_line": pltpu.VMEM((planes, own, 256), low),
        "wv_line": pltpu.VMEM((planes, own, 256), low),
        "wo_line": pltpu.VMEM((planes, own, width), low),
        "wup_rows": pltpu.VMEM((8, own, part), low),
        "wqk_pair": pltpu.VMEM((planes, 8, own, 256), low),
        "wv_pair": pltpu.VMEM((planes, 8, own, 256), low),
        "heads": pltpu.VMEM((planes, rows, 512), low),
        "head_table": pltpu.VMEM((planes, 8, rows, 256), low),
        "table": pltpu.VMEM((tokens, 256), full),
        "sums": pltpu.VMEM((tokens + rows, 256), full),
        "shared": pltpu.VMEM((tokens + BLOCK, HEAD_DIM), low),
        "values": pltpu.VMEM((tokens + BLOCK, HEAD_DIM), low),
        "total_sorted": pltpu.VMEM((tokens, HEAD_DIM), full),
        "mixed_home": pltpu.VMEM((8, planes, rows, HEAD_DIM), low),
        "total_home": pltpu.VMEM((8, 8, rows), full),
        "last_scale": pltpu.VMEM((1, rows), full),
        "wo_all": pltpu.VMEM((planes, 8, own, width), low),
        "wup_part": pltpu.VMEM((planes, 8, own, part), low),
        "wdown_part": pltpu.VMEM((planes, rows, width), low),
        "df_plane": pltpu.VMEM((8, rows, width), low),
        "mixed_in": pltpu.VMEM((8, planes, rows, HEAD_DIM), low),
        "total_in": pltpu.VMEM((8, 8, rows), full),
        "dtotal_in": pltpu.VMEM((8, 8, rows), full),
        "attended": pltpu.VMEM((planes, rows, 256), low),
        "arrived": pltpu.VMEM((planes, rows, 256), low),
        "h2": pltpu.VMEM((8 * rows, width), low),
        "act": pltpu.VMEM((8 * rows, part), low),
        "dpre": pltpu.VMEM((8 * rows, part), low),
        "kept": pltpu.VMEM((4, 2, rows, width), low),
        "from_sibling": pltpu.VMEM((4, rows, width), low),
        "to_chip": pltpu.VMEM((3, rows, width), low),
        "from_chip": pltpu.VMEM((3, rows, width), low),
        "up_grad": pltpu.VMEM((planes, width // planes, part), low),
        "up_parts": pltpu.VMEM((planes, width // planes, part), low),
        "down_grad": pltpu.VMEM((planes, rows, width), low),
        "down_parts": pltpu.VMEM((planes, rows, width), low),
        "dout": pltpu.VMEM((rows, width), low),
        "datt_out": pltpu.VMEM((planes, rows, 256), low),
        "datt": pltpu.VMEM((planes, rows, 256), low),
        "up_bias": pltpu.VMEM((1, part), full),
        "feed_gain": pltpu.VMEM((1, width), full),
        "feed_shift": pltpu.VMEM((1, width), full),
        "grad_sorted": pltpu.VMEM((tokens, HEAD_DIM), low),
        "grad_total_sorted": pltpu.VMEM((tokens, HEAD_DIM), full),
        "scale_sums": pltpu.VMEM((tiles + 8, rows), full),
        "up_sum": pltpu.VMEM((8, own, part), full),
        "up_arrived": pltpu.VMEM((8, own, part), full),
        "dshared": pltpu.VMEM((planes * rows, 256), low),
        "dvalues": pltpu.VMEM((planes * rows, 256), low),
        "de": pltpu.VMEM((planes, rows, width), low),
        "out_sent": pltpu.VMEM((planes, own, width), low),
        "out_arrived": pltpu.VMEM((planes, own, width), low),
        "y2_parts": pltpu.VMEM((8, rows, width), low),
        "out_sibling": pltpu.VMEM((4, rows, width), low),
        "out_chip": pltpu.VMEM((3, rows, width), low),
        "weight_arrived": pltpu.VMEM((8, planes, own, 512), low),
        "weight_sum": pltpu.VMEM((planes, own, 512), low),
        "weight_final": pltpu.VMEM((planes, own, 512), low),
        "tiles_sent": pltpu.VMEM((2, 24, rows), full),
        "tiles_arrived": pltpu.VMEM((8, 24, rows), full),
        "tile": pltpu.VMEM((24, rows), full),
        "tile_line": pltpu.VMEM((planes, 24, rows), full),
    }


def layer_kernel(planes, names, *refs):
    links = Links(planes, *refs[len(names) :])
    held = dict(zip(names, refs))
    links.greet()
    shares = open_part(links, planes, *[held[name] for name in OPEN_REFS])
    shares = feed_part(links, planes, *shares, *[held[name] for name in FEED_REFS])
    close_part(links, planes, *shares, *[held[name] for name in CLOSE_REFS])


def layer_stage(arguments, collective_id, planes):
    rows, width = arguments[LAYER_INPUTS.index("x2")].shape
    own, hidden = arguments[LAYER_INPUTS.index("wup")].shape
    shape = jax.ShapeDtypeStruct
    token, weight = shape((rows, width), jnp.float32), shape((own, width), jnp.float32)
    outputs = [token] * 4 + [weight] * 3 + [
        shape((own, hidden), jnp.float32), token, shape((8, rows), jnp.float32)
    ]
    scratch = layer_scratch(planes, rows, width, own, hidden // 8)
    names = LAYER_INPUTS + LAYER_OUTPUTS + tuple(scratch)
    return pl.pallas_call(
        functools.partial(layer_kernel, planes, names),
        out_shape=outputs,
        in_specs=[VMEM] * len(arguments),
        out_specs=[VMEM] * len(outputs),
        scratch_shapes=list(scratch.values()) + link_scratch(),
        compiler_params=pltpu.CompilerParams(
            vmem_limit_bytes=60 << 20, collective_id=collective_id, has_side_effects=True
        ),
        name="layer",
    )(*arguments)


def finish_kernel(
    y1, y2, g1, g2, shared_grad, value_grad, out_grad, up_grad, down_grad, vectors,
    y1_out, y2_out, g1_out, g2_out, gain_a_out, shift_a_out, shared_out, value_out, out_out,
    gain_f_out, shift_f_out, up_out, up_bias_out, down_out, down_bias_out, arrived,
):
    pairs = (
        (y1, y1_out), (y2, y2_out), (g1, g1_out), (g2, g2_out), (shared_grad, shared_out),
        (value_grad, value_out), (out_grad, out_out), (up_grad, up_out), (down_grad, down_out),
    )
    copies = [
        pltpu.make_async_copy(source, target.at[0], arrived.at[index])
        for index, (source, target) in enumerate(pairs)
    ]
    for copy in copies:
        copy.start()
    sub = lax.axis_index("sub")
    rows = vectors[...]
    own = sum(
        jnp.where(sub == u, rows[:, u * 32 : u * 32 + 32], 0.0) for u in range(4)
    )
    for row, target in enumerate((gain_a_out, shift_a_out, gain_f_out, shift_f_out, down_bias_out)):
        target[...] = own[row : row + 1, :]
    up_bias_out[...] = rows[5:6, :]
    for copy in copies:
        copy.wait()


def finish_stage(arguments):
    full = jnp.float32
    large = [(jax.ShapeDtypeStruct((1,) + a.shape, full), ANY) for a in arguments[:-1]]
    y1, y2, g1, g2, shared_grad, value_grad, out_grad, up_grad, down_grad = large
    small = (jax.ShapeDtypeStruct((1, arguments[4].shape[0]), full), VMEM)
    up_bias = (jax.ShapeDtypeStruct((1, arguments[-1].shape[1]), full), VMEM)
    outputs = [
        y1, y2, g1, g2, small, small, shared_grad, value_grad, out_grad, small, small, up_grad,
        up_bias, down_grad, small,
    ]
    return pl.pallas_call(
        finish_kernel,
        out_shape=[o[0] for o in outputs],
        in_specs=[VMEM] * 10,
        out_specs=[o[1] for o in outputs],
        scratch_shapes=[pltpu.SemaphoreType.DMA((9,))],
        name="finish",
    )(*arguments)


def plane_plan(
    n_seq,
    n_sub,
    first_half,
    second_half,
    grad_first,
    grad_second,
    attend_gain,
    attend_shift,
    query_key_weight,
    value_projection_weight,
    output_projection_weight,
    feed_gain,
    feed_shift,
    upper_projection_weight,
    upper_projection_bias,
    lower_projection_weight,
    lower_projection_bias,
    sort_order,
    sort_place,
):
    planes = n_seq // 2
    x1, x2, g1, g2 = (a[0] for a in (first_half, second_half, grad_first, grad_second))
    wqk, wv, wo = query_key_weight[0], value_projection_weight[0], output_projection_weight[0]
    wup, wdown = upper_projection_weight[0], lower_projection_weight[0]
    results = layer_stage(
        (
            sort_order[0, :, 0], sort_place[0, :, 0], attend_gain, attend_shift, feed_gain, feed_shift,
            upper_projection_bias, lower_projection_bias, x2, wqk, wv, wo, wup, wdown, g2, x1, g1,
        ),
        1,
        planes,
    )
    return finish_stage(results)


def on_device(n_seq, n_sub, *arguments):
    sequences, rows, width = arguments[0].shape
    rounds = arguments[-1].shape[1]
    fits = (
        sequences == 1
        and rows == 2 * BLOCK
        and rounds == n_sub
        and HEADS == n_seq
        and width == HEADS * HEAD_DIM
    )
    if fits:
        return plane_plan(n_seq, n_sub, *arguments)
    return general_plan(*arguments)


def solution(mesh):
    return jax.shard_map(
        functools.partial(on_device, mesh.shape["seq"], mesh.shape["sub"]),
        mesh=mesh,
        in_specs=(
            P(None, ("seq", "sub"), None),
            P(None, ("seq", "sub"), None),
            P(None, ("seq", "sub"), None),
            P(None, ("seq", "sub"), None),
            P(None, ("seq", "sub")),
            P(None, ("seq", "sub")),
            P(None, ("seq", "sub"), None),
            P(None, ("seq", "sub"), None),
            P(None, ("seq", "sub"), None),
            P(None, ("seq", "sub")),
            P(None, ("seq", "sub")),
            P(None, ("seq", "sub"), None),
            P(None, ("seq", "sub")),
            P(None, ("seq", "sub"), None),
            P(None, ("seq", "sub")),
            P(None, None, None, ("seq", "sub")),
            P(None, None, None, ("seq", "sub")),
        ),
        out_specs=(
            P(None, ("seq", "sub"), None),
            P(None, ("seq", "sub"), None),
            P(None, ("seq", "sub"), None),
            P(None, ("seq", "sub"), None),
            P(None, ("seq", "sub")),
            P(None, ("seq", "sub")),
            P(None, ("seq", "sub"), None),
            P(None, ("seq", "sub"), None),
            P(None, ("seq", "sub"), None),
            P(None, ("seq", "sub")),
            P(None, ("seq", "sub")),
            P(None, ("seq", "sub"), None),
            P(None, ("seq", "sub")),
            P(None, ("seq", "sub"), None),
            P(None, ("seq", "sub")),
        ),
        check_vma=False,
    )
```

```python
import functools

import jax
import jax.numpy as jnp
from jax import lax
from jax.experimental import pallas as pl
from jax.experimental.pallas import tpu as pltpu
from jax.sharding import PartitionSpec as P

HEADS = 8
HEAD_DIM = 128
BLOCK = 64
LATER = -1000000000.0
SELF = -100000.0


def from_behind(block, axis, distance):
    devices = range(lax.axis_size(axis))
    route = [((i - distance) % len(devices), i) for i in devices]
    return lax.ppermute(block, axis, route)


def layer_norm(value_vectors, scaling, shifts):
    center = jnp.mean(value_vectors, axis=-1, keepdims=True)
    offset = value_vectors - center
    spread = jnp.mean(offset * offset, axis=-1, keepdims=True)
    return offset * lax.rsqrt(spread + 1e-05) * scaling + shifts


def gelu_exact(value_vectors):
    return jax.nn.gelu(value_vectors, approximate=False)


def combine_rounds(outputs, totals):
    highest = jnp.max(totals, axis=0, keepdims=True)
    weights = jnp.exp(totals - highest)
    weights = weights / jnp.sum(weights, axis=0, keepdims=True)
    by_head = outputs.reshape(outputs.shape[:-1] + (totals.shape[-1], -1))
    return jnp.sum(weights[..., None] * by_head, axis=0).reshape(outputs.shape[1:])


def home_slots(places, row_count):
    target = places // row_count
    prior_state = (target[:, None, :] == target[:, :, None]) & (
        places[:, None, :] < places[:, :, None]
    )
    return (target, jnp.sum(prior_state.astype(jnp.int32), axis=2))


def sorted_slots(orders, row_count):
    source = orders // row_count
    ladder = jnp.arange(row_count, dtype=jnp.int32)
    prior_state = (source[:, None, :] == source[:, :, None]) & (
        ladder[None, None, :] < ladder[None, :, None]
    )
    return (source, jnp.sum(prior_state.astype(jnp.int32), axis=2))


def slot_lookup(owners, slot_index, devices, capacity):
    groups, row_count = owners.shape
    flat_index = owners * capacity + slot_index
    lookup = jnp.full((groups, devices * capacity), row_count, jnp.int32)
    filler = jnp.broadcast_to(jnp.arange(row_count, dtype=jnp.int32), (groups, row_count))
    lookup = lookup.at[jnp.arange(groups)[:, None], flat_index].set(filler)
    return jnp.transpose(lookup.reshape(groups, devices, capacity), (1, 0, 2))


def gather_slots(value_vectors, member, lookup):
    padding = jnp.zeros((value_vectors.shape[0], 1) + value_vectors.shape[2:], value_vectors.dtype)
    padded = jnp.concatenate([value_vectors, padding], axis=1)
    return padded[member[None, :, None], lookup]


def settle(received, owners, slot_index):
    return received[owners, jnp.arange(owners.shape[0])[:, None], slot_index]


def build_routes(orders, places, devices, capacity):
    rounds, sequences, row_count = orders.shape
    order_flat = orders.reshape(rounds * sequences, row_count)
    target, home_slot = home_slots(places.reshape(rounds * sequences, row_count), row_count)
    source, sorted_slot = sorted_slots(order_flat, row_count)
    home_lookup = slot_lookup(target, home_slot, devices, capacity)
    back_lookup = slot_lookup(source, sorted_slot, devices, capacity)
    return (target, home_slot, source, sorted_slot, home_lookup, back_lookup, order_flat)


def trade_rows(first_part, second_part):
    return (
        lax.all_to_all(first_part, ("seq", "sub"), split_axis=0, concat_axis=0, tiled=True),
        lax.all_to_all(second_part, ("seq", "sub"), split_axis=0, concat_axis=0, tiled=True),
    )


def trade_results(first_part, second_part):
    return (
        lax.all_to_all(first_part, ("seq", "sub"), split_axis=0, concat_axis=0, tiled=True),
        lax.all_to_all(second_part, ("seq", "sub"), split_axis=0, concat_axis=0, tiled=True),
    )


def window(rows_here, rows_left):
    groups = rows_here.shape[0]
    extended = jnp.concatenate([rows_left, rows_here], axis=1)
    extended = extended.reshape((groups, -1, BLOCK) + rows_here.shape[2:])
    return jnp.concatenate([extended[:, :-1], extended[:, 1:]], axis=2)


def score_parts(shared_rows, order_rows, halo_shared, halo_order):
    groups, row_count, features = shared_rows.shape
    blocks = row_count // BLOCK
    queries = shared_rows.reshape(groups, blocks, BLOCK, HEADS, HEAD_DIM)
    key_rows = window(shared_rows, halo_shared).reshape(groups, blocks, 2 * BLOCK, HEADS, HEAD_DIM)
    key_float = key_rows.astype(jnp.float32)
    mean_square = jnp.mean(key_float * key_float, axis=-1) + 1e-06
    key_scale = lax.rsqrt(mean_square) / HEAD_DIM
    raw_scores = jnp.einsum(
        "gcqhd,gckhd->gchqk", queries, key_rows, preferred_element_type=jnp.float32
    )
    query_pos = order_rows.reshape(groups, blocks, BLOCK)
    key_pos = window(order_rows, halo_order)
    is_later = (key_pos[:, :, None, :] > query_pos[:, :, :, None])[:, :, None]
    is_self = (key_pos[:, :, None, :] == query_pos[:, :, :, None])[:, :, None]
    scale_row = jnp.transpose(key_scale, (0, 1, 3, 2))[:, :, :, None, :]
    scores = jnp.where(
        is_later, -1000000000.0, jnp.where(is_self, -100000.0, raw_scores * scale_row)
    )
    highest = jnp.max(scores, axis=-1, keepdims=True)
    log_total = highest + jnp.log(jnp.sum(jnp.exp(scores - highest), axis=-1, keepdims=True))
    probability = jnp.exp(scores - log_total)
    return (
        queries,
        key_rows,
        key_float,
        mean_square,
        key_scale,
        scale_row,
        raw_scores,
        is_later | is_self,
        log_total,
        probability,
    )


def attend(shared_rows, value_rows, order_rows, halo):
    halo_shared, halo_value, halo_order = halo
    parts = score_parts(shared_rows, order_rows, halo_shared, halo_order)
    groups, row_count, features = shared_rows.shape
    value_keys = window(value_rows, halo_value).reshape(
        groups, row_count // BLOCK, 2 * BLOCK, HEADS, HEAD_DIM
    )
    mixed = jnp.einsum(
        "gchqk,gckhd->gcqhd",
        parts[9].astype(jnp.bfloat16),
        value_keys,
        preferred_element_type=jnp.float32,
    )
    log_total = jnp.transpose(parts[8][..., 0], (0, 1, 3, 2)).reshape(groups, row_count, HEADS)
    return (mixed.reshape(groups, row_count, features), log_total)


def fold_window(grads_window, groups, row_count, features):
    grads_window = grads_window.reshape(groups, row_count // BLOCK, 2 * BLOCK, features)
    empty = jnp.zeros((groups, 1, BLOCK, features), jnp.float32)
    extended = jnp.concatenate([grads_window[:, :, :BLOCK], empty], axis=1) + jnp.concatenate(
        [empty, grads_window[:, :, BLOCK:]], axis=1
    )
    return (extended[:, 1:].reshape(groups, row_count, features), extended[:, 0])


def attend_back(shared_rows, value_rows, order_rows, halo, grad_out, grad_total):
    halo_shared, halo_value, halo_order = halo
    (
        queries,
        key_rows,
        key_float,
        mean_square,
        key_scale,
        scale_row,
        raw_scores,
        masked,
        log_total,
        probability,
    ) = score_parts(shared_rows, order_rows, halo_shared, halo_order)
    groups, row_count, features = shared_rows.shape
    blocks = row_count // BLOCK
    value_keys = window(value_rows, halo_value).reshape(groups, blocks, 2 * BLOCK, HEADS, HEAD_DIM)
    prob_low = probability.astype(jnp.bfloat16)
    grad_heads = grad_out.reshape(groups, blocks, BLOCK, HEADS, HEAD_DIM)
    grad_log = jnp.transpose(
        grad_total.astype(jnp.float32).reshape(groups, blocks, BLOCK, HEADS), (0, 1, 3, 2)
    )[..., None]
    grad_prob = jnp.einsum(
        "gcqhd,gckhd->gchqk", grad_heads, value_keys, preferred_element_type=jnp.float32
    )
    inner = jnp.sum(probability * grad_prob, axis=-1, keepdims=True)
    grad_score = jnp.where(masked, 0.0, probability * (grad_prob - inner + grad_log))
    grad_scale = jnp.transpose(jnp.sum(grad_score * raw_scores, axis=3), (0, 1, 3, 2))
    grad_raw = (grad_score * scale_row).astype(jnp.bfloat16)
    grad_query = jnp.einsum(
        "gchqk,gckhd->gcqhd", grad_raw, key_rows, preferred_element_type=jnp.float32
    )
    grad_key = jnp.einsum(
        "gchqk,gcqhd->gckhd", grad_raw, queries, preferred_element_type=jnp.float32
    )
    grad_key = grad_key - (grad_scale * key_scale / mean_square)[..., None] * key_float / HEAD_DIM
    grad_value = jnp.einsum(
        "gchqk,gcqhd->gckhd", prob_low, grad_heads, preferred_element_type=jnp.float32
    )
    key_home, key_left = fold_window(grad_key, groups, row_count, features)
    value_home, value_left = fold_window(grad_value, groups, row_count, features)
    back_key, back_value = from_behind((key_left, value_left), ("seq", "sub"), -1)
    grad_shared = grad_query.reshape(groups, row_count, features) + key_home
    grad_shared = grad_shared.at[:, row_count - BLOCK :].add(back_key)
    grad_values = value_home.at[:, row_count - BLOCK :].add(back_value)
    return (grad_shared, grad_values)


def sorted_attention(shared_query_key, value_vectors, routes):
    target, home_slot, source, sorted_slot, home_lookup, back_lookup, order_flat = routes
    groups = target.shape[0]
    member = jnp.arange(groups) % shared_query_key.shape[0]
    got_shared, got_values = trade_rows(
        gather_slots(shared_query_key, member, home_lookup),
        gather_slots(value_vectors, member, home_lookup),
    )
    shared_rows = settle(got_shared, source, sorted_slot)
    value_rows = settle(got_values, source, sorted_slot)
    halo = from_behind(
        (shared_rows[:, -BLOCK:], value_rows[:, -BLOCK:], order_flat[:, -BLOCK:]), ("seq", "sub"), 1
    )
    mixed, log_total = attend(shared_rows, value_rows, order_flat, halo)
    all_groups = jnp.arange(groups)
    got_mixed, got_total = trade_results(
        gather_slots(mixed, all_groups, back_lookup),
        gather_slots(log_total, all_groups, back_lookup),
    )
    return (
        settle(got_mixed, target, home_slot),
        settle(got_total, target, home_slot),
        (shared_rows, value_rows, halo),
    )


def round_outputs(normalized_input, query_key_weight, value_projection_weight, routes, rounds):
    shared_query_key = jnp.einsum(
        "srd,de->sre", normalized_input, query_key_weight, preferred_element_type=jnp.float32
    ).astype(jnp.bfloat16)
    value_vectors = jnp.einsum(
        "srd,de->sre", normalized_input, value_projection_weight, preferred_element_type=jnp.float32
    ).astype(jnp.bfloat16)
    mixed, log_total, kept = sorted_attention(shared_query_key, value_vectors, routes)
    sequences, row_count, features = normalized_input.shape
    outputs = mixed.reshape(rounds, sequences, row_count, features)
    totals = log_total.reshape(rounds, sequences, row_count, HEADS)
    return (shared_query_key, value_vectors, outputs, totals, kept)


def collect(weight_stack, layer_index):
    (
        attend_gain,
        attend_shift,
        query_key_weight,
        value_projection_weight,
        output_projection_weight,
        feed_gain,
        feed_shift,
        upper_projection_weight,
        upper_projection_bias,
        lower_projection_weight,
        lower_projection_bias,
    ) = tuple((shard_piece[layer_index] for shard_piece in weight_stack))
    return (
        lax.all_gather(attend_gain, ("seq", "sub"), axis=0, tiled=True),
        lax.all_gather(attend_shift, ("seq", "sub"), axis=0, tiled=True),
        lax.all_gather(query_key_weight, ("seq", "sub"), axis=0, tiled=True),
        lax.all_gather(value_projection_weight, ("seq", "sub"), axis=0, tiled=True),
        lax.all_gather(output_projection_weight, ("seq", "sub"), axis=0, tiled=True),
        lax.all_gather(feed_gain, ("seq", "sub"), axis=0, tiled=True),
        lax.all_gather(feed_shift, ("seq", "sub"), axis=0, tiled=True),
        lax.all_gather(upper_projection_weight, ("seq", "sub"), axis=0, tiled=True),
        lax.all_gather(upper_projection_bias, ("seq", "sub"), axis=0, tiled=True),
        lax.all_gather(lower_projection_weight, ("seq", "sub"), axis=0, tiled=True),
        lax.all_gather(lower_projection_bias, ("seq", "sub"), axis=0, tiled=True),
    )


def spread_grads(level_grads):
    (
        attend_gain,
        attend_shift,
        query_key_weight,
        value_projection_weight,
        output_projection_weight,
        feed_gain,
        feed_shift,
        upper_projection_weight,
        upper_projection_bias,
        lower_projection_weight,
        lower_projection_bias,
    ) = level_grads
    return (
        lax.psum_scatter(attend_gain, ("seq", "sub"), scatter_dimension=0, tiled=True),
        lax.psum_scatter(attend_shift, ("seq", "sub"), scatter_dimension=0, tiled=True),
        lax.psum_scatter(query_key_weight.astype(jnp.bfloat16), ("seq", "sub"), scatter_dimension=0, tiled=True),
        lax.psum_scatter(value_projection_weight.astype(jnp.bfloat16), ("seq", "sub"), scatter_dimension=0, tiled=True),
        lax.psum_scatter(output_projection_weight.astype(jnp.bfloat16), ("seq", "sub"), scatter_dimension=0, tiled=True),
        lax.psum_scatter(feed_gain, ("seq", "sub"), scatter_dimension=0, tiled=True),
        lax.psum_scatter(feed_shift, ("seq", "sub"), scatter_dimension=0, tiled=True),
        lax.psum_scatter(upper_projection_weight.astype(jnp.bfloat16), ("seq", "sub"), scatter_dimension=0, tiled=True),
        lax.psum_scatter(upper_projection_bias, ("seq", "sub"), scatter_dimension=0, tiled=True),
        lax.psum_scatter(lower_projection_weight.astype(jnp.bfloat16), ("seq", "sub"), scatter_dimension=0, tiled=True),
        lax.psum_scatter(lower_projection_bias, ("seq", "sub"), scatter_dimension=0, tiled=True),
    )


def layer_pass(first_half, second_half, grad_one, grad_two, params, routes, rounds):
    (
        attend_gain,
        attend_shift,
        query_key_weight,
        value_projection_weight,
        output_projection_weight,
        feed_gain,
        feed_shift,
        upper_projection_weight,
        upper_projection_bias,
        lower_projection_weight,
        lower_projection_bias,
    ) = params
    attend_norm, attend_pull = jax.vjp(
        layer_norm, second_half, attend_gain.astype(jnp.float32), attend_shift.astype(jnp.float32)
    )
    normalized_input = attend_norm.astype(jnp.bfloat16)
    shared_query_key, value_vectors, outputs, totals, kept = round_outputs(
        normalized_input, query_key_weight, value_projection_weight, routes, rounds
    )
    attention_result, combine_pull = jax.vjp(combine_rounds, outputs, totals)
    attended_low = attention_result.astype(jnp.bfloat16)
    top_one = first_half + jnp.einsum(
        "srd,de->sre", attended_low, output_projection_weight, preferred_element_type=jnp.float32
    )
    feed_norm, feed_pull = jax.vjp(
        layer_norm, top_one, feed_gain.astype(jnp.float32), feed_shift.astype(jnp.float32)
    )
    feed_forward_input = feed_norm.astype(jnp.bfloat16)
    prior_state = jnp.einsum(
        "srd,df->srf",
        feed_forward_input,
        upper_projection_weight,
        preferred_element_type=jnp.float32,
    ) + upper_projection_bias.astype(jnp.float32)
    hidden_activation, active_pull = jax.vjp(gelu_exact, prior_state)
    active_low = hidden_activation.astype(jnp.bfloat16)
    feed_out = jnp.einsum(
        "srf,fd->srd", active_low, lower_projection_weight, preferred_element_type=jnp.float32
    ) + lower_projection_bias.astype(jnp.float32)
    top_two = second_half + feed_out
    feed_grad = grad_two.astype(jnp.bfloat16)
    down_weight_grad = jnp.einsum(
        "srf,srd->fd", active_low, feed_grad, preferred_element_type=jnp.float32
    )
    down_bias_grad = jnp.sum(feed_grad.astype(jnp.float32), axis=(0, 1))
    active_grad = jnp.einsum(
        "srd,fd->srf", feed_grad, lower_projection_weight, preferred_element_type=jnp.float32
    )
    before_grad = active_pull(active_grad)[0].astype(jnp.bfloat16)
    up_weight_grad = jnp.einsum(
        "srd,srf->df", feed_forward_input, before_grad, preferred_element_type=jnp.float32
    )
    up_bias_grad = jnp.sum(before_grad.astype(jnp.float32), axis=(0, 1))
    norm_grad = jnp.einsum(
        "srf,df->srd", before_grad, upper_projection_weight, preferred_element_type=jnp.float32
    )
    one_part, feed_gain_grad, feed_shift_grad = feed_pull(norm_grad)
    total_one = grad_one + one_part
    out_grad = total_one.astype(jnp.bfloat16)
    output_weight_grad = jnp.einsum(
        "srd,sre->de", attended_low, out_grad, preferred_element_type=jnp.float32
    )
    attended_grad = jnp.einsum(
        "sre,de->srd", out_grad, output_projection_weight, preferred_element_type=jnp.float32
    )
    outputs_grad, totals_grad = combine_pull(attended_grad)
    target, home_slot, source, sorted_slot, home_lookup, back_lookup, order_flat = routes
    sequences, row_count, features = top_one.shape
    groups = rounds * sequences
    all_groups = jnp.arange(groups)
    outputs_low = outputs_grad.astype(jnp.bfloat16).reshape(groups, row_count, features)
    totals_low = totals_grad.astype(jnp.bfloat16).reshape(groups, row_count, HEADS)
    got_out, got_total = trade_rows(
        gather_slots(outputs_low, all_groups, home_lookup),
        gather_slots(totals_low, all_groups, home_lookup),
    )
    shared_rows, value_rows, halo = kept
    grad_shared, grad_values = attend_back(
        shared_rows,
        value_rows,
        order_flat,
        halo,
        settle(got_out, source, sorted_slot),
        settle(got_total, source, sorted_slot),
    )
    home_shared, home_values = trade_rows(
        gather_slots(grad_shared.astype(jnp.bfloat16), all_groups, back_lookup),
        gather_slots(grad_values.astype(jnp.bfloat16), all_groups, back_lookup),
    )
    shared_grad = jnp.sum(
        settle(home_shared, target, home_slot)
        .astype(jnp.float32)
        .reshape(rounds, sequences, row_count, features),
        axis=0,
    ).astype(jnp.bfloat16)
    values_grad = jnp.sum(
        settle(home_values, target, home_slot)
        .astype(jnp.float32)
        .reshape(rounds, sequences, row_count, features),
        axis=0,
    ).astype(jnp.bfloat16)
    shared_weight_grad = jnp.einsum(
        "srd,sre->de", normalized_input, shared_grad, preferred_element_type=jnp.float32
    )
    value_weight_grad = jnp.einsum(
        "srd,sre->de", normalized_input, values_grad, preferred_element_type=jnp.float32
    )
    normed_grad = jnp.einsum(
        "sre,de->srd", shared_grad, query_key_weight, preferred_element_type=jnp.float32
    ) + jnp.einsum(
        "sre,de->srd", values_grad, value_projection_weight, preferred_element_type=jnp.float32
    )
    two_part, attend_gain_grad, attend_shift_grad = attend_pull(normed_grad)
    total_two = grad_two + two_part
    level_grads = (
        attend_gain_grad,
        attend_shift_grad,
        shared_weight_grad,
        value_weight_grad,
        output_weight_grad,
        feed_gain_grad,
        feed_shift_grad,
        up_weight_grad,
        up_bias_grad,
        down_weight_grad,
        down_bias_grad,
    )
    return (top_one, top_two, total_one, total_two, level_grads)


def general_plan(
    first_half,
    second_half,
    grad_first,
    grad_second,
    attend_gain,
    attend_shift,
    query_key_weight,
    value_projection_weight,
    output_projection_weight,
    feed_gain,
    feed_shift,
    upper_projection_weight,
    upper_projection_bias,
    lower_projection_weight,
    lower_projection_bias,
    sort_order,
    sort_place,
):
    weight_stack = (
        attend_gain,
        attend_shift,
        query_key_weight,
        value_projection_weight,
        output_projection_weight,
        feed_gain,
        feed_shift,
        upper_projection_weight,
        upper_projection_bias,
        lower_projection_weight,
        lower_projection_bias,
    )
    devices = lax.axis_size(("seq", "sub"))
    rounds = sort_order.shape[1]
    row_count = first_half.shape[1]
    capacity = 2 * max(1, row_count // devices)
    params = collect(weight_stack, 0)
    routes = build_routes(sort_order[0], sort_place[0], devices, capacity)
    first_out, second_out, first_grad, second_grad, level_grads = layer_pass(
        first_half, second_half, grad_first, grad_second, params, routes, rounds
    )
    stacked = tuple((entry[None].astype(jnp.float32) for entry in spread_grads(level_grads)))
    return (first_out, second_out, first_grad, second_grad) + stacked


class Links:
    def __init__(self, planes, send, receive, local):
        self.send, self.receive, self.local = send, receive, local
        self.used, self.used_local = 0, 0
        self.planes = planes
        seq, sub = lax.axis_index("seq"), lax.axis_index("sub")
        self.z, self.x = seq // 2, lax.rem(seq, 2)
        self.y, self.core = sub // 2, lax.rem(sub, 2)
        self.p = self.x * 4 + sub

    def near(self, step):
        x = 1 - self.x if step & 4 else self.x
        y = 1 - self.y if step & 2 else self.y
        core = 1 - self.core if step & 1 else self.core
        return (self.z * 2 + x, y * 2 + core), x * 4 + y * 2 + core

    def along(self, step):
        to = lax.rem(self.z + step, self.planes)
        back = lax.rem(self.z + self.planes - step, self.planes)
        return (to * 2 + self.x, self.y * 2 + self.core), to, back

    def greet(self):
        barrier = pltpu.get_barrier_semaphore()
        targets = [self.near(step)[0] for step in range(1, 8)]
        targets += [self.along(step)[0] for step in range(1, self.planes)]
        for target in targets:
            pl.semaphore_signal(barrier, inc=1, device_id=target, device_id_type=pl.DeviceIdType.MESH)
        self.greeted = len(targets)

    def meet(self):
        pl.semaphore_wait(pltpu.get_barrier_semaphore(), self.greeted)

    def push(self, source, target, device, start=True):
        copy = pltpu.make_async_remote_copy(
            src_ref=source,
            dst_ref=target,
            send_sem=self.send.at[self.used],
            recv_sem=self.receive.at[self.used],
            device_id=device,
            device_id_type=pl.DeviceIdType.MESH,
        )
        self.used += 1
        if start:
            copy.start()
        return copy

    def keep(self, source, target):
        copy = pltpu.make_async_copy(source, target, self.local.at[self.used_local])
        self.used_local += 1
        copy.start()
        return copy


class Chain:
    def __init__(self, links, ref):
        self.links, self.ref, self.first, self.sent = links, ref, links.used, []
        links.used += 5
        self.hand_on(links.z, links.z < 3, links.z > 0, 2)

    def hand_on(self, shard, rightward, leftward, ways):
        links = self.links
        steps = ((1, rightward), (-1, leftward)) if ways == 2 else ((None, rightward | leftward),)
        for step, wanted in steps:
            if step is None:
                step = jnp.where(rightward, 1, -1)
            to = jnp.clip(links.z + step, 0, 3)
            middle = jnp.where(to == 1, jnp.where(shard == 0, 0, shard - 1), jnp.where(shard == 3, 0, 2 - shard))
            arrival = jnp.where((to == 0) | (to == 3), jnp.abs(to - shard) - 1, middle)
            arrival = jnp.clip(arrival, 0, 2)
            copy = pltpu.make_async_remote_copy(
                src_ref=self.ref.at[shard],
                dst_ref=self.ref.at[shard],
                send_sem=links.send.at[self.first + len(self.sent)],
                recv_sem=links.receive.at[self.first + arrival],
                device_id=(to * 2 + links.x, links.y * 2 + links.core),
                device_id_type=pl.DeviceIdType.MESH,
            )
            self.sent.append((wanted, copy))
            pl.when(wanted)(copy.start)

    def arrive(self, index):
        links, z = self.links, self.links.z
        ends = jnp.where(z == 0, index + 1, 2 - index)
        inner = jnp.where(z == 1, (0, 2, 3)[index], (3, 1, 0)[index])
        shard = jnp.where((z == 0) | (z == 3), ends, inner)
        pltpu.make_async_remote_copy(
            src_ref=self.ref.at[shard],
            dst_ref=self.ref.at[shard],
            send_sem=links.send.at[self.first],
            recv_sem=links.receive.at[self.first + index],
            device_id=(z * 2 + links.x, links.y * 2 + links.core),
            device_id_type=pl.DeviceIdType.MESH,
        ).wait_recv()
        self.hand_on(shard, (shard < z) & (z < 3), (shard > z) & (z > 0), 1)
        return shard

    def finish(self):
        for wanted, copy in self.sent:
            pl.when(wanted)(copy.wait_send)


COPIES = 320


def link_scratch():
    return [
        pltpu.SemaphoreType.DMA((COPIES,)),
        pltpu.SemaphoreType.DMA((COPIES,)),
        pltpu.SemaphoreType.DMA((64,)),
    ]


def along_z(source, target):
    def transfer(links, here, there):
        own = links.keep(source(here, links.z), target(there, links.z))
        copies = []
        for step in range(1, links.planes):
            device, to, _ = links.along(step)
            copies.append(links.push(source(here, to), target(there, links.z), device))
        yield
        own.wait()
        for copy in copies:
            copy.wait()

    return transfer


def along_z_in_turn(source, target):
    def transfer(links, here, there):
        own = links.keep(source(here, links.z), target(there, links.z))
        copies = []
        for step in range(1, links.planes):
            device, to, _ = links.along(step)
            copies.append(links.push(source(here, to), target(there, links.z), device, start=False))
        outer = (links.z == 0) | (links.z == links.planes - 1)
        for copy in copies:
            pl.when(outer)(copy.start)
        yield
        for copy in copies:
            pl.when(jnp.logical_not(outer))(copy.start)
        yield
        own.wait()
        for copy in copies:
            copy.wait()

    return transfer


def over_plane(source, target):
    def transfer(links, here, there):
        own = links.keep(source(here, links.p), target(there, links.p))
        copies = []
        for step in (6, 7, 4, 5, 2, 3, 1):
            device, to = links.near(step)
            copies.append(links.push(source(here, to), target(there, links.p), device))
        yield
        own.wait()
        for copy in copies:
            copy.wait()

    return transfer


def over_chips(source, target):
    def transfer(links, here, there):
        own = links.keep(source(here, links.p), target(there, links.p))
        copies = []
        for step in (6, 4, 2):
            device, to = links.near(step)
            copies.append(links.push(source(here, to), target(there, links.p), device))
        sibling, _ = links.near(1)
        passed = [links.push(source(here, links.p), target(there, links.p), sibling)]
        yield
        for step, copy in zip((6, 4, 2), copies):
            copy.wait_recv()
            _, sender = links.near(step)
            passed.append(links.push(target(there, sender), target(there, sender), sibling))
        yield
        own.wait()
        for copy in copies:
            copy.wait_send()
        for copy in passed:
            copy.wait()

    return transfer


def everywhere(links, here, there):
    own = links.keep(here, there.at[links.z, links.p])
    copies = []
    for step in (6, 7, 4, 5, 2, 3, 1):
        copies.append(links.push(here, there.at[links.z, links.p], links.near(step)[0]))
    yield
    own.wait()
    for copy in copies:
        copy.wait()
    copies = []
    for step in range(1, links.planes):
        copies.append(links.push(there.at[links.z], there.at[links.z], links.along(step)[0]))
    yield
    for copy in copies:
        copy.wait()


def drive(transfers):
    while transfers:
        left = []
        for transfer in transfers:
            try:
                next(transfer)
                left.append(transfer)
            except StopIteration:
                pass
        transfers = left


def whole(ref, index):
    return ref


def block(ref, index):
    return ref.at[index]


def second(ref, index):
    return ref.at[:, index]


def rows_of(index):
    return pl.ds(pl.multiple_of(index * 128, 128), 128)


def pick_tile(table, index_ref, tile, part):
    return jnp.concatenate(
        [table[pl.ds(index_ref[tile, part * 32 + row], 1), :] for row in range(32)], axis=0
    )


def sort_tile(order, table, first, second, offset, tile):
    for part in range(4):
        start = pl.multiple_of(tile * 128 + part * 32 + offset, 32)
        picked = pick_tile(table, order, tile, part)
        first[pl.ds(start, 32), :] = picked[:, :128].astype(first.dtype)
        second[pl.ds(start, 32), :] = picked[:, 128:].astype(second.dtype)


def across(column):
    return jnp.broadcast_to(column, (128, 128)).T[:1, :]


def down(row):
    return jnp.broadcast_to(row, (128, 128)).T


def dot(a, b, contract):
    return lax.dot_general(a, b, (contract, ((), ())), preferred_element_type=jnp.float32)


def key_scales(keys):
    rows = keys.astype(jnp.float32)
    mean_square = jnp.mean(rows * rows, axis=-1, keepdims=True) + 1e-06
    return rows, mean_square, lax.rsqrt(mean_square) / HEAD_DIM


def half_turned(row):
    return jnp.concatenate([row[:, 64:], row[:, :64]], axis=1)


def windows(before, here):
    return [jnp.concatenate([before[:, 64:], here[:, :64]], axis=1), here]


def masked_scores(raw, scale, query_pos, key_pos):
    return jnp.where(
        key_pos > query_pos, LATER, jnp.where(key_pos == query_pos, SELF, raw * scale)
    )


def attend_tiles(tiles, unroll, order, order_rows, table, shared, values, mixed, total_sorted, last_scale):
    sort = functools.partial(sort_tile, order, table, shared, values, BLOCK)
    end = tiles * 128
    for tile in [tiles - 1] + list(range(unroll)):
        sort(tile)
    shared[:BLOCK, :] = shared[end : end + BLOCK, :]
    values[:BLOCK, :] = values[end : end + BLOCK, :]
    last_scale[...] = across(key_scales(shared[end - BLOCK : end + BLOCK, :])[2])

    def step_tiles(step, carry):
        first = step * unroll
        numbers = [lax.rem(first + tiles - 1, tiles)] + [first + k for k in range(unroll)]
        places = [order_rows[pl.ds(t, 1), :] for t in numbers]
        scale = [last_scale[...]]
        work = []
        for k in range(unroll):
            start = pl.multiple_of((first + k) * 128, 128)
            keys = [shared[pl.ds(pl.multiple_of(start + half * 64, 64), 128), :] for half in range(2)]
            vals = [values[pl.ds(pl.multiple_of(start + half * 64, 64), 128), :] for half in range(2)]
            own = jnp.concatenate([keys[0][64:], keys[1][64:]], axis=0)
            scale.append(across(key_scales(own)[2]))
            work.append((keys, vals))
        last_scale[...] = scale[-1]
        for k in range(unroll):
            sort(lax.rem(first + unroll + k, tiles))
        query_pos = jnp.concatenate([down(place) for place in places[1:]], axis=0)
        key_pos, key_scale = [], []
        for k in range(unroll):
            key_pos += windows(places[k], places[k + 1])
            key_scale += windows(scale[k], scale[k + 1])
        raw = [dot(k[64:], k, ((1,), (1,))) for keys, _ in work for k in keys]
        raw, key_pos, key_scale = (
            jnp.concatenate([jnp.broadcast_to(a, (64, 128)) for a in parts], axis=0)
            for parts in (raw, key_pos, key_scale)
        )
        scores = masked_scores(raw, key_scale, query_pos, key_pos)
        highest = jnp.max(scores, axis=-1, keepdims=True)
        total = highest + jnp.log(jnp.sum(jnp.exp(scores - highest), axis=-1, keepdims=True))
        prob = jnp.exp(scores - total).astype(jnp.bfloat16)
        rows = pl.ds(pl.multiple_of(first * 128, 128), unroll * 128)
        total = jnp.broadcast_to(total, (unroll * 128, 128))
        mixed[rows, 128:] = total
        total_sorted[rows, :] = total
        vals = [v for _, vals in work for v in vals]
        mixed[rows, :128] = jnp.concatenate(
            [dot(prob[64 * i : 64 * i + 64], v, ((1,), (0,))) for i, v in enumerate(vals)], axis=0
        )
        return carry

    lax.fori_loop(0, tiles // unroll, step_tiles, 0)


def attend_back_tiles(
    tiles, unroll, order, order_rows, table, shared, values, total_sorted,
    grad_sorted, grad_total_sorted, sums, scale_sums, last_scale,
):
    sort = functools.partial(sort_tile, order, table, grad_sorted, grad_total_sorted, 0)
    end = tiles * 128
    for tile in range(unroll):
        sort(tile)
    last_scale[...] = across(key_scales(shared[end - BLOCK : end + BLOCK, :])[2])
    scale_sums[...] = jnp.zeros_like(scale_sums)
    sums[end : end + 128, :] = jnp.zeros((128, 256), jnp.float32)
    early = lax.broadcasted_iota(jnp.int32, (1, 128), 1) < 64

    def step_tiles(step, carry):
        first = step * unroll
        numbers = [lax.rem(first + tiles - 1, tiles)] + [first + k for k in range(unroll)]
        places = [order_rows[pl.ds(t, 1), :] for t in numbers]
        scale = [last_scale[...]]
        work = []
        for k in range(unroll):
            start = pl.multiple_of((first + k) * 128, 128)
            keys = [shared[pl.ds(pl.multiple_of(start + half * 64, 64), 128), :] for half in range(2)]
            vals = [values[pl.ds(pl.multiple_of(start + half * 64, 64), 128), :] for half in range(2)]
            own = jnp.concatenate([keys[0][64:], keys[1][64:]], axis=0)
            scale.append(across(key_scales(own)[2]))
            tile = pl.ds(start, 128)
            work.append(
                (keys, vals, grad_sorted[tile, :], grad_total_sorted[tile, :], total_sorted[tile, :])
            )
        last_scale[...] = scale[-1]
        for k in range(unroll):
            sort(lax.rem(first + unroll + k, tiles))
        blocks = 2 * unroll
        scale_parts = [0.0] * (unroll + 1)
        query_pos = jnp.concatenate([down(place) for place in places[1:]], axis=0)
        key_pos, key_scale = [], []
        for k in range(unroll):
            key_pos += windows(places[k], places[k + 1])
            key_scale += windows(scale[k], scale[k + 1])
        keys = [k for item in work for k in item[0]]
        vals = [v for item in work for v in item[1]]
        grads, grad_totals, totals = (
            jnp.concatenate([item[n] for item in work], axis=0) for n in (2, 3, 4)
        )
        own = [slice(64 * i, 64 * i + 64) for i in range(blocks)]
        raw = [dot(k[64:], k, ((1,), (1,))) for k in keys]
        grad_prob = [dot(grads[own[i]], v, ((1,), (1,))) for i, v in enumerate(vals)]
        raw, grad_prob, key_pos, key_scale = (
            jnp.concatenate([jnp.broadcast_to(a, (64, 128)) for a in parts], axis=0)
            for parts in (raw, grad_prob, key_pos, key_scale)
        )
        prob = jnp.exp(masked_scores(raw, key_scale, query_pos, key_pos) - totals)
        inner = jnp.sum(prob * grad_prob, axis=-1, keepdims=True)
        grad_score = jnp.where(
            key_pos < query_pos, prob * (grad_prob + (grad_totals - inner)), 0.0
        )
        product = grad_score * raw
        for index in range(blocks):
            k, half = index // 2, index % 2
            part = jnp.sum(product[own[index]], axis=0, keepdims=True)
            if half == 0:
                turned = half_turned(part)
                scale_parts[k] += jnp.where(early, 0.0, turned)
                scale_parts[k + 1] += jnp.where(early, turned, 0.0)
            else:
                scale_parts[k + 1] += part
        grad_raw = (grad_score * key_scale).astype(jnp.bfloat16)
        prob = prob.astype(jnp.bfloat16)
        key_parts = [dot(grad_raw[own[i]], keys[i][64:], ((0,), (0,))) for i in range(blocks)]
        value_parts = [dot(prob[own[i]], grads[own[i]], ((0,), (0,))) for i in range(blocks)]
        query_parts = [dot(grad_raw[own[i]], keys[i], ((1,), (0,))) for i in range(blocks)]
        key_sums = [key_parts[0][:64]] + [
            key_parts[i][64:] + query_parts[i] + (key_parts[i + 1][:64] if i + 1 < blocks else 0.0)
            for i in range(blocks)
        ]
        value_sums = [value_parts[0][:64]] + [
            value_parts[i][64:] + (value_parts[i + 1][:64] if i + 1 < blocks else 0.0)
            for i in range(blocks)
        ]
        for index in range(blocks):
            rows = pl.ds(pl.multiple_of(first * 128 + index * 64, 64), 64)
            sums[rows, :128] = key_sums[index + 1]
            sums[rows, 128:] = value_sums[index + 1]
        for k in range(unroll):
            scale_sums[pl.ds(first + k, 1), :] = scale_parts[k + 1]
        before = jnp.where(step == 0, tiles, numbers[0])
        rows = pl.ds(pl.multiple_of(before * 128 + 64, 64), 64)
        sums[rows, :128] += key_sums[0]
        sums[rows, 128:] += value_sums[0]
        scale_sums[pl.ds(before, 1), :] += scale_parts[0]
        return carry

    lax.fori_loop(0, tiles // unroll, step_tiles, 0)
    sums[end - 128 : end, :] += sums[end : end + 128, :]
    scale_sums[pl.ds(tiles - 1, 1), :] += scale_sums[pl.ds(tiles, 1), :]

    def finish(step, carry):
        for part in range(2):
            tile = step * 2 + part
            rows = rows_of(tile)
            start = pl.multiple_of(tile * 128 + 64, 64)
            keys, mean_square, scale = key_scales(shared[pl.ds(start, 128), :])
            factor = down(scale_sums[pl.ds(tile, 1), :]) * (scale / (mean_square * HEAD_DIM))
            sums[rows, :128] -= factor * keys
        return carry

    lax.fori_loop(0, tiles // 2, finish, 0)


VMEM = pl.BlockSpec(memory_space=pltpu.VMEM)
ANY = pl.BlockSpec(memory_space=pl.ANY)


def narrow(ref, index):
    return ref.at[:, index, :, pl.ds(0, HEAD_DIM)]


def normal_parts(rows):
    center = jnp.mean(rows, axis=-1, keepdims=True)
    offset = rows - center
    spread = jnp.mean(offset * offset, axis=-1, keepdims=True)
    inverse = lax.rsqrt(spread + 1e-05)
    return offset * inverse, inverse


def norm_back(grad, rows, gain):
    unit, inverse = normal_parts(rows)
    scaled = grad * gain
    shared = jnp.mean(scaled, axis=-1, keepdims=True)
    along = jnp.mean(scaled * unit, axis=-1, keepdims=True)
    return (
        (scaled - shared - unit * along) * inverse,
        jnp.sum(grad * unit, axis=0, keepdims=True),
        jnp.sum(grad, axis=0, keepdims=True),
    )


def gelu_parts(rows):
    below = 0.5 * (1.0 + lax.erf(rows * 0.7071067811865476))
    bell = jnp.exp(-0.5 * rows * rows) * 0.3989422804014327
    return rows * below, below + rows * bell


def open_part(
    links, planes,
    sort_order, sort_place, gain_a_in, shift_a_in, gain_f_in, shift_f_in, bias_up_in, bias_down_in,
    x2, wqk, wv, wo, wup, wdown, g2,
    ints, all_ints, floats, all_floats, gains, bias_up, order_rows, place_rows, order_s, place_s, normed, df,
    wqk_line, wv_line, wo_line, wup_rows, wqk_pair, wv_pair, heads, head_table, table, sums,
    shared, values, total_sorted, mixed_home, total_home, last_scale,
    wo_all, wup_part, wdown_part, df_plane, mixed_in, total_in,
):
    low, full = jnp.bfloat16, jnp.float32
    sub = links.y * 2 + links.core
    tiles = planes * 8
    ints[...] = jnp.concatenate([sort_order[...], sort_place[...]], axis=0)
    lane = lax.broadcasted_iota(jnp.int32, (1, 128), 1) // 32

    def spread(vector):
        wide = jnp.concatenate([vector[...].astype(full)] * 4, axis=1)
        return jnp.where(lane == sub, wide, 0.0)

    floats[...] = jnp.concatenate(
        [spread(v) for v in (gain_a_in, shift_a_in, gain_f_in, shift_f_in, bias_down_in)]
        + [bias_up_in[...].astype(full), jnp.zeros((2, 128), full)],
        axis=0,
    )
    df[...] = g2[...].astype(low)
    links.meet()
    share_floats = everywhere(links, floats, all_floats)
    next(share_floats)
    share_ints = everywhere(links, ints, all_ints)
    next(share_ints)

    def pair_columns(ref, z):
        return ref.at[:, pl.ds(pl.multiple_of(z * 256, 256), 256)]

    pair_shares = [
        along_z(pair_columns, block)(links, a, b) for a, b in ((wqk, wqk_line), (wv, wv_line))
    ]
    for transfer in pair_shares:
        next(transfer)
    wo_share = along_z(whole, block)(links, wo, wo_line)
    next(wo_share)
    df_share = over_chips(whole, block)(links, df, df_plane)
    next(df_share)
    unit, _ = normal_parts(x2[...])
    next(share_floats)

    def upper_columns(chunk):
        def columns(ref, p):
            return ref.at[:, pl.ds(pl.multiple_of((chunk * 8 + p) * 128, 128), 128)]

        def landing(ref, p):
            return ref.at[p, :, pl.ds(chunk * 128, 128)]

        return over_plane(columns, landing)

    drive([share_floats])

    def vector_of(row, z_step=2):
        chunks = []
        for chunk in range(8):
            z, x = chunk // 2, chunk % 2
            parts = [all_floats[z, x * 4 + u, row : row + 1, :] for u in range(4)]
            chunks.append(parts[0] + parts[1] + parts[2] + parts[3])
        return jnp.concatenate(chunks, axis=1)

    gain, shift = vector_of(0), vector_of(1)
    normed[links.z] = (unit * gain + shift).astype(low)
    normed_chain = Chain(links, normed)
    for transfer in pair_shares:
        drive([transfer])
    pair_shares = [
        over_chips(whole, second)(links, a, b) for a, b in ((wqk_line, wqk_pair), (wv_line, wv_pair))
    ]
    for transfer in pair_shares:
        next(transfer)
    next(share_ints)
    upper_shares = [upper_columns(chunk)(links, wup, wup_rows) for chunk in range(planes)]
    for transfer in upper_shares:
        next(transfer)
    for transfer in pair_shares:
        next(transfer)
    gains[0:1, :] = gain
    gains[1:2, :] = shift
    for row in (2, 3, 4):
        gains[row : row + 1, :] = vector_of(row)
    for z in range(planes):
        bias_up[:, z * 128 : (z + 1) * 128] = all_floats[z, links.p, 5:6, :]
    drive(pair_shares)
    drive([share_ints])
    for z in range(planes):
        for p in range(8):
            tile = z * 8 + p
            order_rows[tile : tile + 1, :] = all_ints[z, p, pl.ds(sub, 1), :]
            place_rows[tile : tile + 1, :] = all_ints[z, p, pl.ds(sub + 4, 1), :]
    to_scalars = [links.keep(order_rows, order_s), links.keep(place_rows, place_s)]

    def head_columns(z):
        def columns(ref, p):
            return ref.at[z, :, pl.ds(pl.multiple_of((p // 4) * 256, 256), 256)]

        return columns

    def landing(z):
        return lambda ref, p: ref.at[z, p]

    def project(z):
        rows = normed[z]
        for weights, offset in ((wqk_pair, 0), (wv_pair, 128)):
            result = dot(rows, weights[...].reshape(-1, 256), ((1,), (0,))).astype(low)
            heads[z, :, offset : offset + 128] = result[:, :128]
            heads[z, :, 256 + offset : 384 + offset] = result[:, 128:]
        transfer = over_chips(head_columns(z), landing(z))(links, heads, head_table)
        next(transfer)
        return transfer

    head_shares = [project(links.z)]
    next(df_share)
    for index in range(3):
        head_shares.append(project(normed_chain.arrive(index)))
        next(head_shares[-2])
    for transfer in upper_shares:
        drive([transfer])
    up_share = along_z_in_turn(whole, block)(links, wup_rows, wup_part)
    next(up_share)

    def first_rows(ref, z):
        return ref.at[pl.ds(0, 64), :]

    def first_landing(ref, z):
        return ref.at[z, pl.ds(0, 64), :]

    down_share = along_z_in_turn(first_rows, first_landing)(links, wdown, wdown_part)
    next(down_share)
    next(head_shares[-1])
    drive([wo_share])
    wo_share = over_chips(whole, second)(links, wo_line, wo_all)
    for copy in to_scalars:
        copy.wait()
    drive(head_shares)
    shares = [df_share, up_share, down_share]
    next(up_share)
    next(down_share)
    next(wo_share)

    def load(tile, carry):
        table[rows_of(tile), :] = head_table[tile // 8, lax.rem(tile, 8)].astype(full)
        return carry

    lax.fori_loop(0, tiles, load, 0)
    attend_tiles(
        tiles, 2, order_s, order_rows, table, shared, values, sums, total_sorted, last_scale
    )
    next(wo_share)
    kept = []
    sent = []
    for step in (6, 7, 4, 5, 2, 3, 1, 0):
        device, p = links.near(step)

        def unsort(z, carry):
            totals = []
            for part in range(4):
                picked = pick_tile(sums, place_s, z * 8 + p, part)
                mixed_home[p, z, part * 32 : part * 32 + 32, :] = picked[:, :128].astype(low)
                totals.append(picked[:, 128:])
            total_home[p, pl.ds(z, 1), :] = jnp.concatenate(totals, axis=0).T[:1, :]
            return carry

        lax.fori_loop(0, planes, unsort, 0)
        for here, there in ((mixed_home, mixed_in), (total_home, total_in)):
            source, target = here.at[p], there.at[links.p]
            if step:
                sent.append(links.push(source, target, device))
            else:
                kept.append(links.keep(source, target))
    normed_chain.finish()
    for copy in kept + sent:
        copy.wait()
    return wo_share, shares


def feed_part(
    links, planes, wo_share, weight_shares,
    x1, g1, y1_out, g1_out, gains, bias_up, sums, table, head_table, mixed_home, total_home,
    wo_all, wup_part, wdown_part, df_plane, mixed_in, total_in, dtotal_in, attended, arrived, h2, act, dpre,
    kept, from_sibling, to_chip, from_chip, up_grad, up_parts, down_grad, down_parts, dout, datt_out, datt,
    up_bias, feed_gain, feed_shift, y2_sibling, y2_chip, out_sibling, wdown,
):
    low, full = jnp.bfloat16, jnp.float32

    def weight_rows(head, z):
        return pl.ds(pl.multiple_of((head * planes + z) * 128, 128), 128)

    def wo_rows(z):
        return wo_all[z].reshape(256, -1)

    def combine(z, carry):
        for x in range(2):
            totals = [down(total_in[x * 4 + u, pl.ds(z, 1), :]) for u in range(4)]
            highest = jnp.maximum(
                jnp.maximum(totals[0], totals[1]), jnp.maximum(totals[2], totals[3])
            )
            parts = [jnp.exp(t - highest) for t in totals]
            inverse = 1.0 / (parts[0] + parts[1] + parts[2] + parts[3])
            result = 0.0
            for u in range(4):
                weight = parts[u] * inverse
                sums[weight_rows(x * 4 + u, z), :128] = weight
                result += weight * mixed_in[x * 4 + u, z].astype(full)
            attended[z, :, x * 128 : (x + 1) * 128] = result.astype(low)
        return carry

    lax.fori_loop(0, planes, combine, 0)
    share = along_z(block, block)(links, attended, arrived)
    next(share)

    def last_rows(ref, z):
        return ref.at[pl.ds(64, 64), :]

    def last_landing(ref, z):
        return ref.at[z, pl.ds(64, 64), :]

    down_share = along_z(last_rows, last_landing)(links, wdown, wdown_part)
    next(down_share)
    drive([wo_share])
    drive([share])
    y1 = x1[...]
    for z in range(planes):
        y1 += dot(arrived[z], wo_rows(z), ((1,), (0,)))
    y1_out[...] = y1
    unit, _ = normal_parts(y1)
    own_rows = pl.ds(pl.multiple_of(links.p * 128, 128), 128)
    h2[own_rows, :] = (unit * gains[2:3, :] + gains[3:4, :]).astype(low)

    sibling, _ = links.near(1)
    own_h2 = h2.at[own_rows, :]
    direct = {step: links.push(own_h2, own_h2, links.near(step)[0]) for step in (2, 4)}
    handed = {0: links.push(own_h2, own_h2, sibling)}
    drive(weight_shares + [down_share])

    half = wup_part.shape[3] // 2

    def upper_back(part, carry):
        rows = pl.ds(pl.multiple_of(part * 256, 256), 256)
        grad = df_plane[pl.ds(part * 2, 2)].reshape(256, -1)
        result = dot(grad, wdown_part[...].reshape(half * 2, -1), ((1,), (1,)))
        table[rows, :] = result[:, :half]
        table[pl.ds(pl.multiple_of(1024 + part * 256, 256), 256), :] = result[:, half:]
        return carry

    lax.fori_loop(0, 4, upper_back, 0)

    def pass_on(step):
        direct[step].wait_recv()
        block_rows = h2.at[rows_of(links.near(step)[1]), :]
        handed[step] = links.push(block_rows, block_rows, sibling)

    def feed(slot, step):
        handed[step].wait_recv()
        chip = links.near(step)[1] // 2
        rows = pl.ds(pl.multiple_of(chip * 256, 256), 256)
        before = dot(h2[rows, :], wup_part[...].reshape(-1, 2 * half), ((1,), (0,))) + bias_up[...]
        value, slope = gelu_parts(before)
        act[rows, :] = value.astype(low)
        grad = jnp.concatenate(
            [table[rows, :], table[pl.ds(pl.multiple_of(1024 + chip * 256, 256), 256), :]], axis=1
        )
        grad = (grad * slope).astype(low)
        dpre[rows, :] = grad
        kept[slot] = dot(grad, wup_part[...].reshape(-1, 2 * half), ((1,), (1,))).reshape(2, 128, -1).astype(low)
        return links.push(kept.at[slot, 1 - links.core], from_sibling.at[slot], sibling)

    def chip_sum(slot, step, traded):
        traded.wait_recv()
        result = kept[slot, links.core].astype(full) + from_sibling[slot].astype(full)
        if slot == 0:
            return result
        to_chip[slot - 1] = result.astype(low)
        return links.push(to_chip.at[slot - 1], from_chip.at[slot - 1], links.near(step)[0])

    traded = [feed(0, 0)]
    for step in (2, 4):
        direct[step].wait_send()
    direct[6] = links.push(own_h2, own_h2, links.near(6)[0])
    pass_on(2)
    pass_on(4)
    traded.append(feed(1, 2))
    sent = [chip_sum(1, 2, traded[1])]
    pass_on(6)
    traded.append(feed(2, 4))
    sent.append(chip_sum(2, 4, traded[2]))
    traded.append(feed(3, 6))
    sent.append(chip_sum(3, 6, traded[3]))
    own_sum = chip_sum(0, 0, traded[0])

    def upper_grad(part, carry):
        rows = pl.ds(pl.multiple_of(part * 256, 256), 256)
        up_grad[part] = dot(h2[:, rows], dpre[...], ((0,), (0,))).astype(low)
        return carry

    lax.fori_loop(0, planes, upper_grad, 0)

    def lower_grad(part, carry):
        rows = pl.ds(pl.multiple_of(part * 128, 128), 128)
        down_grad[part] = dot(act[:, rows], df_plane[...].reshape(act.shape[0], -1), ((0,), (0,))).astype(low)
        return carry

    lax.fori_loop(0, planes, lower_grad, 0)

    def lower(part, carry):
        rows = pl.ds(pl.multiple_of(part * 128, 128), 128)
        df_plane[part] = dot(
            act[rows, :], wdown_part[...].reshape(2 * half, -1), ((1,), (0,))
        ).astype(low)
        return carry

    lax.fori_loop(0, 8, lower, 0)

    def of_chip(step, core):
        return links.near(step)[1] // 2 * 2 + core

    y2_traded = [
        links.push(df_plane.at[of_chip(step, 1 - links.core)], y2_sibling.at[slot], sibling)
        for slot, step in enumerate((6, 4, 2, 0))
    ]
    for copy in sent:
        copy.wait_recv()
    grad = own_sum + (
        from_chip[0].astype(full) + from_chip[1].astype(full) + from_chip[2].astype(full)
    )
    part, gain_grad, shift_grad = norm_back(grad, y1_out[...], gains[2:3, :])
    feed_gain[...] = gain_grad
    feed_shift[...] = shift_grad
    g1_new = g1[...] + part
    g1_out[...] = g1_new
    dout[...] = g1_new.astype(low)
    for z in range(planes):
        datt_out[z] = dot(dout[...], wo_rows(z), ((1,), (1,))).astype(low)
    share = along_z(block, block)(links, datt_out, datt)
    next(share)
    y2_pushed = []
    for slot, step in enumerate((6, 4, 2, 0)):
        y2_traded[slot].wait()
        mine = of_chip(step, links.core)
        df_plane[mine] = (
            df_plane[mine].astype(full) + y2_sibling[slot].astype(full)
        ).astype(low)
        if step:
            y2_pushed.append(
                links.push(df_plane.at[mine], y2_chip.at[slot], links.near(step)[0])
            )
    for copy in [direct[6]] + list(handed.values()):
        copy.wait_send()
    for z in range(planes):
        part = dot(arrived[z], dout[...], ((0,), (0,))).astype(low)
        for p in range(8):
            row = p * 128 + z * 32
            h2[row : row + 32, :] = part[p * 32 : p * 32 + 32]
    out_traded = [
        links.push(
            h2.at[rows_of(links.near(step)[1] // 2 * 2 + 1 - links.core), :],
            out_sibling.at[slot],
            sibling,
        )
        for slot, step in enumerate((6, 4, 2, 0))
    ]
    up_bias[...] = jnp.sum(dpre[...].astype(full), axis=0, keepdims=True)
    drive([share])
    share_up = along_z(block, block)(links, up_grad, up_parts)
    next(share_up)
    share_down = along_z(block, block)(links, down_grad, down_parts)
    next(share_down)
    def combine_back(z, carry):
        for x in range(2):
            grad = datt[z, :, x * 128 : (x + 1) * 128].astype(full)
            chosen = [sums[weight_rows(x * 4 + u, z), :128] for u in range(4)]
            inner = [
                jnp.sum(grad * mixed_in[x * 4 + u, z].astype(full), axis=-1, keepdims=True)
                for u in range(4)
            ]
            mean = sum(chosen[u] * inner[u] for u in range(4))
            for u in range(4):
                mixed_home[x * 4 + u, z] = (chosen[u] * grad).astype(low)
                change = (chosen[u] * (inner[u] - mean)).astype(low).astype(full)
                total_home[x * 4 + u, pl.ds(z, 1), :] = change.T[:1, :]
        return carry

    lax.fori_loop(0, planes, combine_back, 0)
    shares = [
        over_plane(block, narrow)(links, mixed_home, head_table),
        over_plane(block, block)(links, total_home, dtotal_in),
    ]
    for transfer in shares:
        next(transfer)
    for copy in traded + sent:
        copy.wait_send()
    return shares, y2_pushed, share_up, share_down, out_traded


def close_part(
    links, planes, shares, y2_pushed, share_up, share_down, out_traded,
    x2, g2, y2_out, g2_out, shared_grad_out, value_grad_out, out_grad_out, up_out, down_out, vectors_out,
    gains, order_rows, order_s, place_s, normed, wqk_pair, wv_pair, shared, values, total_sorted, head_table,
    table, sums, last_scale, dtotal_in, attended, df_plane, h2, wup_part, wdown_part, up_parts, down_grad,
    down_parts, kept, from_sibling, to_chip, from_chip, up_bias, feed_gain, feed_shift, grad_sorted,
    grad_total_sorted, scale_sums, up_sum, up_arrived, dshared, dvalues, de, out_sent, out_arrived,
    weight_arrived, weight_sum, weight_final, tiles_sent, tiles_arrived, tile, tile_line, y2_chip,
    out_sibling, out_chip,
):
    low, full = jnp.bfloat16, jnp.float32
    tiles = planes * 8
    line = planes * 128
    out_sums = []
    for slot, step in enumerate((6, 4, 2, 0)):
        out_traded[slot].wait()
        rows = rows_of(links.near(step)[1] // 2 * 2 + links.core)
        total = h2[rows, :].astype(full) + out_sibling[slot].astype(full)
        h2[rows, :] = total.astype(low)
        out_sums.append(rows)
    drive(shares)
    out_pushed = [
        links.push(h2.at[out_sums[slot], :], out_chip.at[slot], links.near(step)[0])
        for slot, step in enumerate((6, 4, 2))
    ]

    def load(index, carry):
        z, p = index // 8, lax.rem(index, 8)
        table[rows_of(index), :128] = head_table[z, p, :, :HEAD_DIM].astype(full)
        table[rows_of(index), 128:] = down(dtotal_in[p, pl.ds(z, 1), :])
        return carry

    lax.fori_loop(0, tiles, load, 0)
    attend_back_tiles(
        tiles, 4, order_s, order_rows, table, shared, values, total_sorted,
        grad_sorted, grad_total_sorted, sums, scale_sums, last_scale,
    )
    sibling, _ = links.near(1)

    def unsort(slot, step):
        chip = links.near(step)[1] // 2
        for core, goal in ((0, 1 - links.core), (1, links.core)):

            def rows(z, carry):
                columns = pl.ds(pl.multiple_of(z * 256, 256), 256)
                for part in range(4):
                    picked = pick_tile(sums, place_s, z * 8 + chip * 2 + goal, part)
                    kept[slot, core, part * 32 : part * 32 + 32, columns] = picked.astype(low)
                return carry

            lax.fori_loop(0, planes, rows, 0)
            if core == 0:
                traded = links.push(kept.at[slot, 0], from_sibling.at[slot], sibling)
        return traded

    def chip_sum(slot, step, traded):
        traded.wait_recv()
        result = kept[slot, 1].astype(full) + from_sibling[slot].astype(full)
        if step == 0:
            return result
        to_chip[slot] = result.astype(low)
        return links.push(to_chip.at[slot], from_chip.at[slot], links.near(step)[0])

    steps = (6, 4, 2, 0)
    traded, sent = [], []
    for slot, step in enumerate(steps):
        traded.append(unsort(slot, step))
        if slot:
            sent.append(chip_sum(slot - 1, steps[slot - 1], traded[slot - 1]))
    total = h2[out_sums[3], :].astype(full)
    for slot, copy in enumerate(out_pushed):
        copy.wait()
        total += out_chip[slot].astype(full)
    out_sent[...] = total.astype(low).reshape(out_sent.shape)
    own_sum = chip_sum(3, 0, traded[3])
    share_out = along_z(block, block)(links, out_sent, out_arrived)
    next(share_out)
    own_columns = pl.ds(pl.multiple_of(links.x * 128, 128), 128)
    far_columns = pl.ds(pl.multiple_of((1 - links.x) * 128, 128), 128)

    def settle_sum(columns, result):
        for z in range(planes):
            part = result[:, z * 256 : z * 256 + 256].astype(low)
            dshared[z * 128 : z * 128 + 128, columns] = part[:, :128]
            dvalues[z * 128 : z * 128 + 128, columns] = part[:, 128:]

    sent[2].wait_recv()
    settle_sum(own_columns, own_sum + from_chip[2].astype(full))
    sent[1].wait_recv()
    sent[0].wait_recv()
    settle_sum(far_columns, from_chip[1].astype(full) + from_chip[0].astype(full))
    all_wqk, all_wv = wqk_pair[...].reshape(-1, 256), wv_pair[...].reshape(-1, 256)
    drive([share_down])

    def input_grad(z, carry):
        rows = rows_of(z)
        down_grad[z] = (
            dot(dshared[rows, :], all_wqk, ((1,), (1,))) + dot(dvalues[rows, :], all_wv, ((1,), (1,)))
        ).astype(low)
        return carry

    lax.fori_loop(0, planes, input_grad, 0)
    share_de = along_z(block, block)(links, down_grad, de)
    next(share_de)
    drive([share_up])
    up_sum[...] = sum(up_parts[z].astype(full) for z in range(planes)).reshape(up_sum.shape)
    share_up = over_plane(block, block)(links, up_sum, up_arrived)
    next(share_up)
    all_normed = normed[...].reshape(line, -1)
    for index, grad in enumerate((dshared, dvalues)):
        wup_part[:, :, :, index * 256 : index * 256 + 256] = (
            dot(all_normed, grad[...], ((0,), (0,))).astype(low).reshape(wup_part.shape[:3] + (256,))
        )
    share_weights = over_plane(second, block)(links, wup_part, weight_arrived)
    next(share_weights)
    for copy in y2_pushed:
        copy.wait()
    y2_out[...] = x2[...] + (
        df_plane[links.p].astype(full)
        + sum(y2_chip[slot].astype(full) for slot in range(3))
        + gains[4:5, :]
    )
    drive([share_up])
    for p in range(8):
        for z in range(planes):
            up_out[:, (z * 8 + p) * 128 : (z * 8 + p + 1) * 128] = up_arrived[
                p, :, z * 128 : (z + 1) * 128
            ]
    down_out[...] = sum(down_parts[z].astype(full) for z in range(planes))
    drive([share_out])
    out_grad_out[...] = sum(out_arrived[z].astype(full) for z in range(planes))
    down_bias = jnp.sum(g2[...].astype(low).astype(full), axis=0, keepdims=True)
    drive([share_weights])
    weight_sum[...] = sum(weight_arrived[p].astype(full) for p in range(8)).astype(low)

    share_final = along_z(block, block)(links, weight_sum, weight_final)
    next(share_final)
    drive([share_de])
    part, gain_grad, shift_grad = norm_back(
        sum(de[z].astype(full) for z in range(planes)), x2[...], gains[0:1, :]
    )
    vectors = [gain_grad, shift_grad, feed_gain[...], feed_shift[...], down_bias]
    for x in range(2):
        for index, vector in enumerate(vectors):
            for z in range(planes):
                chunk = (z * 2 + x) * 128
                row = index * planes + z
                tiles_sent[x, row : row + 1, :] = vector[:, chunk : chunk + 128]
        tiles_sent[x, 5 * planes :, :] = jnp.zeros((24 - 5 * planes, 128), full)

    def of_x(ref, p):
        return ref.at[p // 4]

    share_tiles = over_plane(of_x, block)(links, tiles_sent, tiles_arrived)
    next(share_tiles)
    g2_out[...] = g2[...] + part
    drive([share_tiles])
    tile[...] = jnp.sum(tiles_arrived[...], axis=0)
    for z in range(planes):
        tile[5 * planes + z : 5 * planes + z + 1, :] = up_bias[:, z * 128 : (z + 1) * 128]
    share_tile = along_z(whole, block)(links, tile, tile_line)
    next(share_tile)
    drive([share_final])
    for z in range(planes):
        columns = slice(z * 256, z * 256 + 256)
        shared_grad_out[:, columns] = weight_final[z, :, :256].astype(full)
        value_grad_out[:, columns] = weight_final[z, :, 256:].astype(full)
    drive([share_tile])
    tile[...] = jnp.sum(tile_line[...], axis=0)
    for index in range(6):
        vectors_out[index : index + 1, :] = tile[pl.ds(index * planes + links.z, 1), :]
    vectors_out[6:8, :] = jnp.zeros((2, 128), full)
    for copy in traded + sent:
        copy.wait_send()


LAYER_INPUTS = (
    "sort_order", "sort_place", "gain_a_in", "shift_a_in", "gain_f_in", "shift_f_in", "bias_up_in",
    "bias_down_in", "x2", "wqk", "wv", "wo", "wup", "wdown", "g2", "x1", "g1",
)
LAYER_OUTPUTS = (
    "y1_out", "y2_out", "g1_out", "g2_out", "shared_grad_out", "value_grad_out", "out_grad_out",
    "up_out", "down_out", "vectors_out",
)
OPEN_REFS = (
    "sort_order", "sort_place", "gain_a_in", "shift_a_in", "gain_f_in", "shift_f_in", "bias_up_in",
    "bias_down_in", "x2", "wqk", "wv", "wo", "wup", "wdown", "g2", "ints", "all_ints", "floats",
    "all_floats", "gains", "bias_up", "order_rows", "place_rows", "order_s", "place_s", "normed",
    "df", "wqk_line", "wv_line", "wo_line", "wup_rows", "wqk_pair", "wv_pair", "heads",
    "head_table", "table", "sums", "shared", "values", "total_sorted", "mixed_home", "total_home",
    "last_scale", "wo_all", "wup_part", "wdown_part", "df_plane", "mixed_in", "total_in",
)
FEED_REFS = (
    "x1", "g1", "y1_out", "g1_out", "gains", "bias_up", "sums", "table", "head_table", "mixed_home",
    "total_home", "wo_all", "wup_part", "wdown_part", "df_plane", "mixed_in", "total_in",
    "dtotal_in", "attended", "arrived", "h2", "act", "dpre", "kept", "from_sibling", "to_chip",
    "from_chip", "up_grad", "up_parts", "down_grad", "down_parts", "dout", "datt_out", "datt",
    "up_bias", "feed_gain", "feed_shift", "y2_sibling", "y2_chip", "out_sibling", "wdown",
)
CLOSE_REFS = (
    "x2", "g2", "y2_out", "g2_out", "shared_grad_out", "value_grad_out", "out_grad_out", "up_out",
    "down_out", "vectors_out", "gains", "order_rows", "order_s", "place_s", "normed", "wqk_pair",
    "wv_pair", "shared", "values", "total_sorted", "head_table", "table", "sums", "last_scale",
    "dtotal_in", "attended", "df_plane", "h2", "wup_part", "wdown_part", "up_parts", "down_grad",
    "down_parts", "kept", "from_sibling", "to_chip", "from_chip", "up_bias", "feed_gain",
    "feed_shift", "grad_sorted", "grad_total_sorted", "scale_sums", "up_sum", "up_arrived",
    "dshared", "dvalues", "de", "out_sent", "out_arrived", "weight_arrived", "weight_sum",
    "weight_final", "tiles_sent", "tiles_arrived", "tile", "tile_line",
    "y2_chip", "out_sibling", "out_chip",
)


def layer_scratch(planes, rows, width, own, part):
    low, full, whole_number = jnp.bfloat16, jnp.float32, jnp.int32
    tiles = planes * 8
    tokens = tiles * rows
    return {
        "ints": pltpu.VMEM((8, rows), whole_number),
        "all_ints": pltpu.VMEM((planes, 8, 8, rows), whole_number),
        "floats": pltpu.VMEM((8, rows), full),
        "all_floats": pltpu.VMEM((planes, 8, 8, rows), full),
        "gains": pltpu.VMEM((8, width), full),
        "bias_up": pltpu.VMEM((1, part), full),
        "order_rows": pltpu.VMEM((tiles, rows), whole_number),
        "place_rows": pltpu.VMEM((tiles, rows), whole_number),
        "order_s": pltpu.SMEM((tiles, rows), whole_number),
        "place_s": pltpu.SMEM((tiles, rows), whole_number),
        "normed": pltpu.VMEM((planes, rows, width), low),
        "df": pltpu.VMEM((rows, width), low),
        "wqk_line": pltpu.VMEM((planes, own, 256), low),
        "wv_line": pltpu.VMEM((planes, own, 256), low),
        "wo_line": pltpu.VMEM((planes, own, width), low),
        "wup_rows": pltpu.VMEM((8, own, part), low),
        "wqk_pair": pltpu.VMEM((planes, 8, own, 256), low),
        "wv_pair": pltpu.VMEM((planes, 8, own, 256), low),
        "heads": pltpu.VMEM((planes, rows, 512), low),
        "head_table": pltpu.VMEM((planes, 8, rows, 256), low),
        "table": pltpu.VMEM((tokens, 256), full),
        "sums": pltpu.VMEM((tokens + rows, 256), full),
        "shared": pltpu.VMEM((tokens + BLOCK, HEAD_DIM), low),
        "values": pltpu.VMEM((tokens + BLOCK, HEAD_DIM), low),
        "total_sorted": pltpu.VMEM((tokens, HEAD_DIM), full),
        "mixed_home": pltpu.VMEM((8, planes, rows, HEAD_DIM), low),
        "total_home": pltpu.VMEM((8, 8, rows), full),
        "last_scale": pltpu.VMEM((1, rows), full),
        "wo_all": pltpu.VMEM((planes, 8, own, width), low),
        "wup_part": pltpu.VMEM((planes, 8, own, part), low),
        "wdown_part": pltpu.VMEM((planes, rows, width), low),
        "df_plane": pltpu.VMEM((8, rows, width), low),
        "mixed_in": pltpu.VMEM((8, planes, rows, HEAD_DIM), low),
        "total_in": pltpu.VMEM((8, 8, rows), full),
        "dtotal_in": pltpu.VMEM((8, 8, rows), full),
        "attended": pltpu.VMEM((planes, rows, 256), low),
        "arrived": pltpu.VMEM((planes, rows, 256), low),
        "h2": pltpu.VMEM((8 * rows, width), low),
        "act": pltpu.VMEM((8 * rows, part), low),
        "dpre": pltpu.VMEM((8 * rows, part), low),
        "kept": pltpu.VMEM((4, 2, rows, width), low),
        "from_sibling": pltpu.VMEM((4, rows, width), low),
        "to_chip": pltpu.VMEM((3, rows, width), low),
        "from_chip": pltpu.VMEM((3, rows, width), low),
        "up_grad": pltpu.VMEM((planes, width // planes, part), low),
        "up_parts": pltpu.VMEM((planes, width // planes, part), low),
        "down_grad": pltpu.VMEM((planes, rows, width), low),
        "down_parts": pltpu.VMEM((planes, rows, width), low),
        "dout": pltpu.VMEM((rows, width), low),
        "datt_out": pltpu.VMEM((planes, rows, 256), low),
        "datt": pltpu.VMEM((planes, rows, 256), low),
        "up_bias": pltpu.VMEM((1, part), full),
        "feed_gain": pltpu.VMEM((1, width), full),
        "feed_shift": pltpu.VMEM((1, width), full),
        "grad_sorted": pltpu.VMEM((tokens, HEAD_DIM), low),
        "grad_total_sorted": pltpu.VMEM((tokens, HEAD_DIM), full),
        "scale_sums": pltpu.VMEM((tiles + 8, rows), full),
        "up_sum": pltpu.VMEM((8, own, part), full),
        "up_arrived": pltpu.VMEM((8, own, part), full),
        "dshared": pltpu.VMEM((planes * rows, 256), low),
        "dvalues": pltpu.VMEM((planes * rows, 256), low),
        "de": pltpu.VMEM((planes, rows, width), low),
        "out_sent": pltpu.VMEM((planes, own, width), low),
        "out_arrived": pltpu.VMEM((planes, own, width), low),
        "y2_sibling": pltpu.VMEM((4, rows, width), low),
        "y2_chip": pltpu.VMEM((3, rows, width), low),
        "out_sibling": pltpu.VMEM((4, rows, width), low),
        "out_chip": pltpu.VMEM((3, rows, width), low),
        "weight_arrived": pltpu.VMEM((8, planes, own, 512), low),
        "weight_sum": pltpu.VMEM((planes, own, 512), low),
        "weight_final": pltpu.VMEM((planes, own, 512), low),
        "tiles_sent": pltpu.VMEM((2, 24, rows), full),
        "tiles_arrived": pltpu.VMEM((8, 24, rows), full),
        "tile": pltpu.VMEM((24, rows), full),
        "tile_line": pltpu.VMEM((planes, 24, rows), full),
    }


def layer_kernel(planes, names, *refs):
    links = Links(planes, *refs[len(names) :])
    held = dict(zip(names, refs))
    links.greet()
    shares = open_part(links, planes, *[held[name] for name in OPEN_REFS])
    shares = feed_part(links, planes, *shares, *[held[name] for name in FEED_REFS])
    close_part(links, planes, *shares, *[held[name] for name in CLOSE_REFS])


def layer_stage(arguments, collective_id, planes):
    rows, width = arguments[LAYER_INPUTS.index("x2")].shape
    own, hidden = arguments[LAYER_INPUTS.index("wup")].shape
    shape = jax.ShapeDtypeStruct
    token, weight = shape((rows, width), jnp.float32), shape((own, width), jnp.float32)
    outputs = [token] * 4 + [weight] * 3 + [
        shape((own, hidden), jnp.float32), token, shape((8, rows), jnp.float32)
    ]
    scratch = layer_scratch(planes, rows, width, own, hidden // 8)
    names = LAYER_INPUTS + LAYER_OUTPUTS + tuple(scratch)
    return pl.pallas_call(
        functools.partial(layer_kernel, planes, names),
        out_shape=outputs,
        in_specs=[VMEM] * len(arguments),
        out_specs=[VMEM] * len(outputs),
        scratch_shapes=list(scratch.values()) + link_scratch(),
        compiler_params=pltpu.CompilerParams(
            vmem_limit_bytes=60 << 20, collective_id=collective_id, has_side_effects=True
        ),
        name="layer",
    )(*arguments)


def finish_kernel(
    y1, y2, g1, g2, shared_grad, value_grad, out_grad, up_grad, down_grad, vectors,
    y1_out, y2_out, g1_out, g2_out, gain_a_out, shift_a_out, shared_out, value_out, out_out,
    gain_f_out, shift_f_out, up_out, up_bias_out, down_out, down_bias_out, arrived,
):
    pairs = (
        (y1, y1_out), (y2, y2_out), (g1, g1_out), (g2, g2_out), (shared_grad, shared_out),
        (value_grad, value_out), (out_grad, out_out), (up_grad, up_out), (down_grad, down_out),
    )
    copies = [
        pltpu.make_async_copy(source, target.at[0], arrived.at[index])
        for index, (source, target) in enumerate(pairs)
    ]
    for copy in copies:
        copy.start()
    sub = lax.axis_index("sub")
    rows = vectors[...]
    own = sum(
        jnp.where(sub == u, rows[:, u * 32 : u * 32 + 32], 0.0) for u in range(4)
    )
    for row, target in enumerate((gain_a_out, shift_a_out, gain_f_out, shift_f_out, down_bias_out)):
        target[...] = own[row : row + 1, :]
    up_bias_out[...] = rows[5:6, :]
    for copy in copies:
        copy.wait()


def finish_stage(arguments):
    full = jnp.float32
    large = [(jax.ShapeDtypeStruct((1,) + a.shape, full), ANY) for a in arguments[:-1]]
    y1, y2, g1, g2, shared_grad, value_grad, out_grad, up_grad, down_grad = large
    small = (jax.ShapeDtypeStruct((1, arguments[4].shape[0]), full), VMEM)
    up_bias = (jax.ShapeDtypeStruct((1, arguments[-1].shape[1]), full), VMEM)
    outputs = [
        y1, y2, g1, g2, small, small, shared_grad, value_grad, out_grad, small, small, up_grad,
        up_bias, down_grad, small,
    ]
    return pl.pallas_call(
        finish_kernel,
        out_shape=[o[0] for o in outputs],
        in_specs=[VMEM] * 10,
        out_specs=[o[1] for o in outputs],
        scratch_shapes=[pltpu.SemaphoreType.DMA((9,))],
        name="finish",
    )(*arguments)


def plane_plan(
    n_seq,
    n_sub,
    first_half,
    second_half,
    grad_first,
    grad_second,
    attend_gain,
    attend_shift,
    query_key_weight,
    value_projection_weight,
    output_projection_weight,
    feed_gain,
    feed_shift,
    upper_projection_weight,
    upper_projection_bias,
    lower_projection_weight,
    lower_projection_bias,
    sort_order,
    sort_place,
):
    planes = n_seq // 2
    x1, x2, g1, g2 = (a[0] for a in (first_half, second_half, grad_first, grad_second))
    wqk, wv, wo = query_key_weight[0], value_projection_weight[0], output_projection_weight[0]
    wup, wdown = upper_projection_weight[0], lower_projection_weight[0]
    results = layer_stage(
        (
            sort_order[0, :, 0], sort_place[0, :, 0], attend_gain, attend_shift, feed_gain, feed_shift,
            upper_projection_bias, lower_projection_bias, x2, wqk, wv, wo, wup, wdown, g2, x1, g1,
        ),
        1,
        planes,
    )
    return finish_stage(results)


def on_device(n_seq, n_sub, *arguments):
    sequences, rows, width = arguments[0].shape
    rounds = arguments[-1].shape[1]
    fits = (
        sequences == 1
        and rows == 2 * BLOCK
        and rounds == n_sub
        and HEADS == n_seq
        and width == HEADS * HEAD_DIM
    )
    if fits:
        return plane_plan(n_seq, n_sub, *arguments)
    return general_plan(*arguments)


def solution(mesh):
    return jax.shard_map(
        functools.partial(on_device, mesh.shape["seq"], mesh.shape["sub"]),
        mesh=mesh,
        in_specs=(
            P(None, ("seq", "sub"), None),
            P(None, ("seq", "sub"), None),
            P(None, ("seq", "sub"), None),
            P(None, ("seq", "sub"), None),
            P(None, ("seq", "sub")),
            P(None, ("seq", "sub")),
            P(None, ("seq", "sub"), None),
            P(None, ("seq", "sub"), None),
            P(None, ("seq", "sub"), None),
            P(None, ("seq", "sub")),
            P(None, ("seq", "sub")),
            P(None, ("seq", "sub"), None),
            P(None, ("seq", "sub")),
            P(None, ("seq", "sub"), None),
            P(None, ("seq", "sub")),
            P(None, None, None, ("seq", "sub")),
            P(None, None, None, ("seq", "sub")),
        ),
        out_specs=(
            P(None, ("seq", "sub"), None),
            P(None, ("seq", "sub"), None),
            P(None, ("seq", "sub"), None),
            P(None, ("seq", "sub"), None),
            P(None, ("seq", "sub")),
            P(None, ("seq", "sub")),
            P(None, ("seq", "sub"), None),
            P(None, ("seq", "sub"), None),
            P(None, ("seq", "sub"), None),
            P(None, ("seq", "sub")),
            P(None, ("seq", "sub")),
            P(None, ("seq", "sub"), None),
            P(None, ("seq", "sub")),
            P(None, ("seq", "sub"), None),
            P(None, ("seq", "sub")),
        ),
        check_vma=False,
    )
```

```python
import functools

import jax
import jax.numpy as jnp
from jax import lax
from jax.experimental import pallas as pl
from jax.experimental.pallas import tpu as pltpu
from jax.sharding import PartitionSpec as P

HEADS = 8
HEAD_DIM = 128
BLOCK = 64
LATER = -1000000000.0
SELF = -100000.0


def from_behind(block, axis, distance):
    devices = range(lax.axis_size(axis))
    route = [((i - distance) % len(devices), i) for i in devices]
    return lax.ppermute(block, axis, route)


def layer_norm(value_vectors, scaling, shifts):
    center = jnp.mean(value_vectors, axis=-1, keepdims=True)
    offset = value_vectors - center
    spread = jnp.mean(offset * offset, axis=-1, keepdims=True)
    return offset * lax.rsqrt(spread + 1e-05) * scaling + shifts


def gelu_exact(value_vectors):
    return jax.nn.gelu(value_vectors, approximate=False)


def combine_rounds(outputs, totals):
    highest = jnp.max(totals, axis=0, keepdims=True)
    weights = jnp.exp(totals - highest)
    weights = weights / jnp.sum(weights, axis=0, keepdims=True)
    by_head = outputs.reshape(outputs.shape[:-1] + (totals.shape[-1], -1))
    return jnp.sum(weights[..., None] * by_head, axis=0).reshape(outputs.shape[1:])


def home_slots(places, row_count):
    target = places // row_count
    prior_state = (target[:, None, :] == target[:, :, None]) & (
        places[:, None, :] < places[:, :, None]
    )
    return (target, jnp.sum(prior_state.astype(jnp.int32), axis=2))


def sorted_slots(orders, row_count):
    source = orders // row_count
    ladder = jnp.arange(row_count, dtype=jnp.int32)
    prior_state = (source[:, None, :] == source[:, :, None]) & (
        ladder[None, None, :] < ladder[None, :, None]
    )
    return (source, jnp.sum(prior_state.astype(jnp.int32), axis=2))


def slot_lookup(owners, slot_index, devices, capacity):
    groups, row_count = owners.shape
    flat_index = owners * capacity + slot_index
    lookup = jnp.full((groups, devices * capacity), row_count, jnp.int32)
    filler = jnp.broadcast_to(jnp.arange(row_count, dtype=jnp.int32), (groups, row_count))
    lookup = lookup.at[jnp.arange(groups)[:, None], flat_index].set(filler)
    return jnp.transpose(lookup.reshape(groups, devices, capacity), (1, 0, 2))


def gather_slots(value_vectors, member, lookup):
    padding = jnp.zeros((value_vectors.shape[0], 1) + value_vectors.shape[2:], value_vectors.dtype)
    padded = jnp.concatenate([value_vectors, padding], axis=1)
    return padded[member[None, :, None], lookup]


def settle(received, owners, slot_index):
    return received[owners, jnp.arange(owners.shape[0])[:, None], slot_index]


def build_routes(orders, places, devices, capacity):
    rounds, sequences, row_count = orders.shape
    order_flat = orders.reshape(rounds * sequences, row_count)
    target, home_slot = home_slots(places.reshape(rounds * sequences, row_count), row_count)
    source, sorted_slot = sorted_slots(order_flat, row_count)
    home_lookup = slot_lookup(target, home_slot, devices, capacity)
    back_lookup = slot_lookup(source, sorted_slot, devices, capacity)
    return (target, home_slot, source, sorted_slot, home_lookup, back_lookup, order_flat)


def trade_rows(first_part, second_part):
    return (
        lax.all_to_all(first_part, ("seq", "sub"), split_axis=0, concat_axis=0, tiled=True),
        lax.all_to_all(second_part, ("seq", "sub"), split_axis=0, concat_axis=0, tiled=True),
    )


def trade_results(first_part, second_part):
    return (
        lax.all_to_all(first_part, ("seq", "sub"), split_axis=0, concat_axis=0, tiled=True),
        lax.all_to_all(second_part, ("seq", "sub"), split_axis=0, concat_axis=0, tiled=True),
    )


def window(rows_here, rows_left):
    groups = rows_here.shape[0]
    extended = jnp.concatenate([rows_left, rows_here], axis=1)
    extended = extended.reshape((groups, -1, BLOCK) + rows_here.shape[2:])
    return jnp.concatenate([extended[:, :-1], extended[:, 1:]], axis=2)


def score_parts(shared_rows, order_rows, halo_shared, halo_order):
    groups, row_count, features = shared_rows.shape
    blocks = row_count // BLOCK
    queries = shared_rows.reshape(groups, blocks, BLOCK, HEADS, HEAD_DIM)
    key_rows = window(shared_rows, halo_shared).reshape(groups, blocks, 2 * BLOCK, HEADS, HEAD_DIM)
    key_float = key_rows.astype(jnp.float32)
    mean_square = jnp.mean(key_float * key_float, axis=-1) + 1e-06
    key_scale = lax.rsqrt(mean_square) / HEAD_DIM
    raw_scores = jnp.einsum(
        "gcqhd,gckhd->gchqk", queries, key_rows, preferred_element_type=jnp.float32
    )
    query_pos = order_rows.reshape(groups, blocks, BLOCK)
    key_pos = window(order_rows, halo_order)
    is_later = (key_pos[:, :, None, :] > query_pos[:, :, :, None])[:, :, None]
    is_self = (key_pos[:, :, None, :] == query_pos[:, :, :, None])[:, :, None]
    scale_row = jnp.transpose(key_scale, (0, 1, 3, 2))[:, :, :, None, :]
    scores = jnp.where(
        is_later, -1000000000.0, jnp.where(is_self, -100000.0, raw_scores * scale_row)
    )
    highest = jnp.max(scores, axis=-1, keepdims=True)
    log_total = highest + jnp.log(jnp.sum(jnp.exp(scores - highest), axis=-1, keepdims=True))
    probability = jnp.exp(scores - log_total)
    return (
        queries,
        key_rows,
        key_float,
        mean_square,
        key_scale,
        scale_row,
        raw_scores,
        is_later | is_self,
        log_total,
        probability,
    )


def attend(shared_rows, value_rows, order_rows, halo):
    halo_shared, halo_value, halo_order = halo
    parts = score_parts(shared_rows, order_rows, halo_shared, halo_order)
    groups, row_count, features = shared_rows.shape
    value_keys = window(value_rows, halo_value).reshape(
        groups, row_count // BLOCK, 2 * BLOCK, HEADS, HEAD_DIM
    )
    mixed = jnp.einsum(
        "gchqk,gckhd->gcqhd",
        parts[9].astype(jnp.bfloat16),
        value_keys,
        preferred_element_type=jnp.float32,
    )
    log_total = jnp.transpose(parts[8][..., 0], (0, 1, 3, 2)).reshape(groups, row_count, HEADS)
    return (mixed.reshape(groups, row_count, features), log_total)


def fold_window(grads_window, groups, row_count, features):
    grads_window = grads_window.reshape(groups, row_count // BLOCK, 2 * BLOCK, features)
    empty = jnp.zeros((groups, 1, BLOCK, features), jnp.float32)
    extended = jnp.concatenate([grads_window[:, :, :BLOCK], empty], axis=1) + jnp.concatenate(
        [empty, grads_window[:, :, BLOCK:]], axis=1
    )
    return (extended[:, 1:].reshape(groups, row_count, features), extended[:, 0])


def attend_back(shared_rows, value_rows, order_rows, halo, grad_out, grad_total):
    halo_shared, halo_value, halo_order = halo
    (
        queries,
        key_rows,
        key_float,
        mean_square,
        key_scale,
        scale_row,
        raw_scores,
        masked,
        log_total,
        probability,
    ) = score_parts(shared_rows, order_rows, halo_shared, halo_order)
    groups, row_count, features = shared_rows.shape
    blocks = row_count // BLOCK
    value_keys = window(value_rows, halo_value).reshape(groups, blocks, 2 * BLOCK, HEADS, HEAD_DIM)
    prob_low = probability.astype(jnp.bfloat16)
    grad_heads = grad_out.reshape(groups, blocks, BLOCK, HEADS, HEAD_DIM)
    grad_log = jnp.transpose(
        grad_total.astype(jnp.float32).reshape(groups, blocks, BLOCK, HEADS), (0, 1, 3, 2)
    )[..., None]
    grad_prob = jnp.einsum(
        "gcqhd,gckhd->gchqk", grad_heads, value_keys, preferred_element_type=jnp.float32
    )
    inner = jnp.sum(probability * grad_prob, axis=-1, keepdims=True)
    grad_score = jnp.where(masked, 0.0, probability * (grad_prob - inner + grad_log))
    grad_scale = jnp.transpose(jnp.sum(grad_score * raw_scores, axis=3), (0, 1, 3, 2))
    grad_raw = (grad_score * scale_row).astype(jnp.bfloat16)
    grad_query = jnp.einsum(
        "gchqk,gckhd->gcqhd", grad_raw, key_rows, preferred_element_type=jnp.float32
    )
    grad_key = jnp.einsum(
        "gchqk,gcqhd->gckhd", grad_raw, queries, preferred_element_type=jnp.float32
    )
    grad_key = grad_key - (grad_scale * key_scale / mean_square)[..., None] * key_float / HEAD_DIM
    grad_value = jnp.einsum(
        "gchqk,gcqhd->gckhd", prob_low, grad_heads, preferred_element_type=jnp.float32
    )
    key_home, key_left = fold_window(grad_key, groups, row_count, features)
    value_home, value_left = fold_window(grad_value, groups, row_count, features)
    back_key, back_value = from_behind((key_left, value_left), ("seq", "sub"), -1)
    grad_shared = grad_query.reshape(groups, row_count, features) + key_home
    grad_shared = grad_shared.at[:, row_count - BLOCK :].add(back_key)
    grad_values = value_home.at[:, row_count - BLOCK :].add(back_value)
    return (grad_shared, grad_values)


def sorted_attention(shared_query_key, value_vectors, routes):
    target, home_slot, source, sorted_slot, home_lookup, back_lookup, order_flat = routes
    groups = target.shape[0]
    member = jnp.arange(groups) % shared_query_key.shape[0]
    got_shared, got_values = trade_rows(
        gather_slots(shared_query_key, member, home_lookup),
        gather_slots(value_vectors, member, home_lookup),
    )
    shared_rows = settle(got_shared, source, sorted_slot)
    value_rows = settle(got_values, source, sorted_slot)
    halo = from_behind(
        (shared_rows[:, -BLOCK:], value_rows[:, -BLOCK:], order_flat[:, -BLOCK:]), ("seq", "sub"), 1
    )
    mixed, log_total = attend(shared_rows, value_rows, order_flat, halo)
    all_groups = jnp.arange(groups)
    got_mixed, got_total = trade_results(
        gather_slots(mixed, all_groups, back_lookup),
        gather_slots(log_total, all_groups, back_lookup),
    )
    return (
        settle(got_mixed, target, home_slot),
        settle(got_total, target, home_slot),
        (shared_rows, value_rows, halo),
    )


def round_outputs(normalized_input, query_key_weight, value_projection_weight, routes, rounds):
    shared_query_key = jnp.einsum(
        "srd,de->sre", normalized_input, query_key_weight, preferred_element_type=jnp.float32
    ).astype(jnp.bfloat16)
    value_vectors = jnp.einsum(
        "srd,de->sre", normalized_input, value_projection_weight, preferred_element_type=jnp.float32
    ).astype(jnp.bfloat16)
    mixed, log_total, kept = sorted_attention(shared_query_key, value_vectors, routes)
    sequences, row_count, features = normalized_input.shape
    outputs = mixed.reshape(rounds, sequences, row_count, features)
    totals = log_total.reshape(rounds, sequences, row_count, HEADS)
    return (shared_query_key, value_vectors, outputs, totals, kept)


def collect(weight_stack, layer_index):
    (
        attend_gain,
        attend_shift,
        query_key_weight,
        value_projection_weight,
        output_projection_weight,
        feed_gain,
        feed_shift,
        upper_projection_weight,
        upper_projection_bias,
        lower_projection_weight,
        lower_projection_bias,
    ) = tuple((shard_piece[layer_index] for shard_piece in weight_stack))
    return (
        lax.all_gather(attend_gain, ("seq", "sub"), axis=0, tiled=True),
        lax.all_gather(attend_shift, ("seq", "sub"), axis=0, tiled=True),
        lax.all_gather(query_key_weight, ("seq", "sub"), axis=0, tiled=True),
        lax.all_gather(value_projection_weight, ("seq", "sub"), axis=0, tiled=True),
        lax.all_gather(output_projection_weight, ("seq", "sub"), axis=0, tiled=True),
        lax.all_gather(feed_gain, ("seq", "sub"), axis=0, tiled=True),
        lax.all_gather(feed_shift, ("seq", "sub"), axis=0, tiled=True),
        lax.all_gather(upper_projection_weight, ("seq", "sub"), axis=0, tiled=True),
        lax.all_gather(upper_projection_bias, ("seq", "sub"), axis=0, tiled=True),
        lax.all_gather(lower_projection_weight, ("seq", "sub"), axis=0, tiled=True),
        lax.all_gather(lower_projection_bias, ("seq", "sub"), axis=0, tiled=True),
    )


def spread_grads(level_grads):
    (
        attend_gain,
        attend_shift,
        query_key_weight,
        value_projection_weight,
        output_projection_weight,
        feed_gain,
        feed_shift,
        upper_projection_weight,
        upper_projection_bias,
        lower_projection_weight,
        lower_projection_bias,
    ) = level_grads
    return (
        lax.psum_scatter(attend_gain, ("seq", "sub"), scatter_dimension=0, tiled=True),
        lax.psum_scatter(attend_shift, ("seq", "sub"), scatter_dimension=0, tiled=True),
        lax.psum_scatter(query_key_weight.astype(jnp.bfloat16), ("seq", "sub"), scatter_dimension=0, tiled=True),
        lax.psum_scatter(value_projection_weight.astype(jnp.bfloat16), ("seq", "sub"), scatter_dimension=0, tiled=True),
        lax.psum_scatter(output_projection_weight.astype(jnp.bfloat16), ("seq", "sub"), scatter_dimension=0, tiled=True),
        lax.psum_scatter(feed_gain, ("seq", "sub"), scatter_dimension=0, tiled=True),
        lax.psum_scatter(feed_shift, ("seq", "sub"), scatter_dimension=0, tiled=True),
        lax.psum_scatter(upper_projection_weight.astype(jnp.bfloat16), ("seq", "sub"), scatter_dimension=0, tiled=True),
        lax.psum_scatter(upper_projection_bias, ("seq", "sub"), scatter_dimension=0, tiled=True),
        lax.psum_scatter(lower_projection_weight.astype(jnp.bfloat16), ("seq", "sub"), scatter_dimension=0, tiled=True),
        lax.psum_scatter(lower_projection_bias, ("seq", "sub"), scatter_dimension=0, tiled=True),
    )


def layer_pass(first_half, second_half, grad_one, grad_two, params, routes, rounds):
    (
        attend_gain,
        attend_shift,
        query_key_weight,
        value_projection_weight,
        output_projection_weight,
        feed_gain,
        feed_shift,
        upper_projection_weight,
        upper_projection_bias,
        lower_projection_weight,
        lower_projection_bias,
    ) = params
    attend_norm, attend_pull = jax.vjp(
        layer_norm, second_half, attend_gain.astype(jnp.float32), attend_shift.astype(jnp.float32)
    )
    normalized_input = attend_norm.astype(jnp.bfloat16)
    shared_query_key, value_vectors, outputs, totals, kept = round_outputs(
        normalized_input, query_key_weight, value_projection_weight, routes, rounds
    )
    attention_result, combine_pull = jax.vjp(combine_rounds, outputs, totals)
    attended_low = attention_result.astype(jnp.bfloat16)
    top_one = first_half + jnp.einsum(
        "srd,de->sre", attended_low, output_projection_weight, preferred_element_type=jnp.float32
    )
    feed_norm, feed_pull = jax.vjp(
        layer_norm, top_one, feed_gain.astype(jnp.float32), feed_shift.astype(jnp.float32)
    )
    feed_forward_input = feed_norm.astype(jnp.bfloat16)
    prior_state = jnp.einsum(
        "srd,df->srf",
        feed_forward_input,
        upper_projection_weight,
        preferred_element_type=jnp.float32,
    ) + upper_projection_bias.astype(jnp.float32)
    hidden_activation, active_pull = jax.vjp(gelu_exact, prior_state)
    active_low = hidden_activation.astype(jnp.bfloat16)
    feed_out = jnp.einsum(
        "srf,fd->srd", active_low, lower_projection_weight, preferred_element_type=jnp.float32
    ) + lower_projection_bias.astype(jnp.float32)
    top_two = second_half + feed_out
    feed_grad = grad_two.astype(jnp.bfloat16)
    down_weight_grad = jnp.einsum(
        "srf,srd->fd", active_low, feed_grad, preferred_element_type=jnp.float32
    )
    down_bias_grad = jnp.sum(feed_grad.astype(jnp.float32), axis=(0, 1))
    active_grad = jnp.einsum(
        "srd,fd->srf", feed_grad, lower_projection_weight, preferred_element_type=jnp.float32
    )
    before_grad = active_pull(active_grad)[0].astype(jnp.bfloat16)
    up_weight_grad = jnp.einsum(
        "srd,srf->df", feed_forward_input, before_grad, preferred_element_type=jnp.float32
    )
    up_bias_grad = jnp.sum(before_grad.astype(jnp.float32), axis=(0, 1))
    norm_grad = jnp.einsum(
        "srf,df->srd", before_grad, upper_projection_weight, preferred_element_type=jnp.float32
    )
    one_part, feed_gain_grad, feed_shift_grad = feed_pull(norm_grad)
    total_one = grad_one + one_part
    out_grad = total_one.astype(jnp.bfloat16)
    output_weight_grad = jnp.einsum(
        "srd,sre->de", attended_low, out_grad, preferred_element_type=jnp.float32
    )
    attended_grad = jnp.einsum(
        "sre,de->srd", out_grad, output_projection_weight, preferred_element_type=jnp.float32
    )
    outputs_grad, totals_grad = combine_pull(attended_grad)
    target, home_slot, source, sorted_slot, home_lookup, back_lookup, order_flat = routes
    sequences, row_count, features = top_one.shape
    groups = rounds * sequences
    all_groups = jnp.arange(groups)
    outputs_low = outputs_grad.astype(jnp.bfloat16).reshape(groups, row_count, features)
    totals_low = totals_grad.astype(jnp.bfloat16).reshape(groups, row_count, HEADS)
    got_out, got_total = trade_rows(
        gather_slots(outputs_low, all_groups, home_lookup),
        gather_slots(totals_low, all_groups, home_lookup),
    )
    shared_rows, value_rows, halo = kept
    grad_shared, grad_values = attend_back(
        shared_rows,
        value_rows,
        order_flat,
        halo,
        settle(got_out, source, sorted_slot),
        settle(got_total, source, sorted_slot),
    )
    home_shared, home_values = trade_rows(
        gather_slots(grad_shared.astype(jnp.bfloat16), all_groups, back_lookup),
        gather_slots(grad_values.astype(jnp.bfloat16), all_groups, back_lookup),
    )
    shared_grad = jnp.sum(
        settle(home_shared, target, home_slot)
        .astype(jnp.float32)
        .reshape(rounds, sequences, row_count, features),
        axis=0,
    ).astype(jnp.bfloat16)
    values_grad = jnp.sum(
        settle(home_values, target, home_slot)
        .astype(jnp.float32)
        .reshape(rounds, sequences, row_count, features),
        axis=0,
    ).astype(jnp.bfloat16)
    shared_weight_grad = jnp.einsum(
        "srd,sre->de", normalized_input, shared_grad, preferred_element_type=jnp.float32
    )
    value_weight_grad = jnp.einsum(
        "srd,sre->de", normalized_input, values_grad, preferred_element_type=jnp.float32
    )
    normed_grad = jnp.einsum(
        "sre,de->srd", shared_grad, query_key_weight, preferred_element_type=jnp.float32
    ) + jnp.einsum(
        "sre,de->srd", values_grad, value_projection_weight, preferred_element_type=jnp.float32
    )
    two_part, attend_gain_grad, attend_shift_grad = attend_pull(normed_grad)
    total_two = grad_two + two_part
    level_grads = (
        attend_gain_grad,
        attend_shift_grad,
        shared_weight_grad,
        value_weight_grad,
        output_weight_grad,
        feed_gain_grad,
        feed_shift_grad,
        up_weight_grad,
        up_bias_grad,
        down_weight_grad,
        down_bias_grad,
    )
    return (top_one, top_two, total_one, total_two, level_grads)


def general_plan(
    first_half,
    second_half,
    grad_first,
    grad_second,
    attend_gain,
    attend_shift,
    query_key_weight,
    value_projection_weight,
    output_projection_weight,
    feed_gain,
    feed_shift,
    upper_projection_weight,
    upper_projection_bias,
    lower_projection_weight,
    lower_projection_bias,
    sort_order,
    sort_place,
):
    weight_stack = (
        attend_gain,
        attend_shift,
        query_key_weight,
        value_projection_weight,
        output_projection_weight,
        feed_gain,
        feed_shift,
        upper_projection_weight,
        upper_projection_bias,
        lower_projection_weight,
        lower_projection_bias,
    )
    devices = lax.axis_size(("seq", "sub"))
    rounds = sort_order.shape[1]
    row_count = first_half.shape[1]
    capacity = 2 * max(1, row_count // devices)
    params = collect(weight_stack, 0)
    routes = build_routes(sort_order[0], sort_place[0], devices, capacity)
    first_out, second_out, first_grad, second_grad, level_grads = layer_pass(
        first_half, second_half, grad_first, grad_second, params, routes, rounds
    )
    stacked = tuple((entry[None].astype(jnp.float32) for entry in spread_grads(level_grads)))
    return (first_out, second_out, first_grad, second_grad) + stacked


class Links:
    def __init__(self, planes, send, receive, local):
        self.send, self.receive, self.local = send, receive, local
        self.used, self.used_local = 0, 0
        self.planes = planes
        seq, sub = lax.axis_index("seq"), lax.axis_index("sub")
        self.z, self.x = seq // 2, lax.rem(seq, 2)
        self.y, self.core = sub // 2, lax.rem(sub, 2)
        self.p = self.x * 4 + sub

    def near(self, step):
        x = 1 - self.x if step & 4 else self.x
        y = 1 - self.y if step & 2 else self.y
        core = 1 - self.core if step & 1 else self.core
        return (self.z * 2 + x, y * 2 + core), x * 4 + y * 2 + core

    def along(self, step):
        to = lax.rem(self.z + step, self.planes)
        back = lax.rem(self.z + self.planes - step, self.planes)
        return (to * 2 + self.x, self.y * 2 + self.core), to, back

    def greet(self):
        barrier = pltpu.get_barrier_semaphore()
        targets = [self.near(step)[0] for step in range(1, 8)]
        targets += [self.along(step)[0] for step in range(1, self.planes)]
        for target in targets:
            pl.semaphore_signal(barrier, inc=1, device_id=target, device_id_type=pl.DeviceIdType.MESH)
        self.greeted = len(targets)

    def meet(self):
        pl.semaphore_wait(pltpu.get_barrier_semaphore(), self.greeted)

    def push(self, source, target, device, start=True):
        copy = pltpu.make_async_remote_copy(
            src_ref=source,
            dst_ref=target,
            send_sem=self.send.at[self.used],
            recv_sem=self.receive.at[self.used],
            device_id=device,
            device_id_type=pl.DeviceIdType.MESH,
        )
        self.used += 1
        if start:
            copy.start()
        return copy

    def keep(self, source, target):
        copy = pltpu.make_async_copy(source, target, self.local.at[self.used_local])
        self.used_local += 1
        copy.start()
        return copy


class Chain:
    def __init__(self, links, ref):
        self.links, self.ref, self.first, self.sent = links, ref, links.used, []
        links.used += 5
        self.hand_on(links.z, links.z < 3, links.z > 0, 2)

    def hand_on(self, shard, rightward, leftward, ways):
        links = self.links
        steps = ((1, rightward), (-1, leftward)) if ways == 2 else ((None, rightward | leftward),)
        for step, wanted in steps:
            if step is None:
                step = jnp.where(rightward, 1, -1)
            to = jnp.clip(links.z + step, 0, 3)
            middle = jnp.where(to == 1, jnp.where(shard == 0, 0, shard - 1), jnp.where(shard == 3, 0, 2 - shard))
            arrival = jnp.where((to == 0) | (to == 3), jnp.abs(to - shard) - 1, middle)
            arrival = jnp.clip(arrival, 0, 2)
            copy = pltpu.make_async_remote_copy(
                src_ref=self.ref.at[shard],
                dst_ref=self.ref.at[shard],
                send_sem=links.send.at[self.first + len(self.sent)],
                recv_sem=links.receive.at[self.first + arrival],
                device_id=(to * 2 + links.x, links.y * 2 + links.core),
                device_id_type=pl.DeviceIdType.MESH,
            )
            self.sent.append((wanted, copy))
            pl.when(wanted)(copy.start)

    def arrive(self, index):
        links, z = self.links, self.links.z
        ends = jnp.where(z == 0, index + 1, 2 - index)
        inner = jnp.where(z == 1, (0, 2, 3)[index], (3, 1, 0)[index])
        shard = jnp.where((z == 0) | (z == 3), ends, inner)
        pltpu.make_async_remote_copy(
            src_ref=self.ref.at[shard],
            dst_ref=self.ref.at[shard],
            send_sem=links.send.at[self.first],
            recv_sem=links.receive.at[self.first + index],
            device_id=(z * 2 + links.x, links.y * 2 + links.core),
            device_id_type=pl.DeviceIdType.MESH,
        ).wait_recv()
        self.hand_on(shard, (shard < z) & (z < 3), (shard > z) & (z > 0), 1)
        return shard

    def finish(self):
        for wanted, copy in self.sent:
            pl.when(wanted)(copy.wait_send)


COPIES = 320


def link_scratch():
    return [
        pltpu.SemaphoreType.DMA((COPIES,)),
        pltpu.SemaphoreType.DMA((COPIES,)),
        pltpu.SemaphoreType.DMA((64,)),
    ]


def along_z(source, target):
    def transfer(links, here, there):
        own = links.keep(source(here, links.z), target(there, links.z))
        copies = []
        for step in range(1, links.planes):
            device, to, _ = links.along(step)
            copies.append(links.push(source(here, to), target(there, links.z), device))
        yield
        own.wait()
        for copy in copies:
            copy.wait()

    return transfer


def along_z_in_turn(source, target):
    def transfer(links, here, there):
        own = links.keep(source(here, links.z), target(there, links.z))
        copies = []
        for step in range(1, links.planes):
            device, to, _ = links.along(step)
            copies.append(links.push(source(here, to), target(there, links.z), device, start=False))
        outer = (links.z == 0) | (links.z == links.planes - 1)
        for copy in copies:
            pl.when(outer)(copy.start)
        yield
        for copy in copies:
            pl.when(jnp.logical_not(outer))(copy.start)
        yield
        own.wait()
        for copy in copies:
            copy.wait()

    return transfer


def along_z_outer_first(source, target):
    def transfer(links, here, there):
        copies = []
        for step in range(1, links.planes):
            device, to, _ = links.along(step)
            copy = links.push(source(here, to), target(there, links.z), device, start=False)
            copies.append(((to == 0) | (to == links.planes - 1), copy))
        for outer, copy in copies:
            pl.when(outer)(copy.start)
        yield
        for outer, copy in copies:
            pl.when(jnp.logical_not(outer))(copy.start)
        own = links.keep(source(here, links.z), target(there, links.z))
        yield
        own.wait()
        for _, copy in copies:
            copy.wait()

    return transfer


def over_plane(source, target):
    def transfer(links, here, there):
        own = links.keep(source(here, links.p), target(there, links.p))
        copies = []
        for step in (6, 7, 4, 5, 2, 3, 1):
            device, to = links.near(step)
            copies.append(links.push(source(here, to), target(there, links.p), device))
        yield
        own.wait()
        for copy in copies:
            copy.wait()

    return transfer


def over_chips(source, target):
    def transfer(links, here, there):
        own = links.keep(source(here, links.p), target(there, links.p))
        copies = []
        for step in (6, 4, 2):
            device, to = links.near(step)
            copies.append(links.push(source(here, to), target(there, links.p), device))
        sibling, _ = links.near(1)
        passed = [links.push(source(here, links.p), target(there, links.p), sibling)]
        yield
        for step, copy in zip((6, 4, 2), copies):
            copy.wait_recv()
            _, sender = links.near(step)
            passed.append(links.push(target(there, sender), target(there, sender), sibling))
        yield
        own.wait()
        for copy in copies:
            copy.wait_send()
        for copy in passed:
            copy.wait()

    return transfer


def everywhere(links, here, there):
    own = links.keep(here, there.at[links.z, links.p])
    copies = []
    for step in (6, 7, 4, 5, 2, 3, 1):
        copies.append(links.push(here, there.at[links.z, links.p], links.near(step)[0]))
    yield
    own.wait()
    for copy in copies:
        copy.wait()
    copies = []
    for step in range(1, links.planes):
        copies.append(links.push(there.at[links.z], there.at[links.z], links.along(step)[0]))
    yield
    for copy in copies:
        copy.wait()


def drive(transfers):
    while transfers:
        left = []
        for transfer in transfers:
            try:
                next(transfer)
                left.append(transfer)
            except StopIteration:
                pass
        transfers = left


def whole(ref, index):
    return ref


def block(ref, index):
    return ref.at[index]


def second(ref, index):
    return ref.at[:, index]


def rows_of(index):
    return pl.ds(pl.multiple_of(index * 128, 128), 128)


def pick_tile(table, index_ref, tile, part):
    return jnp.concatenate(
        [table[pl.ds(index_ref[tile, part * 32 + row], 1), :] for row in range(32)], axis=0
    )


def sort_tile(order, table, first, second, offset, tile):
    for part in range(4):
        start = pl.multiple_of(tile * 128 + part * 32 + offset, 32)
        picked = pick_tile(table, order, tile, part)
        first[pl.ds(start, 32), :] = picked[:, :128].astype(first.dtype)
        second[pl.ds(start, 32), :] = picked[:, 128:].astype(second.dtype)


def across(column):
    return jnp.broadcast_to(column, (128, 128)).T[:1, :]


def down(row):
    return jnp.broadcast_to(row, (128, 128)).T


def dot(a, b, contract):
    return lax.dot_general(a, b, (contract, ((), ())), preferred_element_type=jnp.float32)


def key_scales(keys):
    rows = keys.astype(jnp.float32)
    mean_square = jnp.mean(rows * rows, axis=-1, keepdims=True) + 1e-06
    return rows, mean_square, lax.rsqrt(mean_square) / HEAD_DIM


def half_turned(row):
    return jnp.concatenate([row[:, 64:], row[:, :64]], axis=1)


def windows(before, here):
    return [jnp.concatenate([before[:, 64:], here[:, :64]], axis=1), here]


def masked_scores(raw, scale, query_pos, key_pos):
    return jnp.where(
        key_pos > query_pos, LATER, jnp.where(key_pos == query_pos, SELF, raw * scale)
    )


def attend_tiles(tiles, unroll, order, order_rows, table, shared, values, mixed, total_sorted, last_scale):
    sort = functools.partial(sort_tile, order, table, shared, values, BLOCK)
    end = tiles * 128
    for tile in [tiles - 1] + list(range(unroll)):
        sort(tile)
    shared[:BLOCK, :] = shared[end : end + BLOCK, :]
    values[:BLOCK, :] = values[end : end + BLOCK, :]
    last_scale[...] = across(key_scales(shared[end - BLOCK : end + BLOCK, :])[2])

    def step_tiles(step, carry):
        first = step * unroll
        numbers = [lax.rem(first + tiles - 1, tiles)] + [first + k for k in range(unroll)]
        places = [order_rows[pl.ds(t, 1), :] for t in numbers]
        scale = [last_scale[...]]
        work = []
        for k in range(unroll):
            start = pl.multiple_of((first + k) * 128, 128)
            keys = [shared[pl.ds(pl.multiple_of(start + half * 64, 64), 128), :] for half in range(2)]
            vals = [values[pl.ds(pl.multiple_of(start + half * 64, 64), 128), :] for half in range(2)]
            own = jnp.concatenate([keys[0][64:], keys[1][64:]], axis=0)
            scale.append(across(key_scales(own)[2]))
            work.append((keys, vals))
        last_scale[...] = scale[-1]
        for k in range(unroll):
            sort(lax.rem(first + unroll + k, tiles))
        query_pos = jnp.concatenate([down(place) for place in places[1:]], axis=0)
        key_pos, key_scale = [], []
        for k in range(unroll):
            key_pos += windows(places[k], places[k + 1])
            key_scale += windows(scale[k], scale[k + 1])
        raw = [dot(k[64:], k, ((1,), (1,))) for keys, _ in work for k in keys]
        raw, key_pos, key_scale = (
            jnp.concatenate([jnp.broadcast_to(a, (64, 128)) for a in parts], axis=0)
            for parts in (raw, key_pos, key_scale)
        )
        scores = masked_scores(raw, key_scale, query_pos, key_pos)
        highest = jnp.max(scores, axis=-1, keepdims=True)
        total = highest + jnp.log(jnp.sum(jnp.exp(scores - highest), axis=-1, keepdims=True))
        prob = jnp.exp(scores - total).astype(jnp.bfloat16)
        rows = pl.ds(pl.multiple_of(first * 128, 128), unroll * 128)
        total = jnp.broadcast_to(total, (unroll * 128, 128))
        mixed[rows, 128:] = total
        total_sorted[rows, :] = total
        vals = [v for _, vals in work for v in vals]
        mixed[rows, :128] = jnp.concatenate(
            [dot(prob[64 * i : 64 * i + 64], v, ((1,), (0,))) for i, v in enumerate(vals)], axis=0
        )
        return carry

    lax.fori_loop(0, tiles // unroll, step_tiles, 0)


def attend_back_tiles(
    tiles, unroll, order, order_rows, table, shared, values, total_sorted,
    grad_sorted, grad_total_sorted, sums, scale_sums, last_scale,
):
    sort = functools.partial(sort_tile, order, table, grad_sorted, grad_total_sorted, 0)
    end = tiles * 128
    for tile in range(unroll):
        sort(tile)
    last_scale[...] = across(key_scales(shared[end - BLOCK : end + BLOCK, :])[2])
    scale_sums[...] = jnp.zeros_like(scale_sums)
    sums[end : end + 128, :] = jnp.zeros((128, 256), jnp.float32)
    early = lax.broadcasted_iota(jnp.int32, (1, 128), 1) < 64

    def step_tiles(step, carry):
        first = step * unroll
        numbers = [lax.rem(first + tiles - 1, tiles)] + [first + k for k in range(unroll)]
        places = [order_rows[pl.ds(t, 1), :] for t in numbers]
        scale = [last_scale[...]]
        work = []
        for k in range(unroll):
            start = pl.multiple_of((first + k) * 128, 128)
            keys = [shared[pl.ds(pl.multiple_of(start + half * 64, 64), 128), :] for half in range(2)]
            vals = [values[pl.ds(pl.multiple_of(start + half * 64, 64), 128), :] for half in range(2)]
            own = jnp.concatenate([keys[0][64:], keys[1][64:]], axis=0)
            scale.append(across(key_scales(own)[2]))
            tile = pl.ds(start, 128)
            work.append(
                (keys, vals, grad_sorted[tile, :], grad_total_sorted[tile, :], total_sorted[tile, :])
            )
        last_scale[...] = scale[-1]
        for k in range(unroll):
            sort(lax.rem(first + unroll + k, tiles))
        blocks = 2 * unroll
        scale_parts = [0.0] * (unroll + 1)
        query_pos = jnp.concatenate([down(place) for place in places[1:]], axis=0)
        key_pos, key_scale = [], []
        for k in range(unroll):
            key_pos += windows(places[k], places[k + 1])
            key_scale += windows(scale[k], scale[k + 1])
        keys = [k for item in work for k in item[0]]
        vals = [v for item in work for v in item[1]]
        grads, grad_totals, totals = (
            jnp.concatenate([item[n] for item in work], axis=0) for n in (2, 3, 4)
        )
        own = [slice(64 * i, 64 * i + 64) for i in range(blocks)]
        raw = [dot(k[64:], k, ((1,), (1,))) for k in keys]
        grad_prob = [dot(grads[own[i]], v, ((1,), (1,))) for i, v in enumerate(vals)]
        raw, grad_prob, key_pos, key_scale = (
            jnp.concatenate([jnp.broadcast_to(a, (64, 128)) for a in parts], axis=0)
            for parts in (raw, grad_prob, key_pos, key_scale)
        )
        prob = jnp.exp(masked_scores(raw, key_scale, query_pos, key_pos) - totals)
        inner = jnp.sum(prob * grad_prob, axis=-1, keepdims=True)
        grad_score = jnp.where(
            key_pos < query_pos, prob * (grad_prob + (grad_totals - inner)), 0.0
        )
        product = grad_score * raw
        for index in range(blocks):
            k, half = index // 2, index % 2
            part = jnp.sum(product[own[index]], axis=0, keepdims=True)
            if half == 0:
                turned = half_turned(part)
                scale_parts[k] += jnp.where(early, 0.0, turned)
                scale_parts[k + 1] += jnp.where(early, turned, 0.0)
            else:
                scale_parts[k + 1] += part
        grad_raw = (grad_score * key_scale).astype(jnp.bfloat16)
        prob = prob.astype(jnp.bfloat16)
        key_parts = [dot(grad_raw[own[i]], keys[i][64:], ((0,), (0,))) for i in range(blocks)]
        value_parts = [dot(prob[own[i]], grads[own[i]], ((0,), (0,))) for i in range(blocks)]
        query_parts = [dot(grad_raw[own[i]], keys[i], ((1,), (0,))) for i in range(blocks)]
        key_sums = [key_parts[0][:64]] + [
            key_parts[i][64:] + query_parts[i] + (key_parts[i + 1][:64] if i + 1 < blocks else 0.0)
            for i in range(blocks)
        ]
        value_sums = [value_parts[0][:64]] + [
            value_parts[i][64:] + (value_parts[i + 1][:64] if i + 1 < blocks else 0.0)
            for i in range(blocks)
        ]
        for index in range(blocks):
            rows = pl.ds(pl.multiple_of(first * 128 + index * 64, 64), 64)
            sums[rows, :128] = key_sums[index + 1]
            sums[rows, 128:] = value_sums[index + 1]
        for k in range(unroll):
            scale_sums[pl.ds(first + k, 1), :] = scale_parts[k + 1]
        before = jnp.where(step == 0, tiles, numbers[0])
        rows = pl.ds(pl.multiple_of(before * 128 + 64, 64), 64)
        sums[rows, :128] += key_sums[0]
        sums[rows, 128:] += value_sums[0]
        scale_sums[pl.ds(before, 1), :] += scale_parts[0]
        return carry

    lax.fori_loop(0, tiles // unroll, step_tiles, 0)
    sums[end - 128 : end, :] += sums[end : end + 128, :]
    scale_sums[pl.ds(tiles - 1, 1), :] += scale_sums[pl.ds(tiles, 1), :]

    def finish(step, carry):
        for part in range(2):
            tile = step * 2 + part
            rows = rows_of(tile)
            start = pl.multiple_of(tile * 128 + 64, 64)
            keys, mean_square, scale = key_scales(shared[pl.ds(start, 128), :])
            factor = down(scale_sums[pl.ds(tile, 1), :]) * (scale / (mean_square * HEAD_DIM))
            sums[rows, :128] -= factor * keys
        return carry

    lax.fori_loop(0, tiles // 2, finish, 0)


VMEM = pl.BlockSpec(memory_space=pltpu.VMEM)
ANY = pl.BlockSpec(memory_space=pl.ANY)


def narrow(ref, index):
    return ref.at[:, index, :, pl.ds(0, HEAD_DIM)]


def normal_parts(rows):
    center = jnp.mean(rows, axis=-1, keepdims=True)
    offset = rows - center
    spread = jnp.mean(offset * offset, axis=-1, keepdims=True)
    inverse = lax.rsqrt(spread + 1e-05)
    return offset * inverse, inverse


def norm_back(grad, rows, gain):
    unit, inverse = normal_parts(rows)
    scaled = grad * gain
    shared = jnp.mean(scaled, axis=-1, keepdims=True)
    along = jnp.mean(scaled * unit, axis=-1, keepdims=True)
    return (
        (scaled - shared - unit * along) * inverse,
        jnp.sum(grad * unit, axis=0, keepdims=True),
        jnp.sum(grad, axis=0, keepdims=True),
    )


def gelu_parts(rows):
    below = 0.5 * (1.0 + lax.erf(rows * 0.7071067811865476))
    bell = jnp.exp(-0.5 * rows * rows) * 0.3989422804014327
    return rows * below, below + rows * bell


def open_part(
    links, planes,
    sort_order, sort_place, gain_a_in, shift_a_in, gain_f_in, shift_f_in, bias_up_in, bias_down_in,
    x2, wqk, wv, wo, wup, wdown, g2,
    ints, all_ints, floats, all_floats, gains, bias_up, order_rows, place_rows, order_s, place_s, normed, df,
    wqk_line, wv_line, wo_line, wup_rows, wqk_pair, wv_pair, heads, head_table, table, sums,
    shared, values, total_sorted, mixed_home, total_home, last_scale,
    wo_all, wup_part, wdown_part, df_plane, mixed_in, total_in,
):
    low, full = jnp.bfloat16, jnp.float32
    sub = links.y * 2 + links.core
    tiles = planes * 8
    ints[...] = jnp.concatenate([sort_order[...], sort_place[...]], axis=0)
    lane = lax.broadcasted_iota(jnp.int32, (1, 128), 1) // 32

    def spread(vector):
        wide = jnp.concatenate([vector[...].astype(full)] * 4, axis=1)
        return jnp.where(lane == sub, wide, 0.0)

    floats[...] = jnp.concatenate(
        [spread(v) for v in (gain_a_in, shift_a_in, gain_f_in, shift_f_in, bias_down_in)]
        + [bias_up_in[...].astype(full), jnp.zeros((2, 128), full)],
        axis=0,
    )
    df[...] = g2[...].astype(low)
    links.meet()
    share_floats = everywhere(links, floats, all_floats)
    next(share_floats)
    share_ints = everywhere(links, ints, all_ints)
    next(share_ints)

    def pair_columns(ref, z):
        return ref.at[:, pl.ds(pl.multiple_of(z * 256, 256), 256)]

    pair_shares = [
        along_z(pair_columns, block)(links, a, b) for a, b in ((wqk, wqk_line), (wv, wv_line))
    ]
    for transfer in pair_shares:
        next(transfer)
    wo_share = along_z(whole, block)(links, wo, wo_line)
    next(wo_share)
    df_share = over_chips(whole, block)(links, df, df_plane)
    next(df_share)
    unit, _ = normal_parts(x2[...])
    next(share_floats)

    def upper_columns(chunk):
        def columns(ref, p):
            return ref.at[:, pl.ds(pl.multiple_of((chunk * 8 + p) * 128, 128), 128)]

        def landing(ref, p):
            return ref.at[p, :, pl.ds(chunk * 128, 128)]

        return over_plane(columns, landing)

    drive([share_floats])

    def vector_of(row, z_step=2):
        chunks = []
        for chunk in range(8):
            z, x = chunk // 2, chunk % 2
            parts = [all_floats[z, x * 4 + u, row : row + 1, :] for u in range(4)]
            chunks.append(parts[0] + parts[1] + parts[2] + parts[3])
        return jnp.concatenate(chunks, axis=1)

    gain, shift = vector_of(0), vector_of(1)
    normed[links.z] = (unit * gain + shift).astype(low)
    normed_chain = Chain(links, normed)
    for transfer in pair_shares:
        drive([transfer])
    pair_shares = [
        over_chips(whole, second)(links, a, b) for a, b in ((wqk_line, wqk_pair), (wv_line, wv_pair))
    ]
    for transfer in pair_shares:
        next(transfer)
    next(share_ints)
    upper_shares = [upper_columns(chunk)(links, wup, wup_rows) for chunk in range(planes)]
    for transfer in upper_shares:
        next(transfer)
    for transfer in pair_shares:
        next(transfer)
    gains[0:1, :] = gain
    gains[1:2, :] = shift
    for row in (2, 3, 4):
        gains[row : row + 1, :] = vector_of(row)
    for z in range(planes):
        bias_up[:, z * 128 : (z + 1) * 128] = all_floats[z, links.p, 5:6, :]
    drive(pair_shares)
    drive([share_ints])
    for z in range(planes):
        for p in range(8):
            tile = z * 8 + p
            order_rows[tile : tile + 1, :] = all_ints[z, p, pl.ds(sub, 1), :]
            place_rows[tile : tile + 1, :] = all_ints[z, p, pl.ds(sub + 4, 1), :]
    to_scalars = [links.keep(order_rows, order_s), links.keep(place_rows, place_s)]

    def head_columns(z):
        def columns(ref, p):
            return ref.at[z, :, pl.ds(pl.multiple_of((p // 4) * 256, 256), 256)]

        return columns

    def landing(z):
        return lambda ref, p: ref.at[z, p]

    def project(z):
        rows = normed[z]
        for weights, offset in ((wqk_pair, 0), (wv_pair, 128)):
            result = dot(rows, weights[...].reshape(-1, 256), ((1,), (0,))).astype(low)
            heads[z, :, offset : offset + 128] = result[:, :128]
            heads[z, :, 256 + offset : 384 + offset] = result[:, 128:]
        transfer = over_chips(head_columns(z), landing(z))(links, heads, head_table)
        next(transfer)
        return transfer

    head_shares = [project(links.z)]
    next(df_share)
    for index in range(3):
        head_shares.append(project(normed_chain.arrive(index)))
        next(head_shares[-2])
    for transfer in upper_shares:
        drive([transfer])
    up_share = along_z_in_turn(whole, block)(links, wup_rows, wup_part)
    next(up_share)

    def first_rows(ref, z):
        return ref.at[pl.ds(0, 64), :]

    def first_landing(ref, z):
        return ref.at[z, pl.ds(0, 64), :]

    down_share = along_z_in_turn(first_rows, first_landing)(links, wdown, wdown_part)
    next(down_share)
    next(head_shares[-1])
    drive([wo_share])
    wo_share = over_chips(whole, second)(links, wo_line, wo_all)
    for copy in to_scalars:
        copy.wait()
    drive(head_shares)
    shares = [df_share, up_share, down_share]
    next(up_share)
    next(down_share)
    next(wo_share)

    def load(tile, carry):
        table[rows_of(tile), :] = head_table[tile // 8, lax.rem(tile, 8)].astype(full)
        return carry

    lax.fori_loop(0, tiles, load, 0)
    attend_tiles(
        tiles, 2, order_s, order_rows, table, shared, values, sums, total_sorted, last_scale
    )
    next(wo_share)
    kept = []
    sent = []
    for step in (6, 7, 4, 5, 2, 3, 1, 0):
        device, p = links.near(step)

        def unsort(z, carry):
            totals = []
            for part in range(4):
                picked = pick_tile(sums, place_s, z * 8 + p, part)
                mixed_home[p, z, part * 32 : part * 32 + 32, :] = picked[:, :128].astype(low)
                totals.append(picked[:, 128:])
            total_home[p, pl.ds(z, 1), :] = jnp.concatenate(totals, axis=0).T[:1, :]
            return carry

        lax.fori_loop(0, planes, unsort, 0)
        for here, there in ((mixed_home, mixed_in), (total_home, total_in)):
            source, target = here.at[p], there.at[links.p]
            if step:
                sent.append(links.push(source, target, device))
            else:
                kept.append(links.keep(source, target))
    normed_chain.finish()
    for copy in kept + sent:
        copy.wait()
    return wo_share, shares


def feed_part(
    links, planes, wo_share, weight_shares,
    x1, g1, y1_out, g1_out, gains, bias_up, sums, table, head_table, mixed_home, total_home,
    wo_all, wup_part, wdown_part, df_plane, mixed_in, total_in, dtotal_in, attended, arrived, h2, act, dpre,
    kept, from_sibling, to_chip, from_chip, up_grad, up_parts, down_grad, down_parts, dout, datt_out, datt,
    up_bias, feed_gain, feed_shift, y2_sibling, y2_chip, out_sibling, wdown,
):
    low, full = jnp.bfloat16, jnp.float32

    def weight_rows(head, z):
        return pl.ds(pl.multiple_of((head * planes + z) * 128, 128), 128)

    def wo_rows(z):
        return wo_all[z].reshape(256, -1)

    def combine(z, carry):
        for x in range(2):
            totals = [down(total_in[x * 4 + u, pl.ds(z, 1), :]) for u in range(4)]
            highest = jnp.maximum(
                jnp.maximum(totals[0], totals[1]), jnp.maximum(totals[2], totals[3])
            )
            parts = [jnp.exp(t - highest) for t in totals]
            inverse = 1.0 / (parts[0] + parts[1] + parts[2] + parts[3])
            result = 0.0
            for u in range(4):
                weight = parts[u] * inverse
                sums[weight_rows(x * 4 + u, z), :128] = weight
                result += weight * mixed_in[x * 4 + u, z].astype(full)
            attended[z, :, x * 128 : (x + 1) * 128] = result.astype(low)
        return carry

    lax.fori_loop(0, planes, combine, 0)
    share = along_z(block, block)(links, attended, arrived)
    next(share)

    def last_rows(ref, z):
        return ref.at[pl.ds(64, 64), :]

    def last_landing(ref, z):
        return ref.at[z, pl.ds(64, 64), :]

    down_share = along_z(last_rows, last_landing)(links, wdown, wdown_part)
    next(down_share)
    drive([wo_share])
    drive([share])
    y1 = x1[...]
    for z in range(planes):
        y1 += dot(arrived[z], wo_rows(z), ((1,), (0,)))
    y1_out[...] = y1
    unit, _ = normal_parts(y1)
    own_rows = pl.ds(pl.multiple_of(links.p * 128, 128), 128)
    h2[own_rows, :] = (unit * gains[2:3, :] + gains[3:4, :]).astype(low)

    sibling, _ = links.near(1)
    own_h2 = h2.at[own_rows, :]
    direct = {step: links.push(own_h2, own_h2, links.near(step)[0]) for step in (2, 4)}
    handed = {0: links.push(own_h2, own_h2, sibling)}
    drive(weight_shares + [down_share])

    half = wup_part.shape[3] // 2

    def upper_back(part, carry):
        rows = pl.ds(pl.multiple_of(part * 256, 256), 256)
        grad = df_plane[pl.ds(part * 2, 2)].reshape(256, -1)
        result = dot(grad, wdown_part[...].reshape(half * 2, -1), ((1,), (1,)))
        table[rows, :] = result[:, :half]
        table[pl.ds(pl.multiple_of(1024 + part * 256, 256), 256), :] = result[:, half:]
        return carry

    lax.fori_loop(0, 4, upper_back, 0)

    def pass_on(step):
        direct[step].wait_recv()
        block_rows = h2.at[rows_of(links.near(step)[1]), :]
        handed[step] = links.push(block_rows, block_rows, sibling)

    def feed(slot, step):
        handed[step].wait_recv()
        chip = links.near(step)[1] // 2
        rows = pl.ds(pl.multiple_of(chip * 256, 256), 256)
        before = dot(h2[rows, :], wup_part[...].reshape(-1, 2 * half), ((1,), (0,))) + bias_up[...]
        value, slope = gelu_parts(before)
        act[rows, :] = value.astype(low)
        grad = jnp.concatenate(
            [table[rows, :], table[pl.ds(pl.multiple_of(1024 + chip * 256, 256), 256), :]], axis=1
        )
        grad = (grad * slope).astype(low)
        dpre[rows, :] = grad
        kept[slot] = dot(grad, wup_part[...].reshape(-1, 2 * half), ((1,), (1,))).reshape(2, 128, -1).astype(low)
        return links.push(kept.at[slot, 1 - links.core], from_sibling.at[slot], sibling)

    def chip_sum(slot, step, traded):
        traded.wait_recv()
        result = kept[slot, links.core].astype(full) + from_sibling[slot].astype(full)
        if slot == 0:
            return result
        to_chip[slot - 1] = result.astype(low)
        return links.push(to_chip.at[slot - 1], from_chip.at[slot - 1], links.near(step)[0])

    traded = [feed(0, 0)]
    for step in (2, 4):
        direct[step].wait_send()
    direct[6] = links.push(own_h2, own_h2, links.near(6)[0])
    pass_on(2)
    pass_on(4)
    traded.append(feed(1, 2))
    sent = [chip_sum(1, 2, traded[1])]
    pass_on(6)
    traded.append(feed(2, 4))
    sent.append(chip_sum(2, 4, traded[2]))
    traded.append(feed(3, 6))
    sent.append(chip_sum(3, 6, traded[3]))
    own_sum = chip_sum(0, 0, traded[0])

    def upper_grad(part, carry):
        rows = pl.ds(pl.multiple_of(part * 256, 256), 256)
        up_grad[part] = dot(h2[:, rows], dpre[...], ((0,), (0,))).astype(low)
        return carry

    lax.fori_loop(0, planes, upper_grad, 0)

    def lower_grad(part, carry):
        rows = pl.ds(pl.multiple_of(part * 128, 128), 128)
        down_grad[part] = dot(act[:, rows], df_plane[...].reshape(act.shape[0], -1), ((0,), (0,))).astype(low)
        return carry

    lax.fori_loop(0, planes, lower_grad, 0)

    def lower(part, carry):
        rows = pl.ds(pl.multiple_of(part * 128, 128), 128)
        df_plane[part] = dot(
            act[rows, :], wdown_part[...].reshape(2 * half, -1), ((1,), (0,))
        ).astype(low)
        return carry

    lax.fori_loop(0, 8, lower, 0)

    def of_chip(step, core):
        return links.near(step)[1] // 2 * 2 + core

    y2_traded = [
        links.push(df_plane.at[of_chip(step, 1 - links.core)], y2_sibling.at[slot], sibling)
        for slot, step in enumerate((6, 4, 2, 0))
    ]
    for copy in sent:
        copy.wait_recv()
    grad = own_sum + (
        from_chip[0].astype(full) + from_chip[1].astype(full) + from_chip[2].astype(full)
    )
    part, gain_grad, shift_grad = norm_back(grad, y1_out[...], gains[2:3, :])
    feed_gain[...] = gain_grad
    feed_shift[...] = shift_grad
    g1_new = g1[...] + part
    g1_out[...] = g1_new
    dout[...] = g1_new.astype(low)
    for z in range(planes):
        datt_out[z] = dot(dout[...], wo_rows(z), ((1,), (1,))).astype(low)
    share = along_z(block, block)(links, datt_out, datt)
    next(share)
    y2_pushed = []
    for slot, step in enumerate((6, 4, 2, 0)):
        y2_traded[slot].wait()
        mine = of_chip(step, links.core)
        df_plane[mine] = (
            df_plane[mine].astype(full) + y2_sibling[slot].astype(full)
        ).astype(low)
        if step:
            y2_pushed.append(
                links.push(df_plane.at[mine], y2_chip.at[slot], links.near(step)[0])
            )
    for copy in [direct[6]] + list(handed.values()):
        copy.wait_send()
    for z in range(planes):
        part = dot(arrived[z], dout[...], ((0,), (0,))).astype(low)
        for p in range(8):
            row = p * 128 + z * 32
            h2[row : row + 32, :] = part[p * 32 : p * 32 + 32]
    out_traded = [
        links.push(
            h2.at[rows_of(links.near(step)[1] // 2 * 2 + 1 - links.core), :],
            out_sibling.at[slot],
            sibling,
        )
        for slot, step in enumerate((6, 4, 2, 0))
    ]
    up_bias[...] = jnp.sum(dpre[...].astype(full), axis=0, keepdims=True)
    drive([share])
    share_up = along_z(block, block)(links, up_grad, up_parts)
    next(share_up)
    share_down = along_z(block, block)(links, down_grad, down_parts)
    next(share_down)
    def combine_back(z, carry):
        for x in range(2):
            grad = datt[z, :, x * 128 : (x + 1) * 128].astype(full)
            chosen = [sums[weight_rows(x * 4 + u, z), :128] for u in range(4)]
            inner = [
                jnp.sum(grad * mixed_in[x * 4 + u, z].astype(full), axis=-1, keepdims=True)
                for u in range(4)
            ]
            mean = sum(chosen[u] * inner[u] for u in range(4))
            for u in range(4):
                mixed_home[x * 4 + u, z] = (chosen[u] * grad).astype(low)
                change = (chosen[u] * (inner[u] - mean)).astype(low).astype(full)
                total_home[x * 4 + u, pl.ds(z, 1), :] = change.T[:1, :]
        return carry

    lax.fori_loop(0, planes, combine_back, 0)
    shares = [
        over_plane(block, narrow)(links, mixed_home, head_table),
        over_plane(block, block)(links, total_home, dtotal_in),
    ]
    for transfer in shares:
        next(transfer)
    for copy in traded + sent:
        copy.wait_send()
    return shares, y2_pushed, share_up, share_down, out_traded


def close_part(
    links, planes, shares, y2_pushed, share_up, share_down, out_traded,
    x2, g2, y2_out, g2_out, shared_grad_out, value_grad_out, out_grad_out, up_out, down_out, vectors_out,
    gains, order_rows, order_s, place_s, normed, wqk_pair, wv_pair, shared, values, total_sorted, head_table,
    table, sums, last_scale, dtotal_in, attended, df_plane, h2, wup_part, wdown_part, up_parts, down_grad,
    down_parts, kept, from_sibling, to_chip, from_chip, up_bias, feed_gain, feed_shift, grad_sorted,
    grad_total_sorted, scale_sums, up_sum, up_arrived, dshared, dvalues, de, out_sent, out_arrived,
    weight_arrived, weight_sum, weight_final, tiles_sent, tiles_arrived, tile, tile_line, y2_sibling, y2_chip,
    out_sibling, out_chip,
):
    low, full = jnp.bfloat16, jnp.float32
    tiles = planes * 8
    line = planes * 128
    out_sums = []
    for slot, step in enumerate((6, 4, 2, 0)):
        out_traded[slot].wait()
        rows = rows_of(links.near(step)[1] // 2 * 2 + links.core)
        total = h2[rows, :].astype(full) + out_sibling[slot].astype(full)
        h2[rows, :] = total.astype(low)
        out_sums.append(rows)
    drive(shares)
    out_pushed = [
        links.push(h2.at[out_sums[slot], :], out_chip.at[slot], links.near(step)[0])
        for slot, step in enumerate((6, 4, 2))
    ]

    def load(index, carry):
        z, p = index // 8, lax.rem(index, 8)
        table[rows_of(index), :128] = head_table[z, p, :, :HEAD_DIM].astype(full)
        table[rows_of(index), 128:] = down(dtotal_in[p, pl.ds(z, 1), :])
        return carry

    lax.fori_loop(0, tiles, load, 0)
    attend_back_tiles(
        tiles, 4, order_s, order_rows, table, shared, values, total_sorted,
        grad_sorted, grad_total_sorted, sums, scale_sums, last_scale,
    )
    total = h2[out_sums[3], :].astype(full)
    for slot, copy in enumerate(out_pushed):
        copy.wait()
        total += out_chip[slot].astype(full)
    out_sent[...] = total.astype(low).reshape(out_sent.shape)
    share_out = along_z(block, block)(links, out_sent, out_arrived)
    next(share_out)
    sibling, _ = links.near(1)
    steps = (6, 4, 2, 0)
    halves = ((0, 3), (1, 2))

    def unsort(half, slot, step):
        chip = links.near(step)[1] // 2
        columns = pl.ds(half * 512, 512)
        for core, goal in ((0, 1 - links.core), (1, links.core)):

            def rows(index, carry):
                z = index * 3 if half == 0 else index + 1
                place = pl.ds(pl.multiple_of(half * 512 + index * 256, 256), 256)
                for part in range(4):
                    picked = pick_tile(sums, place_s, z * 8 + chip * 2 + goal, part)
                    kept[slot, core, part * 32 : part * 32 + 32, place] = picked.astype(low)
                return carry

            lax.fori_loop(0, 2, rows, 0)
            if core == 0:
                traded = links.push(
                    kept.at[slot, 0, :, columns], from_sibling.at[slot, :, columns], sibling
                )
        return traded

    def chip_sum(half, slot, traded):
        traded.wait_recv()
        columns = slice(half * 512, half * 512 + 512)
        result = kept[slot, 1, :, columns].astype(full) + from_sibling[slot, :, columns].astype(full)
        if steps[slot] == 0:
            return result
        to_chip[slot, :, columns] = result.astype(low)
        columns = pl.ds(half * 512, 512)
        return links.push(
            to_chip.at[slot, :, columns], from_chip.at[slot, :, columns], links.near(steps[slot])[0]
        )

    traded, sent = [[], []], [[], []]
    for half in range(2):
        for slot, step in enumerate(steps):
            traded[half].append(unsort(half, slot, step))
            if slot:
                sent[half].append(chip_sum(half, slot - 1, traded[half][slot - 1]))
    own_columns = pl.ds(pl.multiple_of(links.x * 128, 128), 128)
    far_columns = pl.ds(pl.multiple_of((1 - links.x) * 128, 128), 128)
    all_wqk, all_wv = wqk_pair[...].reshape(-1, 256), wv_pair[...].reshape(-1, 256)

    def settle_sum(half, columns, result):
        for index, z in enumerate(halves[half]):
            part = result[:, index * 256 : index * 256 + 256].astype(low)
            dshared[z * 128 : z * 128 + 128, columns] = part[:, :128]
            dvalues[z * 128 : z * 128 + 128, columns] = part[:, 128:]

    share_de = along_z_outer_first(block, block)(links, y2_sibling, de)
    for half in range(2):
        own_sum = chip_sum(half, 3, traded[half][3])
        columns = slice(half * 512, half * 512 + 512)
        for copy in sent[half]:
            copy.wait_recv()
        settle_sum(half, own_columns, own_sum + from_chip[2, :, columns].astype(full))
        settle_sum(
            half, far_columns, from_chip[1, :, columns].astype(full) + from_chip[0, :, columns].astype(full)
        )
        for z in halves[half]:
            rows = slice(z * 128, z * 128 + 128)
            y2_sibling[z] = (
                dot(dshared[rows, :], all_wqk, ((1,), (1,))) + dot(dvalues[rows, :], all_wv, ((1,), (1,)))
            ).astype(low)
        next(share_de)
    drive([share_up])
    up_sum[...] = sum(up_parts[z].astype(full) for z in range(planes)).reshape(up_sum.shape)
    share_up = over_plane(block, block)(links, up_sum, up_arrived)
    next(share_up)
    all_normed = normed[...].reshape(line, -1)
    for index, grad in enumerate((dshared, dvalues)):
        wup_part[:, :, :, index * 256 : index * 256 + 256] = (
            dot(all_normed, grad[...], ((0,), (0,))).astype(low).reshape(wup_part.shape[:3] + (256,))
        )
    share_weights = over_plane(second, block)(links, wup_part, weight_arrived)
    next(share_weights)
    for copy in y2_pushed:
        copy.wait()
    y2_out[...] = x2[...] + (
        df_plane[links.p].astype(full)
        + sum(y2_chip[slot].astype(full) for slot in range(3))
        + gains[4:5, :]
    )
    drive([share_up])
    for p in range(8):
        for z in range(planes):
            up_out[:, (z * 8 + p) * 128 : (z * 8 + p + 1) * 128] = up_arrived[
                p, :, z * 128 : (z + 1) * 128
            ]
    drive([share_down])
    down_out[...] = sum(down_parts[z].astype(full) for z in range(planes))
    drive([share_out])
    out_grad_out[...] = sum(out_arrived[z].astype(full) for z in range(planes))
    down_bias = jnp.sum(g2[...].astype(low).astype(full), axis=0, keepdims=True)
    drive([share_weights])
    weight_sum[...] = sum(weight_arrived[p].astype(full) for p in range(8)).astype(low)

    share_final = along_z(block, block)(links, weight_sum, weight_final)
    next(share_final)
    drive([share_de])
    part, gain_grad, shift_grad = norm_back(
        sum(de[z].astype(full) for z in range(planes)), x2[...], gains[0:1, :]
    )
    vectors = [gain_grad, shift_grad, feed_gain[...], feed_shift[...], down_bias]
    for x in range(2):
        for index, vector in enumerate(vectors):
            for z in range(planes):
                chunk = (z * 2 + x) * 128
                row = index * planes + z
                tiles_sent[x, row : row + 1, :] = vector[:, chunk : chunk + 128]
        tiles_sent[x, 5 * planes :, :] = jnp.zeros((24 - 5 * planes, 128), full)

    def of_x(ref, p):
        return ref.at[p // 4]

    share_tiles = over_plane(of_x, block)(links, tiles_sent, tiles_arrived)
    next(share_tiles)
    g2_out[...] = g2[...] + part
    drive([share_tiles])
    tile[...] = jnp.sum(tiles_arrived[...], axis=0)
    for z in range(planes):
        tile[5 * planes + z : 5 * planes + z + 1, :] = up_bias[:, z * 128 : (z + 1) * 128]
    share_tile = along_z(whole, block)(links, tile, tile_line)
    next(share_tile)
    drive([share_final])
    for z in range(planes):
        columns = slice(z * 256, z * 256 + 256)
        shared_grad_out[:, columns] = weight_final[z, :, :256].astype(full)
        value_grad_out[:, columns] = weight_final[z, :, 256:].astype(full)
    drive([share_tile])
    tile[...] = jnp.sum(tile_line[...], axis=0)
    for index in range(6):
        vectors_out[index : index + 1, :] = tile[pl.ds(index * planes + links.z, 1), :]
    vectors_out[6:8, :] = jnp.zeros((2, 128), full)
    for copy in traded[0] + traded[1] + sent[0] + sent[1]:
        copy.wait_send()


LAYER_INPUTS = (
    "sort_order", "sort_place", "gain_a_in", "shift_a_in", "gain_f_in", "shift_f_in", "bias_up_in",
    "bias_down_in", "x2", "wqk", "wv", "wo", "wup", "wdown", "g2", "x1", "g1",
)
LAYER_OUTPUTS = (
    "y1_out", "y2_out", "g1_out", "g2_out", "shared_grad_out", "value_grad_out", "out_grad_out",
    "up_out", "down_out", "vectors_out",
)
OPEN_REFS = (
    "sort_order", "sort_place", "gain_a_in", "shift_a_in", "gain_f_in", "shift_f_in", "bias_up_in",
    "bias_down_in", "x2", "wqk", "wv", "wo", "wup", "wdown", "g2", "ints", "all_ints", "floats",
    "all_floats", "gains", "bias_up", "order_rows", "place_rows", "order_s", "place_s", "normed",
    "df", "wqk_line", "wv_line", "wo_line", "wup_rows", "wqk_pair", "wv_pair", "heads",
    "head_table", "table", "sums", "shared", "values", "total_sorted", "mixed_home", "total_home",
    "last_scale", "wo_all", "wup_part", "wdown_part", "df_plane", "mixed_in", "total_in",
)
FEED_REFS = (
    "x1", "g1", "y1_out", "g1_out", "gains", "bias_up", "sums", "table", "head_table", "mixed_home",
    "total_home", "wo_all", "wup_part", "wdown_part", "df_plane", "mixed_in", "total_in",
    "dtotal_in", "attended", "arrived", "h2", "act", "dpre", "kept", "from_sibling", "to_chip",
    "from_chip", "up_grad", "up_parts", "down_grad", "down_parts", "dout", "datt_out", "datt",
    "up_bias", "feed_gain", "feed_shift", "y2_sibling", "y2_chip", "out_sibling", "wdown",
)
CLOSE_REFS = (
    "x2", "g2", "y2_out", "g2_out", "shared_grad_out", "value_grad_out", "out_grad_out", "up_out",
    "down_out", "vectors_out", "gains", "order_rows", "order_s", "place_s", "normed", "wqk_pair",
    "wv_pair", "shared", "values", "total_sorted", "head_table", "table", "sums", "last_scale",
    "dtotal_in", "attended", "df_plane", "h2", "wup_part", "wdown_part", "up_parts", "down_grad",
    "down_parts", "kept", "from_sibling", "to_chip", "from_chip", "up_bias", "feed_gain",
    "feed_shift", "grad_sorted", "grad_total_sorted", "scale_sums", "up_sum", "up_arrived",
    "dshared", "dvalues", "de", "out_sent", "out_arrived", "weight_arrived", "weight_sum",
    "weight_final", "tiles_sent", "tiles_arrived", "tile", "tile_line",
    "y2_sibling", "y2_chip", "out_sibling", "out_chip",
)


def layer_scratch(planes, rows, width, own, part):
    low, full, whole_number = jnp.bfloat16, jnp.float32, jnp.int32
    tiles = planes * 8
    tokens = tiles * rows
    return {
        "ints": pltpu.VMEM((8, rows), whole_number),
        "all_ints": pltpu.VMEM((planes, 8, 8, rows), whole_number),
        "floats": pltpu.VMEM((8, rows), full),
        "all_floats": pltpu.VMEM((planes, 8, 8, rows), full),
        "gains": pltpu.VMEM((8, width), full),
        "bias_up": pltpu.VMEM((1, part), full),
        "order_rows": pltpu.VMEM((tiles, rows), whole_number),
        "place_rows": pltpu.VMEM((tiles, rows), whole_number),
        "order_s": pltpu.SMEM((tiles, rows), whole_number),
        "place_s": pltpu.SMEM((tiles, rows), whole_number),
        "normed": pltpu.VMEM((planes, rows, width), low),
        "df": pltpu.VMEM((rows, width), low),
        "wqk_line": pltpu.VMEM((planes, own, 256), low),
        "wv_line": pltpu.VMEM((planes, own, 256), low),
        "wo_line": pltpu.VMEM((planes, own, width), low),
        "wup_rows": pltpu.VMEM((8, own, part), low),
        "wqk_pair": pltpu.VMEM((planes, 8, own, 256), low),
        "wv_pair": pltpu.VMEM((planes, 8, own, 256), low),
        "heads": pltpu.VMEM((planes, rows, 512), low),
        "head_table": pltpu.VMEM((planes, 8, rows, 256), low),
        "table": pltpu.VMEM((tokens, 256), full),
        "sums": pltpu.VMEM((tokens + rows, 256), full),
        "shared": pltpu.VMEM((tokens + BLOCK, HEAD_DIM), low),
        "values": pltpu.VMEM((tokens + BLOCK, HEAD_DIM), low),
        "total_sorted": pltpu.VMEM((tokens, HEAD_DIM), full),
        "mixed_home": pltpu.VMEM((8, planes, rows, HEAD_DIM), low),
        "total_home": pltpu.VMEM((8, 8, rows), full),
        "last_scale": pltpu.VMEM((1, rows), full),
        "wo_all": pltpu.VMEM((planes, 8, own, width), low),
        "wup_part": pltpu.VMEM((planes, 8, own, part), low),
        "wdown_part": pltpu.VMEM((planes, rows, width), low),
        "df_plane": pltpu.VMEM((8, rows, width), low),
        "mixed_in": pltpu.VMEM((8, planes, rows, HEAD_DIM), low),
        "total_in": pltpu.VMEM((8, 8, rows), full),
        "dtotal_in": pltpu.VMEM((8, 8, rows), full),
        "attended": pltpu.VMEM((planes, rows, 256), low),
        "arrived": pltpu.VMEM((planes, rows, 256), low),
        "h2": pltpu.VMEM((8 * rows, width), low),
        "act": pltpu.VMEM((8 * rows, part), low),
        "dpre": pltpu.VMEM((8 * rows, part), low),
        "kept": pltpu.VMEM((4, 2, rows, width), low),
        "from_sibling": pltpu.VMEM((4, rows, width), low),
        "to_chip": pltpu.VMEM((3, rows, width), low),
        "from_chip": pltpu.VMEM((3, rows, width), low),
        "up_grad": pltpu.VMEM((planes, width // planes, part), low),
        "up_parts": pltpu.VMEM((planes, width // planes, part), low),
        "down_grad": pltpu.VMEM((planes, rows, width), low),
        "down_parts": pltpu.VMEM((planes, rows, width), low),
        "dout": pltpu.VMEM((rows, width), low),
        "datt_out": pltpu.VMEM((planes, rows, 256), low),
        "datt": pltpu.VMEM((planes, rows, 256), low),
        "up_bias": pltpu.VMEM((1, part), full),
        "feed_gain": pltpu.VMEM((1, width), full),
        "feed_shift": pltpu.VMEM((1, width), full),
        "grad_sorted": pltpu.VMEM((tokens, HEAD_DIM), low),
        "grad_total_sorted": pltpu.VMEM((tokens, HEAD_DIM), full),
        "scale_sums": pltpu.VMEM((tiles + 8, rows), full),
        "up_sum": pltpu.VMEM((8, own, part), full),
        "up_arrived": pltpu.VMEM((8, own, part), full),
        "dshared": pltpu.VMEM((planes * rows, 256), low),
        "dvalues": pltpu.VMEM((planes * rows, 256), low),
        "de": pltpu.VMEM((planes, rows, width), low),
        "out_sent": pltpu.VMEM((planes, own, width), low),
        "out_arrived": pltpu.VMEM((planes, own, width), low),
        "y2_sibling": pltpu.VMEM((4, rows, width), low),
        "y2_chip": pltpu.VMEM((3, rows, width), low),
        "out_sibling": pltpu.VMEM((4, rows, width), low),
        "out_chip": pltpu.VMEM((3, rows, width), low),
        "weight_arrived": pltpu.VMEM((8, planes, own, 512), low),
        "weight_sum": pltpu.VMEM((planes, own, 512), low),
        "weight_final": pltpu.VMEM((planes, own, 512), low),
        "tiles_sent": pltpu.VMEM((2, 24, rows), full),
        "tiles_arrived": pltpu.VMEM((8, 24, rows), full),
        "tile": pltpu.VMEM((24, rows), full),
        "tile_line": pltpu.VMEM((planes, 24, rows), full),
    }


def layer_kernel(planes, names, *refs):
    links = Links(planes, *refs[len(names) :])
    held = dict(zip(names, refs))
    links.greet()
    shares = open_part(links, planes, *[held[name] for name in OPEN_REFS])
    shares = feed_part(links, planes, *shares, *[held[name] for name in FEED_REFS])
    close_part(links, planes, *shares, *[held[name] for name in CLOSE_REFS])


def layer_stage(arguments, collective_id, planes):
    rows, width = arguments[LAYER_INPUTS.index("x2")].shape
    own, hidden = arguments[LAYER_INPUTS.index("wup")].shape
    shape = jax.ShapeDtypeStruct
    token, weight = shape((rows, width), jnp.float32), shape((own, width), jnp.float32)
    outputs = [token] * 4 + [weight] * 3 + [
        shape((own, hidden), jnp.float32), token, shape((8, rows), jnp.float32)
    ]
    scratch = layer_scratch(planes, rows, width, own, hidden // 8)
    names = LAYER_INPUTS + LAYER_OUTPUTS + tuple(scratch)
    return pl.pallas_call(
        functools.partial(layer_kernel, planes, names),
        out_shape=outputs,
        in_specs=[VMEM] * len(arguments),
        out_specs=[VMEM] * len(outputs),
        scratch_shapes=list(scratch.values()) + link_scratch(),
        compiler_params=pltpu.CompilerParams(
            vmem_limit_bytes=60 << 20, collective_id=collective_id, has_side_effects=True
        ),
        name="layer",
    )(*arguments)


def finish_kernel(
    y1, y2, g1, g2, shared_grad, value_grad, out_grad, up_grad, down_grad, vectors,
    y1_out, y2_out, g1_out, g2_out, gain_a_out, shift_a_out, shared_out, value_out, out_out,
    gain_f_out, shift_f_out, up_out, up_bias_out, down_out, down_bias_out, arrived,
):
    pairs = (
        (y1, y1_out), (y2, y2_out), (g1, g1_out), (g2, g2_out), (shared_grad, shared_out),
        (value_grad, value_out), (out_grad, out_out), (up_grad, up_out), (down_grad, down_out),
    )
    copies = [
        pltpu.make_async_copy(source, target.at[0], arrived.at[index])
        for index, (source, target) in enumerate(pairs)
    ]
    for copy in copies:
        copy.start()
    sub = lax.axis_index("sub")
    rows = vectors[...]
    own = sum(
        jnp.where(sub == u, rows[:, u * 32 : u * 32 + 32], 0.0) for u in range(4)
    )
    for row, target in enumerate((gain_a_out, shift_a_out, gain_f_out, shift_f_out, down_bias_out)):
        target[...] = own[row : row + 1, :]
    up_bias_out[...] = rows[5:6, :]
    for copy in copies:
        copy.wait()


def finish_stage(arguments):
    full = jnp.float32
    large = [(jax.ShapeDtypeStruct((1,) + a.shape, full), ANY) for a in arguments[:-1]]
    y1, y2, g1, g2, shared_grad, value_grad, out_grad, up_grad, down_grad = large
    small = (jax.ShapeDtypeStruct((1, arguments[4].shape[0]), full), VMEM)
    up_bias = (jax.ShapeDtypeStruct((1, arguments[-1].shape[1]), full), VMEM)
    outputs = [
        y1, y2, g1, g2, small, small, shared_grad, value_grad, out_grad, small, small, up_grad,
        up_bias, down_grad, small,
    ]
    return pl.pallas_call(
        finish_kernel,
        out_shape=[o[0] for o in outputs],
        in_specs=[VMEM] * 10,
        out_specs=[o[1] for o in outputs],
        scratch_shapes=[pltpu.SemaphoreType.DMA((9,))],
        name="finish",
    )(*arguments)


def plane_plan(
    n_seq,
    n_sub,
    first_half,
    second_half,
    grad_first,
    grad_second,
    attend_gain,
    attend_shift,
    query_key_weight,
    value_projection_weight,
    output_projection_weight,
    feed_gain,
    feed_shift,
    upper_projection_weight,
    upper_projection_bias,
    lower_projection_weight,
    lower_projection_bias,
    sort_order,
    sort_place,
):
    planes = n_seq // 2
    x1, x2, g1, g2 = (a[0] for a in (first_half, second_half, grad_first, grad_second))
    wqk, wv, wo = query_key_weight[0], value_projection_weight[0], output_projection_weight[0]
    wup, wdown = upper_projection_weight[0], lower_projection_weight[0]
    results = layer_stage(
        (
            sort_order[0, :, 0], sort_place[0, :, 0], attend_gain, attend_shift, feed_gain, feed_shift,
            upper_projection_bias, lower_projection_bias, x2, wqk, wv, wo, wup, wdown, g2, x1, g1,
        ),
        1,
        planes,
    )
    return finish_stage(results)


def on_device(n_seq, n_sub, *arguments):
    sequences, rows, width = arguments[0].shape
    rounds = arguments[-1].shape[1]
    fits = (
        sequences == 1
        and rows == 2 * BLOCK
        and rounds == n_sub
        and HEADS == n_seq
        and width == HEADS * HEAD_DIM
    )
    if fits:
        return plane_plan(n_seq, n_sub, *arguments)
    return general_plan(*arguments)


def solution(mesh):
    return jax.shard_map(
        functools.partial(on_device, mesh.shape["seq"], mesh.shape["sub"]),
        mesh=mesh,
        in_specs=(
            P(None, ("seq", "sub"), None),
            P(None, ("seq", "sub"), None),
            P(None, ("seq", "sub"), None),
            P(None, ("seq", "sub"), None),
            P(None, ("seq", "sub")),
            P(None, ("seq", "sub")),
            P(None, ("seq", "sub"), None),
            P(None, ("seq", "sub"), None),
            P(None, ("seq", "sub"), None),
            P(None, ("seq", "sub")),
            P(None, ("seq", "sub")),
            P(None, ("seq", "sub"), None),
            P(None, ("seq", "sub")),
            P(None, ("seq", "sub"), None),
            P(None, ("seq", "sub")),
            P(None, None, None, ("seq", "sub")),
            P(None, None, None, ("seq", "sub")),
        ),
        out_specs=(
            P(None, ("seq", "sub"), None),
            P(None, ("seq", "sub"), None),
            P(None, ("seq", "sub"), None),
            P(None, ("seq", "sub"), None),
            P(None, ("seq", "sub")),
            P(None, ("seq", "sub")),
            P(None, ("seq", "sub"), None),
            P(None, ("seq", "sub"), None),
            P(None, ("seq", "sub"), None),
            P(None, ("seq", "sub")),
            P(None, ("seq", "sub")),
            P(None, ("seq", "sub"), None),
            P(None, ("seq", "sub")),
            P(None, ("seq", "sub"), None),
            P(None, ("seq", "sub")),
        ),
        check_vma=False,
    )
```

```python
import functools

import jax
import jax.numpy as jnp
from jax import lax
from jax.experimental import pallas as pl
from jax.experimental.pallas import tpu as pltpu
from jax.sharding import PartitionSpec as P

HEADS = 8
HEAD_DIM = 128
BLOCK = 64
LATER = -1000000000.0
SELF = -100000.0


def from_behind(block, axis, distance):
    devices = range(lax.axis_size(axis))
    route = [((i - distance) % len(devices), i) for i in devices]
    return lax.ppermute(block, axis, route)


def layer_norm(value_vectors, scaling, shifts):
    center = jnp.mean(value_vectors, axis=-1, keepdims=True)
    offset = value_vectors - center
    spread = jnp.mean(offset * offset, axis=-1, keepdims=True)
    return offset * lax.rsqrt(spread + 1e-05) * scaling + shifts


def gelu_exact(value_vectors):
    return jax.nn.gelu(value_vectors, approximate=False)


def combine_rounds(outputs, totals):
    highest = jnp.max(totals, axis=0, keepdims=True)
    weights = jnp.exp(totals - highest)
    weights = weights / jnp.sum(weights, axis=0, keepdims=True)
    by_head = outputs.reshape(outputs.shape[:-1] + (totals.shape[-1], -1))
    return jnp.sum(weights[..., None] * by_head, axis=0).reshape(outputs.shape[1:])


def home_slots(places, row_count):
    target = places // row_count
    prior_state = (target[:, None, :] == target[:, :, None]) & (
        places[:, None, :] < places[:, :, None]
    )
    return (target, jnp.sum(prior_state.astype(jnp.int32), axis=2))


def sorted_slots(orders, row_count):
    source = orders // row_count
    ladder = jnp.arange(row_count, dtype=jnp.int32)
    prior_state = (source[:, None, :] == source[:, :, None]) & (
        ladder[None, None, :] < ladder[None, :, None]
    )
    return (source, jnp.sum(prior_state.astype(jnp.int32), axis=2))


def slot_lookup(owners, slot_index, devices, capacity):
    groups, row_count = owners.shape
    flat_index = owners * capacity + slot_index
    lookup = jnp.full((groups, devices * capacity), row_count, jnp.int32)
    filler = jnp.broadcast_to(jnp.arange(row_count, dtype=jnp.int32), (groups, row_count))
    lookup = lookup.at[jnp.arange(groups)[:, None], flat_index].set(filler)
    return jnp.transpose(lookup.reshape(groups, devices, capacity), (1, 0, 2))


def gather_slots(value_vectors, member, lookup):
    padding = jnp.zeros((value_vectors.shape[0], 1) + value_vectors.shape[2:], value_vectors.dtype)
    padded = jnp.concatenate([value_vectors, padding], axis=1)
    return padded[member[None, :, None], lookup]


def settle(received, owners, slot_index):
    return received[owners, jnp.arange(owners.shape[0])[:, None], slot_index]


def build_routes(orders, places, devices, capacity):
    rounds, sequences, row_count = orders.shape
    order_flat = orders.reshape(rounds * sequences, row_count)
    target, home_slot = home_slots(places.reshape(rounds * sequences, row_count), row_count)
    source, sorted_slot = sorted_slots(order_flat, row_count)
    home_lookup = slot_lookup(target, home_slot, devices, capacity)
    back_lookup = slot_lookup(source, sorted_slot, devices, capacity)
    return (target, home_slot, source, sorted_slot, home_lookup, back_lookup, order_flat)


def trade_rows(first_part, second_part):
    return (
        lax.all_to_all(first_part, ("seq", "sub"), split_axis=0, concat_axis=0, tiled=True),
        lax.all_to_all(second_part, ("seq", "sub"), split_axis=0, concat_axis=0, tiled=True),
    )


def trade_results(first_part, second_part):
    return (
        lax.all_to_all(first_part, ("seq", "sub"), split_axis=0, concat_axis=0, tiled=True),
        lax.all_to_all(second_part, ("seq", "sub"), split_axis=0, concat_axis=0, tiled=True),
    )


def window(rows_here, rows_left):
    groups = rows_here.shape[0]
    extended = jnp.concatenate([rows_left, rows_here], axis=1)
    extended = extended.reshape((groups, -1, BLOCK) + rows_here.shape[2:])
    return jnp.concatenate([extended[:, :-1], extended[:, 1:]], axis=2)


def score_parts(shared_rows, order_rows, halo_shared, halo_order):
    groups, row_count, features = shared_rows.shape
    blocks = row_count // BLOCK
    queries = shared_rows.reshape(groups, blocks, BLOCK, HEADS, HEAD_DIM)
    key_rows = window(shared_rows, halo_shared).reshape(groups, blocks, 2 * BLOCK, HEADS, HEAD_DIM)
    key_float = key_rows.astype(jnp.float32)
    mean_square = jnp.mean(key_float * key_float, axis=-1) + 1e-06
    key_scale = lax.rsqrt(mean_square) / HEAD_DIM
    raw_scores = jnp.einsum(
        "gcqhd,gckhd->gchqk", queries, key_rows, preferred_element_type=jnp.float32
    )
    query_pos = order_rows.reshape(groups, blocks, BLOCK)
    key_pos = window(order_rows, halo_order)
    is_later = (key_pos[:, :, None, :] > query_pos[:, :, :, None])[:, :, None]
    is_self = (key_pos[:, :, None, :] == query_pos[:, :, :, None])[:, :, None]
    scale_row = jnp.transpose(key_scale, (0, 1, 3, 2))[:, :, :, None, :]
    scores = jnp.where(
        is_later, -1000000000.0, jnp.where(is_self, -100000.0, raw_scores * scale_row)
    )
    highest = jnp.max(scores, axis=-1, keepdims=True)
    log_total = highest + jnp.log(jnp.sum(jnp.exp(scores - highest), axis=-1, keepdims=True))
    probability = jnp.exp(scores - log_total)
    return (
        queries,
        key_rows,
        key_float,
        mean_square,
        key_scale,
        scale_row,
        raw_scores,
        is_later | is_self,
        log_total,
        probability,
    )


def attend(shared_rows, value_rows, order_rows, halo):
    halo_shared, halo_value, halo_order = halo
    parts = score_parts(shared_rows, order_rows, halo_shared, halo_order)
    groups, row_count, features = shared_rows.shape
    value_keys = window(value_rows, halo_value).reshape(
        groups, row_count // BLOCK, 2 * BLOCK, HEADS, HEAD_DIM
    )
    mixed = jnp.einsum(
        "gchqk,gckhd->gcqhd",
        parts[9].astype(jnp.bfloat16),
        value_keys,
        preferred_element_type=jnp.float32,
    )
    log_total = jnp.transpose(parts[8][..., 0], (0, 1, 3, 2)).reshape(groups, row_count, HEADS)
    return (mixed.reshape(groups, row_count, features), log_total)


def fold_window(grads_window, groups, row_count, features):
    grads_window = grads_window.reshape(groups, row_count // BLOCK, 2 * BLOCK, features)
    empty = jnp.zeros((groups, 1, BLOCK, features), jnp.float32)
    extended = jnp.concatenate([grads_window[:, :, :BLOCK], empty], axis=1) + jnp.concatenate(
        [empty, grads_window[:, :, BLOCK:]], axis=1
    )
    return (extended[:, 1:].reshape(groups, row_count, features), extended[:, 0])


def attend_back(shared_rows, value_rows, order_rows, halo, grad_out, grad_total):
    halo_shared, halo_value, halo_order = halo
    (
        queries,
        key_rows,
        key_float,
        mean_square,
        key_scale,
        scale_row,
        raw_scores,
        masked,
        log_total,
        probability,
    ) = score_parts(shared_rows, order_rows, halo_shared, halo_order)
    groups, row_count, features = shared_rows.shape
    blocks = row_count // BLOCK
    value_keys = window(value_rows, halo_value).reshape(groups, blocks, 2 * BLOCK, HEADS, HEAD_DIM)
    prob_low = probability.astype(jnp.bfloat16)
    grad_heads = grad_out.reshape(groups, blocks, BLOCK, HEADS, HEAD_DIM)
    grad_log = jnp.transpose(
        grad_total.astype(jnp.float32).reshape(groups, blocks, BLOCK, HEADS), (0, 1, 3, 2)
    )[..., None]
    grad_prob = jnp.einsum(
        "gcqhd,gckhd->gchqk", grad_heads, value_keys, preferred_element_type=jnp.float32
    )
    inner = jnp.sum(probability * grad_prob, axis=-1, keepdims=True)
    grad_score = jnp.where(masked, 0.0, probability * (grad_prob - inner + grad_log))
    grad_scale = jnp.transpose(jnp.sum(grad_score * raw_scores, axis=3), (0, 1, 3, 2))
    grad_raw = (grad_score * scale_row).astype(jnp.bfloat16)
    grad_query = jnp.einsum(
        "gchqk,gckhd->gcqhd", grad_raw, key_rows, preferred_element_type=jnp.float32
    )
    grad_key = jnp.einsum(
        "gchqk,gcqhd->gckhd", grad_raw, queries, preferred_element_type=jnp.float32
    )
    grad_key = grad_key - (grad_scale * key_scale / mean_square)[..., None] * key_float / HEAD_DIM
    grad_value = jnp.einsum(
        "gchqk,gcqhd->gckhd", prob_low, grad_heads, preferred_element_type=jnp.float32
    )
    key_home, key_left = fold_window(grad_key, groups, row_count, features)
    value_home, value_left = fold_window(grad_value, groups, row_count, features)
    back_key, back_value = from_behind((key_left, value_left), ("seq", "sub"), -1)
    grad_shared = grad_query.reshape(groups, row_count, features) + key_home
    grad_shared = grad_shared.at[:, row_count - BLOCK :].add(back_key)
    grad_values = value_home.at[:, row_count - BLOCK :].add(back_value)
    return (grad_shared, grad_values)


def sorted_attention(shared_query_key, value_vectors, routes):
    target, home_slot, source, sorted_slot, home_lookup, back_lookup, order_flat = routes
    groups = target.shape[0]
    member = jnp.arange(groups) % shared_query_key.shape[0]
    got_shared, got_values = trade_rows(
        gather_slots(shared_query_key, member, home_lookup),
        gather_slots(value_vectors, member, home_lookup),
    )
    shared_rows = settle(got_shared, source, sorted_slot)
    value_rows = settle(got_values, source, sorted_slot)
    halo = from_behind(
        (shared_rows[:, -BLOCK:], value_rows[:, -BLOCK:], order_flat[:, -BLOCK:]), ("seq", "sub"), 1
    )
    mixed, log_total = attend(shared_rows, value_rows, order_flat, halo)
    all_groups = jnp.arange(groups)
    got_mixed, got_total = trade_results(
        gather_slots(mixed, all_groups, back_lookup),
        gather_slots(log_total, all_groups, back_lookup),
    )
    return (
        settle(got_mixed, target, home_slot),
        settle(got_total, target, home_slot),
        (shared_rows, value_rows, halo),
    )


def round_outputs(normalized_input, query_key_weight, value_projection_weight, routes, rounds):
    shared_query_key = jnp.einsum(
        "srd,de->sre", normalized_input, query_key_weight, preferred_element_type=jnp.float32
    ).astype(jnp.bfloat16)
    value_vectors = jnp.einsum(
        "srd,de->sre", normalized_input, value_projection_weight, preferred_element_type=jnp.float32
    ).astype(jnp.bfloat16)
    mixed, log_total, kept = sorted_attention(shared_query_key, value_vectors, routes)
    sequences, row_count, features = normalized_input.shape
    outputs = mixed.reshape(rounds, sequences, row_count, features)
    totals = log_total.reshape(rounds, sequences, row_count, HEADS)
    return (shared_query_key, value_vectors, outputs, totals, kept)


def collect(weight_stack, layer_index):
    (
        attend_gain,
        attend_shift,
        query_key_weight,
        value_projection_weight,
        output_projection_weight,
        feed_gain,
        feed_shift,
        upper_projection_weight,
        upper_projection_bias,
        lower_projection_weight,
        lower_projection_bias,
    ) = tuple((shard_piece[layer_index] for shard_piece in weight_stack))
    return (
        lax.all_gather(attend_gain, ("seq", "sub"), axis=0, tiled=True),
        lax.all_gather(attend_shift, ("seq", "sub"), axis=0, tiled=True),
        lax.all_gather(query_key_weight, ("seq", "sub"), axis=0, tiled=True),
        lax.all_gather(value_projection_weight, ("seq", "sub"), axis=0, tiled=True),
        lax.all_gather(output_projection_weight, ("seq", "sub"), axis=0, tiled=True),
        lax.all_gather(feed_gain, ("seq", "sub"), axis=0, tiled=True),
        lax.all_gather(feed_shift, ("seq", "sub"), axis=0, tiled=True),
        lax.all_gather(upper_projection_weight, ("seq", "sub"), axis=0, tiled=True),
        lax.all_gather(upper_projection_bias, ("seq", "sub"), axis=0, tiled=True),
        lax.all_gather(lower_projection_weight, ("seq", "sub"), axis=0, tiled=True),
        lax.all_gather(lower_projection_bias, ("seq", "sub"), axis=0, tiled=True),
    )


def spread_grads(level_grads):
    (
        attend_gain,
        attend_shift,
        query_key_weight,
        value_projection_weight,
        output_projection_weight,
        feed_gain,
        feed_shift,
        upper_projection_weight,
        upper_projection_bias,
        lower_projection_weight,
        lower_projection_bias,
    ) = level_grads
    return (
        lax.psum_scatter(attend_gain, ("seq", "sub"), scatter_dimension=0, tiled=True),
        lax.psum_scatter(attend_shift, ("seq", "sub"), scatter_dimension=0, tiled=True),
        lax.psum_scatter(query_key_weight.astype(jnp.bfloat16), ("seq", "sub"), scatter_dimension=0, tiled=True),
        lax.psum_scatter(value_projection_weight.astype(jnp.bfloat16), ("seq", "sub"), scatter_dimension=0, tiled=True),
        lax.psum_scatter(output_projection_weight.astype(jnp.bfloat16), ("seq", "sub"), scatter_dimension=0, tiled=True),
        lax.psum_scatter(feed_gain, ("seq", "sub"), scatter_dimension=0, tiled=True),
        lax.psum_scatter(feed_shift, ("seq", "sub"), scatter_dimension=0, tiled=True),
        lax.psum_scatter(upper_projection_weight.astype(jnp.bfloat16), ("seq", "sub"), scatter_dimension=0, tiled=True),
        lax.psum_scatter(upper_projection_bias, ("seq", "sub"), scatter_dimension=0, tiled=True),
        lax.psum_scatter(lower_projection_weight.astype(jnp.bfloat16), ("seq", "sub"), scatter_dimension=0, tiled=True),
        lax.psum_scatter(lower_projection_bias, ("seq", "sub"), scatter_dimension=0, tiled=True),
    )


def layer_pass(first_half, second_half, grad_one, grad_two, params, routes, rounds):
    (
        attend_gain,
        attend_shift,
        query_key_weight,
        value_projection_weight,
        output_projection_weight,
        feed_gain,
        feed_shift,
        upper_projection_weight,
        upper_projection_bias,
        lower_projection_weight,
        lower_projection_bias,
    ) = params
    attend_norm, attend_pull = jax.vjp(
        layer_norm, second_half, attend_gain.astype(jnp.float32), attend_shift.astype(jnp.float32)
    )
    normalized_input = attend_norm.astype(jnp.bfloat16)
    shared_query_key, value_vectors, outputs, totals, kept = round_outputs(
        normalized_input, query_key_weight, value_projection_weight, routes, rounds
    )
    attention_result, combine_pull = jax.vjp(combine_rounds, outputs, totals)
    attended_low = attention_result.astype(jnp.bfloat16)
    top_one = first_half + jnp.einsum(
        "srd,de->sre", attended_low, output_projection_weight, preferred_element_type=jnp.float32
    )
    feed_norm, feed_pull = jax.vjp(
        layer_norm, top_one, feed_gain.astype(jnp.float32), feed_shift.astype(jnp.float32)
    )
    feed_forward_input = feed_norm.astype(jnp.bfloat16)
    prior_state = jnp.einsum(
        "srd,df->srf",
        feed_forward_input,
        upper_projection_weight,
        preferred_element_type=jnp.float32,
    ) + upper_projection_bias.astype(jnp.float32)
    hidden_activation, active_pull = jax.vjp(gelu_exact, prior_state)
    active_low = hidden_activation.astype(jnp.bfloat16)
    feed_out = jnp.einsum(
        "srf,fd->srd", active_low, lower_projection_weight, preferred_element_type=jnp.float32
    ) + lower_projection_bias.astype(jnp.float32)
    top_two = second_half + feed_out
    feed_grad = grad_two.astype(jnp.bfloat16)
    down_weight_grad = jnp.einsum(
        "srf,srd->fd", active_low, feed_grad, preferred_element_type=jnp.float32
    )
    down_bias_grad = jnp.sum(feed_grad.astype(jnp.float32), axis=(0, 1))
    active_grad = jnp.einsum(
        "srd,fd->srf", feed_grad, lower_projection_weight, preferred_element_type=jnp.float32
    )
    before_grad = active_pull(active_grad)[0].astype(jnp.bfloat16)
    up_weight_grad = jnp.einsum(
        "srd,srf->df", feed_forward_input, before_grad, preferred_element_type=jnp.float32
    )
    up_bias_grad = jnp.sum(before_grad.astype(jnp.float32), axis=(0, 1))
    norm_grad = jnp.einsum(
        "srf,df->srd", before_grad, upper_projection_weight, preferred_element_type=jnp.float32
    )
    one_part, feed_gain_grad, feed_shift_grad = feed_pull(norm_grad)
    total_one = grad_one + one_part
    out_grad = total_one.astype(jnp.bfloat16)
    output_weight_grad = jnp.einsum(
        "srd,sre->de", attended_low, out_grad, preferred_element_type=jnp.float32
    )
    attended_grad = jnp.einsum(
        "sre,de->srd", out_grad, output_projection_weight, preferred_element_type=jnp.float32
    )
    outputs_grad, totals_grad = combine_pull(attended_grad)
    target, home_slot, source, sorted_slot, home_lookup, back_lookup, order_flat = routes
    sequences, row_count, features = top_one.shape
    groups = rounds * sequences
    all_groups = jnp.arange(groups)
    outputs_low = outputs_grad.astype(jnp.bfloat16).reshape(groups, row_count, features)
    totals_low = totals_grad.astype(jnp.bfloat16).reshape(groups, row_count, HEADS)
    got_out, got_total = trade_rows(
        gather_slots(outputs_low, all_groups, home_lookup),
        gather_slots(totals_low, all_groups, home_lookup),
    )
    shared_rows, value_rows, halo = kept
    grad_shared, grad_values = attend_back(
        shared_rows,
        value_rows,
        order_flat,
        halo,
        settle(got_out, source, sorted_slot),
        settle(got_total, source, sorted_slot),
    )
    home_shared, home_values = trade_rows(
        gather_slots(grad_shared.astype(jnp.bfloat16), all_groups, back_lookup),
        gather_slots(grad_values.astype(jnp.bfloat16), all_groups, back_lookup),
    )
    shared_grad = jnp.sum(
        settle(home_shared, target, home_slot)
        .astype(jnp.float32)
        .reshape(rounds, sequences, row_count, features),
        axis=0,
    ).astype(jnp.bfloat16)
    values_grad = jnp.sum(
        settle(home_values, target, home_slot)
        .astype(jnp.float32)
        .reshape(rounds, sequences, row_count, features),
        axis=0,
    ).astype(jnp.bfloat16)
    shared_weight_grad = jnp.einsum(
        "srd,sre->de", normalized_input, shared_grad, preferred_element_type=jnp.float32
    )
    value_weight_grad = jnp.einsum(
        "srd,sre->de", normalized_input, values_grad, preferred_element_type=jnp.float32
    )
    normed_grad = jnp.einsum(
        "sre,de->srd", shared_grad, query_key_weight, preferred_element_type=jnp.float32
    ) + jnp.einsum(
        "sre,de->srd", values_grad, value_projection_weight, preferred_element_type=jnp.float32
    )
    two_part, attend_gain_grad, attend_shift_grad = attend_pull(normed_grad)
    total_two = grad_two + two_part
    level_grads = (
        attend_gain_grad,
        attend_shift_grad,
        shared_weight_grad,
        value_weight_grad,
        output_weight_grad,
        feed_gain_grad,
        feed_shift_grad,
        up_weight_grad,
        up_bias_grad,
        down_weight_grad,
        down_bias_grad,
    )
    return (top_one, top_two, total_one, total_two, level_grads)


def general_plan(
    first_half,
    second_half,
    grad_first,
    grad_second,
    attend_gain,
    attend_shift,
    query_key_weight,
    value_projection_weight,
    output_projection_weight,
    feed_gain,
    feed_shift,
    upper_projection_weight,
    upper_projection_bias,
    lower_projection_weight,
    lower_projection_bias,
    sort_order,
    sort_place,
):
    weight_stack = (
        attend_gain,
        attend_shift,
        query_key_weight,
        value_projection_weight,
        output_projection_weight,
        feed_gain,
        feed_shift,
        upper_projection_weight,
        upper_projection_bias,
        lower_projection_weight,
        lower_projection_bias,
    )
    devices = lax.axis_size(("seq", "sub"))
    rounds = sort_order.shape[1]
    row_count = first_half.shape[1]
    capacity = 2 * max(1, row_count // devices)
    params = collect(weight_stack, 0)
    routes = build_routes(sort_order[0], sort_place[0], devices, capacity)
    first_out, second_out, first_grad, second_grad, level_grads = layer_pass(
        first_half, second_half, grad_first, grad_second, params, routes, rounds
    )
    stacked = tuple((entry[None].astype(jnp.float32) for entry in spread_grads(level_grads)))
    return (first_out, second_out, first_grad, second_grad) + stacked


class Links:
    def __init__(self, planes, send, receive, local):
        self.send, self.receive, self.local = send, receive, local
        self.used, self.used_local = 0, 0
        self.planes = planes
        seq, sub = lax.axis_index("seq"), lax.axis_index("sub")
        self.z, self.x = seq // 2, lax.rem(seq, 2)
        self.y, self.core = sub // 2, lax.rem(sub, 2)
        self.p = self.x * 4 + sub

    def near(self, step):
        x = 1 - self.x if step & 4 else self.x
        y = 1 - self.y if step & 2 else self.y
        core = 1 - self.core if step & 1 else self.core
        return (self.z * 2 + x, y * 2 + core), x * 4 + y * 2 + core

    def along(self, step):
        to = lax.rem(self.z + step, self.planes)
        back = lax.rem(self.z + self.planes - step, self.planes)
        return (to * 2 + self.x, self.y * 2 + self.core), to, back

    def greet(self):
        barrier = pltpu.get_barrier_semaphore()
        targets = [self.near(step)[0] for step in range(1, 8)]
        targets += [self.along(step)[0] for step in range(1, self.planes)]
        for target in targets:
            pl.semaphore_signal(barrier, inc=1, device_id=target, device_id_type=pl.DeviceIdType.MESH)
        self.greeted = len(targets)

    def meet(self):
        pl.semaphore_wait(pltpu.get_barrier_semaphore(), self.greeted)

    def push(self, source, target, device, start=True):
        copy = pltpu.make_async_remote_copy(
            src_ref=source,
            dst_ref=target,
            send_sem=self.send.at[self.used],
            recv_sem=self.receive.at[self.used],
            device_id=device,
            device_id_type=pl.DeviceIdType.MESH,
        )
        self.used += 1
        if start:
            copy.start()
        return copy

    def keep(self, source, target):
        copy = pltpu.make_async_copy(source, target, self.local.at[self.used_local])
        self.used_local += 1
        copy.start()
        return copy


class Chain:
    def __init__(self, links, ref):
        self.links, self.ref, self.first, self.sent = links, ref, links.used, []
        links.used += 5
        self.hand_on(links.z, links.z < 3, links.z > 0, 2)

    def hand_on(self, shard, rightward, leftward, ways):
        links = self.links
        steps = ((1, rightward), (-1, leftward)) if ways == 2 else ((None, rightward | leftward),)
        for step, wanted in steps:
            if step is None:
                step = jnp.where(rightward, 1, -1)
            to = jnp.clip(links.z + step, 0, 3)
            middle = jnp.where(to == 1, jnp.where(shard == 0, 0, shard - 1), jnp.where(shard == 3, 0, 2 - shard))
            arrival = jnp.where((to == 0) | (to == 3), jnp.abs(to - shard) - 1, middle)
            arrival = jnp.clip(arrival, 0, 2)
            copy = pltpu.make_async_remote_copy(
                src_ref=self.ref.at[shard],
                dst_ref=self.ref.at[shard],
                send_sem=links.send.at[self.first + len(self.sent)],
                recv_sem=links.receive.at[self.first + arrival],
                device_id=(to * 2 + links.x, links.y * 2 + links.core),
                device_id_type=pl.DeviceIdType.MESH,
            )
            self.sent.append((wanted, copy))
            pl.when(wanted)(copy.start)

    def arrive(self, index):
        links, z = self.links, self.links.z
        ends = jnp.where(z == 0, index + 1, 2 - index)
        inner = jnp.where(z == 1, (0, 2, 3)[index], (3, 1, 0)[index])
        shard = jnp.where((z == 0) | (z == 3), ends, inner)
        pltpu.make_async_remote_copy(
            src_ref=self.ref.at[shard],
            dst_ref=self.ref.at[shard],
            send_sem=links.send.at[self.first],
            recv_sem=links.receive.at[self.first + index],
            device_id=(z * 2 + links.x, links.y * 2 + links.core),
            device_id_type=pl.DeviceIdType.MESH,
        ).wait_recv()
        self.hand_on(shard, (shard < z) & (z < 3), (shard > z) & (z > 0), 1)
        return shard

    def finish(self):
        for wanted, copy in self.sent:
            pl.when(wanted)(copy.wait_send)


COPIES = 320


def link_scratch():
    return [
        pltpu.SemaphoreType.DMA((COPIES,)),
        pltpu.SemaphoreType.DMA((COPIES,)),
        pltpu.SemaphoreType.DMA((64,)),
    ]


def along_z(source, target):
    def transfer(links, here, there):
        own = links.keep(source(here, links.z), target(there, links.z))
        copies = []
        for step in range(1, links.planes):
            device, to, _ = links.along(step)
            copies.append(links.push(source(here, to), target(there, links.z), device))
        yield
        own.wait()
        for copy in copies:
            copy.wait()

    return transfer


def along_z_in_turn(source, target):
    def transfer(links, here, there):
        own = links.keep(source(here, links.z), target(there, links.z))
        copies = []
        for step in range(1, links.planes):
            device, to, _ = links.along(step)
            copies.append(links.push(source(here, to), target(there, links.z), device, start=False))
        outer = (links.z == 0) | (links.z == links.planes - 1)
        for copy in copies:
            pl.when(outer)(copy.start)
        yield
        for copy in copies:
            pl.when(jnp.logical_not(outer))(copy.start)
        yield
        own.wait()
        for copy in copies:
            copy.wait()

    return transfer


def along_z_outer_first(source, target):
    def transfer(links, here, there):
        copies = []
        for step in range(1, links.planes):
            device, to, _ = links.along(step)
            copy = links.push(source(here, to), target(there, links.z), device, start=False)
            copies.append(((to == 0) | (to == links.planes - 1), copy))
        for outer, copy in copies:
            pl.when(outer)(copy.start)
        yield
        for outer, copy in copies:
            pl.when(jnp.logical_not(outer))(copy.start)
        own = links.keep(source(here, links.z), target(there, links.z))
        yield
        own.wait()
        for _, copy in copies:
            copy.wait()

    return transfer


def over_plane(source, target):
    def transfer(links, here, there):
        own = links.keep(source(here, links.p), target(there, links.p))
        copies = []
        for step in (6, 7, 4, 5, 2, 3, 1):
            device, to = links.near(step)
            copies.append(links.push(source(here, to), target(there, links.p), device))
        yield
        own.wait()
        for copy in copies:
            copy.wait()

    return transfer


def over_chips(source, target):
    def transfer(links, here, there):
        own = links.keep(source(here, links.p), target(there, links.p))
        copies = []
        for step in (6, 4, 2):
            device, to = links.near(step)
            copies.append(links.push(source(here, to), target(there, links.p), device))
        sibling, _ = links.near(1)
        passed = [links.push(source(here, links.p), target(there, links.p), sibling)]
        yield
        for step, copy in zip((6, 4, 2), copies):
            copy.wait_recv()
            _, sender = links.near(step)
            passed.append(links.push(target(there, sender), target(there, sender), sibling))
        yield
        own.wait()
        for copy in copies:
            copy.wait_send()
        for copy in passed:
            copy.wait()

    return transfer


def everywhere(links, here, there):
    own = links.keep(here, there.at[links.z, links.p])
    copies = []
    for step in (6, 7, 4, 5, 2, 3, 1):
        copies.append(links.push(here, there.at[links.z, links.p], links.near(step)[0]))
    yield
    own.wait()
    for copy in copies:
        copy.wait()
    copies = []
    for step in range(1, links.planes):
        copies.append(links.push(there.at[links.z], there.at[links.z], links.along(step)[0]))
    yield
    for copy in copies:
        copy.wait()


def drive(transfers):
    while transfers:
        left = []
        for transfer in transfers:
            try:
                next(transfer)
                left.append(transfer)
            except StopIteration:
                pass
        transfers = left


def whole(ref, index):
    return ref


def block(ref, index):
    return ref.at[index]


def second(ref, index):
    return ref.at[:, index]


def rows_of(index):
    return pl.ds(pl.multiple_of(index * 128, 128), 128)


def pick_tile(table, index_ref, tile, part):
    return jnp.concatenate(
        [table[pl.ds(index_ref[tile, part * 32 + row], 1), :] for row in range(32)], axis=0
    )


def sort_tile(order, table, first, second, offset, tile):
    for part in range(4):
        start = pl.multiple_of(tile * 128 + part * 32 + offset, 32)
        picked = pick_tile(table, order, tile, part)
        first[pl.ds(start, 32), :] = picked[:, :128].astype(first.dtype)
        second[pl.ds(start, 32), :] = picked[:, 128:].astype(second.dtype)


def across(column):
    return jnp.broadcast_to(column, (128, 128)).T[:1, :]


def down(row):
    return jnp.broadcast_to(row, (128, 128)).T


def dot(a, b, contract):
    return lax.dot_general(a, b, (contract, ((), ())), preferred_element_type=jnp.float32)


def key_scales(keys):
    rows = keys.astype(jnp.float32)
    mean_square = jnp.mean(rows * rows, axis=-1, keepdims=True) + 1e-06
    return rows, mean_square, lax.rsqrt(mean_square) / HEAD_DIM


def half_turned(row):
    return jnp.concatenate([row[:, 64:], row[:, :64]], axis=1)


def windows(before, here):
    return [jnp.concatenate([before[:, 64:], here[:, :64]], axis=1), here]


def masked_scores(raw, scale, query_pos, key_pos):
    return jnp.where(
        key_pos > query_pos, LATER, jnp.where(key_pos == query_pos, SELF, raw * scale)
    )


def attend_tiles(tiles, unroll, order, order_rows, table, shared, values, mixed, total_sorted, last_scale):
    sort = functools.partial(sort_tile, order, table, shared, values, BLOCK)
    end = tiles * 128
    for tile in [tiles - 1] + list(range(unroll)):
        sort(tile)
    shared[:BLOCK, :] = shared[end : end + BLOCK, :]
    values[:BLOCK, :] = values[end : end + BLOCK, :]
    last_scale[...] = across(key_scales(shared[end - BLOCK : end + BLOCK, :])[2])

    def step_tiles(step, carry):
        first = step * unroll
        numbers = [lax.rem(first + tiles - 1, tiles)] + [first + k for k in range(unroll)]
        places = [order_rows[pl.ds(t, 1), :] for t in numbers]
        scale = [last_scale[...]]
        work = []
        for k in range(unroll):
            start = pl.multiple_of((first + k) * 128, 128)
            keys = [shared[pl.ds(pl.multiple_of(start + half * 64, 64), 128), :] for half in range(2)]
            vals = [values[pl.ds(pl.multiple_of(start + half * 64, 64), 128), :] for half in range(2)]
            own = jnp.concatenate([keys[0][64:], keys[1][64:]], axis=0)
            scale.append(across(key_scales(own)[2]))
            work.append((keys, vals))
        last_scale[...] = scale[-1]
        for k in range(unroll):
            sort(lax.rem(first + unroll + k, tiles))
        query_pos = jnp.concatenate([down(place) for place in places[1:]], axis=0)
        key_pos, key_scale = [], []
        for k in range(unroll):
            key_pos += windows(places[k], places[k + 1])
            key_scale += windows(scale[k], scale[k + 1])
        raw = [dot(k[64:], k, ((1,), (1,))) for keys, _ in work for k in keys]
        raw, key_pos, key_scale = (
            jnp.concatenate([jnp.broadcast_to(a, (64, 128)) for a in parts], axis=0)
            for parts in (raw, key_pos, key_scale)
        )
        scores = masked_scores(raw, key_scale, query_pos, key_pos)
        highest = jnp.max(scores, axis=-1, keepdims=True)
        total = highest + jnp.log(jnp.sum(jnp.exp(scores - highest), axis=-1, keepdims=True))
        prob = jnp.exp(scores - total).astype(jnp.bfloat16)
        rows = pl.ds(pl.multiple_of(first * 128, 128), unroll * 128)
        total = jnp.broadcast_to(total, (unroll * 128, 128))
        mixed[rows, 128:] = total
        total_sorted[rows, :] = total
        vals = [v for _, vals in work for v in vals]
        mixed[rows, :128] = jnp.concatenate(
            [dot(prob[64 * i : 64 * i + 64], v, ((1,), (0,))) for i, v in enumerate(vals)], axis=0
        )
        return carry

    lax.fori_loop(0, tiles // unroll, step_tiles, 0)


def attend_back_tiles(
    tiles, unroll, order, order_rows, table, shared, values, total_sorted,
    grad_sorted, grad_total_sorted, sums, scale_sums, last_scale,
):
    sort = functools.partial(sort_tile, order, table, grad_sorted, grad_total_sorted, 0)
    end = tiles * 128
    for tile in range(unroll):
        sort(tile)
    last_scale[...] = across(key_scales(shared[end - BLOCK : end + BLOCK, :])[2])
    scale_sums[...] = jnp.zeros_like(scale_sums)
    sums[end : end + 128, :] = jnp.zeros((128, 256), jnp.float32)
    early = lax.broadcasted_iota(jnp.int32, (1, 128), 1) < 64

    def step_tiles(step, carry):
        first = step * unroll
        numbers = [lax.rem(first + tiles - 1, tiles)] + [first + k for k in range(unroll)]
        places = [order_rows[pl.ds(t, 1), :] for t in numbers]
        scale = [last_scale[...]]
        work = []
        for k in range(unroll):
            start = pl.multiple_of((first + k) * 128, 128)
            keys = [shared[pl.ds(pl.multiple_of(start + half * 64, 64), 128), :] for half in range(2)]
            vals = [values[pl.ds(pl.multiple_of(start + half * 64, 64), 128), :] for half in range(2)]
            own = jnp.concatenate([keys[0][64:], keys[1][64:]], axis=0)
            scale.append(across(key_scales(own)[2]))
            tile = pl.ds(start, 128)
            work.append(
                (keys, vals, grad_sorted[tile, :], grad_total_sorted[tile, :], total_sorted[tile, :])
            )
        last_scale[...] = scale[-1]
        for k in range(unroll):
            sort(lax.rem(first + unroll + k, tiles))
        blocks = 2 * unroll
        scale_parts = [0.0] * (unroll + 1)
        query_pos = jnp.concatenate([down(place) for place in places[1:]], axis=0)
        key_pos, key_scale = [], []
        for k in range(unroll):
            key_pos += windows(places[k], places[k + 1])
            key_scale += windows(scale[k], scale[k + 1])
        keys = [k for item in work for k in item[0]]
        vals = [v for item in work for v in item[1]]
        grads, grad_totals, totals = (
            jnp.concatenate([item[n] for item in work], axis=0) for n in (2, 3, 4)
        )
        own = [slice(64 * i, 64 * i + 64) for i in range(blocks)]
        raw = [dot(k[64:], k, ((1,), (1,))) for k in keys]
        grad_prob = [dot(grads[own[i]], v, ((1,), (1,))) for i, v in enumerate(vals)]
        raw, grad_prob, key_pos, key_scale = (
            jnp.concatenate([jnp.broadcast_to(a, (64, 128)) for a in parts], axis=0)
            for parts in (raw, grad_prob, key_pos, key_scale)
        )
        prob = jnp.exp(masked_scores(raw, key_scale, query_pos, key_pos) - totals)
        inner = jnp.sum(prob * grad_prob, axis=-1, keepdims=True)
        grad_score = jnp.where(
            key_pos < query_pos, prob * (grad_prob + (grad_totals - inner)), 0.0
        )
        product = grad_score * raw
        for index in range(blocks):
            k, half = index // 2, index % 2
            part = jnp.sum(product[own[index]], axis=0, keepdims=True)
            if half == 0:
                turned = half_turned(part)
                scale_parts[k] += jnp.where(early, 0.0, turned)
                scale_parts[k + 1] += jnp.where(early, turned, 0.0)
            else:
                scale_parts[k + 1] += part
        grad_raw = (grad_score * key_scale).astype(jnp.bfloat16)
        prob = prob.astype(jnp.bfloat16)
        key_parts = [dot(grad_raw[own[i]], keys[i][64:], ((0,), (0,))) for i in range(blocks)]
        value_parts = [dot(prob[own[i]], grads[own[i]], ((0,), (0,))) for i in range(blocks)]
        query_parts = [dot(grad_raw[own[i]], keys[i], ((1,), (0,))) for i in range(blocks)]
        key_sums = [key_parts[0][:64]] + [
            key_parts[i][64:] + query_parts[i] + (key_parts[i + 1][:64] if i + 1 < blocks else 0.0)
            for i in range(blocks)
        ]
        value_sums = [value_parts[0][:64]] + [
            value_parts[i][64:] + (value_parts[i + 1][:64] if i + 1 < blocks else 0.0)
            for i in range(blocks)
        ]
        for index in range(blocks):
            rows = pl.ds(pl.multiple_of(first * 128 + index * 64, 64), 64)
            sums[rows, :128] = key_sums[index + 1]
            sums[rows, 128:] = value_sums[index + 1]
        for k in range(unroll):
            scale_sums[pl.ds(first + k, 1), :] = scale_parts[k + 1]
        before = jnp.where(step == 0, tiles, numbers[0])
        rows = pl.ds(pl.multiple_of(before * 128 + 64, 64), 64)
        sums[rows, :128] += key_sums[0]
        sums[rows, 128:] += value_sums[0]
        scale_sums[pl.ds(before, 1), :] += scale_parts[0]
        return carry

    lax.fori_loop(0, tiles // unroll, step_tiles, 0)
    sums[end - 128 : end, :] += sums[end : end + 128, :]
    scale_sums[pl.ds(tiles - 1, 1), :] += scale_sums[pl.ds(tiles, 1), :]

    def finish(step, carry):
        for part in range(2):
            tile = step * 2 + part
            rows = rows_of(tile)
            start = pl.multiple_of(tile * 128 + 64, 64)
            keys, mean_square, scale = key_scales(shared[pl.ds(start, 128), :])
            factor = down(scale_sums[pl.ds(tile, 1), :]) * (scale / (mean_square * HEAD_DIM))
            sums[rows, :128] -= factor * keys
        return carry

    lax.fori_loop(0, tiles // 2, finish, 0)


VMEM = pl.BlockSpec(memory_space=pltpu.VMEM)
ANY = pl.BlockSpec(memory_space=pl.ANY)


def narrow(ref, index):
    return ref.at[:, index, :, pl.ds(0, HEAD_DIM)]


def normal_parts(rows):
    center = jnp.mean(rows, axis=-1, keepdims=True)
    offset = rows - center
    spread = jnp.mean(offset * offset, axis=-1, keepdims=True)
    inverse = lax.rsqrt(spread + 1e-05)
    return offset * inverse, inverse


def norm_back(grad, rows, gain):
    unit, inverse = normal_parts(rows)
    scaled = grad * gain
    shared = jnp.mean(scaled, axis=-1, keepdims=True)
    along = jnp.mean(scaled * unit, axis=-1, keepdims=True)
    return (
        (scaled - shared - unit * along) * inverse,
        jnp.sum(grad * unit, axis=0, keepdims=True),
        jnp.sum(grad, axis=0, keepdims=True),
    )


def gelu_parts(rows):
    below = 0.5 * (1.0 + lax.erf(rows * 0.7071067811865476))
    bell = jnp.exp(-0.5 * rows * rows) * 0.3989422804014327
    return rows * below, below + rows * bell


def open_part(
    links, planes,
    sort_order, sort_place, gain_a_in, shift_a_in, gain_f_in, shift_f_in, bias_up_in, bias_down_in,
    x2, wqk, wv, wo, wup, wdown, g2,
    ints, all_ints, floats, all_floats, gains, bias_up, order_rows, place_rows, order_s, place_s, normed, df,
    wqk_line, wv_line, wo_line, wup_rows, wqk_pair, wv_pair, heads, head_table, table, sums,
    shared, values, total_sorted, mixed_home, total_home, last_scale,
    wo_all, wup_part, wdown_part, df_plane, mixed_in, total_in,
):
    low, full = jnp.bfloat16, jnp.float32
    sub = links.y * 2 + links.core
    tiles = planes * 8
    ints[...] = jnp.concatenate([sort_order[...], sort_place[...]], axis=0)
    lane = lax.broadcasted_iota(jnp.int32, (1, 128), 1) // 32

    def spread(vector):
        wide = jnp.concatenate([vector[...].astype(full)] * 4, axis=1)
        return jnp.where(lane == sub, wide, 0.0)

    floats[...] = jnp.concatenate(
        [spread(v) for v in (gain_a_in, shift_a_in, gain_f_in, shift_f_in, bias_down_in)]
        + [bias_up_in[...].astype(full), jnp.zeros((2, 128), full)],
        axis=0,
    )
    df[...] = g2[...].astype(low)
    links.meet()
    share_floats = everywhere(links, floats, all_floats)
    next(share_floats)
    share_ints = everywhere(links, ints, all_ints)
    next(share_ints)

    def pair_columns(ref, z):
        return ref.at[:, pl.ds(pl.multiple_of(z * 256, 256), 256)]

    pair_shares = [
        along_z(pair_columns, block)(links, a, b) for a, b in ((wqk, wqk_line), (wv, wv_line))
    ]
    for transfer in pair_shares:
        next(transfer)
    wo_share = along_z(whole, block)(links, wo, wo_line)
    next(wo_share)
    df_share = over_chips(whole, block)(links, df, df_plane)
    next(df_share)
    unit, _ = normal_parts(x2[...])
    next(share_floats)

    def upper_columns(chunk):
        def columns(ref, p):
            return ref.at[:, pl.ds(pl.multiple_of((chunk * 8 + p) * 128, 128), 128)]

        def landing(ref, p):
            return ref.at[p, :, pl.ds(chunk * 128, 128)]

        return over_plane(columns, landing)

    drive([share_floats])

    def vector_of(row, z_step=2):
        chunks = []
        for chunk in range(8):
            z, x = chunk // 2, chunk % 2
            parts = [all_floats[z, x * 4 + u, row : row + 1, :] for u in range(4)]
            chunks.append(parts[0] + parts[1] + parts[2] + parts[3])
        return jnp.concatenate(chunks, axis=1)

    gain, shift = vector_of(0), vector_of(1)
    normed[links.z] = (unit * gain + shift).astype(low)
    normed_chain = Chain(links, normed)
    for transfer in pair_shares:
        drive([transfer])
    pair_shares = [
        over_chips(whole, second)(links, a, b) for a, b in ((wqk_line, wqk_pair), (wv_line, wv_pair))
    ]
    for transfer in pair_shares:
        next(transfer)
    next(share_ints)
    upper_shares = [upper_columns(chunk)(links, wup, wup_rows) for chunk in range(planes)]
    for transfer in upper_shares:
        next(transfer)
    for transfer in pair_shares:
        next(transfer)
    gains[0:1, :] = gain
    gains[1:2, :] = shift
    for row in (2, 3, 4):
        gains[row : row + 1, :] = vector_of(row)
    for z in range(planes):
        bias_up[:, z * 128 : (z + 1) * 128] = all_floats[z, links.p, 5:6, :]
    drive(pair_shares)
    drive([share_ints])
    for z in range(planes):
        for p in range(8):
            tile = z * 8 + p
            order_rows[tile : tile + 1, :] = all_ints[z, p, pl.ds(sub, 1), :]
            place_rows[tile : tile + 1, :] = all_ints[z, p, pl.ds(sub + 4, 1), :]
    to_scalars = [links.keep(order_rows, order_s), links.keep(place_rows, place_s)]

    def head_columns(z):
        def columns(ref, p):
            return ref.at[z, :, pl.ds(pl.multiple_of((p // 4) * 256, 256), 256)]

        return columns

    def landing(z):
        return lambda ref, p: ref.at[z, p]

    def project(z):
        rows = normed[z]
        for weights, offset in ((wqk_pair, 0), (wv_pair, 128)):
            result = dot(rows, weights[...].reshape(-1, 256), ((1,), (0,))).astype(low)
            heads[z, :, offset : offset + 128] = result[:, :128]
            heads[z, :, 256 + offset : 384 + offset] = result[:, 128:]
        transfer = over_chips(head_columns(z), landing(z))(links, heads, head_table)
        next(transfer)
        return transfer

    head_shares = [project(links.z)]
    next(df_share)
    for index in range(3):
        head_shares.append(project(normed_chain.arrive(index)))
        next(head_shares[-2])
    for transfer in upper_shares:
        drive([transfer])
    up_share = along_z_in_turn(whole, block)(links, wup_rows, wup_part)
    next(up_share)
    down_share = along_z_in_turn(whole, block)(links, wdown, wdown_part)
    next(down_share)
    next(head_shares[-1])
    drive([wo_share])
    wo_share = over_chips(whole, second)(links, wo_line, wo_all)
    for copy in to_scalars:
        copy.wait()
    drive(head_shares)
    shares = [df_share, up_share, down_share]
    next(up_share)
    next(down_share)
    next(wo_share)

    def load(tile, carry):
        table[rows_of(tile), :] = head_table[tile // 8, lax.rem(tile, 8)].astype(full)
        return carry

    lax.fori_loop(0, tiles, load, 0)
    attend_tiles(
        tiles, 2, order_s, order_rows, table, shared, values, sums, total_sorted, last_scale
    )
    next(wo_share)
    kept = []
    sent = []
    for step in (6, 7, 4, 5, 2, 3, 1, 0):
        device, p = links.near(step)

        def unsort(z, carry):
            totals = []
            for part in range(4):
                picked = pick_tile(sums, place_s, z * 8 + p, part)
                mixed_home[p, z, part * 32 : part * 32 + 32, :] = picked[:, :128].astype(low)
                totals.append(picked[:, 128:])
            total_home[p, pl.ds(z, 1), :] = jnp.concatenate(totals, axis=0).T[:1, :]
            return carry

        lax.fori_loop(0, planes, unsort, 0)
        for here, there in ((mixed_home, mixed_in), (total_home, total_in)):
            source, target = here.at[p], there.at[links.p]
            if step:
                sent.append(links.push(source, target, device))
            else:
                kept.append(links.keep(source, target))
    normed_chain.finish()
    for copy in kept + sent:
        copy.wait()
    return wo_share, shares


def feed_part(
    links, planes, wo_share, weight_shares,
    x1, g1, y1_out, g1_out, gains, bias_up, sums, table, head_table, mixed_home, total_home,
    wo_all, wup_part, wdown_part, df_plane, mixed_in, total_in, dtotal_in, attended, arrived, h2, act, dpre,
    kept, from_sibling, to_chip, from_chip, up_grad, up_parts, down_grad, down_parts, dout, datt_out, datt,
    up_bias, feed_gain, feed_shift, y2_sibling, y2_chip, out_sibling,
):
    low, full = jnp.bfloat16, jnp.float32

    def weight_rows(head, z):
        return pl.ds(pl.multiple_of((head * planes + z) * 128, 128), 128)

    def wo_rows(z):
        return wo_all[z].reshape(256, -1)

    def combine(z, carry):
        for x in range(2):
            totals = [down(total_in[x * 4 + u, pl.ds(z, 1), :]) for u in range(4)]
            highest = jnp.maximum(
                jnp.maximum(totals[0], totals[1]), jnp.maximum(totals[2], totals[3])
            )
            parts = [jnp.exp(t - highest) for t in totals]
            inverse = 1.0 / (parts[0] + parts[1] + parts[2] + parts[3])
            result = 0.0
            for u in range(4):
                weight = parts[u] * inverse
                sums[weight_rows(x * 4 + u, z), :128] = weight
                result += weight * mixed_in[x * 4 + u, z].astype(full)
            attended[z, :, x * 128 : (x + 1) * 128] = result.astype(low)
        return carry

    lax.fori_loop(0, planes, combine, 0)
    share = along_z(block, block)(links, attended, arrived)
    next(share)
    drive([wo_share])
    drive([share])
    y1 = x1[...]
    for z in range(planes):
        y1 += dot(arrived[z], wo_rows(z), ((1,), (0,)))
    y1_out[...] = y1
    unit, _ = normal_parts(y1)
    own_rows = pl.ds(pl.multiple_of(links.p * 128, 128), 128)
    h2[own_rows, :] = (unit * gains[2:3, :] + gains[3:4, :]).astype(low)

    sibling, _ = links.near(1)
    own_h2 = h2.at[own_rows, :]
    direct = {step: links.push(own_h2, own_h2, links.near(step)[0]) for step in (2, 4)}
    handed = {0: links.push(own_h2, own_h2, sibling)}
    drive(weight_shares)

    half = wup_part.shape[3] // 2

    def upper_back(part, carry):
        rows = pl.ds(pl.multiple_of(part * 256, 256), 256)
        grad = df_plane[pl.ds(part * 2, 2)].reshape(256, -1)
        result = dot(grad, wdown_part[...].reshape(half * 2, -1), ((1,), (1,)))
        table[rows, :] = result[:, :half]
        table[pl.ds(pl.multiple_of(1024 + part * 256, 256), 256), :] = result[:, half:]
        return carry

    lax.fori_loop(0, 4, upper_back, 0)

    def pass_on(step):
        direct[step].wait_recv()
        block_rows = h2.at[rows_of(links.near(step)[1]), :]
        handed[step] = links.push(block_rows, block_rows, sibling)

    def feed(slot, step):
        handed[step].wait_recv()
        chip = links.near(step)[1] // 2
        rows = pl.ds(pl.multiple_of(chip * 256, 256), 256)
        before = dot(h2[rows, :], wup_part[...].reshape(-1, 2 * half), ((1,), (0,))) + bias_up[...]
        value, slope = gelu_parts(before)
        act[rows, :] = value.astype(low)
        grad = jnp.concatenate(
            [table[rows, :], table[pl.ds(pl.multiple_of(1024 + chip * 256, 256), 256), :]], axis=1
        )
        grad = (grad * slope).astype(low)
        dpre[rows, :] = grad
        kept[slot] = dot(grad, wup_part[...].reshape(-1, 2 * half), ((1,), (1,))).reshape(2, 128, -1).astype(low)
        return links.push(kept.at[slot, 1 - links.core], from_sibling.at[slot], sibling)

    def chip_sum(slot, step, traded):
        traded.wait_recv()
        result = kept[slot, links.core].astype(full) + from_sibling[slot].astype(full)
        if slot == 0:
            return result
        to_chip[slot - 1] = result.astype(low)
        return links.push(to_chip.at[slot - 1], from_chip.at[slot - 1], links.near(step)[0])

    traded = [feed(0, 0)]
    for step in (2, 4):
        direct[step].wait_send()
    direct[6] = links.push(own_h2, own_h2, links.near(6)[0])
    pass_on(2)
    pass_on(4)
    traded.append(feed(1, 2))
    sent = [chip_sum(1, 2, traded[1])]
    pass_on(6)
    traded.append(feed(2, 4))
    sent.append(chip_sum(2, 4, traded[2]))
    traded.append(feed(3, 6))
    sent.append(chip_sum(3, 6, traded[3]))
    own_sum = chip_sum(0, 0, traded[0])

    def upper_grad(part, carry):
        rows = pl.ds(pl.multiple_of(part * 256, 256), 256)
        up_grad[part] = dot(h2[:, rows], dpre[...], ((0,), (0,))).astype(low)
        return carry

    lax.fori_loop(0, planes, upper_grad, 0)

    def lower_grad(part, carry):
        rows = pl.ds(pl.multiple_of(part * 128, 128), 128)
        down_grad[part] = dot(act[:, rows], df_plane[...].reshape(act.shape[0], -1), ((0,), (0,))).astype(low)
        return carry

    lax.fori_loop(0, planes, lower_grad, 0)

    def lower(part, carry):
        rows = pl.ds(pl.multiple_of(part * 128, 128), 128)
        df_plane[part] = dot(
            act[rows, :], wdown_part[...].reshape(2 * half, -1), ((1,), (0,))
        ).astype(low)
        return carry

    lax.fori_loop(0, 8, lower, 0)

    def of_chip(step, core):
        return links.near(step)[1] // 2 * 2 + core

    y2_traded = [
        links.push(df_plane.at[of_chip(step, 1 - links.core)], y2_sibling.at[slot], sibling)
        for slot, step in enumerate((6, 4, 2, 0))
    ]
    for copy in sent:
        copy.wait_recv()
    grad = own_sum + (
        from_chip[0].astype(full) + from_chip[1].astype(full) + from_chip[2].astype(full)
    )
    part, gain_grad, shift_grad = norm_back(grad, y1_out[...], gains[2:3, :])
    feed_gain[...] = gain_grad
    feed_shift[...] = shift_grad
    g1_new = g1[...] + part
    g1_out[...] = g1_new
    dout[...] = g1_new.astype(low)
    for z in range(planes):
        datt_out[z] = dot(dout[...], wo_rows(z), ((1,), (1,))).astype(low)
    share = along_z(block, block)(links, datt_out, datt)
    next(share)
    y2_pushed = []
    for slot, step in enumerate((6, 4, 2, 0)):
        y2_traded[slot].wait()
        mine = of_chip(step, links.core)
        df_plane[mine] = (
            df_plane[mine].astype(full) + y2_sibling[slot].astype(full)
        ).astype(low)
        if step:
            y2_pushed.append(
                links.push(df_plane.at[mine], y2_chip.at[slot], links.near(step)[0])
            )
    for copy in [direct[6]] + list(handed.values()):
        copy.wait_send()
    for z in range(planes):
        part = dot(arrived[z], dout[...], ((0,), (0,))).astype(low)
        for p in range(8):
            row = p * 128 + z * 32
            h2[row : row + 32, :] = part[p * 32 : p * 32 + 32]
    out_traded = [
        links.push(
            h2.at[rows_of(links.near(step)[1] // 2 * 2 + 1 - links.core), :],
            out_sibling.at[slot],
            sibling,
        )
        for slot, step in enumerate((6, 4, 2, 0))
    ]
    up_bias[...] = jnp.sum(dpre[...].astype(full), axis=0, keepdims=True)
    drive([share])
    share_up = along_z(block, block)(links, up_grad, up_parts)
    next(share_up)
    share_down = along_z(block, block)(links, down_grad, down_parts)
    next(share_down)
    def combine_back(z, carry):
        for x in range(2):
            grad = datt[z, :, x * 128 : (x + 1) * 128].astype(full)
            chosen = [sums[weight_rows(x * 4 + u, z), :128] for u in range(4)]
            inner = [
                jnp.sum(grad * mixed_in[x * 4 + u, z].astype(full), axis=-1, keepdims=True)
                for u in range(4)
            ]
            mean = sum(chosen[u] * inner[u] for u in range(4))
            for u in range(4):
                mixed_home[x * 4 + u, z] = (chosen[u] * grad).astype(low)
                change = (chosen[u] * (inner[u] - mean)).astype(low).astype(full)
                total_home[x * 4 + u, pl.ds(z, 1), :] = change.T[:1, :]
        return carry

    lax.fori_loop(0, planes, combine_back, 0)
    shares = [
        over_plane(block, narrow)(links, mixed_home, head_table),
        over_plane(block, block)(links, total_home, dtotal_in),
    ]
    for transfer in shares:
        next(transfer)
    for copy in traded + sent:
        copy.wait_send()
    return shares, y2_pushed, share_up, share_down, out_traded


def close_part(
    links, planes, shares, y2_pushed, share_up, share_down, out_traded,
    x2, g2, y2_out, g2_out, shared_grad_out, value_grad_out, out_grad_out, up_out, down_out, vectors_out,
    gains, order_rows, order_s, place_s, normed, wqk_pair, wv_pair, shared, values, total_sorted, head_table,
    table, sums, last_scale, dtotal_in, attended, df_plane, h2, wup_part, wdown_part, up_parts, down_grad,
    down_parts, kept, from_sibling, to_chip, from_chip, up_bias, feed_gain, feed_shift, grad_sorted,
    grad_total_sorted, scale_sums, up_sum, up_arrived, dshared, dvalues, de, out_sent, out_arrived,
    weight_arrived, weight_sum, weight_final, tiles_sent, tiles_arrived, tile, tile_line, y2_sibling, y2_chip,
    out_sibling, out_chip,
):
    low, full = jnp.bfloat16, jnp.float32
    tiles = planes * 8
    line = planes * 128
    out_sums = []
    for slot, step in enumerate((6, 4, 2, 0)):
        out_traded[slot].wait()
        rows = rows_of(links.near(step)[1] // 2 * 2 + links.core)
        total = h2[rows, :].astype(full) + out_sibling[slot].astype(full)
        h2[rows, :] = total.astype(low)
        out_sums.append(rows)
    drive(shares)
    out_pushed = [
        links.push(h2.at[out_sums[slot], :], out_chip.at[slot], links.near(step)[0])
        for slot, step in enumerate((6, 4, 2))
    ]

    def load(index, carry):
        z, p = index // 8, lax.rem(index, 8)
        table[rows_of(index), :128] = head_table[z, p, :, :HEAD_DIM].astype(full)
        table[rows_of(index), 128:] = down(dtotal_in[p, pl.ds(z, 1), :])
        return carry

    lax.fori_loop(0, tiles, load, 0)
    attend_back_tiles(
        tiles, 4, order_s, order_rows, table, shared, values, total_sorted,
        grad_sorted, grad_total_sorted, sums, scale_sums, last_scale,
    )
    total = h2[out_sums[3], :].astype(full)
    for slot, copy in enumerate(out_pushed):
        copy.wait()
        total += out_chip[slot].astype(full)
    out_sent[...] = total.astype(low).reshape(out_sent.shape)
    share_out = along_z(block, block)(links, out_sent, out_arrived)
    next(share_out)
    sibling, _ = links.near(1)
    steps = (6, 4, 2, 0)
    halves = ((0, 3), (1, 2))

    def unsort(half, slot, step):
        chip = links.near(step)[1] // 2
        columns = pl.ds(half * 512, 512)
        for core, goal in ((0, 1 - links.core), (1, links.core)):

            def rows(index, carry):
                z = index * 3 if half == 0 else index + 1
                place = pl.ds(pl.multiple_of(half * 512 + index * 256, 256), 256)
                for part in range(4):
                    picked = pick_tile(sums, place_s, z * 8 + chip * 2 + goal, part)
                    kept[slot, core, part * 32 : part * 32 + 32, place] = picked.astype(low)
                return carry

            lax.fori_loop(0, 2, rows, 0)
            if core == 0:
                traded = links.push(
                    kept.at[slot, 0, :, columns], from_sibling.at[slot, :, columns], sibling
                )
        return traded

    def chip_sum(half, slot, traded):
        traded.wait_recv()
        columns = slice(half * 512, half * 512 + 512)
        result = kept[slot, 1, :, columns].astype(full) + from_sibling[slot, :, columns].astype(full)
        if steps[slot] == 0:
            return result
        to_chip[slot, :, columns] = result.astype(low)
        columns = pl.ds(half * 512, 512)
        return links.push(
            to_chip.at[slot, :, columns], from_chip.at[slot, :, columns], links.near(steps[slot])[0]
        )

    traded, sent = [[], []], [[], []]
    for half in range(2):
        for slot, step in enumerate(steps):
            traded[half].append(unsort(half, slot, step))
            if slot:
                sent[half].append(chip_sum(half, slot - 1, traded[half][slot - 1]))
    own_columns = pl.ds(pl.multiple_of(links.x * 128, 128), 128)
    far_columns = pl.ds(pl.multiple_of((1 - links.x) * 128, 128), 128)
    all_wqk, all_wv = wqk_pair[...].reshape(-1, 256), wv_pair[...].reshape(-1, 256)

    def settle_sum(half, columns, result):
        for index, z in enumerate(halves[half]):
            part = result[:, index * 256 : index * 256 + 256].astype(low)
            dshared[z * 128 : z * 128 + 128, columns] = part[:, :128]
            dvalues[z * 128 : z * 128 + 128, columns] = part[:, 128:]

    share_de = along_z_outer_first(block, block)(links, y2_sibling, de)
    for half in range(2):
        own_sum = chip_sum(half, 3, traded[half][3])
        columns = slice(half * 512, half * 512 + 512)
        for copy in sent[half]:
            copy.wait_recv()
        settle_sum(half, own_columns, own_sum + from_chip[2, :, columns].astype(full))
        settle_sum(
            half, far_columns, from_chip[1, :, columns].astype(full) + from_chip[0, :, columns].astype(full)
        )
        for z in halves[half]:
            rows = slice(z * 128, z * 128 + 128)
            y2_sibling[z] = (
                dot(dshared[rows, :], all_wqk, ((1,), (1,))) + dot(dvalues[rows, :], all_wv, ((1,), (1,)))
            ).astype(low)
        next(share_de)
    drive([share_up])
    up_sum[...] = sum(up_parts[z].astype(full) for z in range(planes)).reshape(up_sum.shape)
    share_up = over_plane(block, block)(links, up_sum, up_arrived)
    next(share_up)
    all_normed = normed[...].reshape(line, -1)
    for index, grad in enumerate((dshared, dvalues)):
        wup_part[:, :, :, index * 256 : index * 256 + 256] = (
            dot(all_normed, grad[...], ((0,), (0,))).astype(low).reshape(wup_part.shape[:3] + (256,))
        )
    share_weights = over_plane(second, block)(links, wup_part, weight_arrived)
    next(share_weights)
    for copy in y2_pushed:
        copy.wait()
    y2_out[...] = x2[...] + (
        df_plane[links.p].astype(full)
        + sum(y2_chip[slot].astype(full) for slot in range(3))
        + gains[4:5, :]
    )
    drive([share_up])
    for p in range(8):
        for z in range(planes):
            up_out[:, (z * 8 + p) * 128 : (z * 8 + p + 1) * 128] = up_arrived[
                p, :, z * 128 : (z + 1) * 128
            ]
    drive([share_down])
    down_out[...] = sum(down_parts[z].astype(full) for z in range(planes))
    drive([share_out])
    out_grad_out[...] = sum(out_arrived[z].astype(full) for z in range(planes))
    down_bias = jnp.sum(g2[...].astype(low).astype(full), axis=0, keepdims=True)
    drive([share_weights])
    weight_sum[...] = sum(weight_arrived[p].astype(full) for p in range(8)).astype(low)

    share_final = along_z(block, block)(links, weight_sum, weight_final)
    next(share_final)
    drive([share_de])
    part, gain_grad, shift_grad = norm_back(
        sum(de[z].astype(full) for z in range(planes)), x2[...], gains[0:1, :]
    )
    vectors = [gain_grad, shift_grad, feed_gain[...], feed_shift[...], down_bias]
    for x in range(2):
        for index, vector in enumerate(vectors):
            for z in range(planes):
                chunk = (z * 2 + x) * 128
                row = index * planes + z
                tiles_sent[x, row : row + 1, :] = vector[:, chunk : chunk + 128]
        tiles_sent[x, 5 * planes :, :] = jnp.zeros((24 - 5 * planes, 128), full)

    def of_x(ref, p):
        return ref.at[p // 4]

    share_tiles = over_plane(of_x, block)(links, tiles_sent, tiles_arrived)
    next(share_tiles)
    g2_out[...] = g2[...] + part
    drive([share_tiles])
    tile[...] = jnp.sum(tiles_arrived[...], axis=0)
    for z in range(planes):
        tile[5 * planes + z : 5 * planes + z + 1, :] = up_bias[:, z * 128 : (z + 1) * 128]
    share_tile = along_z(whole, block)(links, tile, tile_line)
    next(share_tile)
    drive([share_final])
    for z in range(planes):
        columns = slice(z * 256, z * 256 + 256)
        shared_grad_out[:, columns] = weight_final[z, :, :256].astype(full)
        value_grad_out[:, columns] = weight_final[z, :, 256:].astype(full)
    drive([share_tile])
    tile[...] = jnp.sum(tile_line[...], axis=0)
    for index in range(6):
        vectors_out[index : index + 1, :] = tile[pl.ds(index * planes + links.z, 1), :]
    vectors_out[6:8, :] = jnp.zeros((2, 128), full)
    for copy in traded[0] + traded[1] + sent[0] + sent[1]:
        copy.wait_send()


LAYER_INPUTS = (
    "sort_order", "sort_place", "gain_a_in", "shift_a_in", "gain_f_in", "shift_f_in", "bias_up_in",
    "bias_down_in", "x2", "wqk", "wv", "wo", "wup", "wdown", "g2", "x1", "g1",
)
LAYER_OUTPUTS = (
    "y1_out", "y2_out", "g1_out", "g2_out", "shared_grad_out", "value_grad_out", "out_grad_out",
    "up_out", "down_out", "vectors_out",
)
OPEN_REFS = (
    "sort_order", "sort_place", "gain_a_in", "shift_a_in", "gain_f_in", "shift_f_in", "bias_up_in",
    "bias_down_in", "x2", "wqk", "wv", "wo", "wup", "wdown", "g2", "ints", "all_ints", "floats",
    "all_floats", "gains", "bias_up", "order_rows", "place_rows", "order_s", "place_s", "normed",
    "df", "wqk_line", "wv_line", "wo_line", "wup_rows", "wqk_pair", "wv_pair", "heads",
    "head_table", "table", "sums", "shared", "values", "total_sorted", "mixed_home", "total_home",
    "last_scale", "wo_all", "wup_part", "wdown_part", "df_plane", "mixed_in", "total_in",
)
FEED_REFS = (
    "x1", "g1", "y1_out", "g1_out", "gains", "bias_up", "sums", "table", "head_table", "mixed_home",
    "total_home", "wo_all", "wup_part", "wdown_part", "df_plane", "mixed_in", "total_in",
    "dtotal_in", "attended", "arrived", "h2", "act", "dpre", "kept", "from_sibling", "to_chip",
    "from_chip", "up_grad", "up_parts", "down_grad", "down_parts", "dout", "datt_out", "datt",
    "up_bias", "feed_gain", "feed_shift", "y2_sibling", "y2_chip", "out_sibling",
)
CLOSE_REFS = (
    "x2", "g2", "y2_out", "g2_out", "shared_grad_out", "value_grad_out", "out_grad_out", "up_out",
    "down_out", "vectors_out", "gains", "order_rows", "order_s", "place_s", "normed", "wqk_pair",
    "wv_pair", "shared", "values", "total_sorted", "head_table", "table", "sums", "last_scale",
    "dtotal_in", "attended", "df_plane", "h2", "wup_part", "wdown_part", "up_parts", "down_grad",
    "down_parts", "kept", "from_sibling", "to_chip", "from_chip", "up_bias", "feed_gain",
    "feed_shift", "grad_sorted", "grad_total_sorted", "scale_sums", "up_sum", "up_arrived",
    "dshared", "dvalues", "de", "out_sent", "out_arrived", "weight_arrived", "weight_sum",
    "weight_final", "tiles_sent", "tiles_arrived", "tile", "tile_line",
    "y2_sibling", "y2_chip", "out_sibling", "out_chip",
)


def layer_scratch(planes, rows, width, own, part):
    low, full, whole_number = jnp.bfloat16, jnp.float32, jnp.int32
    tiles = planes * 8
    tokens = tiles * rows
    return {
        "ints": pltpu.VMEM((8, rows), whole_number),
        "all_ints": pltpu.VMEM((planes, 8, 8, rows), whole_number),
        "floats": pltpu.VMEM((8, rows), full),
        "all_floats": pltpu.VMEM((planes, 8, 8, rows), full),
        "gains": pltpu.VMEM((8, width), full),
        "bias_up": pltpu.VMEM((1, part), full),
        "order_rows": pltpu.VMEM((tiles, rows), whole_number),
        "place_rows": pltpu.VMEM((tiles, rows), whole_number),
        "order_s": pltpu.SMEM((tiles, rows), whole_number),
        "place_s": pltpu.SMEM((tiles, rows), whole_number),
        "normed": pltpu.VMEM((planes, rows, width), low),
        "df": pltpu.VMEM((rows, width), low),
        "wqk_line": pltpu.VMEM((planes, own, 256), low),
        "wv_line": pltpu.VMEM((planes, own, 256), low),
        "wo_line": pltpu.VMEM((planes, own, width), low),
        "wup_rows": pltpu.VMEM((8, own, part), low),
        "wqk_pair": pltpu.VMEM((planes, 8, own, 256), low),
        "wv_pair": pltpu.VMEM((planes, 8, own, 256), low),
        "heads": pltpu.VMEM((planes, rows, 512), low),
        "head_table": pltpu.VMEM((planes, 8, rows, 256), low),
        "table": pltpu.VMEM((tokens, 256), full),
        "sums": pltpu.VMEM((tokens + rows, 256), full),
        "shared": pltpu.VMEM((tokens + BLOCK, HEAD_DIM), low),
        "values": pltpu.VMEM((tokens + BLOCK, HEAD_DIM), low),
        "total_sorted": pltpu.VMEM((tokens, HEAD_DIM), full),
        "mixed_home": pltpu.VMEM((8, planes, rows, HEAD_DIM), low),
        "total_home": pltpu.VMEM((8, 8, rows), full),
        "last_scale": pltpu.VMEM((1, rows), full),
        "wo_all": pltpu.VMEM((planes, 8, own, width), low),
        "wup_part": pltpu.VMEM((planes, 8, own, part), low),
        "wdown_part": pltpu.VMEM((planes, rows, width), low),
        "df_plane": pltpu.VMEM((8, rows, width), low),
        "mixed_in": pltpu.VMEM((8, planes, rows, HEAD_DIM), low),
        "total_in": pltpu.VMEM((8, 8, rows), full),
        "dtotal_in": pltpu.VMEM((8, 8, rows), full),
        "attended": pltpu.VMEM((planes, rows, 256), low),
        "arrived": pltpu.VMEM((planes, rows, 256), low),
        "h2": pltpu.VMEM((8 * rows, width), low),
        "act": pltpu.VMEM((8 * rows, part), low),
        "dpre": pltpu.VMEM((8 * rows, part), low),
        "kept": pltpu.VMEM((4, 2, rows, width), low),
        "from_sibling": pltpu.VMEM((4, rows, width), low),
        "to_chip": pltpu.VMEM((3, rows, width), low),
        "from_chip": pltpu.VMEM((3, rows, width), low),
        "up_grad": pltpu.VMEM((planes, width // planes, part), low),
        "up_parts": pltpu.VMEM((planes, width // planes, part), low),
        "down_grad": pltpu.VMEM((planes, rows, width), low),
        "down_parts": pltpu.VMEM((planes, rows, width), low),
        "dout": pltpu.VMEM((rows, width), low),
        "datt_out": pltpu.VMEM((planes, rows, 256), low),
        "datt": pltpu.VMEM((planes, rows, 256), low),
        "up_bias": pltpu.VMEM((1, part), full),
        "feed_gain": pltpu.VMEM((1, width), full),
        "feed_shift": pltpu.VMEM((1, width), full),
        "grad_sorted": pltpu.VMEM((tokens, HEAD_DIM), low),
        "grad_total_sorted": pltpu.VMEM((tokens, HEAD_DIM), full),
        "scale_sums": pltpu.VMEM((tiles + 8, rows), full),
        "up_sum": pltpu.VMEM((8, own, part), full),
        "up_arrived": pltpu.VMEM((8, own, part), full),
        "dshared": pltpu.VMEM((planes * rows, 256), low),
        "dvalues": pltpu.VMEM((planes * rows, 256), low),
        "de": pltpu.VMEM((planes, rows, width), low),
        "out_sent": pltpu.VMEM((planes, own, width), low),
        "out_arrived": pltpu.VMEM((planes, own, width), low),
        "y2_sibling": pltpu.VMEM((4, rows, width), low),
        "y2_chip": pltpu.VMEM((3, rows, width), low),
        "out_sibling": pltpu.VMEM((4, rows, width), low),
        "out_chip": pltpu.VMEM((3, rows, width), low),
        "weight_arrived": pltpu.VMEM((8, planes, own, 512), low),
        "weight_sum": pltpu.VMEM((planes, own, 512), low),
        "weight_final": pltpu.VMEM((planes, own, 512), low),
        "tiles_sent": pltpu.VMEM((2, 24, rows), full),
        "tiles_arrived": pltpu.VMEM((8, 24, rows), full),
        "tile": pltpu.VMEM((24, rows), full),
        "tile_line": pltpu.VMEM((planes, 24, rows), full),
    }


def layer_kernel(planes, names, *refs):
    links = Links(planes, *refs[len(names) :])
    held = dict(zip(names, refs))
    links.greet()
    shares = open_part(links, planes, *[held[name] for name in OPEN_REFS])
    shares = feed_part(links, planes, *shares, *[held[name] for name in FEED_REFS])
    close_part(links, planes, *shares, *[held[name] for name in CLOSE_REFS])


def layer_stage(arguments, collective_id, planes):
    rows, width = arguments[LAYER_INPUTS.index("x2")].shape
    own, hidden = arguments[LAYER_INPUTS.index("wup")].shape
    shape = jax.ShapeDtypeStruct
    token, weight = shape((rows, width), jnp.float32), shape((own, width), jnp.float32)
    outputs = [token] * 4 + [weight] * 3 + [
        shape((own, hidden), jnp.float32), token, shape((8, rows), jnp.float32)
    ]
    scratch = layer_scratch(planes, rows, width, own, hidden // 8)
    names = LAYER_INPUTS + LAYER_OUTPUTS + tuple(scratch)
    return pl.pallas_call(
        functools.partial(layer_kernel, planes, names),
        out_shape=outputs,
        in_specs=[VMEM] * len(arguments),
        out_specs=[VMEM] * len(outputs),
        scratch_shapes=list(scratch.values()) + link_scratch(),
        compiler_params=pltpu.CompilerParams(
            vmem_limit_bytes=60 << 20, collective_id=collective_id, has_side_effects=True
        ),
        name="layer",
    )(*arguments)


def finish_kernel(
    y1, y2, g1, g2, shared_grad, value_grad, out_grad, up_grad, down_grad, vectors,
    y1_out, y2_out, g1_out, g2_out, gain_a_out, shift_a_out, shared_out, value_out, out_out,
    gain_f_out, shift_f_out, up_out, up_bias_out, down_out, down_bias_out, arrived,
):
    pairs = (
        (y1, y1_out), (y2, y2_out), (g1, g1_out), (g2, g2_out), (shared_grad, shared_out),
        (value_grad, value_out), (out_grad, out_out), (up_grad, up_out), (down_grad, down_out),
    )
    copies = [
        pltpu.make_async_copy(source, target.at[0], arrived.at[index])
        for index, (source, target) in enumerate(pairs)
    ]
    for copy in copies:
        copy.start()
    sub = lax.axis_index("sub")
    rows = vectors[...]
    own = sum(
        jnp.where(sub == u, rows[:, u * 32 : u * 32 + 32], 0.0) for u in range(4)
    )
    for row, target in enumerate((gain_a_out, shift_a_out, gain_f_out, shift_f_out, down_bias_out)):
        target[...] = own[row : row + 1, :]
    up_bias_out[...] = rows[5:6, :]
    for copy in copies:
        copy.wait()


def finish_stage(arguments):
    full = jnp.float32
    large = [(jax.ShapeDtypeStruct((1,) + a.shape, full), ANY) for a in arguments[:-1]]
    y1, y2, g1, g2, shared_grad, value_grad, out_grad, up_grad, down_grad = large
    small = (jax.ShapeDtypeStruct((1, arguments[4].shape[0]), full), VMEM)
    up_bias = (jax.ShapeDtypeStruct((1, arguments[-1].shape[1]), full), VMEM)
    outputs = [
        y1, y2, g1, g2, small, small, shared_grad, value_grad, out_grad, small, small, up_grad,
        up_bias, down_grad, small,
    ]
    return pl.pallas_call(
        finish_kernel,
        out_shape=[o[0] for o in outputs],
        in_specs=[VMEM] * 10,
        out_specs=[o[1] for o in outputs],
        scratch_shapes=[pltpu.SemaphoreType.DMA((9,))],
        name="finish",
    )(*arguments)


def plane_plan(
    n_seq,
    n_sub,
    first_half,
    second_half,
    grad_first,
    grad_second,
    attend_gain,
    attend_shift,
    query_key_weight,
    value_projection_weight,
    output_projection_weight,
    feed_gain,
    feed_shift,
    upper_projection_weight,
    upper_projection_bias,
    lower_projection_weight,
    lower_projection_bias,
    sort_order,
    sort_place,
):
    planes = n_seq // 2
    x1, x2, g1, g2 = (a[0] for a in (first_half, second_half, grad_first, grad_second))
    wqk, wv, wo = query_key_weight[0], value_projection_weight[0], output_projection_weight[0]
    wup, wdown = upper_projection_weight[0], lower_projection_weight[0]
    results = layer_stage(
        (
            sort_order[0, :, 0], sort_place[0, :, 0], attend_gain, attend_shift, feed_gain, feed_shift,
            upper_projection_bias, lower_projection_bias, x2, wqk, wv, wo, wup, wdown, g2, x1, g1,
        ),
        1,
        planes,
    )
    return finish_stage(results)


def on_device(n_seq, n_sub, *arguments):
    sequences, rows, width = arguments[0].shape
    rounds = arguments[-1].shape[1]
    fits = (
        sequences == 1
        and rows == 2 * BLOCK
        and rounds == n_sub
        and HEADS == n_seq
        and width == HEADS * HEAD_DIM
    )
    if fits:
        return plane_plan(n_seq, n_sub, *arguments)
    return general_plan(*arguments)


def solution(mesh):
    return jax.shard_map(
        functools.partial(on_device, mesh.shape["seq"], mesh.shape["sub"]),
        mesh=mesh,
        in_specs=(
            P(None, ("seq", "sub"), None),
            P(None, ("seq", "sub"), None),
            P(None, ("seq", "sub"), None),
            P(None, ("seq", "sub"), None),
            P(None, ("seq", "sub")),
            P(None, ("seq", "sub")),
            P(None, ("seq", "sub"), None),
            P(None, ("seq", "sub"), None),
            P(None, ("seq", "sub"), None),
            P(None, ("seq", "sub")),
            P(None, ("seq", "sub")),
            P(None, ("seq", "sub"), None),
            P(None, ("seq", "sub")),
            P(None, ("seq", "sub"), None),
            P(None, ("seq", "sub")),
            P(None, None, None, ("seq", "sub")),
            P(None, None, None, ("seq", "sub")),
        ),
        out_specs=(
            P(None, ("seq", "sub"), None),
            P(None, ("seq", "sub"), None),
            P(None, ("seq", "sub"), None),
            P(None, ("seq", "sub"), None),
            P(None, ("seq", "sub")),
            P(None, ("seq", "sub")),
            P(None, ("seq", "sub"), None),
            P(None, ("seq", "sub"), None),
            P(None, ("seq", "sub"), None),
            P(None, ("seq", "sub")),
            P(None, ("seq", "sub")),
            P(None, ("seq", "sub"), None),
            P(None, ("seq", "sub")),
            P(None, ("seq", "sub"), None),
            P(None, ("seq", "sub")),
        ),
        check_vma=False,
    )
```
